32 devices in a mesh: theta: 16 (over z, x, core), gz: 2 (over y).
Axes of the slice: x: 2, y: 2, z: 4, core: 2. Of those that a mesh axis runs over, the one named last changes fastest.
Arguments:
- velocity: float32 [3, 256, 16, 512], P(None, 'theta', 'gz'), may hold values from -2 to 3.5
- radial_op: float32 [512, 544], replicated, may hold values from -0.25 to 0.25
- azimuth_stencil: float32 [21], replicated, may hold values from -1.25 to 1.25
- viscous_factor: float32 [1], replicated, may hold values from 1000000 to 10000000
Outputs:
- new_velocity: float32 [3, 256, 16, 512], P(None, 'theta', 'gz')
- nonlinear: float32 [3, 256, 16, 512], P(None, 'theta', 'gz')
The draws below stay inside these ranges and needn't reach their ends.
All inputs are finite; a program needn't handle non-finite values.
Results may differ from the reference program's by a relative error of at most 0.000098.
Values sent between devices are 32-bit elements; how exact they have to be, the bound alone decides.
No kernel may reach another device: no remote copies, remote signals or barrier semaphores. Data moves between devices by JAX's collectives and lax.ppermute only.
A program may use at most 64 MiB of HBM per device.

```python
import math
import jax
import jax.numpy as jnp
from jax import lax

NR = 512
RT = 32
AZ_REACH = 10
NT = 256
NZ = 16


def draw_velocity(key, part):
    radius = (jnp.arange(NR).astype(jnp.float32) + 0.5) / NR
    profile = 1.5 * (1.0 - radius * radius)
    fluctuation = 0.5 * jax.random.truncated_normal(key, -4.0, 4.0, (3, NT, NZ, NR), jnp.float32)
    mean_flow = jnp.stack([jnp.zeros_like(profile), jnp.zeros_like(profile), profile])
    return fluctuation + mean_flow[:, None, None, :]


def scatter_about(rng, shape, spread, reach, held_as=jnp.bfloat16):
    return jnp.clip(spread * jax.random.normal(rng, shape, jnp.float32), -reach, reach).astype(held_as)


def setup_inputs(seed: int = 0) -> dict:
    streams_of = jax.random.split(jax.random.key(seed), 5)
    return {
        "velocity": draw_velocity(jax.random.fold_in(streams_of[4], 71), 0),
        "radial_op": scatter_about(streams_of[1], (NR, NR + RT), (NR + RT) ** -0.5, 0.25, jnp.float32),
        "azimuth_stencil": scatter_about(streams_of[2], (2 * AZ_REACH + 1,), (2 * AZ_REACH + 1) ** -0.5, 1.25, jnp.float32),
        "viscous_factor": jnp.clip(jnp.exp(jax.random.uniform(streams_of[3], (1,), jnp.float32, math.log(1000000), math.log(10000000))), 1000000, 10000000),
    }


AXIAL_WEIGHTS = (0.75, -0.15, 1.0 / 60.0)
STEP_WEIGHT = 0.2
MIRROR_SIGNS = (-1.0, -1.0, 1.0)


def reference(velocity, radial_op, azimuth_stencil, viscous_factor):
    highest = lax.Precision.HIGHEST
    radius = jnp.arange(NR).astype(jnp.float32) + 0.5
    inverse_r = 1.0 / radius
    sign_flip = jnp.array(MIRROR_SIGNS, jnp.float32).reshape(3, 1, 1, 1)
    mirror = sign_flip * jnp.roll(velocity[:, :, :, :RT], -(NT // 2), axis=1)
    radial_grad = jnp.einsum("ctzj,ij->ctzi", velocity, radial_op[:, :NR], precision=highest)
    radial_grad = radial_grad + jnp.einsum("ctzj,ij->ctzi", mirror, radial_op[:, NR:], precision=highest)
    theta_grad = jnp.zeros_like(velocity)
    for shift_by in range(-AZ_REACH, AZ_REACH + 1):
        theta_grad = theta_grad + azimuth_stencil[shift_by + AZ_REACH] * jnp.roll(velocity, -shift_by, axis=1)
    axial_grad = jnp.zeros_like(velocity)
    for position, weight in enumerate(AXIAL_WEIGHTS):
        shift_by = position + 1
        axial_grad = axial_grad + weight * (jnp.roll(velocity, -shift_by, axis=2) - jnp.roll(velocity, shift_by, axis=2))
    radial_vel = velocity[0]
    azimuth_vel = velocity[1]
    axial_vel = velocity[2]
    convective = radial_vel[None] * radial_grad + (azimuth_vel * inverse_r)[None] * theta_grad + axial_vel[None] * axial_grad
    metric = jnp.stack([-azimuth_vel * azimuth_vel * inverse_r, radial_vel * azimuth_vel * inverse_r, jnp.zeros_like(axial_vel)])
    nonlinear = convective + metric
    right_side = velocity - STEP_WEIGHT * nonlinear
    implicit_coef = viscous_factor[0] * inverse_r * inverse_r
    spectrum = jnp.fft.rfft(right_side, axis=1)
    wavenumber = jnp.arange(NT // 2 + 1).astype(jnp.float32)
    half_sine = jnp.sin(jnp.pi * wavenumber / NT)
    eigenvalue = 1.0 + 4.0 * implicit_coef[None, :] * (half_sine * half_sine)[:, None]
    new_velocity = jnp.fft.irfft(spectrum / eigenvalue[None, :, None, :], n=NT, axis=1).astype(jnp.float32)
    return (new_velocity, nonlinear)
```

```python
import functools

import jax
import jax.numpy as jnp
from jax import lax
from jax.experimental import pallas as pl
from jax.experimental.pallas import tpu as pltpu
from jax.sharding import PartitionSpec as P

AXIAL_WEIGHTS = (0.75, -0.15, 1.0 / 60.0)
AXIAL_REACH = len(AXIAL_WEIGHTS)
STEP_WEIGHT = 0.2
MIRROR_SIGNS = (-1.0, -1.0, 1.0)
LANES = 128
UNROLL = 16

VMEM = pl.BlockSpec(memory_space=pltpu.VMEM)
SMEM = pl.BlockSpec(memory_space=pltpu.SMEM)


def params(block_bytes, blocks):
    return pltpu.CompilerParams(vmem_limit_bytes=(6 << 20) + blocks * block_bytes)


def each(count, body):
    if count <= UNROLL:
        for i in range(count):
            body(i)
    else:
        pl.loop(0, count)(body)


def swap(block, axis, bit):
    size = lax.axis_size(axis)
    return lax.ppermute(block, axis, [(i, i ^ bit) for i in range(size)])


def swap_across(block, axis):
    size = lax.axis_size(axis)
    route = []
    for odd in range(1, size, 2):
        route += [(odd, (odd + 1) % size), ((odd + 1) % size, odd)]
    return lax.ppermute(block, axis, route)


def split(x):
    high = x.astype(jnp.bfloat16)
    return high, (x - high.astype(jnp.float32)).astype(jnp.bfloat16)


def product(left, right):
    dot = functools.partial(jnp.dot, preferred_element_type=jnp.float32)
    return dot(left[0], right[0]) + (dot(left[0], right[1]) + dot(left[1], right[0]))


def pack_planes_kernel(v_ref, y_ref):
    carriers = y_ref.shape[1]
    riders = v_ref.shape[1] - carriers
    lo, hi = AXIAL_REACH, v_ref.shape[2] - AXIAL_REACH

    def carry(t):
        for c in range(3):
            y_ref[c, t] = v_ref[c, t]

    def ride(j):
        for c in range(3):
            t = carriers + j
            y_ref[c, 3 * j, lo:hi] = v_ref[c, t, 0:2]
            y_ref[c, 3 * j + 1, lo : lo + 1] = v_ref[c, t, 2:3]
            y_ref[c, 3 * j + 1, lo + 1 : hi] = v_ref[c, t, hi : hi + 1]
            y_ref[c, 3 * j + 2, lo:hi] = v_ref[c, t, hi + 1 :]

    each(carriers, carry)
    each(riders, ride)


def pack_planes(v):
    comps, points, planes, radial = v.shape
    return pl.pallas_call(
        pack_planes_kernel,
        name="pack_planes",
        out_shape=jax.ShapeDtypeStruct((comps, points - points // 4, planes, radial), v.dtype),
        in_specs=[VMEM],
        out_specs=VMEM,
        compiler_params=params(v.size * 4, 2),
    )(v)


def pack_sides_kernel(me_ref, v_ref, core_ref, chip_ref, mirror_ref):
    points = v_ref.shape[1]
    reach = core_ref.shape[1]
    even = me_ref[0] % 2 == 0
    to_core = jnp.where(even, points - reach, 0)
    to_chip = jnp.where(even, 0, points - reach)
    for c in range(3):
        for h in range(reach):
            core_ref[c, h] = v_ref[c, to_core + h]
            chip_ref[c, h] = v_ref[c, to_chip + h]
    tiles = mirror_ref.shape[1]
    width = LANES // (points // tiles)
    lane = lax.broadcasted_iota(jnp.int32, mirror_ref.shape[2:], 1)

    def put(p):
        for c in range(3):
            tile = v_ref[c, p, :, :LANES]
            for q in range(1, points // tiles):
                part = pltpu.roll(v_ref[c, q * tiles + p, :, :LANES], q * width, 1)
                tile = jnp.where(lane < q * width, tile, part)
            mirror_ref[c, p] = tile

    each(tiles, put)


def pack_sides(me, v, reach, width):
    comps, points, planes, radial = v.shape
    tiles = points // (LANES // width)
    side = jax.ShapeDtypeStruct((comps, reach, planes, radial), v.dtype)
    return pl.pallas_call(
        pack_sides_kernel,
        name="pack_sides",
        out_shape=(side, side, jax.ShapeDtypeStruct((comps, tiles, planes, LANES), v.dtype)),
        in_specs=[SMEM, VMEM],
        out_specs=(VMEM, VMEM, VMEM),
        compiler_params=params(v.size * 4, 3),
    )(me, v)


def inverse_radius(radial):
    return 1.0 / (lax.broadcasted_iota(jnp.int32, (1, radial), 1).astype(jnp.float32) + 0.5)


def axial_weights(planes, inside):
    row = lax.broadcasted_iota(jnp.int32, (planes, 1), 0)
    weights = []
    for m, w in enumerate(AXIAL_WEIGHTS, 1):
        for shift, own, sign in ((m, row < planes - m, 1.0), (planes - m, row >= m, -1.0)):
            keep = own if inside else jnp.logical_not(own)
            weights.append((shift, jnp.where(keep, sign * w, 0.0)))
    return weights


def axial_part(tile, weights):
    planes = tile.shape[0]
    total = None
    for shift, weight in weights:
        term = weight * pltpu.roll(tile, planes - shift, 0)
        total = term if total is None else total + term
    return total


def inner_kernel(stencil_ref, v_ref, op_ref, n_ref, grad_ref):
    comps, points, planes, radial = v_ref.shape
    reach = (stencil_ref.shape[0] - 1) // 2
    rows = points * planes
    right = split(op_ref[:radial])
    for c in range(comps):
        grad_ref[c * rows : (c + 1) * rows] = product(split(v_ref[c].reshape(rows, radial)), right)
    inv_r = inverse_radius(radial)
    weights = axial_weights(planes, True)

    def point(t, lows, highs):
        a, b, e = v_ref[0, t], v_ref[1, t], v_ref[2, t]
        b_inv = b * inv_r
        for c in range(comps):
            around = None
            for m in range(-lows, highs + 1):
                term = stencil_ref[m + reach] * v_ref[c, t + m]
                around = term if around is None else around + term
            start = c * rows + t * planes
            grad = grad_ref[pl.ds(pl.multiple_of(start, planes), planes)]
            n = a * grad + b_inv * around + e * axial_part(v_ref[c, t], weights)
            if c == 0:
                n = n - b_inv * b
            elif c == 1:
                n = n + a * b_inv
            n_ref[c, t] = n

    for t in range(reach):
        point(t, t, min(reach, points - 1 - t))
    each(points - 2 * reach, lambda i: point(i + reach, reach, reach)) if points >= 2 * reach else None
    for t in range(max(reach, points - reach), points):
        point(t, min(reach, t), points - 1 - t)


def inner_terms(stencil, v, op):
    return pl.pallas_call(
        inner_kernel,
        name="inner_terms",
        out_shape=jax.ShapeDtypeStruct(v.shape, v.dtype),
        in_specs=[SMEM, VMEM, VMEM],
        out_specs=VMEM,
        scratch_shapes=[pltpu.VMEM((v.size // v.shape[3], v.shape[3]), jnp.float32)],
        compiler_params=params(v.size * 4, 6),
        cost_estimate=pl.CostEstimate(flops=6 * v.size * v.shape[3], bytes_accessed=16 * v.size, transcendentals=0),
    )(stencil, v, op)


def sides_kernel(me_ref, stencil_ref, v_ref, op_ref, core_ref, chip_ref, mirror_ref, n_in_ref, n_ref, grad_ref):
    comps, points, planes, radial = v_ref.shape
    reach = core_ref.shape[1]
    tiles = mirror_ref.shape[1]
    count = points // tiles
    width = LANES // count
    rows = tiles * planes
    right = split(jnp.concatenate([op_ref[radial:]] * count, axis=0))
    lane = lax.broadcasted_iota(jnp.int32, (rows, LANES), 1)
    for c in range(comps):
        high, low = split(MIRROR_SIGNS[c] * mirror_ref[c].reshape(rows, LANES))
        zero = jnp.zeros_like(high)
        parts = [
            [jnp.where((lane >= q * width) & (lane < (q + 1) * width), x, zero) for q in range(count)]
            for x in (high, low)
        ]
        left = [jnp.concatenate(x, axis=0) for x in parts]
        grad_ref[c * points * planes : (c + 1) * points * planes] = product(left, right)
    inv_r = inverse_radius(radial)

    def finish(t, taps):
        a = v_ref[0, t]
        b_inv = v_ref[1, t] * inv_r
        for c in range(comps):
            start = (c * points + t) * planes
            n = n_in_ref[c, t] + a * grad_ref[pl.ds(pl.multiple_of(start, planes), planes)]
            around = None
            for ref, h, k in taps:
                term = stencil_ref[k] * ref[c, h]
                around = term if around is None else around + term
            if around is not None:
                n = n + b_inv * around
            n_ref[c, t] = n

    def all_points(before, after):
        def taps(t):
            found = [(before, h, h - t) for h in range(t, reach)]
            found += [(after, h, points + h - t + reach) for h in range(min(reach, reach - points + t + 1))]
            return found

        for t in range(reach):
            finish(t, taps(t))
        if points > 2 * reach:
            each(points - 2 * reach, lambda i: finish(i + reach, []))
        for t in range(max(reach, points - reach), points):
            finish(t, taps(t))

    even = me_ref[0] % 2 == 0
    pl.when(even)(lambda: all_points(chip_ref, core_ref))
    pl.when(jnp.logical_not(even))(lambda: all_points(core_ref, chip_ref))


def sides_terms(me, stencil, v, op, core, chip, mirror, n):
    return pl.pallas_call(
        sides_kernel,
        name="sides_terms",
        out_shape=jax.ShapeDtypeStruct(v.shape, v.dtype),
        in_specs=[SMEM, SMEM, VMEM, VMEM, VMEM, VMEM, VMEM, VMEM],
        out_specs=VMEM,
        scratch_shapes=[pltpu.VMEM((v.size // v.shape[3], v.shape[3]), jnp.float32)],
        input_output_aliases={7: 0},
        compiler_params=params(v.size * 4, 8),
        cost_estimate=pl.CostEstimate(flops=2 * v.size * LANES, bytes_accessed=16 * v.size, transcendentals=0),
    )(me, stencil, v, op, core, chip, mirror, n)


def planes_kernel(v_ref, y_ref, power_ref, n_in_ref, n_ref, ends_ref, tile_ref):
    comps, points, planes, radial = v_ref.shape
    carriers = y_ref.shape[1]
    lo, hi = AXIAL_REACH, planes - AXIAL_REACH
    weights = axial_weights(planes, False)
    decay = power_ref[1:2]
    ends_ref[...] = jnp.zeros_like(ends_ref)

    def finish(t, c, tile):
        n = n_in_ref[c, t] + v_ref[2, t] * axial_part(tile, weights)
        n_ref[c, t] = n
        right_side = v_ref[c, t] - STEP_WEIGHT * n
        ends_ref[0, c] = decay * ends_ref[0, c] + right_side
        ends_ref[1, c] = ends_ref[1, c] + power_ref[pl.ds(t, 1)] * right_side

    def carried(t):
        for c in range(comps):
            finish(t, c, y_ref[c, t])

    def ridden(j):
        for c in range(comps):
            tile_ref[c, 0:2] = y_ref[c, 3 * j, lo:hi]
            tile_ref[c, 2:3] = y_ref[c, 3 * j + 1, lo : lo + 1]
            tile_ref[c, lo:hi] = jnp.zeros_like(tile_ref[c, lo:hi])
            tile_ref[c, hi : hi + 1] = y_ref[c, 3 * j + 1, lo + 1 : hi]
            tile_ref[c, hi + 1 :] = y_ref[c, 3 * j + 2, lo:hi]
            finish(carriers + j, c, tile_ref[c])

    each(carriers, carried)
    each(points - carriers, ridden)


def planes_terms(v, y, power, n):
    comps, points, planes, radial = v.shape
    return pl.pallas_call(
        planes_kernel,
        name="planes_terms",
        out_shape=(
            jax.ShapeDtypeStruct(v.shape, v.dtype),
            jax.ShapeDtypeStruct((2, comps, planes, radial), v.dtype),
        ),
        in_specs=[VMEM] * 4,
        out_specs=(VMEM, VMEM),
        scratch_shapes=[pltpu.VMEM((comps, planes, radial), jnp.float32)],
        input_output_aliases={3: 0},
        compiler_params=params(v.size * 4, 6),
        cost_estimate=pl.CostEstimate(flops=20 * v.size, bytes_accessed=16 * v.size, transcendentals=0),
    )(v, y, power, n)


def powers(viscous_factor, points, sectors, radial):
    radius = jnp.arange(radial).astype(jnp.float32) + 0.5
    half = 0.5 * radius * lax.rsqrt(viscous_factor[0])
    root = jnp.sqrt(1.0 + half * half)
    loss = 2.0 * half * (root - half)
    rows = [jnp.ones_like(loss)]
    for _ in range(points):
        rows.append(rows[-1] * (1.0 - loss))
    total, have = loss, 1
    left, result = points * sectors, None
    while left:
        if left & 1:
            result = total if result is None else result + total - result * total
        total = total * (2.0 - total)
        left >>= 1
    return jnp.stack(rows + [half / root, 1.0 / result])


def sweep_kernel(v_ref, n_ref, power_ref, s_ref):
    comps, points, planes, radial = v_ref.shape
    decay = power_ref[1:2]
    height = power_ref[points + 1 : points + 2]
    for c in range(comps):
        s_ref[c, 0] = height * (v_ref[c, 0] - STEP_WEIGHT * n_ref[c, 0])

        def forward(i):
            t = i + 1
            s_ref[c, t] = decay * s_ref[c, t - 1] + height * (v_ref[c, t] - STEP_WEIGHT * n_ref[c, t])

        each(points - 1, forward)

    def backward(i, carry):
        t = points - 1 - i
        after = []
        for c in range(comps):
            s_ref[c, t] = s_ref[c, t] + carry[c]
            after.append(decay * (carry[c] + height * (v_ref[c, t] - STEP_WEIGHT * n_ref[c, t])))
        return tuple(after)

    start = (jnp.zeros((planes, radial), jnp.float32),) * comps
    lax.fori_loop(0, points, backward, start, unroll=points <= UNROLL)


def sweep(v, n, power):
    return pl.pallas_call(
        sweep_kernel,
        name="sweep",
        out_shape=jax.ShapeDtypeStruct(v.shape, v.dtype),
        in_specs=[VMEM] * 3,
        out_specs=VMEM,
        compiler_params=params(v.size * 4, 4),
        cost_estimate=pl.CostEstimate(flops=10 * v.size, bytes_accessed=12 * v.size, transcendentals=0),
    )(v, n, power)


def close_kernel(me_ref, s_ref, power_ref, ends_ref, x_ref):
    comps, points, planes, radial = s_ref.shape
    sectors = ends_ref.shape[0]
    me = me_ref[0]
    hop = power_ref[points : points + 1]
    scale = power_ref[points + 1 : points + 2] * power_ref[points + 2 : points + 3]
    for c in range(comps):
        before = jnp.zeros((planes, radial), jnp.float32)
        after = before
        for j in range(sectors, 0, -1):
            before = hop * before + ends_ref[lax.rem(me + sectors - j, sectors), 0, c]
            after = hop * after + ends_ref[lax.rem(me + j, sectors), 1, c]
        before = scale * before
        after = scale * after

        def point(t):
            x_ref[c, t] = s_ref[c, t] + power_ref[pl.ds(t + 1, 1)] * before + power_ref[pl.ds(points - t, 1)] * after

        each(points, point)


def close(me, s, power, ends):
    return pl.pallas_call(
        close_kernel,
        name="close",
        out_shape=jax.ShapeDtypeStruct(s.shape, s.dtype),
        in_specs=[SMEM, VMEM, VMEM, VMEM],
        out_specs=VMEM,
        compiler_params=params(s.size * 4, 5),
    )(me, s, power, ends)


def local(velocity, radial_op, azimuth_stencil, viscous_factor):
    sectors = lax.axis_size("theta")
    comps, points, planes, radial = velocity.shape
    reach = (azimuth_stencil.shape[0] - 1) // 2
    width = radial_op.shape[1] - radial
    me = lax.axis_index("theta").astype(jnp.int32).reshape(1)
    op = radial_op.T

    planes_out = pack_planes(velocity)
    planes_in = swap(planes_out, "gz", 1)
    core_out, chip_out, mirror_out = pack_sides(me, velocity, reach, width)
    chip_in = swap_across(chip_out, "theta")
    core_in = swap(core_out, "theta", 1)
    mirror_in = swap(mirror_out, "theta", sectors // 2)
    power = powers(viscous_factor, points, sectors, radial)
    n = inner_terms(azimuth_stencil, velocity, op)
    n = sides_terms(me, azimuth_stencil, velocity, op, core_in, chip_in, mirror_in, n)
    nonlinear, ends = planes_terms(velocity, planes_in, power, n)
    everyone = lax.all_gather(ends, "theta")
    s = sweep(velocity, nonlinear, power)
    new_velocity = close(me, s, power, everyone)
    return (new_velocity, nonlinear)


def solution(mesh):
    in_specs = (P(None, "theta", "gz", None), P(), P(), P())
    out_specs = (P(None, "theta", "gz", None), P(None, "theta", "gz", None))
    return jax.shard_map(local, mesh=mesh, in_specs=in_specs, out_specs=out_specs, check_vma=False)
```

```python
import functools

import jax
import jax.numpy as jnp
from jax import lax
from jax.experimental import pallas as pl
from jax.experimental.pallas import tpu as pltpu
from jax.sharding import PartitionSpec as P

AXIAL_WEIGHTS = (0.75, -0.15, 1.0 / 60.0)
AXIAL_REACH = len(AXIAL_WEIGHTS)
STEP_WEIGHT = 0.2
MIRROR_SIGNS = (-1.0, -1.0, 1.0)
LANES = 128
UNROLL = 16

VMEM = pl.BlockSpec(memory_space=pltpu.VMEM)
SMEM = pl.BlockSpec(memory_space=pltpu.SMEM)


def params(block_bytes, blocks):
    return pltpu.CompilerParams(vmem_limit_bytes=(6 << 20) + blocks * block_bytes)


def each(count, body):
    if count <= UNROLL:
        for i in range(count):
            body(i)
    else:
        pl.loop(0, count)(body)


def swap(block, axis, bit):
    size = lax.axis_size(axis)
    return lax.ppermute(block, axis, [(i, i ^ bit) for i in range(size)])


def swap_across(block, axis):
    size = lax.axis_size(axis)
    route = []
    for odd in range(1, size, 2):
        route += [(odd, (odd + 1) % size), ((odd + 1) % size, odd)]
    return lax.ppermute(block, axis, route)


def split(x):
    high = x.astype(jnp.bfloat16)
    return high, (x - high.astype(jnp.float32)).astype(jnp.bfloat16)


def product(left, right):
    dot = functools.partial(jnp.dot, preferred_element_type=jnp.float32)
    return dot(left[0], right[0]) + (dot(left[0], right[1]) + dot(left[1], right[0]))


def pack_planes_kernel(v_ref, y_ref):
    carriers = y_ref.shape[1]
    riders = v_ref.shape[1] - carriers
    lo, hi = AXIAL_REACH, v_ref.shape[2] - AXIAL_REACH

    def carry(t):
        for c in range(3):
            y_ref[c, t] = v_ref[c, t]

    def ride(j):
        for c in range(3):
            t = carriers + j
            y_ref[c, 3 * j, lo:hi] = v_ref[c, t, 0:2]
            y_ref[c, 3 * j + 1, lo : lo + 1] = v_ref[c, t, 2:3]
            y_ref[c, 3 * j + 1, lo + 1 : hi] = v_ref[c, t, hi : hi + 1]
            y_ref[c, 3 * j + 2, lo:hi] = v_ref[c, t, hi + 1 :]

    each(carriers, carry)
    each(riders, ride)


def pack_planes(v):
    comps, points, planes, radial = v.shape
    return pl.pallas_call(
        pack_planes_kernel,
        name="pack_planes",
        out_shape=jax.ShapeDtypeStruct((comps, points - points // 4, planes, radial), v.dtype),
        in_specs=[VMEM],
        out_specs=VMEM,
        compiler_params=params(v.size * 4, 2),
    )(v)


def pack_sides_kernel(me_ref, v_ref, core_ref, chip_ref, mirror_ref):
    points = v_ref.shape[1]
    reach = core_ref.shape[1]
    even = me_ref[0] % 2 == 0
    to_core = jnp.where(even, points - reach, 0)
    to_chip = jnp.where(even, 0, points - reach)
    for c in range(3):
        for h in range(reach):
            core_ref[c, h] = v_ref[c, to_core + h]
            chip_ref[c, h] = v_ref[c, to_chip + h]
    tiles = mirror_ref.shape[1]
    width = LANES // (points // tiles)
    lane = lax.broadcasted_iota(jnp.int32, mirror_ref.shape[2:], 1)

    def put(p):
        for c in range(3):
            tile = v_ref[c, p, :, :LANES]
            for q in range(1, points // tiles):
                part = pltpu.roll(v_ref[c, q * tiles + p, :, :LANES], q * width, 1)
                tile = jnp.where(lane < q * width, tile, part)
            mirror_ref[c, p] = tile

    each(tiles, put)


def pack_sides(me, v, reach, width):
    comps, points, planes, radial = v.shape
    tiles = points // (LANES // width)
    side = jax.ShapeDtypeStruct((comps, reach, planes, radial), v.dtype)
    return pl.pallas_call(
        pack_sides_kernel,
        name="pack_sides",
        out_shape=(side, side, jax.ShapeDtypeStruct((comps, tiles, planes, LANES), v.dtype)),
        in_specs=[SMEM, VMEM],
        out_specs=(VMEM, VMEM, VMEM),
        compiler_params=params(v.size * 4, 3),
    )(me, v)


def inverse_radius(radial):
    return 1.0 / (lax.broadcasted_iota(jnp.int32, (1, radial), 1).astype(jnp.float32) + 0.5)


def axial_weights(planes, inside):
    row = lax.broadcasted_iota(jnp.int32, (planes, 1), 0)
    weights = []
    for m, w in enumerate(AXIAL_WEIGHTS, 1):
        for shift, own, sign in ((m, row < planes - m, 1.0), (planes - m, row >= m, -1.0)):
            keep = own if inside else jnp.logical_not(own)
            weights.append((shift, jnp.where(keep, sign * w, 0.0)))
    return weights


def axial_part(tile, weights):
    planes = tile.shape[0]
    total = None
    for shift, weight in weights:
        term = weight * pltpu.roll(tile, planes - shift, 0)
        total = term if total is None else total + term
    return total


def inner_kernel(stencil_ref, v_ref, op_ref, n_ref, grad_ref):
    comps, points, planes, radial = v_ref.shape
    reach = (stencil_ref.shape[0] - 1) // 2
    rows = points * planes
    right = split(op_ref[:radial])
    for c in range(comps):
        grad_ref[c * rows : (c + 1) * rows] = product(split(v_ref[c].reshape(rows, radial)), right)
    inv_r = inverse_radius(radial)
    weights = axial_weights(planes, True)

    def point(t, lows, highs):
        a, b, e = v_ref[0, t], v_ref[1, t], v_ref[2, t]
        b_inv = b * inv_r
        for c in range(comps):
            around = None
            for m in range(-lows, highs + 1):
                term = stencil_ref[m + reach] * v_ref[c, t + m]
                around = term if around is None else around + term
            start = c * rows + t * planes
            grad = grad_ref[pl.ds(pl.multiple_of(start, planes), planes)]
            n = a * grad + b_inv * around + e * axial_part(v_ref[c, t], weights)
            if c == 0:
                n = n - b_inv * b
            elif c == 1:
                n = n + a * b_inv
            n_ref[c, t] = n

    for t in range(reach):
        point(t, t, min(reach, points - 1 - t))
    each(points - 2 * reach, lambda i: point(i + reach, reach, reach)) if points >= 2 * reach else None
    for t in range(max(reach, points - reach), points):
        point(t, min(reach, t), points - 1 - t)


def inner_terms(stencil, v, op):
    return pl.pallas_call(
        inner_kernel,
        name="inner_terms",
        out_shape=jax.ShapeDtypeStruct(v.shape, v.dtype),
        in_specs=[SMEM, VMEM, VMEM],
        out_specs=VMEM,
        scratch_shapes=[pltpu.VMEM((v.size // v.shape[3], v.shape[3]), jnp.float32)],
        compiler_params=params(v.size * 4, 6),
        cost_estimate=pl.CostEstimate(flops=6 * v.size * v.shape[3], bytes_accessed=16 * v.size, transcendentals=0),
    )(stencil, v, op)


def sides_kernel(me_ref, stencil_ref, v_ref, op_ref, core_ref, chip_ref, mirror_ref, n_in_ref, n_ref, grad_ref):
    comps, points, planes, radial = v_ref.shape
    reach = core_ref.shape[1]
    tiles = mirror_ref.shape[1]
    count = points // tiles
    width = LANES // count
    rows = tiles * planes
    right = split(jnp.concatenate([op_ref[radial:]] * count, axis=0))
    lane = lax.broadcasted_iota(jnp.int32, (rows, LANES), 1)
    for c in range(comps):
        high, low = split(MIRROR_SIGNS[c] * mirror_ref[c].reshape(rows, LANES))
        zero = jnp.zeros_like(high)
        parts = [
            [jnp.where((lane >= q * width) & (lane < (q + 1) * width), x, zero) for q in range(count)]
            for x in (high, low)
        ]
        left = [jnp.concatenate(x, axis=0) for x in parts]
        grad_ref[c * points * planes : (c + 1) * points * planes] = product(left, right)
    inv_r = inverse_radius(radial)

    def finish(t, taps):
        a = v_ref[0, t]
        b_inv = v_ref[1, t] * inv_r
        for c in range(comps):
            start = (c * points + t) * planes
            n = n_in_ref[c, t] + a * grad_ref[pl.ds(pl.multiple_of(start, planes), planes)]
            around = None
            for ref, h, k in taps:
                term = stencil_ref[k] * ref[c, h]
                around = term if around is None else around + term
            if around is not None:
                n = n + b_inv * around
            n_ref[c, t] = n

    def all_points(before, after):
        def taps(t):
            found = [(before, h, h - t) for h in range(t, reach)]
            found += [(after, h, points + h - t + reach) for h in range(min(reach, reach - points + t + 1))]
            return found

        for t in range(reach):
            finish(t, taps(t))
        if points > 2 * reach:
            each(points - 2 * reach, lambda i: finish(i + reach, []))
        for t in range(max(reach, points - reach), points):
            finish(t, taps(t))

    even = me_ref[0] % 2 == 0
    pl.when(even)(lambda: all_points(chip_ref, core_ref))
    pl.when(jnp.logical_not(even))(lambda: all_points(core_ref, chip_ref))


def sides_terms(me, stencil, v, op, core, chip, mirror, n):
    return pl.pallas_call(
        sides_kernel,
        name="sides_terms",
        out_shape=jax.ShapeDtypeStruct(v.shape, v.dtype),
        in_specs=[SMEM, SMEM, VMEM, VMEM, VMEM, VMEM, VMEM, VMEM],
        out_specs=VMEM,
        scratch_shapes=[pltpu.VMEM((v.size // v.shape[3], v.shape[3]), jnp.float32)],
        input_output_aliases={7: 0},
        compiler_params=params(v.size * 4, 8),
        cost_estimate=pl.CostEstimate(flops=2 * v.size * LANES, bytes_accessed=16 * v.size, transcendentals=0),
    )(me, stencil, v, op, core, chip, mirror, n)


def share(sectors, shape):
    comps, _, planes, radial = shape
    return -(-comps * planes * (radial // LANES) // sectors)


def dealt(sectors, shape):
    comps, _, planes, radial = shape
    per = share(sectors, shape)
    for q in range(comps * planes * (radial // LANES)):
        tile, c = divmod(q, comps)
        z, k = divmod(tile, radial // LANES)
        yield q // per, q % per, (c, slice(z, z + 1), slice(k * LANES, (k + 1) * LANES))


def planes_kernel(v_ref, y_ref, power_ref, n_in_ref, n_ref, out_ref, tile_ref, ends_ref):
    comps, points, planes, radial = v_ref.shape
    carriers = y_ref.shape[1]
    lo, hi = AXIAL_REACH, planes - AXIAL_REACH
    weights = axial_weights(planes, False)
    decay = power_ref[1:2]
    ends_ref[...] = jnp.zeros_like(ends_ref)

    def finish(t, c, tile):
        n = n_in_ref[c, t] + v_ref[2, t] * axial_part(tile, weights)
        n_ref[c, t] = n
        right_side = v_ref[c, t] - STEP_WEIGHT * n
        ends_ref[0, c] = decay * ends_ref[0, c] + right_side
        ends_ref[1, c] = ends_ref[1, c] + power_ref[pl.ds(t, 1)] * right_side

    def carried(t):
        for c in range(comps):
            finish(t, c, y_ref[c, t])

    def ridden(j):
        for c in range(comps):
            tile_ref[c, 0:2] = y_ref[c, 3 * j, lo:hi]
            tile_ref[c, 2:3] = y_ref[c, 3 * j + 1, lo : lo + 1]
            tile_ref[c, lo:hi] = jnp.zeros_like(tile_ref[c, lo:hi])
            tile_ref[c, hi : hi + 1] = y_ref[c, 3 * j + 1, lo + 1 : hi]
            tile_ref[c, hi + 1 :] = y_ref[c, 3 * j + 2, lo:hi]
            finish(carriers + j, c, tile_ref[c])

    each(carriers, carried)
    each(points - carriers, ridden)
    for j, row, index in dealt(out_ref.shape[0], v_ref.shape):
        for side in range(2):
            out_ref[j, side, row : row + 1] = ends_ref[(side,) + index]


def planes_terms(v, y, power, n, sectors):
    comps, points, planes, radial = v.shape
    return pl.pallas_call(
        planes_kernel,
        name="planes_terms",
        out_shape=(
            jax.ShapeDtypeStruct(v.shape, v.dtype),
            jax.ShapeDtypeStruct((sectors, 2, share(sectors, v.shape), LANES), v.dtype),
        ),
        in_specs=[VMEM] * 4,
        out_specs=(VMEM, VMEM),
        scratch_shapes=[
            pltpu.VMEM((comps, planes, radial), jnp.float32),
            pltpu.VMEM((2, comps, planes, radial), jnp.float32),
        ],
        input_output_aliases={3: 0},
        compiler_params=params(v.size * 4, 6),
        cost_estimate=pl.CostEstimate(flops=20 * v.size, bytes_accessed=16 * v.size, transcendentals=0),
    )(v, y, power, n)


def powers(viscous_factor, points, sectors, radial):
    radius = jnp.arange(radial).astype(jnp.float32) + 0.5
    half = 0.5 * radius * lax.rsqrt(viscous_factor[0])
    root = jnp.sqrt(1.0 + half * half)
    loss = 2.0 * half * (root - half)
    rows = [jnp.ones_like(loss)]
    for _ in range(points):
        rows.append(rows[-1] * (1.0 - loss))
    total, have = loss, 1
    left, result = points * sectors, None
    while left:
        if left & 1:
            result = total if result is None else result + total - result * total
        total = total * (2.0 - total)
        left >>= 1
    return jnp.stack(rows + [half / root, 1.0 / result])


def sweep_kernel(v_ref, n_ref, power_ref, s_ref):
    comps, points, planes, radial = v_ref.shape
    decay = power_ref[1:2]
    height = power_ref[points + 1 : points + 2]
    for c in range(comps):
        s_ref[c, 0] = height * (v_ref[c, 0] - STEP_WEIGHT * n_ref[c, 0])

        def forward(i):
            t = i + 1
            s_ref[c, t] = decay * s_ref[c, t - 1] + height * (v_ref[c, t] - STEP_WEIGHT * n_ref[c, t])

        each(points - 1, forward)

    def backward(i, carry):
        t = points - 1 - i
        after = []
        for c in range(comps):
            s_ref[c, t] = s_ref[c, t] + carry[c]
            after.append(decay * (carry[c] + height * (v_ref[c, t] - STEP_WEIGHT * n_ref[c, t])))
        return tuple(after)

    start = (jnp.zeros((planes, radial), jnp.float32),) * comps
    lax.fori_loop(0, points, backward, start, unroll=points <= UNROLL)


def sweep(v, n, power):
    return pl.pallas_call(
        sweep_kernel,
        name="sweep",
        out_shape=jax.ShapeDtypeStruct(v.shape, v.dtype),
        in_specs=[VMEM] * 3,
        out_specs=VMEM,
        compiler_params=params(v.size * 4, 4),
        cost_estimate=pl.CostEstimate(flops=10 * v.size, bytes_accessed=12 * v.size, transcendentals=0),
    )(v, n, power)


def link_kernel(me_ref, power_ref, ends_ref, out_ref, hop_ref, height_ref, wrap_ref, *, points, comps):
    sectors, _, per, _ = ends_ref.shape
    tiles = power_ref.shape[1] // LANES
    for row in range(per):
        tile = lax.rem(lax.div(me_ref[0] * per + row, comps), tiles)
        lanes = pl.ds(pl.multiple_of(tile * LANES, LANES), LANES)
        for k, ref in enumerate((hop_ref, height_ref, wrap_ref)):
            ref[row : row + 1] = power_ref[points + k : points + k + 1, lanes]
    hop, height = hop_ref[...], height_ref[...]
    scale = height * wrap_ref[...]
    before = jnp.zeros((per, LANES), jnp.float32)
    after = before
    for j in range(sectors):
        before = hop * before + ends_ref[j, 0]
        after = hop * after + ends_ref[sectors - 1 - j, 1]
    before = scale * before
    after = scale * after
    for j in range(sectors):
        out_ref[j, 0] = before
        out_ref[sectors - 1 - j, 1] = after
        before = hop * before + height * ends_ref[j, 0]
        after = hop * after + height * ends_ref[sectors - 1 - j, 1]


def link(me, power, ends, points, comps):
    row = pltpu.VMEM(ends.shape[2:], jnp.float32)
    return pl.pallas_call(
        functools.partial(link_kernel, points=points, comps=comps),
        name="link",
        out_shape=jax.ShapeDtypeStruct(ends.shape, ends.dtype),
        in_specs=[SMEM, VMEM, VMEM],
        out_specs=VMEM,
        scratch_shapes=[row, row, row],
        compiler_params=params(ends.size * 4, 8),
    )(me, power, ends)


def close_kernel(s_ref, power_ref, entries_ref, x_ref, both_ref):
    comps, points, planes, radial = s_ref.shape
    for j, row, index in dealt(entries_ref.shape[0], s_ref.shape):
        for side in range(2):
            both_ref[(side,) + index] = entries_ref[j, side, row : row + 1]
    for c in range(comps):
        before, after = both_ref[0, c], both_ref[1, c]

        def point(t):
            x_ref[c, t] = s_ref[c, t] + power_ref[pl.ds(t + 1, 1)] * before + power_ref[pl.ds(points - t, 1)] * after

        each(points, point)


def close(s, power, entries):
    return pl.pallas_call(
        close_kernel,
        name="close",
        out_shape=jax.ShapeDtypeStruct(s.shape, s.dtype),
        in_specs=[VMEM, VMEM, VMEM],
        out_specs=VMEM,
        scratch_shapes=[pltpu.VMEM((2,) + s.shape[:1] + s.shape[2:], jnp.float32)],
        compiler_params=params(s.size * 4, 5),
    )(s, power, entries)


def local(velocity, radial_op, azimuth_stencil, viscous_factor):
    sectors = lax.axis_size("theta")
    comps, points, planes, radial = velocity.shape
    reach = (azimuth_stencil.shape[0] - 1) // 2
    width = radial_op.shape[1] - radial
    me = lax.axis_index("theta").astype(jnp.int32).reshape(1)
    op = radial_op.T

    planes_out = pack_planes(velocity)
    planes_in = swap(planes_out, "gz", 1)
    core_out, chip_out, mirror_out = pack_sides(me, velocity, reach, width)
    chip_in = swap_across(chip_out, "theta")
    core_in = swap(core_out, "theta", 1)
    mirror_in = swap(mirror_out, "theta", sectors // 2)
    power = powers(viscous_factor, points, sectors, radial)
    n = inner_terms(azimuth_stencil, velocity, op)
    n = sides_terms(me, azimuth_stencil, velocity, op, core_in, chip_in, mirror_in, n)
    nonlinear, ends = planes_terms(velocity, planes_in, power, n, sectors)
    lines = lax.all_to_all(ends, "theta", 0, 0)
    s = sweep(velocity, nonlinear, power)
    entries = lax.all_to_all(link(me, power, lines, points, comps), "theta", 0, 0)
    new_velocity = close(s, power, entries)
    return (new_velocity, nonlinear)


def solution(mesh):
    in_specs = (P(None, "theta", "gz", None), P(), P(), P())
    out_specs = (P(None, "theta", "gz", None), P(None, "theta", "gz", None))
    return jax.shard_map(local, mesh=mesh, in_specs=in_specs, out_specs=out_specs, check_vma=False)
```

```python
import functools

import jax
import jax.numpy as jnp
from jax import lax
from jax.experimental import pallas as pl
from jax.experimental.pallas import tpu as pltpu
from jax.sharding import PartitionSpec as P

AXIAL_WEIGHTS = (0.75, -0.15, 1.0 / 60.0)
AXIAL_REACH = len(AXIAL_WEIGHTS)
STEP_WEIGHT = 0.2
MIRROR_SIGNS = (-1.0, -1.0, 1.0)
LANES = 128
UNROLL = 16

VMEM = pl.BlockSpec(memory_space=pltpu.VMEM)
SMEM = pl.BlockSpec(memory_space=pltpu.SMEM)
ANY = pl.BlockSpec(memory_space=pl.ANY)


def params(block_bytes, blocks):
    return pltpu.CompilerParams(vmem_limit_bytes=(6 << 20) + blocks * block_bytes)


def held(*shape):
    return pltpu.VMEM(shape, jnp.float32)


def each(count, body):
    if count <= UNROLL:
        for i in range(count):
            body(i)
    else:
        pl.loop(0, count)(body)


def swap(block, axis, bit):
    size = lax.axis_size(axis)
    return lax.ppermute(block, axis, [(i, i ^ bit) for i in range(size)])


def swap_across(block, axis):
    size = lax.axis_size(axis)
    route = []
    for odd in range(1, size, 2):
        route += [(odd, (odd + 1) % size), ((odd + 1) % size, odd)]
    return lax.ppermute(block, axis, route)


def split(x):
    high = x.astype(jnp.bfloat16)
    return high, (x - high.astype(jnp.float32)).astype(jnp.bfloat16)


def product(left, right):
    dot = functools.partial(jnp.dot, preferred_element_type=jnp.float32)
    return dot(left[0], right[0]) + (dot(left[0], right[1]) + dot(left[1], right[0]))


def pack_planes_kernel(v_ref, y_ref):
    carriers = y_ref.shape[1]
    riders = v_ref.shape[1] - carriers
    lo, hi = AXIAL_REACH, v_ref.shape[2] - AXIAL_REACH

    def carry(t):
        for c in range(3):
            y_ref[c, t] = v_ref[c, t]

    def ride(j):
        for c in range(3):
            t = carriers + j
            y_ref[c, 3 * j, lo:hi] = v_ref[c, t, 0:2]
            y_ref[c, 3 * j + 1, lo : lo + 1] = v_ref[c, t, 2:3]
            y_ref[c, 3 * j + 1, lo + 1 : hi] = v_ref[c, t, hi : hi + 1]
            y_ref[c, 3 * j + 2, lo:hi] = v_ref[c, t, hi + 1 :]

    each(carriers, carry)
    each(riders, ride)


def pack_planes(v):
    comps, points, planes, radial = v.shape
    return pl.pallas_call(
        pack_planes_kernel,
        name="pack_planes",
        out_shape=held(comps, points - points // 4, planes, radial),
        in_specs=[VMEM],
        out_specs=VMEM,
        compiler_params=params(v.size * 4, 2),
    )(v)


def pack_sides_kernel(me_ref, v_ref, first_ref, core_ref, chip_ref, mirror_ref):
    points = v_ref.shape[1]
    reach = core_ref.shape[1]
    even = me_ref[0] % 2 == 0
    to_core = jnp.where(even, points - reach, 0)
    to_chip = jnp.where(even, 0, points - reach)
    for c in range(3):
        for h in range(reach):
            core_ref[c, h] = v_ref[c, to_core + h]
            chip_ref[c, h] = v_ref[c, to_chip + h]
    tiles = mirror_ref.shape[1]
    width = LANES // (points // tiles)
    lane = lax.broadcasted_iota(jnp.int32, mirror_ref.shape[2:], 1)

    def put(p):
        for c in range(3):
            tile = v_ref[c, p, :, :LANES]
            for q in range(1, points // tiles):
                part = pltpu.roll(v_ref[c, q * tiles + p, :, :LANES], q * width, 1)
                tile = jnp.where(lane < q * width, tile, part)
            mirror_ref[c, p] = tile

    each(tiles, put)


def pack_sides(me, v, first, reach, width):
    comps, points, planes, radial = v.shape
    tiles = points // (LANES // width)
    side = held(comps, reach, planes, radial)
    return pl.pallas_call(
        pack_sides_kernel,
        name="pack_sides",
        out_shape=(side, side, held(comps, tiles, planes, LANES)),
        in_specs=[SMEM, VMEM, ANY],
        out_specs=(VMEM, VMEM, VMEM),
        compiler_params=params(v.size * 4, 3),
    )(me, v, first)


def inverse_radius(radial):
    return 1.0 / (lax.broadcasted_iota(jnp.int32, (1, radial), 1).astype(jnp.float32) + 0.5)


def axial_weights(planes, inside):
    row = lax.broadcasted_iota(jnp.int32, (planes, 1), 0)
    weights = []
    for m, w in enumerate(AXIAL_WEIGHTS, 1):
        for shift, own, sign in ((m, row < planes - m, 1.0), (planes - m, row >= m, -1.0)):
            keep = own if inside else jnp.logical_not(own)
            weights.append((shift, jnp.where(keep, sign * w, 0.0)))
    return weights


def axial_part(tile, weights):
    planes = tile.shape[0]
    total = None
    for shift, weight in weights:
        term = weight * pltpu.roll(tile, planes - shift, 0)
        total = term if total is None else total + term
    return total


def inner_kernel(stencil_ref, v_ref, op_ref, n_ref, grad_ref):
    comps, points, planes, radial = v_ref.shape
    reach = (stencil_ref.shape[0] - 1) // 2
    rows = points * planes
    right = split(op_ref[:radial])
    for c in range(comps):
        grad_ref[c * rows : (c + 1) * rows] = product(split(v_ref[c].reshape(rows, radial)), right)
    inv_r = inverse_radius(radial)
    weights = axial_weights(planes, True)

    def point(t, lows, highs):
        a, b, e = v_ref[0, t], v_ref[1, t], v_ref[2, t]
        b_inv = b * inv_r
        for c in range(comps):
            around = None
            for m in range(-lows, highs + 1):
                term = stencil_ref[m + reach] * v_ref[c, t + m]
                around = term if around is None else around + term
            start = c * rows + t * planes
            grad = grad_ref[pl.ds(pl.multiple_of(start, planes), planes)]
            n = a * grad + b_inv * around + e * axial_part(v_ref[c, t], weights)
            if c == 0:
                n = n - b_inv * b
            elif c == 1:
                n = n + a * b_inv
            n_ref[c, t] = n

    for t in range(reach):
        point(t, t, min(reach, points - 1 - t))
    each(points - 2 * reach, lambda i: point(i + reach, reach, reach)) if points >= 2 * reach else None
    for t in range(max(reach, points - reach), points):
        point(t, min(reach, t), points - 1 - t)


def inner_terms(stencil, v, op):
    return pl.pallas_call(
        inner_kernel,
        name="inner_terms",
        out_shape=held(*v.shape),
        in_specs=[SMEM, VMEM, VMEM],
        out_specs=VMEM,
        scratch_shapes=[pltpu.VMEM((v.size // v.shape[3], v.shape[3]), jnp.float32)],
        compiler_params=params(v.size * 4, 6),
        cost_estimate=pl.CostEstimate(flops=6 * v.size * v.shape[3], bytes_accessed=16 * v.size, transcendentals=0),
    )(stencil, v, op)


def add_side(stencil_ref, v_ref, side_ref, n_in_ref, n_ref, inv_r, before):
    comps, points, _, _ = v_ref.shape
    reach = side_ref.shape[1]
    for u in range(reach):
        t = u if before else points - reach + u
        taps = [(h, h - u) for h in range(u, reach)] if before else [(h, 2 * reach + h - u) for h in range(u + 1)]
        b_inv = v_ref[1, t] * inv_r
        for c in range(comps):
            around = None
            for h, k in taps:
                term = stencil_ref[k] * side_ref[c, h]
                around = term if around is None else around + term
            n_ref[c, t] = n_in_ref[c, t] + b_inv * around


def early_kernel(me_ref, stencil_ref, v_ref, op_ref, core_ref, mirror_ref, n_in_ref, n_ref, grad_ref):
    comps, points, planes, radial = v_ref.shape
    tiles = mirror_ref.shape[1]
    count = points // tiles
    width = LANES // count
    rows = tiles * planes
    right = split(jnp.concatenate([op_ref[radial:]] * count, axis=0))
    lane = lax.broadcasted_iota(jnp.int32, (rows, LANES), 1)
    for c in range(comps):
        high, low = split(MIRROR_SIGNS[c] * mirror_ref[c].reshape(rows, LANES))
        zero = jnp.zeros_like(high)
        parts = [
            [jnp.where((lane >= q * width) & (lane < (q + 1) * width), x, zero) for q in range(count)]
            for x in (high, low)
        ]
        left = [jnp.concatenate(x, axis=0) for x in parts]
        grad_ref[c * points * planes : (c + 1) * points * planes] = product(left, right)

    def finish(t):
        for c in range(comps):
            start = pl.multiple_of((c * points + t) * planes, planes)
            n_ref[c, t] = n_in_ref[c, t] + v_ref[0, t] * grad_ref[pl.ds(start, planes)]

    each(points, finish)
    even = me_ref[0] % 2 == 0
    add = functools.partial(add_side, stencil_ref, v_ref, core_ref, n_ref, n_ref, inverse_radius(radial))
    pl.when(even)(lambda: add(False))
    pl.when(jnp.logical_not(even))(lambda: add(True))


def early_terms(me, stencil, v, op, core, mirror, n):
    return pl.pallas_call(
        early_kernel,
        name="early_terms",
        out_shape=held(*v.shape),
        in_specs=[SMEM, SMEM, VMEM, VMEM, VMEM, VMEM, VMEM],
        out_specs=VMEM,
        scratch_shapes=[pltpu.VMEM((v.size // v.shape[3], v.shape[3]), jnp.float32)],
        input_output_aliases={6: 0},
        compiler_params=params(v.size * 4, 8),
        cost_estimate=pl.CostEstimate(flops=2 * v.size * LANES, bytes_accessed=16 * v.size, transcendentals=0),
    )(me, stencil, v, op, core, mirror, n)


def late_kernel(me_ref, stencil_ref, v_ref, chip_ref, n_in_ref, n_ref):
    even = me_ref[0] % 2 == 0
    add = functools.partial(
        add_side, stencil_ref, v_ref, chip_ref, n_in_ref, n_ref, inverse_radius(v_ref.shape[3])
    )
    pl.when(even)(lambda: add(True))
    pl.when(jnp.logical_not(even))(lambda: add(False))


def late_terms(me, stencil, v, chip, n):
    return pl.pallas_call(
        late_kernel,
        name="late_terms",
        out_shape=held(*v.shape),
        in_specs=[SMEM, SMEM, VMEM, VMEM, VMEM],
        out_specs=VMEM,
        input_output_aliases={4: 0},
        compiler_params=params(v.size * 4, 5),
        cost_estimate=pl.CostEstimate(flops=20 * v.size, bytes_accessed=12 * v.size, transcendentals=0),
    )(me, stencil, v, chip, n)


def planes_kernel(me_ref, v_ref, y_ref, power_ref, n_in_ref, n_ref, keep_ref, send_ref, tile_ref, ends_ref):
    comps, points, planes, radial = v_ref.shape
    carriers = y_ref.shape[1]
    lo, hi = AXIAL_REACH, planes - AXIAL_REACH
    weights = axial_weights(planes, False)
    decay = power_ref[1:2]
    ends_ref[...] = jnp.zeros_like(ends_ref)

    def finish(t, c, tile):
        n = n_in_ref[c, t] + v_ref[2, t] * axial_part(tile, weights)
        n_ref[c, t] = n
        right_side = v_ref[c, t] - STEP_WEIGHT * n
        ends_ref[0, c] = decay * ends_ref[0, c] + right_side
        ends_ref[1, c] = ends_ref[1, c] + power_ref[pl.ds(t, 1)] * right_side

    def carried(t):
        for c in range(comps):
            finish(t, c, y_ref[c, t])

    def ridden(j):
        for c in range(comps):
            tile_ref[c, 0:2] = y_ref[c, 3 * j, lo:hi]
            tile_ref[c, 2:3] = y_ref[c, 3 * j + 1, lo : lo + 1]
            tile_ref[c, lo:hi] = jnp.zeros_like(tile_ref[c, lo:hi])
            tile_ref[c, hi : hi + 1] = y_ref[c, 3 * j + 1, lo + 1 : hi]
            tile_ref[c, hi + 1 :] = y_ref[c, 3 * j + 2, lo:hi]
            finish(carriers + j, c, tile_ref[c])

    each(carriers, carried)
    each(points - carriers, ridden)
    half = radial // 2
    core = me_ref[0] % 2
    keep_ref[...] = ends_ref[:, :, :, pl.ds(pl.multiple_of(core * half, half), half)]
    send_ref[...] = ends_ref[:, :, :, pl.ds(pl.multiple_of((1 - core) * half, half), half)]


def planes_terms(me, v, y, power, n):
    comps, points, planes, radial = v.shape
    part = held(2, comps, planes, radial // 2)
    return pl.pallas_call(
        planes_kernel,
        name="planes_terms",
        out_shape=(held(*v.shape), part, part),
        in_specs=[SMEM] + [VMEM] * 4,
        out_specs=(VMEM, VMEM, VMEM),
        scratch_shapes=[
            pltpu.VMEM((comps, planes, radial), jnp.float32),
            pltpu.VMEM((2, comps, planes, radial), jnp.float32),
        ],
        input_output_aliases={4: 0},
        compiler_params=params(v.size * 4, 6),
        cost_estimate=pl.CostEstimate(flops=20 * v.size, bytes_accessed=16 * v.size, transcendentals=0),
    )(me, v, y, power, n)


def powers(me, viscous_factor, points, sectors, radial):
    radius = jnp.arange(radial).astype(jnp.float32) + 0.5
    half = 0.5 * radius * lax.rsqrt(viscous_factor[0])
    root = jnp.sqrt(1.0 + half * half)
    loss = 2.0 * half * (root - half)
    rows = [jnp.ones_like(loss)]
    for _ in range(points):
        rows.append(rows[-1] * (1.0 - loss))
    total = loss
    left, result = points * sectors, None
    while left:
        if left & 1:
            result = total if result is None else result + total - result * total
        total = total * (2.0 - total)
        left >>= 1
    across = rows[points] * rows[points]
    rows += [half / root, 1.0 / result]
    before = after = rows[0]
    for bit in range(1, sectors.bit_length() - 1):
        upper = (me >> bit) % 2 == 1
        rows += [across, before, after]
        before, after = jnp.where(upper, before * across, before), jnp.where(upper, after, after * across)
        across = across * across
    return jnp.stack(rows + [before, after])


def sweep_kernel(v_ref, n_ref, power_ref, s_ref, nonlinear_ref, sem):
    leave = pltpu.make_async_copy(n_ref, nonlinear_ref, sem)
    leave.start()
    comps, points, planes, radial = v_ref.shape
    decay = power_ref[1:2]
    height = power_ref[points + 1 : points + 2]
    for c in range(comps):
        s_ref[c, 0] = height * (v_ref[c, 0] - STEP_WEIGHT * n_ref[c, 0])

        def forward(i):
            t = i + 1
            s_ref[c, t] = decay * s_ref[c, t - 1] + height * (v_ref[c, t] - STEP_WEIGHT * n_ref[c, t])

        each(points - 1, forward)

    def backward(i, carry):
        t = points - 1 - i
        after = []
        for c in range(comps):
            s_ref[c, t] = s_ref[c, t] + carry[c]
            after.append(decay * (carry[c] + height * (v_ref[c, t] - STEP_WEIGHT * n_ref[c, t])))
        return tuple(after)

    start = (jnp.zeros((planes, radial), jnp.float32),) * comps
    lax.fori_loop(0, points, backward, start, unroll=points <= UNROLL)
    leave.wait()


def sweep(v, n, power):
    return pl.pallas_call(
        sweep_kernel,
        name="sweep",
        out_shape=(held(*v.shape), jax.ShapeDtypeStruct(v.shape, v.dtype)),
        in_specs=[VMEM] * 3,
        out_specs=(VMEM, ANY),
        scratch_shapes=[pltpu.SemaphoreType.DMA],
        compiler_params=params(v.size * 4, 4),
        cost_estimate=pl.CostEstimate(flops=10 * v.size, bytes_accessed=12 * v.size, transcendentals=0),
    )(v, n, power)


def my_lanes(me_ref, radial, half):
    core = me_ref[0] % 2
    return pl.ds(pl.multiple_of(core * half, half), half)


def pair_kernel(me_ref, power_ref, own_ref, other_ref, block_ref, *, points):
    half = own_ref.shape[3]
    hop = power_ref[points : points + 1, my_lanes(me_ref, power_ref.shape[1], half)]
    odd = me_ref[0] % 2 == 1
    for c in range(own_ref.shape[1]):
        for side in range(2):
            own, other = own_ref[side, c], other_ref[side, c]
            far, near = (own, other) if side == 0 else (other, own)
            block_ref[side, c] = jnp.where(odd, hop * near + far, hop * far + near)


def pair(me, power, own, other, points):
    return pl.pallas_call(
        functools.partial(pair_kernel, points=points),
        name="pair",
        out_shape=held(*own.shape),
        in_specs=[SMEM, VMEM, VMEM, VMEM],
        out_specs=VMEM,
        compiler_params=params(own.size * 4, 8),
    )(me, power, own, other)


def merge_kernel(me_ref, power_ref, block_ref, entry_ref, other_ref, block_out_ref, entry_out_ref, *, points, bit):
    comps, half = block_ref.shape[1], block_ref.shape[3]
    lanes = my_lanes(me_ref, power_ref.shape[1], half)
    first = points + 3 * bit
    across, before, after = [power_ref[first + k : first + k + 1, lanes] for k in range(3)]
    upper = (me_ref[0] >> bit) % 2 == 1
    before = jnp.where(upper, before, 0.0)
    after = jnp.where(upper, 0.0, after)
    for c in range(comps):
        low, high = block_ref[0, c], block_ref[1, c]
        other_low, other_high = other_ref[0, c], other_ref[1, c]
        block_out_ref[0, c] = jnp.where(upper, across * other_low + low, across * low + other_low)
        block_out_ref[1, c] = jnp.where(upper, other_high + across * high, high + across * other_high)
        entry_out_ref[0, c] = entry_ref[0, c] + before * other_low
        entry_out_ref[1, c] = entry_ref[1, c] + after * other_high


def merge(me, power, block, entry, other, points, bit):
    return pl.pallas_call(
        functools.partial(merge_kernel, points=points, bit=bit),
        name="merge",
        out_shape=(held(*block.shape), held(*block.shape)),
        in_specs=[SMEM, VMEM, VMEM, VMEM, VMEM],
        out_specs=(VMEM, VMEM),
        compiler_params=params(block.size * 4, 8),
    )(me, power, block, entry, other)


def enter_kernel(me_ref, power_ref, block_ref, entry_ref, own_ref, other_ref, mine_ref, send_ref, *, points):
    comps, half = block_ref.shape[1], block_ref.shape[3]
    lanes = my_lanes(me_ref, power_ref.shape[1], half)
    row = lambda k: power_ref[k : k + 1, lanes]
    hop, height, wrap = row(points), row(points + 1), row(points + 2)
    last = power_ref.shape[0]
    before, after = row(last - 2) * wrap, row(last - 1) * wrap
    odd = me_ref[0] % 2 == 1
    for c in range(comps):
        low = height * (entry_ref[0, c] + before * block_ref[0, c])
        high = height * (entry_ref[1, c] + after * block_ref[1, c])
        even_low = height * jnp.where(odd, other_ref[0, c], own_ref[0, c])
        odd_high = height * jnp.where(odd, own_ref[1, c], other_ref[1, c])
        even_in = (low, odd_high + hop * high)
        odd_in = (even_low + hop * low, high)
        for side in range(2):
            mine_ref[side, c] = jnp.where(odd, odd_in[side], even_in[side])
            send_ref[side, c] = jnp.where(odd, even_in[side], odd_in[side])


def enter(me, power, block, entry, own, other, points):
    return pl.pallas_call(
        functools.partial(enter_kernel, points=points),
        name="enter",
        out_shape=(held(*block.shape), held(*block.shape)),
        in_specs=[SMEM] + [VMEM] * 5,
        out_specs=(VMEM, VMEM),
        compiler_params=params(block.size * 4, 12),
    )(me, power, block, entry, own, other)


def close_kernel(me_ref, s_ref, power_ref, mine_ref, got_ref, out_ref, x_ref, both_ref, sems):
    comps, points, planes, radial = s_ref.shape
    half = mine_ref.shape[3]
    core = me_ref[0] % 2
    both_ref[:, :, :, pl.ds(pl.multiple_of(core * half, half), half)] = mine_ref[...]
    both_ref[:, :, :, pl.ds(pl.multiple_of((1 - core) * half, half), half)] = got_ref[...]
    leaves = []
    for c in range(comps):
        before, after = both_ref[0, c], both_ref[1, c]

        def point(t):
            x_ref[c, t] = s_ref[c, t] + power_ref[pl.ds(t + 1, 1)] * before + power_ref[pl.ds(points - t, 1)] * after

        each(points, point)
        leaves.append(pltpu.make_async_copy(x_ref.at[c], out_ref.at[c], sems.at[c]))
        leaves[c].start()
    for leave in leaves:
        leave.wait()


def close(me, s, power, mine, got):
    return pl.pallas_call(
        close_kernel,
        name="close",
        out_shape=jax.ShapeDtypeStruct(s.shape, s.dtype),
        in_specs=[SMEM] + [VMEM] * 4,
        out_specs=ANY,
        scratch_shapes=[
            pltpu.VMEM(s.shape, jnp.float32),
            pltpu.VMEM((2,) + s.shape[:1] + s.shape[2:], jnp.float32),
            pltpu.SemaphoreType.DMA((s.shape[0],)),
        ],
        compiler_params=params(s.size * 4, 5),
    )(me, s, power, mine, got)


def local(velocity, radial_op, azimuth_stencil, viscous_factor):
    sectors = lax.axis_size("theta")
    comps, points, planes, radial = velocity.shape
    reach = (azimuth_stencil.shape[0] - 1) // 2
    width = radial_op.shape[1] - radial
    me = lax.axis_index("theta").astype(jnp.int32).reshape(1)
    op = radial_op.T

    planes_out = pack_planes(velocity)
    planes_in = swap(planes_out, "gz", 1)
    core_out, chip_out, mirror_out = pack_sides(me, velocity, planes_out, reach, width)
    chip_in = swap_across(chip_out, "theta")
    core_in = swap(core_out, "theta", 1)
    mirror_in = swap(mirror_out, "theta", sectors // 2)
    power = powers(me, viscous_factor, points, sectors, radial)
    n = inner_terms(azimuth_stencil, velocity, op)
    n = early_terms(me, azimuth_stencil, velocity, op, core_in, mirror_in, n)
    n = late_terms(me, azimuth_stencil, velocity, chip_in, n)
    n, own, send = planes_terms(me, velocity, planes_in, power, n)
    other = swap(send, "theta", 1)
    s, nonlinear = sweep(velocity, n, power)
    block = pair(me, power, own, other, points)
    entry = jnp.zeros_like(block)
    for bit in range(1, sectors.bit_length() - 1):
        block, entry = merge(me, power, block, entry, swap(block, "theta", 1 << bit), points, bit)
    mine, send = enter(me, power, block, entry, own, other, points)
    new_velocity = close(me, s, power, mine, swap(send, "theta", 1))
    return (new_velocity, nonlinear)


def solution(mesh):
    in_specs = (P(None, "theta", "gz", None), P(), P(), P())
    out_specs = (P(None, "theta", "gz", None), P(None, "theta", "gz", None))
    return jax.shard_map(local, mesh=mesh, in_specs=in_specs, out_specs=out_specs, check_vma=False)
```

```python
import functools

import jax
import jax.numpy as jnp
from jax import lax
from jax.experimental import pallas as pl
from jax.experimental.pallas import tpu as pltpu
from jax.sharding import PartitionSpec as P

AXIAL_WEIGHTS = (0.75, -0.15, 1.0 / 60.0)
AXIAL_REACH = len(AXIAL_WEIGHTS)
STEP_WEIGHT = 0.2
MIRROR_SIGNS = (-1.0, -1.0, 1.0)
LANES = 128
UNROLL = 16

VMEM = pl.BlockSpec(memory_space=pltpu.VMEM)
SMEM = pl.BlockSpec(memory_space=pltpu.SMEM)
ANY = pl.BlockSpec(memory_space=pl.ANY)
HBM = pl.BlockSpec(memory_space=pltpu.HBM)


def params(block_bytes, blocks):
    return pltpu.CompilerParams(vmem_limit_bytes=(6 << 20) + blocks * block_bytes)


def held(*shape):
    return pltpu.VMEM(shape, jnp.float32)


def each(count, body):
    if count <= UNROLL:
        for i in range(count):
            body(i)
    else:
        pl.loop(0, count)(body)


def swap(block, axis, bit):
    size = lax.axis_size(axis)
    return lax.ppermute(block, axis, [(i, i ^ bit) for i in range(size)])


def swap_across(block, axis):
    size = lax.axis_size(axis)
    route = []
    for odd in range(1, size, 2):
        route += [(odd, (odd + 1) % size), ((odd + 1) % size, odd)]
    return lax.ppermute(block, axis, route)


def split(x):
    high = x.astype(jnp.bfloat16)
    return high, (x - high.astype(jnp.float32)).astype(jnp.bfloat16)


def product(left, right):
    dot = functools.partial(jnp.dot, preferred_element_type=jnp.float32)
    return dot(left[0], right[0]) + (dot(left[0], right[1]) + dot(left[1], right[0]))


def load_kernel(hbm_ref, v_ref, y_ref, sems):
    comps, points, planes, _ = v_ref.shape
    carriers = y_ref.shape[1]
    lo, hi = AXIAL_REACH, planes - AXIAL_REACH
    loads = [pltpu.make_async_copy(hbm_ref.at[c], v_ref.at[c], sems.at[c]) for c in range(comps)]
    for load in loads:
        load.start()
    for c in range(comps):
        loads[c].wait()

        def carry(t):
            y_ref[c, t] = v_ref[c, t]

        def ride(j):
            t = carriers + j
            y_ref[c, 3 * j, lo:hi] = v_ref[c, t, 0:2]
            y_ref[c, 3 * j + 1, lo : lo + 1] = v_ref[c, t, 2:3]
            y_ref[c, 3 * j + 1, lo + 1 : hi] = v_ref[c, t, hi : hi + 1]
            y_ref[c, 3 * j + 2, lo:hi] = v_ref[c, t, hi + 1 :]

        each(carriers, carry)
        each(points - carriers, ride)


def load(v):
    comps, points, planes, radial = v.shape
    return pl.pallas_call(
        load_kernel,
        name="load",
        out_shape=(held(*v.shape), held(comps, points - points // 4, planes, radial)),
        in_specs=[HBM],
        out_specs=(VMEM, VMEM),
        scratch_shapes=[pltpu.SemaphoreType.DMA((comps,))],
        compiler_params=params(v.size * 4, 2),
    )(v)


def pack_side_kernel(me_ref, v_ref, first_ref, side_ref, *, after):
    points, reach = v_ref.shape[1], side_ref.shape[1]

    def put(start):
        for c in range(v_ref.shape[0]):
            for h in range(reach):
                side_ref[c, h] = v_ref[c, start + h]

    even = me_ref[0] % 2 == 0
    last = even if after else jnp.logical_not(even)
    pl.when(last)(lambda: put(points - reach))
    pl.when(jnp.logical_not(last))(lambda: put(0))


def pack_side(me, v, first, reach, after):
    comps, _, planes, radial = v.shape
    return pl.pallas_call(
        functools.partial(pack_side_kernel, after=after),
        name="pack_core" if after else "pack_chip",
        out_shape=held(comps, reach, planes, radial),
        in_specs=[SMEM, VMEM, ANY],
        out_specs=VMEM,
        compiler_params=params(v.size * 4, 3),
    )(me, v, first)


def pack_mirror_kernel(v_ref, first_ref, mirror_ref):
    points, tiles = v_ref.shape[1], mirror_ref.shape[1]
    width = LANES // (points // tiles)
    lane = lax.broadcasted_iota(jnp.int32, mirror_ref.shape[2:], 1)

    def put(p):
        for c in range(v_ref.shape[0]):
            tile = v_ref[c, p, :, :LANES]
            for q in range(1, points // tiles):
                part = pltpu.roll(v_ref[c, q * tiles + p, :, :LANES], q * width, 1)
                tile = jnp.where(lane < q * width, tile, part)
            mirror_ref[c, p] = tile

    each(tiles, put)


def pack_mirror(v, first, width):
    comps, points, planes, _ = v.shape
    return pl.pallas_call(
        pack_mirror_kernel,
        name="pack_mirror",
        out_shape=held(comps, points // (LANES // width), planes, LANES),
        in_specs=[VMEM, ANY],
        out_specs=VMEM,
        compiler_params=params(v.size * 4, 2),
    )(v, first)


def inverse_radius(radial, start=0):
    return 1.0 / ((lax.broadcasted_iota(jnp.int32, (1, radial), 1) + start).astype(jnp.float32) + 0.5)


def axial_weights(planes, inside):
    row = lax.broadcasted_iota(jnp.int32, (planes, 1), 0)
    weights = []
    for m, w in enumerate(AXIAL_WEIGHTS, 1):
        for shift, own, sign in ((m, row < planes - m, 1.0), (planes - m, row >= m, -1.0)):
            keep = own if inside else jnp.logical_not(own)
            weights.append((shift, jnp.where(keep, sign * w, 0.0)))
    return weights


def axial_part(tile, weights):
    planes = tile.shape[0]
    total = None
    for shift, weight in weights:
        term = weight * pltpu.roll(tile, planes - shift, 0)
        total = term if total is None else total + term
    return total


def inner_kernel(stencil_ref, v_ref, op_ref, n_ref, grad_ref):
    comps, points, planes, radial = v_ref.shape
    reach = (stencil_ref.shape[0] - 1) // 2
    rows = points * planes
    right = split(op_ref[:radial])
    for c in range(comps):
        grad_ref[c * rows : (c + 1) * rows] = product(split(v_ref[c].reshape(rows, radial)), right)
    inv_r = inverse_radius(radial)
    weights = axial_weights(planes, True)

    def point(t, lows, highs):
        a, b, e = v_ref[0, t], v_ref[1, t], v_ref[2, t]
        b_inv = b * inv_r
        for c in range(comps):
            around = None
            for m in range(-lows, highs + 1):
                term = stencil_ref[m + reach] * v_ref[c, t + m]
                around = term if around is None else around + term
            start = c * rows + t * planes
            grad = grad_ref[pl.ds(pl.multiple_of(start, planes), planes)]
            n = a * grad + b_inv * around + e * axial_part(v_ref[c, t], weights)
            if c == 0:
                n = n - b_inv * b
            elif c == 1:
                n = n + a * b_inv
            n_ref[c, t] = n

    for t in range(reach):
        point(t, t, min(reach, points - 1 - t))
    each(points - 2 * reach, lambda i: point(i + reach, reach, reach)) if points >= 2 * reach else None
    for t in range(max(reach, points - reach), points):
        point(t, min(reach, t), points - 1 - t)


def inner_terms(stencil, v, op):
    return pl.pallas_call(
        inner_kernel,
        name="inner_terms",
        out_shape=held(*v.shape),
        in_specs=[SMEM, VMEM, VMEM],
        out_specs=VMEM,
        scratch_shapes=[pltpu.VMEM((v.size // v.shape[3], v.shape[3]), jnp.float32)],
        compiler_params=params(v.size * 4, 6),
        cost_estimate=pl.CostEstimate(flops=6 * v.size * v.shape[3], bytes_accessed=16 * v.size, transcendentals=0),
    )(stencil, v, op)


def add_side(stencil_ref, v_ref, side_ref, n_in_ref, n_ref, before):
    comps, points, _, radial = v_ref.shape
    reach = side_ref.shape[1]
    first = 0 if before else reach + 1
    weights = [stencil_ref[first + k] for k in range(reach)]

    @pl.loop(0, radial // LANES)
    def column(k):
        lanes = pl.ds(pl.multiple_of(k * LANES, LANES), LANES)
        inv_r = inverse_radius(LANES, k * LANES)
        for c in range(comps):
            side = [side_ref[c, h, :, lanes] for h in range(reach)]
            for u in range(reach):
                t = u if before else points - reach + u
                taps = [(h, h - u) for h in range(u, reach)] if before else [(h, reach - 1 + h - u) for h in range(u + 1)]
                around = None
                for h, w in taps:
                    term = weights[w] * side[h]
                    around = term if around is None else around + term
                n_ref[c, t, :, lanes] = n_in_ref[c, t, :, lanes] + v_ref[1, t, :, lanes] * inv_r * around


def early_kernel(me_ref, stencil_ref, v_ref, op_ref, core_ref, mirror_ref, n_in_ref, n_ref, grad_ref):
    comps, points, planes, radial = v_ref.shape
    tiles = mirror_ref.shape[1]
    count = points // tiles
    width = LANES // count
    rows = tiles * planes
    right = split(jnp.concatenate([op_ref[radial:]] * count, axis=0))
    lane = lax.broadcasted_iota(jnp.int32, (rows, LANES), 1)
    for c in range(comps):
        high, low = split(MIRROR_SIGNS[c] * mirror_ref[c].reshape(rows, LANES))
        zero = jnp.zeros_like(high)
        parts = [
            [jnp.where((lane >= q * width) & (lane < (q + 1) * width), x, zero) for q in range(count)]
            for x in (high, low)
        ]
        left = [jnp.concatenate(x, axis=0) for x in parts]
        grad_ref[c * points * planes : (c + 1) * points * planes] = product(left, right)

    def finish(t):
        for c in range(comps):
            start = pl.multiple_of((c * points + t) * planes, planes)
            n_ref[c, t] = n_in_ref[c, t] + v_ref[0, t] * grad_ref[pl.ds(start, planes)]

    each(points, finish)
    even = me_ref[0] % 2 == 0
    add = functools.partial(add_side, stencil_ref, v_ref, core_ref, n_ref, n_ref)
    pl.when(even)(lambda: add(False))
    pl.when(jnp.logical_not(even))(lambda: add(True))


def early_terms(me, stencil, v, op, core, mirror, n):
    return pl.pallas_call(
        early_kernel,
        name="early_terms",
        out_shape=held(*v.shape),
        in_specs=[SMEM, SMEM, VMEM, VMEM, VMEM, VMEM, VMEM],
        out_specs=VMEM,
        scratch_shapes=[pltpu.VMEM((v.size // v.shape[3], v.shape[3]), jnp.float32)],
        input_output_aliases={6: 0},
        compiler_params=params(v.size * 4, 8),
        cost_estimate=pl.CostEstimate(flops=2 * v.size * LANES, bytes_accessed=16 * v.size, transcendentals=0),
    )(me, stencil, v, op, core, mirror, n)


def late_kernel(me_ref, stencil_ref, v_ref, chip_ref, n_in_ref, n_ref):
    even = me_ref[0] % 2 == 0
    add = functools.partial(add_side, stencil_ref, v_ref, chip_ref, n_in_ref, n_ref)
    pl.when(even)(lambda: add(True))
    pl.when(jnp.logical_not(even))(lambda: add(False))


def late_terms(me, stencil, v, chip, n):
    return pl.pallas_call(
        late_kernel,
        name="late_terms",
        out_shape=held(*v.shape),
        in_specs=[SMEM, SMEM, VMEM, VMEM, VMEM],
        out_specs=VMEM,
        input_output_aliases={4: 0},
        compiler_params=params(v.size * 4, 5),
        cost_estimate=pl.CostEstimate(flops=20 * v.size, bytes_accessed=12 * v.size, transcendentals=0),
    )(me, stencil, v, chip, n)


def planes_kernel(me_ref, v_ref, y_ref, power_ref, n_in_ref, n_ref, keep_ref, send_ref, tile_ref, ends_ref):
    comps, points, planes, radial = v_ref.shape
    carriers = y_ref.shape[1]
    lo, hi = AXIAL_REACH, planes - AXIAL_REACH
    weights = axial_weights(planes, False)
    for c in range(comps):
        for j in range(points - carriers):
            tile_ref[c, j, 0:2] = y_ref[c, 3 * j, lo:hi]
            tile_ref[c, j, 2:3] = y_ref[c, 3 * j + 1, lo : lo + 1]
            tile_ref[c, j, lo:hi] = jnp.zeros((hi - lo, radial), jnp.float32)
            tile_ref[c, j, hi : hi + 1] = y_ref[c, 3 * j + 1, lo + 1 : hi]
            tile_ref[c, j, hi + 1 :] = y_ref[c, 3 * j + 2, lo:hi]

    @pl.loop(0, radial // LANES)
    def column(k):
        lanes = pl.ds(pl.multiple_of(k * LANES, LANES), LANES)
        decay = power_ref[1:2, lanes]
        for c in range(comps):
            low = high = None
            for t in range(points):
                tile = y_ref[c, t, :, lanes] if t < carriers else tile_ref[c, t - carriers, :, lanes]
                n = n_in_ref[c, t, :, lanes] + v_ref[2, t, :, lanes] * axial_part(tile, weights)
                n_ref[c, t, :, lanes] = n
                right_side = v_ref[c, t, :, lanes] - STEP_WEIGHT * n
                low = right_side if t == 0 else decay * low + right_side
                high = right_side if t == 0 else high + power_ref[t : t + 1, lanes] * right_side
            ends_ref[0, c, :, lanes] = low
            ends_ref[1, c, :, lanes] = high

    half = radial // 2
    core = me_ref[0] % 2
    keep_ref[...] = ends_ref[:, :, :, pl.ds(pl.multiple_of(core * half, half), half)]
    send_ref[...] = ends_ref[:, :, :, pl.ds(pl.multiple_of((1 - core) * half, half), half)]


def planes_terms(me, v, y, power, n):
    comps, points, planes, radial = v.shape
    part = held(2, comps, planes, radial // 2)
    return pl.pallas_call(
        planes_kernel,
        name="planes_terms",
        out_shape=(held(*v.shape), part, part),
        in_specs=[SMEM] + [VMEM] * 4,
        out_specs=(VMEM, VMEM, VMEM),
        scratch_shapes=[
            pltpu.VMEM((comps, points - y.shape[1], planes, radial), jnp.float32),
            pltpu.VMEM((2, comps, planes, radial), jnp.float32),
        ],
        input_output_aliases={4: 0},
        compiler_params=params(v.size * 4, 6),
        cost_estimate=pl.CostEstimate(flops=20 * v.size, bytes_accessed=16 * v.size, transcendentals=0),
    )(me, v, y, power, n)


def powers(me, viscous_factor, points, sectors, radial):
    radius = jnp.arange(radial).astype(jnp.float32) + 0.5
    half = 0.5 * radius * lax.rsqrt(viscous_factor[0])
    root = jnp.sqrt(1.0 + half * half)
    loss = 2.0 * half * (root - half)
    rows = [jnp.ones_like(loss)]
    for _ in range(points):
        rows.append(rows[-1] * (1.0 - loss))
    total = loss
    left, result = points * sectors, None
    while left:
        if left & 1:
            result = total if result is None else result + total - result * total
        total = total * (2.0 - total)
        left >>= 1
    across = rows[points] * rows[points]
    rows += [half / root, 1.0 / result]
    before = after = rows[0]
    for bit in range(1, sectors.bit_length() - 1):
        upper = (me >> bit) % 2 == 1
        rows += [across, before, after]
        before, after = jnp.where(upper, before * across, before), jnp.where(upper, after, after * across)
        across = across * across
    return jnp.stack(rows + [before, after])


def sweep_kernel(v_ref, n_ref, power_ref, s_ref, nonlinear_ref, sem):
    leave = pltpu.make_async_copy(n_ref, nonlinear_ref, sem)
    leave.start()
    comps, points, planes, radial = v_ref.shape
    decay = power_ref[1:2]
    height = power_ref[points + 1 : points + 2]
    for c in range(comps):
        s_ref[c, 0] = height * (v_ref[c, 0] - STEP_WEIGHT * n_ref[c, 0])

        def forward(i):
            t = i + 1
            s_ref[c, t] = decay * s_ref[c, t - 1] + height * (v_ref[c, t] - STEP_WEIGHT * n_ref[c, t])

        each(points - 1, forward)

    def backward(i, carry):
        t = points - 1 - i
        after = []
        for c in range(comps):
            s_ref[c, t] = s_ref[c, t] + carry[c]
            after.append(decay * (carry[c] + height * (v_ref[c, t] - STEP_WEIGHT * n_ref[c, t])))
        return tuple(after)

    start = (jnp.zeros((planes, radial), jnp.float32),) * comps
    lax.fori_loop(0, points, backward, start, unroll=points <= UNROLL)
    leave.wait()


def sweep(v, n, power):
    return pl.pallas_call(
        sweep_kernel,
        name="sweep",
        out_shape=(held(*v.shape), jax.ShapeDtypeStruct(v.shape, v.dtype)),
        in_specs=[VMEM] * 3,
        out_specs=(VMEM, ANY),
        scratch_shapes=[pltpu.SemaphoreType.DMA],
        compiler_params=params(v.size * 4, 4),
        cost_estimate=pl.CostEstimate(flops=10 * v.size, bytes_accessed=12 * v.size, transcendentals=0),
    )(v, n, power)


def my_lanes(me_ref, radial, half):
    core = me_ref[0] % 2
    return pl.ds(pl.multiple_of(core * half, half), half)


def pair_kernel(me_ref, power_ref, own_ref, other_ref, block_ref, *, points):
    half = own_ref.shape[3]
    hop = power_ref[points : points + 1, my_lanes(me_ref, power_ref.shape[1], half)]
    odd = me_ref[0] % 2 == 1
    for c in range(own_ref.shape[1]):
        for side in range(2):
            own, other = own_ref[side, c], other_ref[side, c]
            far, near = (own, other) if side == 0 else (other, own)
            block_ref[side, c] = jnp.where(odd, hop * near + far, hop * far + near)


def pair(me, power, own, other, points):
    return pl.pallas_call(
        functools.partial(pair_kernel, points=points),
        name="pair",
        out_shape=held(*own.shape),
        in_specs=[SMEM, VMEM, VMEM, VMEM],
        out_specs=VMEM,
        compiler_params=params(own.size * 4, 8),
    )(me, power, own, other)


def merge_kernel(me_ref, power_ref, block_ref, entry_ref, other_ref, block_out_ref, entry_out_ref, *, points, bit):
    comps, half = block_ref.shape[1], block_ref.shape[3]
    lanes = my_lanes(me_ref, power_ref.shape[1], half)
    first = points + 3 * bit
    across, before, after = [power_ref[first + k : first + k + 1, lanes] for k in range(3)]
    upper = (me_ref[0] >> bit) % 2 == 1
    before = jnp.where(upper, before, 0.0)
    after = jnp.where(upper, 0.0, after)
    for c in range(comps):
        low, high = block_ref[0, c], block_ref[1, c]
        other_low, other_high = other_ref[0, c], other_ref[1, c]
        block_out_ref[0, c] = jnp.where(upper, across * other_low + low, across * low + other_low)
        block_out_ref[1, c] = jnp.where(upper, other_high + across * high, high + across * other_high)
        entry_out_ref[0, c] = entry_ref[0, c] + before * other_low
        entry_out_ref[1, c] = entry_ref[1, c] + after * other_high


def merge(me, power, block, entry, other, points, bit):
    return pl.pallas_call(
        functools.partial(merge_kernel, points=points, bit=bit),
        name="merge",
        out_shape=(held(*block.shape), held(*block.shape)),
        in_specs=[SMEM, VMEM, VMEM, VMEM, VMEM],
        out_specs=(VMEM, VMEM),
        compiler_params=params(block.size * 4, 8),
    )(me, power, block, entry, other)


def enter_kernel(me_ref, power_ref, block_ref, entry_ref, own_ref, other_ref, ready_ref, mine_ref, send_ref, *, points):
    comps, half = block_ref.shape[1], block_ref.shape[3]
    lanes = my_lanes(me_ref, power_ref.shape[1], half)
    row = lambda k: power_ref[k : k + 1, lanes]
    hop, height, wrap = row(points), row(points + 1), row(points + 2)
    last = power_ref.shape[0]
    before, after = row(last - 2) * wrap, row(last - 1) * wrap
    odd = me_ref[0] % 2 == 1
    for c in range(comps):
        low = height * (entry_ref[0, c] + before * block_ref[0, c])
        high = height * (entry_ref[1, c] + after * block_ref[1, c])
        even_low = height * jnp.where(odd, other_ref[0, c], own_ref[0, c])
        odd_high = height * jnp.where(odd, own_ref[1, c], other_ref[1, c])
        even_in = (low, odd_high + hop * high)
        odd_in = (even_low + hop * low, high)
        for side in range(2):
            mine_ref[side, c] = jnp.where(odd, odd_in[side], even_in[side])
            send_ref[side, c] = jnp.where(odd, even_in[side], odd_in[side])


def enter(me, power, block, entry, own, other, ready, points):
    return pl.pallas_call(
        functools.partial(enter_kernel, points=points),
        name="enter",
        out_shape=(held(*block.shape), held(*block.shape)),
        in_specs=[SMEM] + [VMEM] * 5 + [ANY],
        out_specs=(VMEM, VMEM),
        compiler_params=params(block.size * 4, 12),
    )(me, power, block, entry, own, other, ready)


def close_kernel(me_ref, s_ref, power_ref, mine_ref, got_ref, out_ref, x_ref, both_ref, sems):
    comps, points, planes, radial = s_ref.shape
    half = mine_ref.shape[3]
    core = me_ref[0] % 2
    both_ref[:, :, :, pl.ds(pl.multiple_of(core * half, half), half)] = mine_ref[...]
    both_ref[:, :, :, pl.ds(pl.multiple_of((1 - core) * half, half), half)] = got_ref[...]
    leaves = []
    for c in range(comps):
        before, after = both_ref[0, c], both_ref[1, c]

        def point(t):
            x_ref[c, t] = s_ref[c, t] + power_ref[pl.ds(t + 1, 1)] * before + power_ref[pl.ds(points - t, 1)] * after

        each(points, point)
        leaves.append(pltpu.make_async_copy(x_ref.at[c], out_ref.at[c], sems.at[c]))
        leaves[c].start()
    for leave in leaves:
        leave.wait()


def close(me, s, power, mine, got):
    return pl.pallas_call(
        close_kernel,
        name="close",
        out_shape=jax.ShapeDtypeStruct(s.shape, s.dtype),
        in_specs=[SMEM] + [VMEM] * 4,
        out_specs=ANY,
        scratch_shapes=[
            pltpu.VMEM(s.shape, jnp.float32),
            pltpu.VMEM((2,) + s.shape[:1] + s.shape[2:], jnp.float32),
            pltpu.SemaphoreType.DMA((s.shape[0],)),
        ],
        compiler_params=params(s.size * 4, 5),
    )(me, s, power, mine, got)


def local(velocity, radial_op, azimuth_stencil, viscous_factor):
    sectors = lax.axis_size("theta")
    comps, points, planes, radial = velocity.shape
    reach = (azimuth_stencil.shape[0] - 1) // 2
    width = radial_op.shape[1] - radial
    me = lax.axis_index("theta").astype(jnp.int32).reshape(1)
    op = radial_op.T

    velocity, planes_out = load(velocity)
    planes_in = swap(planes_out, "gz", 1)
    chip_out = pack_side(me, velocity, planes_out, reach, False)
    chip_in = swap_across(chip_out, "theta")
    mirror_out = pack_mirror(velocity, chip_out, width)
    mirror_in = swap(mirror_out, "theta", sectors // 2)
    core_out = pack_side(me, velocity, mirror_out, reach, True)
    core_in = swap(core_out, "theta", 1)
    power = powers(me, viscous_factor, points, sectors, radial)
    n = inner_terms(azimuth_stencil, velocity, op)
    n = early_terms(me, azimuth_stencil, velocity, op, core_in, mirror_in, n)
    n = late_terms(me, azimuth_stencil, velocity, chip_in, n)
    n, own, send = planes_terms(me, velocity, planes_in, power, n)
    other = swap(send, "theta", 1)
    s, nonlinear = sweep(velocity, n, power)
    block = pair(me, power, own, other, points)
    entry = jnp.zeros_like(block)
    for bit in range(1, sectors.bit_length() - 1):
        block, entry = merge(me, power, block, entry, swap(block, "theta", 1 << bit), points, bit)
    mine, send = enter(me, power, block, entry, own, other, s, points)
    new_velocity = close(me, s, power, mine, swap(send, "theta", 1))
    return (new_velocity, nonlinear)


def solution(mesh):
    in_specs = (P(None, "theta", "gz", None), P(), P(), P())
    out_specs = (P(None, "theta", "gz", None), P(None, "theta", "gz", None))
    return jax.shard_map(local, mesh=mesh, in_specs=in_specs, out_specs=out_specs, check_vma=False)
```

```python
import functools

import jax
import jax.numpy as jnp
from jax import lax
from jax.experimental import pallas as pl
from jax.experimental.pallas import tpu as pltpu
from jax.sharding import PartitionSpec as P

AXIAL_WEIGHTS = (0.75, -0.15, 1.0 / 60.0)
AXIAL_REACH = len(AXIAL_WEIGHTS)
STEP_WEIGHT = 0.2
MIRROR_SIGNS = (-1.0, -1.0, 1.0)
LANES = 128
UNROLL = 16

VMEM = pl.BlockSpec(memory_space=pltpu.VMEM)
SMEM = pl.BlockSpec(memory_space=pltpu.SMEM)
ANY = pl.BlockSpec(memory_space=pl.ANY)
HBM = pl.BlockSpec(memory_space=pltpu.HBM)


def params(block_bytes, blocks):
    return pltpu.CompilerParams(vmem_limit_bytes=(2 << 20) + blocks * block_bytes)


def held(*shape):
    return pltpu.VMEM(shape, jnp.float32)


def each(count, body):
    if count <= UNROLL:
        for i in range(count):
            body(i)
    else:
        pl.loop(0, count)(body)


def swap(block, axis, bit):
    size = lax.axis_size(axis)
    return lax.ppermute(block, axis, [(i, i ^ bit) for i in range(size)])


def swap_across(block, axis):
    size = lax.axis_size(axis)
    route = []
    for odd in range(1, size, 2):
        route += [(odd, (odd + 1) % size), ((odd + 1) % size, odd)]
    return lax.ppermute(block, axis, route)


def split(x):
    high = x.astype(jnp.bfloat16)
    return high, (x - high.astype(jnp.float32)).astype(jnp.bfloat16)


def product(left, right):
    dot = functools.partial(jnp.dot, preferred_element_type=jnp.float32)
    return dot(left[0], right[0]) + (dot(left[0], right[1]) + dot(left[1], right[0]))


def load_kernel(hbm_ref, v_ref, y_ref, sems):
    comps, points, planes, _ = v_ref.shape
    carriers = y_ref.shape[1]
    lo, hi = AXIAL_REACH, planes - AXIAL_REACH
    loads = [pltpu.make_async_copy(hbm_ref.at[c], v_ref.at[c], sems.at[c]) for c in range(comps)]
    for load in loads:
        load.start()
    for c in range(comps):
        loads[c].wait()

        def carry(t):
            y_ref[c, t] = v_ref[c, t]

        def ride(j):
            t = carriers + j
            y_ref[c, 3 * j, lo:hi] = v_ref[c, t, 0:2]
            y_ref[c, 3 * j + 1, lo : lo + 1] = v_ref[c, t, 2:3]
            y_ref[c, 3 * j + 1, lo + 1 : hi] = v_ref[c, t, hi : hi + 1]
            y_ref[c, 3 * j + 2, lo:hi] = v_ref[c, t, hi + 1 :]

        each(carriers, carry)
        each(points - carriers, ride)


def load(v):
    comps, points, planes, radial = v.shape
    return pl.pallas_call(
        load_kernel,
        name="load",
        out_shape=(held(*v.shape), held(comps, points - points // 4, planes, radial)),
        in_specs=[HBM],
        out_specs=(VMEM, VMEM),
        scratch_shapes=[pltpu.SemaphoreType.DMA((comps,))],
        compiler_params=params(v.size * 4, 2),
    )(v)


def pack_side_kernel(me_ref, v_ref, first_ref, side_ref, *, after):
    points, reach = v_ref.shape[1], side_ref.shape[1]

    def put(start):
        for c in range(v_ref.shape[0]):
            for h in range(reach):
                side_ref[c, h] = v_ref[c, start + h]

    even = me_ref[0] % 2 == 0
    last = even if after else jnp.logical_not(even)
    pl.when(last)(lambda: put(points - reach))
    pl.when(jnp.logical_not(last))(lambda: put(0))


def pack_side(me, v, first, reach, after):
    comps, _, planes, radial = v.shape
    return pl.pallas_call(
        functools.partial(pack_side_kernel, after=after),
        name="pack_core" if after else "pack_chip",
        out_shape=held(comps, reach, planes, radial),
        in_specs=[SMEM, VMEM, ANY],
        out_specs=VMEM,
        compiler_params=params(v.size * 4, 3),
    )(me, v, first)


def pack_mirror_kernel(v_ref, first_ref, mirror_ref):
    points, tiles = v_ref.shape[1], mirror_ref.shape[1]
    width = LANES // (points // tiles)
    lane = lax.broadcasted_iota(jnp.int32, mirror_ref.shape[2:], 1)

    def put(p):
        for c in range(v_ref.shape[0]):
            tile = v_ref[c, p, :, :LANES]
            for q in range(1, points // tiles):
                part = pltpu.roll(v_ref[c, q * tiles + p, :, :LANES], q * width, 1)
                tile = jnp.where(lane < q * width, tile, part)
            mirror_ref[c, p] = tile

    each(tiles, put)


def pack_mirror(v, first, width):
    comps, points, planes, _ = v.shape
    return pl.pallas_call(
        pack_mirror_kernel,
        name="pack_mirror",
        out_shape=held(comps, points // (LANES // width), planes, LANES),
        in_specs=[VMEM, ANY],
        out_specs=VMEM,
        compiler_params=params(v.size * 4, 2),
    )(v, first)


def inverse_radius(radial, start=0):
    return 1.0 / ((lax.broadcasted_iota(jnp.int32, (1, radial), 1) + start).astype(jnp.float32) + 0.5)


def axial_weights(planes, inside):
    row = lax.broadcasted_iota(jnp.int32, (planes, LANES), 0)
    weights = []
    for m, w in enumerate(AXIAL_WEIGHTS, 1):
        for shift, own, sign in ((m, row < planes - m, 1.0), (planes - m, row >= m, -1.0)):
            keep = own if inside else jnp.logical_not(own)
            weights.append((shift, jnp.where(keep, sign * w, 0.0)))
    return weights


def axial_part(tile, weights):
    planes = tile.shape[0]
    total = None
    for shift, weight in weights:
        term = weight * pltpu.roll(tile, planes - shift, 0)
        total = term if total is None else total + term
    return total


def inner_kernel(tap_ref, v_ref, op_ref, n_ref, grad_ref):
    comps, points, planes, radial = v_ref.shape
    reach = (tap_ref.shape[0] - 1) // 2
    rows = points * planes
    right = split(op_ref[:radial])
    for c in range(comps):
        grad_ref[c * rows : (c + 1) * rows] = product(split(v_ref[c].reshape(rows, radial)), right)
    weights = axial_weights(planes, True)

    @pl.loop(0, radial // LANES)
    def column(k):
        lanes = pl.ds(pl.multiple_of(k * LANES, LANES), LANES)
        inv_r = inverse_radius(LANES, k * LANES)
        for c in range(comps):
            for t in range(points):
                a, b, e = [v_ref[i, t, :, lanes] for i in range(3)]
                b_inv = b * inv_r
                around = None
                for m in range(max(-reach, -t), min(reach, points - 1 - t) + 1):
                    term = tap_ref[m + reach] * v_ref[c, t + m, :, lanes]
                    around = term if around is None else around + term
                start = c * rows + t * planes
                n = a * grad_ref[start : start + planes, lanes] + b_inv * around
                n = n + e * axial_part(v_ref[c, t, :, lanes], weights)
                if c == 0:
                    n = n - b_inv * b
                elif c == 1:
                    n = n + a * b_inv
                n_ref[c, t, :, lanes] = n


def inner_terms(taps, v, op):
    return pl.pallas_call(
        inner_kernel,
        name="inner_terms",
        out_shape=held(*v.shape),
        in_specs=[VMEM, VMEM, VMEM],
        out_specs=VMEM,
        scratch_shapes=[pltpu.VMEM((v.size // v.shape[3], v.shape[3]), jnp.float32)],
        compiler_params=params(v.size * 4, 6),
        cost_estimate=pl.CostEstimate(flops=6 * v.size * v.shape[3], bytes_accessed=16 * v.size, transcendentals=0),
    )(taps, v, op)


def add_side(tap_ref, v_ref, side_ref, n_in_ref, n_ref, before):
    comps, points, _, radial = v_ref.shape
    reach = side_ref.shape[1]
    first = 0 if before else reach + 1

    @pl.loop(0, radial // LANES)
    def column(k):
        lanes = pl.ds(pl.multiple_of(k * LANES, LANES), LANES)
        inv_r = inverse_radius(LANES, k * LANES)
        weights = [tap_ref[first + i] for i in range(reach)]
        for c in range(comps):
            side = [side_ref[c, h, :, lanes] for h in range(reach)]
            for u in range(reach):
                t = u if before else points - reach + u
                taps = [(h, h - u) for h in range(u, reach)] if before else [(h, reach - 1 + h - u) for h in range(u + 1)]
                around = None
                for h, w in taps:
                    term = weights[w] * side[h]
                    around = term if around is None else around + term
                n_ref[c, t, :, lanes] = n_in_ref[c, t, :, lanes] + v_ref[1, t, :, lanes] * inv_r * around


def early_kernel(me_ref, tap_ref, v_ref, op_ref, core_ref, mirror_ref, n_in_ref, n_ref, grad_ref):
    comps, points, planes, radial = v_ref.shape
    tiles = mirror_ref.shape[1]
    count = points // tiles
    width = LANES // count
    rows = tiles * planes
    right = split(jnp.concatenate([op_ref[radial:]] * count, axis=0))
    lane = lax.broadcasted_iota(jnp.int32, (rows, LANES), 1)
    for c in range(comps):
        high, low = split(MIRROR_SIGNS[c] * mirror_ref[c].reshape(rows, LANES))
        zero = jnp.zeros_like(high)
        parts = [
            [jnp.where((lane >= q * width) & (lane < (q + 1) * width), x, zero) for q in range(count)]
            for x in (high, low)
        ]
        left = [jnp.concatenate(x, axis=0) for x in parts]
        grad_ref[c * points * planes : (c + 1) * points * planes] = product(left, right)

    def finish(t):
        for c in range(comps):
            start = pl.multiple_of((c * points + t) * planes, planes)
            n_ref[c, t] = n_in_ref[c, t] + v_ref[0, t] * grad_ref[pl.ds(start, planes)]

    each(points, finish)
    even = me_ref[0] % 2 == 0
    add = functools.partial(add_side, tap_ref, v_ref, core_ref, n_ref, n_ref)
    pl.when(even)(lambda: add(False))
    pl.when(jnp.logical_not(even))(lambda: add(True))


def early_terms(me, taps, v, op, core, mirror, n):
    return pl.pallas_call(
        early_kernel,
        name="early_terms",
        out_shape=held(*v.shape),
        in_specs=[SMEM, VMEM, VMEM, VMEM, VMEM, VMEM, VMEM],
        out_specs=VMEM,
        scratch_shapes=[pltpu.VMEM((v.size // v.shape[3], v.shape[3]), jnp.float32)],
        input_output_aliases={6: 0},
        compiler_params=params(v.size * 4, 8),
        cost_estimate=pl.CostEstimate(flops=2 * v.size * LANES, bytes_accessed=16 * v.size, transcendentals=0),
    )(me, taps, v, op, core, mirror, n)


def late_kernel(me_ref, tap_ref, v_ref, chip_ref, n_in_ref, n_ref):
    even = me_ref[0] % 2 == 0
    add = functools.partial(add_side, tap_ref, v_ref, chip_ref, n_in_ref, n_ref)
    pl.when(even)(lambda: add(True))
    pl.when(jnp.logical_not(even))(lambda: add(False))


def late_terms(me, taps, v, chip, n):
    return pl.pallas_call(
        late_kernel,
        name="late_terms",
        out_shape=held(*v.shape),
        in_specs=[SMEM, VMEM, VMEM, VMEM, VMEM],
        out_specs=VMEM,
        input_output_aliases={4: 0},
        compiler_params=params(v.size * 4, 5),
        cost_estimate=pl.CostEstimate(flops=20 * v.size, bytes_accessed=12 * v.size, transcendentals=0),
    )(me, taps, v, chip, n)


def planes_kernel(me_ref, v_ref, y_ref, power_ref, n_in_ref, n_ref, keep_ref, send_ref, tile_ref, ends_ref):
    comps, points, planes, radial = v_ref.shape
    carriers = y_ref.shape[1]
    lo, hi = AXIAL_REACH, planes - AXIAL_REACH
    weights = axial_weights(planes, False)
    for c in range(comps):
        for j in range(points - carriers):
            tile_ref[c, j, 0:2] = y_ref[c, 3 * j, lo:hi]
            tile_ref[c, j, 2:3] = y_ref[c, 3 * j + 1, lo : lo + 1]
            tile_ref[c, j, lo:hi] = jnp.zeros((hi - lo, radial), jnp.float32)
            tile_ref[c, j, hi : hi + 1] = y_ref[c, 3 * j + 1, lo + 1 : hi]
            tile_ref[c, j, hi + 1 :] = y_ref[c, 3 * j + 2, lo:hi]

    @pl.loop(0, radial // LANES)
    def column(k):
        lanes = pl.ds(pl.multiple_of(k * LANES, LANES), LANES)
        decay = power_ref[1:2, lanes]
        for c in range(comps):
            low = high = None
            for t in range(points):
                tile = y_ref[c, t, :, lanes] if t < carriers else tile_ref[c, t - carriers, :, lanes]
                n = n_in_ref[c, t, :, lanes] + v_ref[2, t, :, lanes] * axial_part(tile, weights)
                n_ref[c, t, :, lanes] = n
                right_side = v_ref[c, t, :, lanes] - STEP_WEIGHT * n
                low = right_side if t == 0 else decay * low + right_side
                high = right_side if t == 0 else high + power_ref[t : t + 1, lanes] * right_side
            ends_ref[0, c, :, lanes] = low
            ends_ref[1, c, :, lanes] = high

    half = radial // 2
    core = me_ref[0] % 2
    keep_ref[...] = ends_ref[:, :, :, pl.ds(pl.multiple_of(core * half, half), half)]
    send_ref[...] = ends_ref[:, :, :, pl.ds(pl.multiple_of((1 - core) * half, half), half)]


def planes_terms(me, v, y, power, n):
    comps, points, planes, radial = v.shape
    part = held(2, comps, planes, radial // 2)
    return pl.pallas_call(
        planes_kernel,
        name="planes_terms",
        out_shape=(held(*v.shape), part, part),
        in_specs=[SMEM] + [VMEM] * 4,
        out_specs=(VMEM, VMEM, VMEM),
        scratch_shapes=[
            pltpu.VMEM((comps, points - y.shape[1], planes, radial), jnp.float32),
            pltpu.VMEM((2, comps, planes, radial), jnp.float32),
        ],
        input_output_aliases={4: 0},
        compiler_params=params(v.size * 4, 6),
        cost_estimate=pl.CostEstimate(flops=20 * v.size, bytes_accessed=16 * v.size, transcendentals=0),
    )(me, v, y, power, n)


def table_kernel(me_ref, factor_ref, stencil_ref, row_ref, tap_ref, *, points, sectors):
    radial = row_ref.shape[1]
    one = jnp.ones((1, radial), jnp.float32)
    half = (0.5 * lax.rsqrt(factor_ref[0] * one)) / inverse_radius(radial)
    root = jnp.sqrt(1.0 + half * half)
    loss = 2.0 * half * (root - half)
    rows = [one]
    for _ in range(points):
        rows.append(rows[-1] * (1.0 - loss))
    total = loss
    left, result = points * sectors, None
    while left:
        if left & 1:
            result = total if result is None else result + total - result * total
        total = total * (2.0 - total)
        left >>= 1
    across = rows[points] * rows[points]
    rows += [half / root, 1.0 / result]
    before = after = one
    for bit in range(1, sectors.bit_length() - 1):
        upper = (me_ref[0] >> bit) % 2 == 1
        rows += [across, before, after]
        before, after = jnp.where(upper, before * across, before), jnp.where(upper, after, after * across)
        across = across * across
    for k, row in enumerate(rows + [before, after]):
        row_ref[k : k + 1] = row
    for k in range(tap_ref.shape[0]):
        tap_ref[k] = jnp.full(tap_ref.shape[1:], stencil_ref[k], jnp.float32)


def table(me, viscous_factor, stencil, points, sectors, planes, radial):
    count = points + 5 + 3 * (sectors.bit_length() - 2)
    return pl.pallas_call(
        functools.partial(table_kernel, points=points, sectors=sectors),
        name="table",
        out_shape=(held(count, radial), held(stencil.shape[0], planes, LANES)),
        in_specs=[SMEM, SMEM, SMEM],
        out_specs=(VMEM, VMEM),
        compiler_params=params(1 << 20, 1),
        cost_estimate=pl.CostEstimate(flops=1000 * radial, bytes_accessed=400 * radial, transcendentals=0),
    )(me, viscous_factor, stencil)


def sweep_kernel(v_ref, n_ref, power_ref, s_ref, nonlinear_ref, sem):
    leave = pltpu.make_async_copy(n_ref, nonlinear_ref, sem)
    leave.start()
    comps, points, planes, radial = v_ref.shape
    decay = power_ref[1:2]
    height = power_ref[points + 1 : points + 2]
    for c in range(comps):
        s_ref[c, 0] = height * (v_ref[c, 0] - STEP_WEIGHT * n_ref[c, 0])

        def forward(i):
            t = i + 1
            s_ref[c, t] = decay * s_ref[c, t - 1] + height * (v_ref[c, t] - STEP_WEIGHT * n_ref[c, t])

        each(points - 1, forward)

    def backward(i, carry):
        t = points - 1 - i
        after = []
        for c in range(comps):
            s_ref[c, t] = s_ref[c, t] + carry[c]
            after.append(decay * (carry[c] + height * (v_ref[c, t] - STEP_WEIGHT * n_ref[c, t])))
        return tuple(after)

    start = (jnp.zeros((planes, radial), jnp.float32),) * comps
    lax.fori_loop(0, points, backward, start, unroll=points <= UNROLL)
    leave.wait()


def sweep(v, n, power):
    return pl.pallas_call(
        sweep_kernel,
        name="sweep",
        out_shape=(held(*v.shape), jax.ShapeDtypeStruct(v.shape, v.dtype)),
        in_specs=[VMEM] * 3,
        out_specs=(VMEM, ANY),
        scratch_shapes=[pltpu.SemaphoreType.DMA],
        compiler_params=params(v.size * 4, 4),
        cost_estimate=pl.CostEstimate(flops=10 * v.size, bytes_accessed=12 * v.size, transcendentals=0),
    )(v, n, power)


def my_lanes(me_ref, radial, half):
    core = me_ref[0] % 2
    return pl.ds(pl.multiple_of(core * half, half), half)


def pair_kernel(me_ref, power_ref, own_ref, other_ref, block_ref, *, points):
    half = own_ref.shape[3]
    hop = power_ref[points : points + 1, my_lanes(me_ref, power_ref.shape[1], half)]
    odd = me_ref[0] % 2 == 1
    for c in range(own_ref.shape[1]):
        for side in range(2):
            own, other = own_ref[side, c], other_ref[side, c]
            far, near = (own, other) if side == 0 else (other, own)
            block_ref[side, c] = jnp.where(odd, hop * near + far, hop * far + near)


def pair(me, power, own, other, points):
    return pl.pallas_call(
        functools.partial(pair_kernel, points=points),
        name="pair",
        out_shape=held(*own.shape),
        in_specs=[SMEM, VMEM, VMEM, VMEM],
        out_specs=VMEM,
        compiler_params=params(own.size * 4, 8),
    )(me, power, own, other)


def merge_kernel(me_ref, power_ref, block_ref, other_ref, *refs, points, bit):
    *entry_refs, block_out_ref, entry_out_ref = refs
    comps, half = block_ref.shape[1], block_ref.shape[3]
    lanes = my_lanes(me_ref, power_ref.shape[1], half)
    first = points + 3 * bit
    across, before, after = [power_ref[first + k : first + k + 1, lanes] for k in range(3)]
    upper = (me_ref[0] >> bit) % 2 == 1
    before = jnp.where(upper, before, 0.0)
    after = jnp.where(upper, 0.0, after)
    for c in range(comps):
        low, high = block_ref[0, c], block_ref[1, c]
        other_low, other_high = other_ref[0, c], other_ref[1, c]
        block_out_ref[0, c] = jnp.where(upper, across * other_low + low, across * low + other_low)
        block_out_ref[1, c] = jnp.where(upper, other_high + across * high, high + across * other_high)
        for side, enters in enumerate((before * other_low, after * other_high)):
            entry_out_ref[side, c] = entry_refs[0][side, c] + enters if entry_refs else enters


def merge(me, power, block, other, entries, points, bit):
    return pl.pallas_call(
        functools.partial(merge_kernel, points=points, bit=bit),
        name="merge",
        out_shape=(held(*block.shape), held(*block.shape)),
        in_specs=[SMEM] + [VMEM] * (3 + len(entries)),
        out_specs=(VMEM, VMEM),
        compiler_params=params(block.size * 4, 8),
    )(me, power, block, other, *entries)


def enter_kernel(me_ref, power_ref, block_ref, entry_ref, own_ref, other_ref, ready_ref, mine_ref, send_ref, *, points):
    comps, half = block_ref.shape[1], block_ref.shape[3]
    lanes = my_lanes(me_ref, power_ref.shape[1], half)
    row = lambda k: power_ref[k : k + 1, lanes]
    hop, height, wrap = row(points), row(points + 1), row(points + 2)
    last = power_ref.shape[0]
    before, after = row(last - 2) * wrap, row(last - 1) * wrap
    odd = me_ref[0] % 2 == 1
    for c in range(comps):
        low = height * (entry_ref[0, c] + before * block_ref[0, c])
        high = height * (entry_ref[1, c] + after * block_ref[1, c])
        even_low = height * jnp.where(odd, other_ref[0, c], own_ref[0, c])
        odd_high = height * jnp.where(odd, own_ref[1, c], other_ref[1, c])
        even_in = (low, odd_high + hop * high)
        odd_in = (even_low + hop * low, high)
        for side in range(2):
            mine_ref[side, c] = jnp.where(odd, odd_in[side], even_in[side])
            send_ref[side, c] = jnp.where(odd, even_in[side], odd_in[side])


def enter(me, power, block, entry, own, other, ready, points):
    return pl.pallas_call(
        functools.partial(enter_kernel, points=points),
        name="enter",
        out_shape=(held(*block.shape), held(*block.shape)),
        in_specs=[SMEM] + [VMEM] * 5 + [ANY],
        out_specs=(VMEM, VMEM),
        compiler_params=params(block.size * 4, 12),
    )(me, power, block, entry, own, other, ready)


def close_kernel(me_ref, s_ref, power_ref, mine_ref, got_ref, out_ref, x_ref, both_ref, sems):
    comps, points, planes, radial = s_ref.shape
    half = mine_ref.shape[3]
    core = me_ref[0] % 2
    both_ref[:, :, :, pl.ds(pl.multiple_of(core * half, half), half)] = mine_ref[...]
    both_ref[:, :, :, pl.ds(pl.multiple_of((1 - core) * half, half), half)] = got_ref[...]
    leaves = []
    for c in range(comps):
        before, after = both_ref[0, c], both_ref[1, c]

        def point(t):
            x_ref[c, t] = s_ref[c, t] + power_ref[pl.ds(t + 1, 1)] * before + power_ref[pl.ds(points - t, 1)] * after

        each(points, point)
        leaves.append(pltpu.make_async_copy(x_ref.at[c], out_ref.at[c], sems.at[c]))
        leaves[c].start()
    for leave in leaves:
        leave.wait()


def close(me, s, power, mine, got):
    return pl.pallas_call(
        close_kernel,
        name="close",
        out_shape=jax.ShapeDtypeStruct(s.shape, s.dtype),
        in_specs=[SMEM] + [VMEM] * 4,
        out_specs=ANY,
        scratch_shapes=[
            pltpu.VMEM(s.shape, jnp.float32),
            pltpu.VMEM((2,) + s.shape[:1] + s.shape[2:], jnp.float32),
            pltpu.SemaphoreType.DMA((s.shape[0],)),
        ],
        compiler_params=params(s.size * 4, 5),
    )(me, s, power, mine, got)


def local(velocity, radial_op, azimuth_stencil, viscous_factor):
    sectors = lax.axis_size("theta")
    comps, points, planes, radial = velocity.shape
    reach = (azimuth_stencil.shape[0] - 1) // 2
    width = radial_op.shape[1] - radial
    me = lax.axis_index("theta").astype(jnp.int32).reshape(1)
    op = radial_op.T

    velocity, planes_out = load(pltpu.with_memory_space_constraint(velocity, pltpu.HBM))
    planes_in = swap(planes_out, "gz", 1)
    chip_out = pack_side(me, velocity, planes_out, reach, False)
    chip_in = swap_across(chip_out, "theta")
    mirror_out = pack_mirror(velocity, chip_out, width)
    mirror_in = swap(mirror_out, "theta", sectors // 2)
    core_out = pack_side(me, velocity, mirror_out, reach, True)
    core_in = swap(core_out, "theta", 1)
    power, taps = table(me, viscous_factor, azimuth_stencil, points, sectors, planes, radial)
    n = inner_terms(taps, velocity, op)
    n = early_terms(me, taps, velocity, op, core_in, mirror_in, n)
    n = late_terms(me, taps, velocity, chip_in, n)
    n, own, send = planes_terms(me, velocity, planes_in, power, n)
    other = swap(send, "theta", 1)
    s, nonlinear = sweep(velocity, n, power)
    block = pair(me, power, own, other, points)
    entries = ()
    for bit in range(1, sectors.bit_length() - 1):
        block, entry = merge(me, power, block, swap(block, "theta", 1 << bit), entries, points, bit)
        entries = (entry,)
    mine, send = enter(me, power, block, entry, own, other, s, points)
    new_velocity = close(me, s, power, mine, swap(send, "theta", 1))
    return (new_velocity, nonlinear)


def solution(mesh):
    in_specs = (P(None, "theta", "gz", None), P(), P(), P())
    out_specs = (P(None, "theta", "gz", None), P(None, "theta", "gz", None))
    return jax.shard_map(local, mesh=mesh, in_specs=in_specs, out_specs=out_specs, check_vma=False)
```

```python
import functools

import jax
import jax.numpy as jnp
from jax import lax
from jax.experimental import pallas as pl
from jax.experimental.pallas import tpu as pltpu
from jax.sharding import PartitionSpec as P

AXIAL_WEIGHTS = (0.75, -0.15, 1.0 / 60.0)
AXIAL_REACH = len(AXIAL_WEIGHTS)
STEP_WEIGHT = 0.2
MIRROR_SIGNS = (-1.0, -1.0, 1.0)
PIECES = ((0, 1), (2,))
LANES = 128
UNROLL = 16

VMEM = pl.BlockSpec(memory_space=pltpu.VMEM)
SMEM = pl.BlockSpec(memory_space=pltpu.SMEM)
ANY = pl.BlockSpec(memory_space=pl.ANY)
HBM = pl.BlockSpec(memory_space=pltpu.HBM)


def params(block_bytes, blocks):
    return pltpu.CompilerParams(vmem_limit_bytes=(2 << 20) + blocks * block_bytes)


def held(*shape):
    return pltpu.VMEM(shape, jnp.float32)


def each(count, body):
    if count <= UNROLL:
        for i in range(count):
            body(i)
    else:
        pl.loop(0, count)(body)


def swap(block, axis, bit):
    size = lax.axis_size(axis)
    return lax.ppermute(block, axis, [(i, i ^ bit) for i in range(size)])


def swap_across(block, axis):
    size = lax.axis_size(axis)
    route = []
    for odd in range(1, size, 2):
        route += [(odd, (odd + 1) % size), ((odd + 1) % size, odd)]
    return lax.ppermute(block, axis, route)


def split(x):
    high = x.astype(jnp.bfloat16)
    return high, (x - high.astype(jnp.float32)).astype(jnp.bfloat16)


def product(left, right):
    dot = functools.partial(jnp.dot, preferred_element_type=jnp.float32)
    return dot(left[0], right[0]) + (dot(left[0], right[1]) + dot(left[1], right[0]))


def load_kernel(hbm_ref, v_ref, *refs):
    *y_refs, sems = refs
    comps, points, planes, _ = v_ref.shape
    carriers = y_refs[0].shape[1]
    lo, hi = AXIAL_REACH, planes - AXIAL_REACH
    loads = [pltpu.make_async_copy(hbm_ref.at[c], v_ref.at[c], sems.at[c]) for c in range(comps)]
    for load in loads:
        load.start()
    for y_ref, piece in zip(y_refs, PIECES):
        for i, c in enumerate(piece):
            loads[c].wait()

            def carry(t):
                y_ref[i, t] = v_ref[c, t]

            def ride(j):
                t = carriers + j
                y_ref[i, 3 * j, lo:hi] = v_ref[c, t, 0:2]
                y_ref[i, 3 * j + 1, lo : lo + 1] = v_ref[c, t, 2:3]
                y_ref[i, 3 * j + 1, lo + 1 : hi] = v_ref[c, t, hi : hi + 1]
                y_ref[i, 3 * j + 2, lo:hi] = v_ref[c, t, hi + 1 :]

            each(carriers, carry)
            each(points - carriers, ride)


def load(v):
    comps, points, planes, radial = v.shape
    sent = [held(len(piece), points - points // 4, planes, radial) for piece in PIECES]
    return pl.pallas_call(
        load_kernel,
        name="load",
        out_shape=(held(*v.shape), *sent),
        in_specs=[HBM],
        out_specs=(VMEM,) * (1 + len(sent)),
        scratch_shapes=[pltpu.SemaphoreType.DMA((comps,))],
        compiler_params=params(v.size * 4, 2),
    )(v)


def pack_side_kernel(me_ref, v_ref, first_ref, *side_refs, after, pieces):
    points, reach = v_ref.shape[1], side_refs[0].shape[1]

    def put(start):
        for side_ref, piece in zip(side_refs, pieces):
            for i, c in enumerate(piece):
                for h in range(reach):
                    side_ref[i, h] = v_ref[c, start + h]

    even = me_ref[0] % 2 == 0
    last = even if after else jnp.logical_not(even)
    pl.when(last)(lambda: put(points - reach))
    pl.when(jnp.logical_not(last))(lambda: put(0))


def pack_side(me, v, first, reach, after, pieces):
    comps, _, planes, radial = v.shape
    return pl.pallas_call(
        functools.partial(pack_side_kernel, after=after, pieces=pieces),
        name="pack_core" if after else "pack_chip",
        out_shape=tuple(held(len(piece), reach, planes, radial) for piece in pieces),
        in_specs=[SMEM, VMEM, ANY],
        out_specs=(VMEM,) * len(pieces),
        compiler_params=params(v.size * 4, 3),
    )(me, v, first)


def pack_mirror_kernel(v_ref, first_ref, mirror_ref):
    points, tiles = v_ref.shape[1], mirror_ref.shape[1]
    width = LANES // (points // tiles)
    lane = lax.broadcasted_iota(jnp.int32, mirror_ref.shape[2:], 1)

    def put(p):
        for c in range(v_ref.shape[0]):
            tile = v_ref[c, p, :, :LANES]
            for q in range(1, points // tiles):
                part = pltpu.roll(v_ref[c, q * tiles + p, :, :LANES], q * width, 1)
                tile = jnp.where(lane < q * width, tile, part)
            mirror_ref[c, p] = tile

    each(tiles, put)


def pack_mirror(v, first, width):
    comps, points, planes, _ = v.shape
    return pl.pallas_call(
        pack_mirror_kernel,
        name="pack_mirror",
        out_shape=held(comps, points // (LANES // width), planes, LANES),
        in_specs=[VMEM, ANY],
        out_specs=VMEM,
        compiler_params=params(v.size * 4, 2),
    )(v, first)


def inverse_radius(radial, start=0):
    return 1.0 / ((lax.broadcasted_iota(jnp.int32, (1, radial), 1) + start).astype(jnp.float32) + 0.5)


def axial_weights(planes, inside):
    row = lax.broadcasted_iota(jnp.int32, (planes, LANES), 0)
    weights = []
    for m, w in enumerate(AXIAL_WEIGHTS, 1):
        for shift, own, sign in ((m, row < planes - m, 1.0), (planes - m, row >= m, -1.0)):
            keep = own if inside else jnp.logical_not(own)
            weights.append((shift, jnp.where(keep, sign * w, 0.0)))
    return weights


def axial_part(tile, weights):
    planes, width = tile.shape
    weights = [(shift, jnp.concatenate([weight] * (width // LANES), axis=1)) for shift, weight in weights]
    total = None
    for shift, weight in weights:
        term = weight * pltpu.roll(tile, planes - shift, 0)
        total = term if total is None else total + term
    return total


def inner_kernel(tap_ref, v_ref, op_ref, n_ref, grad_ref):
    comps, points, planes, radial = v_ref.shape
    reach = (tap_ref.shape[0] - 1) // 2
    rows = points * planes
    right = split(op_ref[:radial])
    for c in range(comps):
        grad_ref[c * rows : (c + 1) * rows] = product(split(v_ref[c].reshape(rows, radial)), right)
    weights = axial_weights(planes, True)

    @pl.loop(0, radial // LANES)
    def column(k):
        lanes = pl.ds(pl.multiple_of(k * LANES, LANES), LANES)
        inv_r = inverse_radius(LANES, k * LANES)
        for c in range(comps):
            for t in range(points):
                a, b, e = [v_ref[i, t, :, lanes] for i in range(3)]
                b_inv = b * inv_r
                around = None
                for m in range(max(-reach, -t), min(reach, points - 1 - t) + 1):
                    term = tap_ref[m + reach] * v_ref[c, t + m, :, lanes]
                    around = term if around is None else around + term
                start = c * rows + t * planes
                n = a * grad_ref[start : start + planes, lanes] + b_inv * around
                n = n + e * axial_part(v_ref[c, t, :, lanes], weights)
                if c == 0:
                    n = n - b_inv * b
                elif c == 1:
                    n = n + a * b_inv
                n_ref[c, t, :, lanes] = n


def inner_terms(taps, v, op):
    return pl.pallas_call(
        inner_kernel,
        name="inner_terms",
        out_shape=held(*v.shape),
        in_specs=[VMEM, VMEM, VMEM],
        out_specs=VMEM,
        scratch_shapes=[pltpu.VMEM((v.size // v.shape[3], v.shape[3]), jnp.float32)],
        compiler_params=params(v.size * 4, 6),
        cost_estimate=pl.CostEstimate(flops=6 * v.size * v.shape[3], bytes_accessed=16 * v.size, transcendentals=0),
    )(taps, v, op)


def add_side(tap_ref, v_ref, side_ref, n_in_ref, n_ref, before, piece):
    comps, points, _, radial = v_ref.shape
    reach = side_ref.shape[1]
    first = 0 if before else reach + 1

    @pl.loop(0, radial // LANES)
    def column(k):
        lanes = pl.ds(pl.multiple_of(k * LANES, LANES), LANES)
        inv_r = inverse_radius(LANES, k * LANES)
        weights = [tap_ref[first + i] for i in range(reach)]
        for i, c in enumerate(piece):
            side = [side_ref[i, h, :, lanes] for h in range(reach)]
            for u in range(reach):
                t = u if before else points - reach + u
                taps = [(h, h - u) for h in range(u, reach)] if before else [(h, reach - 1 + h - u) for h in range(u + 1)]
                around = None
                for h, w in taps:
                    term = weights[w] * side[h]
                    around = term if around is None else around + term
                n_ref[i, t, :, lanes] = n_in_ref[c, t, :, lanes] + v_ref[1, t, :, lanes] * inv_r * around


def early_kernel(me_ref, tap_ref, v_ref, op_ref, core_ref, mirror_ref, n_in_ref, n_ref, grad_ref):
    comps, points, planes, radial = v_ref.shape
    tiles = mirror_ref.shape[1]
    count = points // tiles
    width = LANES // count
    rows = tiles * planes
    right = split(jnp.concatenate([op_ref[radial:]] * count, axis=0))
    lane = lax.broadcasted_iota(jnp.int32, (rows, LANES), 1)
    for c in range(comps):
        high, low = split(MIRROR_SIGNS[c] * mirror_ref[c].reshape(rows, LANES))
        zero = jnp.zeros_like(high)
        parts = [
            [jnp.where((lane >= q * width) & (lane < (q + 1) * width), x, zero) for q in range(count)]
            for x in (high, low)
        ]
        left = [jnp.concatenate(x, axis=0) for x in parts]
        grad_ref[c * points * planes : (c + 1) * points * planes] = product(left, right)

    def finish(t):
        for c in range(comps):
            start = pl.multiple_of((c * points + t) * planes, planes)
            n_ref[c, t] = n_in_ref[c, t] + v_ref[0, t] * grad_ref[pl.ds(start, planes)]

    each(points, finish)
    even = me_ref[0] % 2 == 0
    add = functools.partial(add_side, tap_ref, v_ref, core_ref, n_ref, n_ref, piece=range(comps))
    pl.when(even)(lambda: add(before=False))
    pl.when(jnp.logical_not(even))(lambda: add(before=True))


def early_terms(me, taps, v, op, core, mirror, n):
    return pl.pallas_call(
        early_kernel,
        name="early_terms",
        out_shape=held(*v.shape),
        in_specs=[SMEM, VMEM, VMEM, VMEM, VMEM, VMEM, VMEM],
        out_specs=VMEM,
        scratch_shapes=[pltpu.VMEM((v.size // v.shape[3], v.shape[3]), jnp.float32)],
        input_output_aliases={6: 0},
        compiler_params=params(v.size * 4, 8),
        cost_estimate=pl.CostEstimate(flops=2 * v.size * LANES, bytes_accessed=16 * v.size, transcendentals=0),
    )(me, taps, v, op, core, mirror, n)


def late_kernel(me_ref, tap_ref, v_ref, chip_ref, n_in_ref, n_ref, *, piece):
    points, reach = v_ref.shape[1], chip_ref.shape[1]

    def add(before):
        add_side(tap_ref, v_ref, chip_ref, n_in_ref, n_ref, before, piece)
        for i, c in enumerate(piece):
            for t in range(reach, points) if before else range(points - reach):
                n_ref[i, t] = n_in_ref[c, t]

    even = me_ref[0] % 2 == 0
    pl.when(even)(lambda: add(True))
    pl.when(jnp.logical_not(even))(lambda: add(False))


def late_terms(me, taps, v, chip, n, piece):
    return pl.pallas_call(
        functools.partial(late_kernel, piece=piece),
        name="late_terms",
        out_shape=held(len(piece), *v.shape[1:]),
        in_specs=[SMEM, VMEM, VMEM, VMEM, VMEM],
        out_specs=VMEM,
        compiler_params=params(v.size * 4, 5),
        cost_estimate=pl.CostEstimate(flops=20 * v.size, bytes_accessed=12 * v.size, transcendentals=0),
    )(me, taps, v, chip, n)


def planes_kernel(v_ref, y_ref, row_ref, n_in_ref, n_ref, ends_ref, tile_ref, *, piece):
    comps, points, planes, radial = v_ref.shape
    carriers = y_ref.shape[1]
    lo, hi = AXIAL_REACH, planes - AXIAL_REACH
    weights = axial_weights(planes, False)
    decay = row_ref[1:2]
    for i in range(len(piece)):
        for j in range(points - carriers):
            tile_ref[i, j, 0:2] = y_ref[i, 3 * j, lo:hi]
            tile_ref[i, j, 2:3] = y_ref[i, 3 * j + 1, lo : lo + 1]
            tile_ref[i, j, lo:hi] = jnp.zeros((hi - lo, radial), jnp.float32)
            tile_ref[i, j, hi : hi + 1] = y_ref[i, 3 * j + 1, lo + 1 : hi]
            tile_ref[i, j, hi + 1 :] = y_ref[i, 3 * j + 2, lo:hi]
        ends_ref[0, i] = jnp.zeros((planes, radial), jnp.float32)
        ends_ref[1, i] = jnp.zeros((planes, radial), jnp.float32)

    def finish(t):
        for i, c in enumerate(piece):
            tile = y_ref[i, t] if t < carriers else tile_ref[i, t - carriers]
            n = n_in_ref[i, t] + v_ref[2, t] * axial_part(tile, weights)
            n_ref[i, t] = n
            right_side = v_ref[c, t] - STEP_WEIGHT * n
            ends_ref[0, i] = decay * ends_ref[0, i] + right_side
            ends_ref[1, i] = ends_ref[1, i] + row_ref[t : t + 1] * right_side

    for t in range(points):
        finish(t)


def planes_terms(v, y, rows, n, piece):
    comps, points, planes, radial = v.shape
    return pl.pallas_call(
        functools.partial(planes_kernel, piece=piece),
        name="planes_terms",
        out_shape=(held(*n.shape), held(2, len(piece), planes, radial)),
        in_specs=[VMEM] * 4,
        out_specs=(VMEM, VMEM),
        scratch_shapes=[pltpu.VMEM((len(piece), points - y.shape[1], planes, radial), jnp.float32)],
        input_output_aliases={3: 0},
        compiler_params=params(v.size * 4, 6),
        cost_estimate=pl.CostEstimate(flops=20 * v.size, bytes_accessed=16 * v.size, transcendentals=0),
    )(v, y, rows, n)


def stages(sectors):
    bits = sectors.bit_length() - 1
    return [(bit, 1 << min(2, bits - bit)) for bit in range(0, bits, 2)]


def stage_rows(points, sectors):
    first, found = points + 2, []
    for _, group in stages(sectors):
        found.append(first)
        first += 4 * group
    return found, first


def table_kernel(me_ref, factor_ref, stencil_ref, row_ref, tap_ref, *, points, sectors):
    radial = row_ref.shape[1]
    one = jnp.ones((1, radial), jnp.float32)
    half = (0.5 * lax.rsqrt(factor_ref[0] * one)) / inverse_radius(radial)
    root = jnp.sqrt(1.0 + half * half)
    loss = 2.0 * half * (root - half)
    rows = [one]
    for _ in range(points):
        rows.append(rows[-1] * (1.0 - loss))
    total = loss
    left, result = points * sectors, None
    while left:
        if left & 1:
            result = total if result is None else result + total - result * total
        total = total * (2.0 - total)
        left >>= 1
    height, wrap = half / root, 1.0 / result
    across = rows[points]
    rows.append(height)
    before = after = one

    def pick(index, choices):
        found = choices[-1]
        for k in range(len(choices) - 2, -1, -1):
            found = jnp.where(index == k, choices[k], found)
        return found

    for bit, group in stages(sectors):
        place = lax.rem(lax.div(me_ref[0], 1 << bit), group)
        powers = [one]
        for _ in range(group):
            powers.append(powers[-1] * across)
        kinds = [[], [], [], []]
        for x in range(group):
            other = place ^ x
            kinds[0].append(pick(group - 1 - other, powers[:group]))
            kinds[1].append(pick(other, powers[:group]))
            kinds[2].append(before * jnp.where(other < place, pick(place - 1 - other, powers[:group]), 0.0))
            kinds[3].append(after * jnp.where(other > place, pick(other - place - 1, powers[:group]), 0.0))
        before = before * pick(place, powers[:group])
        after = after * pick(group - 1 - place, powers[:group])
        across = powers[group]
        if 1 << bit == sectors // group:
            for x in range(group):
                kinds[2][x] = height * (kinds[2][x] + before * wrap * kinds[0][x])
                kinds[3][x] = height * (kinds[3][x] + after * wrap * kinds[1][x])
        for kind in kinds:
            rows += kind
    for k, row in enumerate(rows):
        row_ref[k : k + 1] = row
    for k in range(tap_ref.shape[0]):
        tap_ref[k] = jnp.full(tap_ref.shape[1:], stencil_ref[k], jnp.float32)


def table(me, viscous_factor, stencil, points, sectors, planes, radial):
    return pl.pallas_call(
        functools.partial(table_kernel, points=points, sectors=sectors),
        name="table",
        out_shape=(held(stage_rows(points, sectors)[1], radial), held(stencil.shape[0], planes, LANES)),
        in_specs=[SMEM, SMEM, SMEM],
        out_specs=(VMEM, VMEM),
        compiler_params=params(1 << 20, 1),
        cost_estimate=pl.CostEstimate(flops=1000 * radial, bytes_accessed=400 * radial, transcendentals=0),
    )(me, viscous_factor, stencil)


def sweep_kernel(v_ref, n_ref, row_ref, *refs, piece):
    s_ref, out_ref, sem = refs[-3:]
    leave = pltpu.make_async_copy(n_ref, out_ref.at[pl.ds(piece[0], len(piece))], sem)
    leave.start()
    _, points, planes, radial = v_ref.shape
    decay = row_ref[1:2]
    height = row_ref[points + 1 : points + 2]
    for i, c in enumerate(piece):
        s_ref[i, 0] = height * (v_ref[c, 0] - STEP_WEIGHT * n_ref[i, 0])

        def forward(k):
            t = k + 1
            s_ref[i, t] = decay * s_ref[i, t - 1] + height * (v_ref[c, t] - STEP_WEIGHT * n_ref[i, t])

        each(points - 1, forward)

    def backward(k, carry):
        t = points - 1 - k
        after = []
        for i, c in enumerate(piece):
            s_ref[i, t] = s_ref[i, t] + carry[i]
            after.append(decay * (carry[i] + height * (v_ref[c, t] - STEP_WEIGHT * n_ref[i, t])))
        return tuple(after)

    start = (jnp.zeros((planes, radial), jnp.float32),) * len(piece)
    lax.fori_loop(0, points, backward, start, unroll=points <= UNROLL)
    leave.wait()


def sweep(v, n, rows, out, piece):
    return pl.pallas_call(
        functools.partial(sweep_kernel, piece=piece),
        name="sweep",
        out_shape=(held(*n.shape), jax.ShapeDtypeStruct(v.shape, v.dtype)),
        in_specs=[VMEM] * 3 + [ANY] * len(out),
        out_specs=(VMEM, ANY),
        scratch_shapes=[pltpu.SemaphoreType.DMA],
        input_output_aliases={3: 1} if out else {},
        compiler_params=params(v.size * 4, 4),
        cost_estimate=pl.CostEstimate(flops=10 * v.size, bytes_accessed=12 * v.size, transcendentals=0),
    )(v, n, rows, *out)


def weighted(row_ref, first, refs, side, c):
    total = None
    for x, ref in enumerate(refs):
        term = row_ref[first + x : first + x + 1] * ref[side, c]
        total = term if total is None else total + term
    return total


def merge_kernel(row_ref, *refs, first, group):
    blocks, entries, (block_ref, entry_ref) = refs[:group], refs[group:-2], refs[-2:]
    for side in range(2):
        for c in range(block_ref.shape[1]):
            block_ref[side, c] = weighted(row_ref, first + side * group, blocks, side, c)
            enters = weighted(row_ref, first + (2 + side) * group, blocks, side, c)
            entry_ref[side, c] = entries[0][side, c] + enters if entries else enters


def merge(rows, blocks, entries, first):
    return pl.pallas_call(
        functools.partial(merge_kernel, first=first, group=len(blocks)),
        name="merge",
        out_shape=(held(*blocks[0].shape),) * 2,
        in_specs=[VMEM] * (1 + len(blocks) + len(entries)),
        out_specs=(VMEM, VMEM),
        compiler_params=params(blocks[0].size * 4, 8),
    )(rows, *blocks, *entries)


def close_kernel(s_ref, row_ref, *refs, first, group, piece, chained):
    blocks, entries = refs[:group], refs[group : -4 - chained]
    out_ref, x_ref, both_ref, sems = refs[-4:]
    count, points, _, _ = s_ref.shape
    height = row_ref[points + 1 : points + 2]
    leaves = []
    for i in range(count):
        for side in range(2):
            enters = weighted(row_ref, first + (2 + side) * group, blocks, side, i)
            both_ref[side, i] = enters + height * entries[0][side, i] if entries else enters
        before, after = both_ref[0, i], both_ref[1, i]

        def point(t):
            x_ref[i, t] = s_ref[i, t] + row_ref[pl.ds(t + 1, 1)] * before + row_ref[pl.ds(points - t, 1)] * after

        each(points, point)
        leaves.append(pltpu.make_async_copy(x_ref.at[i], out_ref.at[piece[i]], sems.at[i]))
        leaves[i].start()
    for leave in leaves:
        leave.wait()


def close(s, rows, blocks, entries, out, shape, first, piece):
    return pl.pallas_call(
        functools.partial(close_kernel, first=first, group=len(blocks), piece=piece, chained=len(out)),
        name="close",
        out_shape=jax.ShapeDtypeStruct(shape, s.dtype),
        in_specs=[VMEM] * (2 + len(blocks) + len(entries)) + [ANY] * len(out),
        out_specs=ANY,
        scratch_shapes=[
            pltpu.VMEM(s.shape, jnp.float32),
            pltpu.VMEM(blocks[0].shape, jnp.float32),
            pltpu.SemaphoreType.DMA((len(piece),)),
        ],
        input_output_aliases={2 + len(blocks) + len(entries): 0} if out else {},
        compiler_params=params(s.size * 4, 5),
    )(s, rows, *blocks, *entries, *out)


def local(velocity, radial_op, azimuth_stencil, viscous_factor):
    sectors = lax.axis_size("theta")
    comps, points, planes, radial = velocity.shape
    shape = velocity.shape
    reach = (azimuth_stencil.shape[0] - 1) // 2
    width = radial_op.shape[1] - radial
    me = lax.axis_index("theta").astype(jnp.int32).reshape(1)
    op = radial_op.T

    velocity, *planes_out = load(pltpu.with_memory_space_constraint(velocity, pltpu.HBM))
    chip_out = pack_side(me, velocity, planes_out[0], reach, False, PIECES)
    mirror_out = pack_mirror(velocity, chip_out[0], width)
    (core_out,) = pack_side(me, velocity, mirror_out, reach, True, (tuple(range(comps)),))
    planes_in, chip_in = [], []
    for k in range(len(PIECES)):
        planes_in.append(swap(planes_out[k], "gz", 1))
        chip_in.append(swap_across(chip_out[k], "theta"))
    mirror_in = swap(mirror_out, "theta", sectors // 2)
    core_in = swap(core_out, "theta", 1)
    rows, taps = table(me, viscous_factor, azimuth_stencil, points, sectors, planes, radial)
    firsts, _ = stage_rows(points, sectors)
    n = inner_terms(taps, velocity, op)
    n = early_terms(me, taps, velocity, op, core_in, mirror_in, n)
    nonlinear, solved, parts = (), (), []
    for k, piece in enumerate(PIECES):
        part = late_terms(me, taps, velocity, chip_in[k], n, piece)
        part, block = planes_terms(velocity, planes_in[k], rows, part, piece)
        entries = ()
        for (bit, group), first in zip(stages(sectors), firsts):
            blocks = [block] + [swap(block, "theta", x << bit) for x in range(1, group)]
            if first != firsts[-1]:
                block, entry = merge(rows, blocks, entries, first)
                entries = (entry,)
        s, out = sweep(velocity, part, rows, nonlinear, piece)
        nonlinear = (out,)
        parts.append((s, blocks, entries))
    for (s, blocks, entries), piece in zip(parts, PIECES):
        solved = (close(s, rows, blocks, entries, solved, shape, firsts[-1], piece),)
    return (solved[0], nonlinear[0])


def solution(mesh):
    in_specs = (P(None, "theta", "gz", None), P(), P(), P())
    out_specs = (P(None, "theta", "gz", None), P(None, "theta", "gz", None))
    return jax.shard_map(local, mesh=mesh, in_specs=in_specs, out_specs=out_specs, check_vma=False)
```

```python
import functools

import jax
import jax.numpy as jnp
from jax import lax
from jax.experimental import pallas as pl
from jax.experimental.pallas import tpu as pltpu
from jax.sharding import PartitionSpec as P

AXIAL_WEIGHTS = (0.75, -0.15, 1.0 / 60.0)
AXIAL_REACH = len(AXIAL_WEIGHTS)
STEP_WEIGHT = 0.2
MIRROR_SIGNS = (-1.0, -1.0, 1.0)
PIECES = ((0, 1), (2,))
LANES = 128
UNROLL = 16

VMEM = pl.BlockSpec(memory_space=pltpu.VMEM)
SMEM = pl.BlockSpec(memory_space=pltpu.SMEM)
ANY = pl.BlockSpec(memory_space=pl.ANY)
HBM = pl.BlockSpec(memory_space=pltpu.HBM)


def params(block_bytes, blocks):
    return pltpu.CompilerParams(vmem_limit_bytes=(2 << 20) + blocks * block_bytes)


def held(*shape):
    return pltpu.VMEM(shape, jnp.float32)


def each(count, body):
    if count <= UNROLL:
        for i in range(count):
            body(i)
    else:
        pl.loop(0, count)(body)


def swap(block, axis, bit):
    size = lax.axis_size(axis)
    return lax.ppermute(block, axis, [(i, i ^ bit) for i in range(size)])


def swap_across(block, axis):
    size = lax.axis_size(axis)
    route = []
    for odd in range(1, size, 2):
        route += [(odd, (odd + 1) % size), ((odd + 1) % size, odd)]
    return lax.ppermute(block, axis, route)


def split(x):
    high = x.astype(jnp.bfloat16)
    return high, (x - high.astype(jnp.float32)).astype(jnp.bfloat16)


def product(left, right):
    dot = functools.partial(jnp.dot, preferred_element_type=jnp.float32)
    return dot(left[0], right[0]) + (dot(left[0], right[1]) + dot(left[1], right[0]))


def load_kernel(hbm_ref, v_ref, *refs):
    *y_refs, sems = refs
    comps, points, planes, _ = v_ref.shape
    carriers = y_refs[0].shape[1]
    lo, hi = AXIAL_REACH, planes - AXIAL_REACH
    loads = [pltpu.make_async_copy(hbm_ref.at[c], v_ref.at[c], sems.at[c]) for c in range(comps)]
    for load in loads:
        load.start()
    for y_ref, piece in zip(y_refs, PIECES):
        for i, c in enumerate(piece):
            loads[c].wait()

            def carry(t):
                y_ref[i, t] = v_ref[c, t]

            def ride(j):
                t = carriers + j
                y_ref[i, 3 * j, lo:hi] = v_ref[c, t, 0:2]
                y_ref[i, 3 * j + 1, lo : lo + 1] = v_ref[c, t, 2:3]
                y_ref[i, 3 * j + 1, lo + 1 : hi] = v_ref[c, t, hi : hi + 1]
                y_ref[i, 3 * j + 2, lo:hi] = v_ref[c, t, hi + 1 :]

            each(carriers, carry)
            each(points - carriers, ride)


def load(v):
    comps, points, planes, radial = v.shape
    sent = [held(len(piece), points - points // 4, planes, radial) for piece in PIECES]
    return pl.pallas_call(
        load_kernel,
        name="load",
        out_shape=(held(*v.shape), *sent),
        in_specs=[HBM],
        out_specs=(VMEM,) * (1 + len(sent)),
        scratch_shapes=[pltpu.SemaphoreType.DMA((comps,))],
        compiler_params=params(v.size * 4, 2),
    )(v)


def pack_side_kernel(me_ref, v_ref, first_ref, *side_refs, after, pieces):
    points, reach = v_ref.shape[1], side_refs[0].shape[1]

    def put(start):
        for side_ref, piece in zip(side_refs, pieces):
            for i, c in enumerate(piece):
                for h in range(reach):
                    side_ref[i, h] = v_ref[c, start + h]

    even = me_ref[0] % 2 == 0
    last = even if after else jnp.logical_not(even)
    pl.when(last)(lambda: put(points - reach))
    pl.when(jnp.logical_not(last))(lambda: put(0))


def pack_side(me, v, first, reach, after, pieces):
    comps, _, planes, radial = v.shape
    return pl.pallas_call(
        functools.partial(pack_side_kernel, after=after, pieces=pieces),
        name="pack_core" if after else "pack_chip",
        out_shape=tuple(held(len(piece), reach, planes, radial) for piece in pieces),
        in_specs=[SMEM, VMEM, ANY],
        out_specs=(VMEM,) * len(pieces),
        compiler_params=params(v.size * 4, 3),
    )(me, v, first)


def pack_mirror_kernel(v_ref, first_ref, mirror_ref):
    points, tiles = v_ref.shape[1], mirror_ref.shape[1]
    width = LANES // (points // tiles)
    lane = lax.broadcasted_iota(jnp.int32, mirror_ref.shape[2:], 1)

    def put(p):
        for c in range(v_ref.shape[0]):
            tile = v_ref[c, p, :, :LANES]
            for q in range(1, points // tiles):
                part = pltpu.roll(v_ref[c, q * tiles + p, :, :LANES], q * width, 1)
                tile = jnp.where(lane < q * width, tile, part)
            mirror_ref[c, p] = tile

    each(tiles, put)


def pack_mirror(v, first, width):
    comps, points, planes, _ = v.shape
    return pl.pallas_call(
        pack_mirror_kernel,
        name="pack_mirror",
        out_shape=held(comps, points // (LANES // width), planes, LANES),
        in_specs=[VMEM, ANY],
        out_specs=VMEM,
        compiler_params=params(v.size * 4, 2),
    )(v, first)


def inverse_radius(radial, start=0):
    return 1.0 / ((lax.broadcasted_iota(jnp.int32, (1, radial), 1) + start).astype(jnp.float32) + 0.5)


def axial_weights(planes, inside):
    row = lax.broadcasted_iota(jnp.int32, (planes, LANES), 0)
    weights = []
    for m, w in enumerate(AXIAL_WEIGHTS, 1):
        for shift, own, sign in ((m, row < planes - m, 1.0), (planes - m, row >= m, -1.0)):
            keep = own if inside else jnp.logical_not(own)
            weights.append((shift, jnp.where(keep, sign * w, 0.0)))
    return weights


def axial_part(tile, weights):
    planes, width = tile.shape
    weights = [(shift, jnp.concatenate([weight] * (width // LANES), axis=1)) for shift, weight in weights]
    total = None
    for shift, weight in weights:
        term = weight * pltpu.roll(tile, planes - shift, 0)
        total = term if total is None else total + term
    return total


def inner_kernel(me_ref, tap_ref, v_ref, op_ref, core_ref, n_ref, grad_ref):
    comps, points, planes, radial = v_ref.shape
    reach = (tap_ref.shape[0] - 1) // 2
    rows = points * planes
    right = split(op_ref[:radial])
    for c in range(comps):
        grad_ref[c * rows : (c + 1) * rows] = product(split(v_ref[c].reshape(rows, radial)), right)
    weights = axial_weights(planes, True)

    @pl.loop(0, radial // LANES)
    def column(k):
        lanes = pl.ds(pl.multiple_of(k * LANES, LANES), LANES)
        inv_r = inverse_radius(LANES, k * LANES)
        for c in range(comps):
            for t in range(points):
                a, b, e = [v_ref[i, t, :, lanes] for i in range(3)]
                b_inv = b * inv_r
                around = None
                for m in range(max(-reach, -t), min(reach, points - 1 - t) + 1):
                    term = tap_ref[m + reach] * v_ref[c, t + m, :, lanes]
                    around = term if around is None else around + term
                start = c * rows + t * planes
                n = a * grad_ref[start : start + planes, lanes] + b_inv * around
                n = n + e * axial_part(v_ref[c, t, :, lanes], weights)
                if c == 0:
                    n = n - b_inv * b
                elif c == 1:
                    n = n + a * b_inv
                n_ref[c, t, :, lanes] = n

    even = me_ref[0] % 2 == 0
    add = functools.partial(add_side, tap_ref, v_ref, core_ref, n_ref, n_ref, piece=range(comps))
    pl.when(even)(lambda: add(before=False))
    pl.when(jnp.logical_not(even))(lambda: add(before=True))


def inner_terms(me, taps, v, op, core):
    return pl.pallas_call(
        inner_kernel,
        name="inner_terms",
        out_shape=held(*v.shape),
        in_specs=[SMEM] + [VMEM] * 4,
        out_specs=VMEM,
        scratch_shapes=[pltpu.VMEM((v.size // v.shape[3], v.shape[3]), jnp.float32)],
        compiler_params=params(v.size * 4, 6),
        cost_estimate=pl.CostEstimate(flops=6 * v.size * v.shape[3], bytes_accessed=16 * v.size, transcendentals=0),
    )(me, taps, v, op, core)


def add_side(tap_ref, v_ref, side_ref, n_in_ref, n_ref, before, piece):
    comps, points, _, radial = v_ref.shape
    reach = side_ref.shape[1]
    first = 0 if before else reach + 1

    @pl.loop(0, radial // LANES)
    def column(k):
        lanes = pl.ds(pl.multiple_of(k * LANES, LANES), LANES)
        inv_r = inverse_radius(LANES, k * LANES)
        weights = [tap_ref[first + i] for i in range(reach)]
        for i, c in enumerate(piece):
            side = [side_ref[i, h, :, lanes] for h in range(reach)]
            for u in range(reach):
                t = u if before else points - reach + u
                taps = [(h, h - u) for h in range(u, reach)] if before else [(h, reach - 1 + h - u) for h in range(u + 1)]
                around = None
                for h, w in taps:
                    term = weights[w] * side[h]
                    around = term if around is None else around + term
                n_ref[i, t, :, lanes] = n_in_ref[c, t, :, lanes] + v_ref[1, t, :, lanes] * inv_r * around


def mirror_kernel(v_ref, op_ref, mirror_ref, n_in_ref, n_ref, grad_ref):
    comps, points, planes, radial = v_ref.shape
    tiles = mirror_ref.shape[1]
    count = points // tiles
    width = LANES // count
    rows = tiles * planes
    right = split(jnp.concatenate([op_ref[radial:]] * count, axis=0))
    lane = lax.broadcasted_iota(jnp.int32, (rows, LANES), 1)
    for c in range(comps):
        high, low = split(MIRROR_SIGNS[c] * mirror_ref[c].reshape(rows, LANES))
        zero = jnp.zeros_like(high)
        parts = [
            [jnp.where((lane >= q * width) & (lane < (q + 1) * width), x, zero) for q in range(count)]
            for x in (high, low)
        ]
        left = [jnp.concatenate(x, axis=0) for x in parts]
        grad_ref[c * points * planes : (c + 1) * points * planes] = product(left, right)

    def finish(t):
        for c in range(comps):
            start = pl.multiple_of((c * points + t) * planes, planes)
            n_ref[c, t] = n_in_ref[c, t] + v_ref[0, t] * grad_ref[pl.ds(start, planes)]

    each(points, finish)


def mirror_terms(v, op, mirror, n):
    return pl.pallas_call(
        mirror_kernel,
        name="mirror_terms",
        out_shape=held(*v.shape),
        in_specs=[VMEM] * 4,
        out_specs=VMEM,
        scratch_shapes=[pltpu.VMEM((v.size // v.shape[3], v.shape[3]), jnp.float32)],
        input_output_aliases={3: 0},
        compiler_params=params(v.size * 4, 8),
        cost_estimate=pl.CostEstimate(flops=2 * v.size * LANES, bytes_accessed=16 * v.size, transcendentals=0),
    )(v, op, mirror, n)


def late_kernel(me_ref, tap_ref, v_ref, chip_ref, n_in_ref, n_ref, *, piece):
    points, reach = v_ref.shape[1], chip_ref.shape[1]

    def add(before):
        add_side(tap_ref, v_ref, chip_ref, n_in_ref, n_ref, before, piece)
        for i, c in enumerate(piece):
            for t in range(reach, points) if before else range(points - reach):
                n_ref[i, t] = n_in_ref[c, t]

    even = me_ref[0] % 2 == 0
    pl.when(even)(lambda: add(True))
    pl.when(jnp.logical_not(even))(lambda: add(False))


def late_terms(me, taps, v, chip, n, piece):
    return pl.pallas_call(
        functools.partial(late_kernel, piece=piece),
        name="late_terms",
        out_shape=held(len(piece), *v.shape[1:]),
        in_specs=[SMEM, VMEM, VMEM, VMEM, VMEM],
        out_specs=VMEM,
        compiler_params=params(v.size * 4, 5),
        cost_estimate=pl.CostEstimate(flops=20 * v.size, bytes_accessed=12 * v.size, transcendentals=0),
    )(me, taps, v, chip, n)


def planes_kernel(v_ref, y_ref, row_ref, n_in_ref, n_ref, ends_ref, tile_ref, *, piece):
    comps, points, planes, radial = v_ref.shape
    carriers = y_ref.shape[1]
    lo, hi = AXIAL_REACH, planes - AXIAL_REACH
    weights = axial_weights(planes, False)
    decay = row_ref[1:2]
    for i in range(len(piece)):
        for j in range(points - carriers):
            tile_ref[i, j, 0:2] = y_ref[i, 3 * j, lo:hi]
            tile_ref[i, j, 2:3] = y_ref[i, 3 * j + 1, lo : lo + 1]
            tile_ref[i, j, lo:hi] = jnp.zeros((hi - lo, radial), jnp.float32)
            tile_ref[i, j, hi : hi + 1] = y_ref[i, 3 * j + 1, lo + 1 : hi]
            tile_ref[i, j, hi + 1 :] = y_ref[i, 3 * j + 2, lo:hi]
        ends_ref[0, i] = jnp.zeros((planes, radial), jnp.float32)
        ends_ref[1, i] = jnp.zeros((planes, radial), jnp.float32)

    def finish(t):
        for i, c in enumerate(piece):
            tile = y_ref[i, t] if t < carriers else tile_ref[i, t - carriers]
            n = n_in_ref[i, t] + v_ref[2, t] * axial_part(tile, weights)
            n_ref[i, t] = n
            right_side = v_ref[c, t] - STEP_WEIGHT * n
            ends_ref[0, i] = decay * ends_ref[0, i] + right_side
            ends_ref[1, i] = ends_ref[1, i] + row_ref[t : t + 1] * right_side

    for t in range(points):
        finish(t)


def planes_terms(v, y, rows, n, piece):
    comps, points, planes, radial = v.shape
    return pl.pallas_call(
        functools.partial(planes_kernel, piece=piece),
        name="planes_terms",
        out_shape=(held(*n.shape), held(2, len(piece), planes, radial)),
        in_specs=[VMEM] * 4,
        out_specs=(VMEM, VMEM),
        scratch_shapes=[pltpu.VMEM((len(piece), points - y.shape[1], planes, radial), jnp.float32)],
        input_output_aliases={3: 0},
        compiler_params=params(v.size * 4, 6),
        cost_estimate=pl.CostEstimate(flops=20 * v.size, bytes_accessed=16 * v.size, transcendentals=0),
    )(v, y, rows, n)


def stages(sectors):
    return [(bit, 2) for bit in range(sectors.bit_length() - 1)]


def stage_rows(points, sectors):
    first, found = points + 2, []
    for _, group in stages(sectors):
        found.append(first)
        first += 4 * group
    return found, first


def table_kernel(me_ref, factor_ref, stencil_ref, row_ref, tap_ref, *, points, sectors):
    radial = row_ref.shape[1]
    one = jnp.ones((1, radial), jnp.float32)
    half = (0.5 * lax.rsqrt(factor_ref[0] * one)) / inverse_radius(radial)
    root = jnp.sqrt(1.0 + half * half)
    loss = 2.0 * half * (root - half)
    rows = [one]
    for _ in range(points):
        rows.append(rows[-1] * (1.0 - loss))
    total = loss
    left, result = points * sectors, None
    while left:
        if left & 1:
            result = total if result is None else result + total - result * total
        total = total * (2.0 - total)
        left >>= 1
    height, wrap = half / root, 1.0 / result
    across = rows[points]
    rows.append(height)
    before = after = one

    def pick(index, choices):
        found = choices[-1]
        for k in range(len(choices) - 2, -1, -1):
            found = jnp.where(index == k, choices[k], found)
        return found

    for bit, group in stages(sectors):
        place = lax.rem(lax.div(me_ref[0], 1 << bit), group)
        powers = [one]
        for _ in range(group):
            powers.append(powers[-1] * across)
        kinds = [[], [], [], []]
        for x in range(group):
            other = place ^ x
            kinds[0].append(pick(group - 1 - other, powers[:group]))
            kinds[1].append(pick(other, powers[:group]))
            kinds[2].append(before * jnp.where(other < place, pick(place - 1 - other, powers[:group]), 0.0))
            kinds[3].append(after * jnp.where(other > place, pick(other - place - 1, powers[:group]), 0.0))
        before = before * pick(place, powers[:group])
        after = after * pick(group - 1 - place, powers[:group])
        across = powers[group]
        if 1 << bit == sectors // group:
            for x in range(group):
                kinds[2][x] = height * (kinds[2][x] + before * wrap * kinds[0][x])
                kinds[3][x] = height * (kinds[3][x] + after * wrap * kinds[1][x])
        for kind in kinds:
            rows += kind
    for k, row in enumerate(rows):
        row_ref[k : k + 1] = row
    for k in range(tap_ref.shape[0]):
        tap_ref[k] = jnp.full(tap_ref.shape[1:], stencil_ref[k], jnp.float32)


def table(me, viscous_factor, stencil, points, sectors, planes, radial):
    return pl.pallas_call(
        functools.partial(table_kernel, points=points, sectors=sectors),
        name="table",
        out_shape=(held(stage_rows(points, sectors)[1], radial), held(stencil.shape[0], planes, LANES)),
        in_specs=[SMEM, SMEM, SMEM],
        out_specs=(VMEM, VMEM),
        compiler_params=params(1 << 20, 1),
        cost_estimate=pl.CostEstimate(flops=1000 * radial, bytes_accessed=400 * radial, transcendentals=0),
    )(me, viscous_factor, stencil)


def sweep_kernel(v_ref, n_ref, row_ref, *refs, piece):
    s_ref, out_ref, sem = refs[-3:]
    leave = pltpu.make_async_copy(n_ref, out_ref.at[pl.ds(piece[0], len(piece))], sem)
    leave.start()
    _, points, planes, radial = v_ref.shape
    decay = row_ref[1:2]
    height = row_ref[points + 1 : points + 2]
    for i, c in enumerate(piece):
        s_ref[i, 0] = height * (v_ref[c, 0] - STEP_WEIGHT * n_ref[i, 0])

        def forward(k):
            t = k + 1
            s_ref[i, t] = decay * s_ref[i, t - 1] + height * (v_ref[c, t] - STEP_WEIGHT * n_ref[i, t])

        each(points - 1, forward)

    def backward(k, carry):
        t = points - 1 - k
        after = []
        for i, c in enumerate(piece):
            s_ref[i, t] = s_ref[i, t] + carry[i]
            after.append(decay * (carry[i] + height * (v_ref[c, t] - STEP_WEIGHT * n_ref[i, t])))
        return tuple(after)

    start = (jnp.zeros((planes, radial), jnp.float32),) * len(piece)
    lax.fori_loop(0, points, backward, start, unroll=points <= UNROLL)
    leave.wait()


def sweep(v, n, rows, out, piece):
    return pl.pallas_call(
        functools.partial(sweep_kernel, piece=piece),
        name="sweep",
        out_shape=(held(*n.shape), jax.ShapeDtypeStruct(v.shape, v.dtype)),
        in_specs=[VMEM] * 3 + [ANY] * len(out),
        out_specs=(VMEM, ANY),
        scratch_shapes=[pltpu.SemaphoreType.DMA],
        input_output_aliases={3: 1} if out else {},
        compiler_params=params(v.size * 4, 4),
        cost_estimate=pl.CostEstimate(flops=10 * v.size, bytes_accessed=12 * v.size, transcendentals=0),
    )(v, n, rows, *out)


def weighted(row_ref, first, refs, side, c):
    total = None
    for x, ref in enumerate(refs):
        term = row_ref[first + x : first + x + 1] * ref[side, c]
        total = term if total is None else total + term
    return total


def merge_kernel(row_ref, *refs, first, group):
    blocks, entries, (block_ref, entry_ref) = refs[:group], refs[group:-2], refs[-2:]
    for side in range(2):
        for c in range(block_ref.shape[1]):
            block_ref[side, c] = weighted(row_ref, first + side * group, blocks, side, c)
            enters = weighted(row_ref, first + (2 + side) * group, blocks, side, c)
            entry_ref[side, c] = entries[0][side, c] + enters if entries else enters


def merge(rows, blocks, entries, first):
    return pl.pallas_call(
        functools.partial(merge_kernel, first=first, group=len(blocks)),
        name="merge",
        out_shape=(held(*blocks[0].shape),) * 2,
        in_specs=[VMEM] * (1 + len(blocks) + len(entries)),
        out_specs=(VMEM, VMEM),
        compiler_params=params(blocks[0].size * 4, 8),
    )(rows, *blocks, *entries)


def close_kernel(s_ref, row_ref, *refs, first, group, piece, chained):
    blocks, entries = refs[:group], refs[group : -4 - chained]
    out_ref, x_ref, both_ref, sems = refs[-4:]
    count, points, _, _ = s_ref.shape
    height = row_ref[points + 1 : points + 2]
    leaves = []
    for i in range(count):
        for side in range(2):
            enters = weighted(row_ref, first + (2 + side) * group, blocks, side, i)
            both_ref[side, i] = enters + height * entries[0][side, i] if entries else enters
        before, after = both_ref[0, i], both_ref[1, i]

        def point(t):
            x_ref[i, t] = s_ref[i, t] + row_ref[pl.ds(t + 1, 1)] * before + row_ref[pl.ds(points - t, 1)] * after

        each(points, point)
        leaves.append(pltpu.make_async_copy(x_ref.at[i], out_ref.at[piece[i]], sems.at[i]))
        leaves[i].start()
    for leave in leaves:
        leave.wait()


def close(s, rows, blocks, entries, out, shape, first, piece):
    return pl.pallas_call(
        functools.partial(close_kernel, first=first, group=len(blocks), piece=piece, chained=len(out)),
        name="close",
        out_shape=jax.ShapeDtypeStruct(shape, s.dtype),
        in_specs=[VMEM] * (2 + len(blocks) + len(entries)) + [ANY] * len(out),
        out_specs=ANY,
        scratch_shapes=[
            pltpu.VMEM(s.shape, jnp.float32),
            pltpu.VMEM(blocks[0].shape, jnp.float32),
            pltpu.SemaphoreType.DMA((len(piece),)),
        ],
        input_output_aliases={2 + len(blocks) + len(entries): 0} if out else {},
        compiler_params=params(s.size * 4, 5),
    )(s, rows, *blocks, *entries, *out)


def local(velocity, radial_op, azimuth_stencil, viscous_factor):
    sectors = lax.axis_size("theta")
    comps, points, planes, radial = velocity.shape
    shape = velocity.shape
    reach = (azimuth_stencil.shape[0] - 1) // 2
    width = radial_op.shape[1] - radial
    me = lax.axis_index("theta").astype(jnp.int32).reshape(1)
    op = radial_op.T

    velocity, *planes_out = load(pltpu.with_memory_space_constraint(velocity, pltpu.HBM))
    (core_out,) = pack_side(me, velocity, planes_out[0], reach, True, (tuple(range(comps)),))
    chip_out = pack_side(me, velocity, core_out, reach, False, PIECES)
    mirror_out = pack_mirror(velocity, chip_out[0], width)
    planes_in, chip_in = [], []
    for k in range(len(PIECES)):
        planes_in.append(swap(planes_out[k], "gz", 1))
        chip_in.append(swap_across(chip_out[k], "theta"))
    mirror_in = swap(mirror_out, "theta", sectors // 2)
    core_in = swap(core_out, "theta", 1)
    rows, taps = table(me, viscous_factor, azimuth_stencil, points, sectors, planes, radial)
    firsts, _ = stage_rows(points, sectors)
    n = inner_terms(me, taps, velocity, op, core_in)
    n = mirror_terms(velocity, op, mirror_in, n)
    nonlinear, solved, parts = (), (), []
    for k, piece in enumerate(PIECES):
        part = late_terms(me, taps, velocity, chip_in[k], n, piece)
        part, block = planes_terms(velocity, planes_in[k], rows, part, piece)
        entries = ()
        for (bit, group), first in zip(stages(sectors), firsts):
            blocks = [block] + [swap(block, "theta", x << bit) for x in range(1, group)]
            if first != firsts[-1]:
                block, entry = merge(rows, blocks, entries, first)
                entries = (entry,)
        s, out = sweep(velocity, part, rows, nonlinear, piece)
        nonlinear = (out,)
        parts.append((s, blocks, entries))
    for (s, blocks, entries), piece in zip(parts, PIECES):
        solved = (close(s, rows, blocks, entries, solved, shape, firsts[-1], piece),)
    return (solved[0], nonlinear[0])


def solution(mesh):
    in_specs = (P(None, "theta", "gz", None), P(), P(), P())
    out_specs = (P(None, "theta", "gz", None), P(None, "theta", "gz", None))
    return jax.shard_map(local, mesh=mesh, in_specs=in_specs, out_specs=out_specs, check_vma=False)
```

```python
import functools

import jax
import jax.numpy as jnp
from jax import lax
from jax.experimental import pallas as pl
from jax.experimental.pallas import tpu as pltpu
from jax.sharding import PartitionSpec as P

AXIAL_WEIGHTS = (0.75, -0.15, 1.0 / 60.0)
AXIAL_REACH = len(AXIAL_WEIGHTS)
STEP_WEIGHT = 0.2
MIRROR_SIGNS = (-1.0, -1.0, 1.0)
LANES = 128
UNROLL = 16
INNER = 10 << 29

VMEM = pl.BlockSpec(memory_space=pltpu.VMEM)
SMEM = pl.BlockSpec(memory_space=pltpu.SMEM)
ANY = pl.BlockSpec(memory_space=pl.ANY)
HBM = pl.BlockSpec(memory_space=pltpu.HBM)


def params(block_bytes, blocks):
    return pltpu.CompilerParams(vmem_limit_bytes=(2 << 20) + blocks * block_bytes)


def held(*shape):
    return pltpu.VMEM(shape, jnp.float32)


def each(count, body):
    if count <= UNROLL:
        for i in range(count):
            body(i)
    else:
        pl.loop(0, count)(body)


def swap(block, axis, bit):
    size = lax.axis_size(axis)
    return lax.ppermute(block, axis, [(i, i ^ bit) for i in range(size)])


def swap_across(block, axis):
    size = lax.axis_size(axis)
    route = []
    for odd in range(1, size, 2):
        route += [(odd, (odd + 1) % size), ((odd + 1) % size, odd)]
    return lax.ppermute(block, axis, route)


def split(x):
    high = x.astype(jnp.bfloat16)
    return high, (x - high.astype(jnp.float32)).astype(jnp.bfloat16)


def product(left, right):
    dot = functools.partial(jnp.dot, preferred_element_type=jnp.float32)
    return dot(left[0], right[0]) + (dot(left[0], right[1]) + dot(left[1], right[0]))


def load_kernel(hbm_ref, v_ref, y_ref, sems):
    comps, points, planes, _ = v_ref.shape
    carriers = y_ref.shape[1]
    lo, hi = AXIAL_REACH, planes - AXIAL_REACH
    loads = [pltpu.make_async_copy(hbm_ref.at[c], v_ref.at[c], sems.at[c]) for c in range(comps)]
    for load in loads:
        load.start()
    for c in range(comps):
        loads[c].wait()

        def carry(t):
            y_ref[c, t] = v_ref[c, t]

        def ride(j):
            t = carriers + j
            y_ref[c, 3 * j, lo:hi] = v_ref[c, t, 0:2]
            y_ref[c, 3 * j + 1, lo : lo + 1] = v_ref[c, t, 2:3]
            y_ref[c, 3 * j + 1, lo + 1 : hi] = v_ref[c, t, hi : hi + 1]
            y_ref[c, 3 * j + 2, lo:hi] = v_ref[c, t, hi + 1 :]

        each(carriers, carry)
        each(points - carriers, ride)


def load(v):
    comps, points, planes, radial = v.shape
    return pl.pallas_call(
        load_kernel,
        name="load",
        out_shape=(held(*v.shape), held(comps, points - points // 4, planes, radial)),
        in_specs=[HBM],
        out_specs=(VMEM, VMEM),
        scratch_shapes=[pltpu.SemaphoreType.DMA((comps,))],
        compiler_params=params(v.size * 4, 2),
    )(v)


def pack_side_kernel(me_ref, v_ref, first_ref, side_ref, *, after):
    points, reach = v_ref.shape[1], side_ref.shape[1]

    def put(start):
        for c in range(v_ref.shape[0]):
            for h in range(reach):
                side_ref[c, h] = v_ref[c, start + h]

    even = me_ref[0] % 2 == 0
    last = even if after else jnp.logical_not(even)
    pl.when(last)(lambda: put(points - reach))
    pl.when(jnp.logical_not(last))(lambda: put(0))


def pack_side(me, v, first, reach, after):
    comps, _, planes, radial = v.shape
    return pl.pallas_call(
        functools.partial(pack_side_kernel, after=after),
        name="pack_core" if after else "pack_chip",
        out_shape=held(comps, reach, planes, radial),
        in_specs=[SMEM, VMEM, ANY],
        out_specs=VMEM,
        compiler_params=params(v.size * 4, 3),
    )(me, v, first)


def pack_mirror_kernel(v_ref, first_ref, mirror_ref):
    points, tiles = v_ref.shape[1], mirror_ref.shape[1]
    width = LANES // (points // tiles)
    lane = lax.broadcasted_iota(jnp.int32, mirror_ref.shape[2:], 1)

    def put(p):
        for c in range(v_ref.shape[0]):
            tile = v_ref[c, p, :, :LANES]
            for q in range(1, points // tiles):
                part = pltpu.roll(v_ref[c, q * tiles + p, :, :LANES], q * width, 1)
                tile = jnp.where(lane < q * width, tile, part)
            mirror_ref[c, p] = tile

    each(tiles, put)


def pack_mirror(v, first, width):
    comps, points, planes, _ = v.shape
    return pl.pallas_call(
        pack_mirror_kernel,
        name="pack_mirror",
        out_shape=held(comps, points // (LANES // width), planes, LANES),
        in_specs=[VMEM, ANY],
        out_specs=VMEM,
        compiler_params=params(v.size * 4, 2),
    )(v, first)


def inverse_radius(radial, start=0):
    return 1.0 / ((lax.broadcasted_iota(jnp.int32, (1, radial), 1) + start).astype(jnp.float32) + 0.5)


def axial_weights(planes, inside):
    row = lax.broadcasted_iota(jnp.int32, (planes, LANES), 0)
    weights = []
    for m, w in enumerate(AXIAL_WEIGHTS, 1):
        for shift, own, sign in ((m, row < planes - m, 1.0), (planes - m, row >= m, -1.0)):
            keep = own if inside else jnp.logical_not(own)
            weights.append((shift, jnp.where(keep, sign * w, 0.0)))
    return weights


def axial_part(tile, weights):
    planes, width = tile.shape
    weights = [(shift, jnp.concatenate([weight] * (width // LANES), axis=1)) for shift, weight in weights]
    total = None
    for shift, weight in weights:
        term = weight * pltpu.roll(tile, planes - shift, 0)
        total = term if total is None else total + term
    return total


def mirror_kernel(v_ref, op_ref, mirror_ref, n_ref, grad_ref):
    comps, points, planes, radial = v_ref.shape
    tiles = mirror_ref.shape[1]
    count = points // tiles
    width = LANES // count
    rows = tiles * planes
    right = split(jnp.concatenate([op_ref[radial:]] * count, axis=0))
    lane = lax.broadcasted_iota(jnp.int32, (rows, LANES), 1)
    for c in range(comps):
        high, low = split(MIRROR_SIGNS[c] * mirror_ref[c].reshape(rows, LANES))
        zero = jnp.zeros_like(high)
        parts = [
            [jnp.where((lane >= q * width) & (lane < (q + 1) * width), x, zero) for q in range(count)]
            for x in (high, low)
        ]
        left = [jnp.concatenate(x, axis=0) for x in parts]
        grad_ref[c * points * planes : (c + 1) * points * planes] = product(left, right)

    def finish(t):
        for c in range(comps):
            start = pl.multiple_of((c * points + t) * planes, planes)
            n_ref[c, t] = v_ref[0, t] * grad_ref[pl.ds(start, planes)]

    each(points, finish)


def mirror_terms(v, op, mirror):
    return pl.pallas_call(
        mirror_kernel,
        name="mirror_terms",
        out_shape=held(*v.shape),
        in_specs=[VMEM, VMEM, VMEM],
        out_specs=VMEM,
        scratch_shapes=[pltpu.VMEM((v.size // v.shape[3], v.shape[3]), jnp.float32)],
        compiler_params=params(v.size * 4, 8),
        cost_estimate=pl.CostEstimate(flops=2 * v.size * LANES, bytes_accessed=16 * v.size, transcendentals=0),
    )(v, op, mirror)


def inner_kernel(tap_ref, v_ref, op_ref, n_in_ref, n_ref, grad_ref):
    comps, points, planes, radial = v_ref.shape
    reach = (tap_ref.shape[0] - 1) // 2
    rows = points * planes
    right = split(op_ref[:radial])
    for c in range(comps):
        grad_ref[c * rows : (c + 1) * rows] = product(split(v_ref[c].reshape(rows, radial)), right)
    weights = axial_weights(planes, True)

    @pl.loop(0, radial // LANES)
    def column(k):
        lanes = pl.ds(pl.multiple_of(k * LANES, LANES), LANES)
        inv_r = inverse_radius(LANES, k * LANES)
        for c in range(comps):
            for t in range(points):
                a, b, e = [v_ref[i, t, :, lanes] for i in range(3)]
                b_inv = b * inv_r
                around = None
                for m in range(max(-reach, -t), min(reach, points - 1 - t) + 1):
                    term = tap_ref[m + reach] * v_ref[c, t + m, :, lanes]
                    around = term if around is None else around + term
                start = c * rows + t * planes
                n = a * grad_ref[start : start + planes, lanes] + b_inv * around
                n = n + e * axial_part(v_ref[c, t, :, lanes], weights) + n_in_ref[c, t, :, lanes]
                if c == 0:
                    n = n - b_inv * b
                elif c == 1:
                    n = n + a * b_inv
                n_ref[c, t, :, lanes] = n


def inner_terms(taps, v, op, n):
    return pl.pallas_call(
        inner_kernel,
        name="inner_terms",
        out_shape=held(*v.shape),
        in_specs=[VMEM] * 4,
        out_specs=VMEM,
        scratch_shapes=[pltpu.VMEM((v.size // v.shape[3], v.shape[3]), jnp.float32)],
        input_output_aliases={3: 0},
        compiler_params=params(v.size * 4, 7),
        cost_estimate=pl.CostEstimate(flops=INNER, bytes_accessed=16 * v.size, transcendentals=0),
    )(taps, v, op, n)


def add_side(tap_ref, v_ref, side_ref, n_in_ref, n_ref, before):
    comps, points, _, radial = v_ref.shape
    reach = side_ref.shape[1]
    first = 0 if before else reach + 1

    @pl.loop(0, radial // LANES)
    def column(k):
        lanes = pl.ds(pl.multiple_of(k * LANES, LANES), LANES)
        inv_r = inverse_radius(LANES, k * LANES)
        weights = [tap_ref[first + i] for i in range(reach)]
        for c in range(comps):
            side = [side_ref[c, h, :, lanes] for h in range(reach)]
            for u in range(reach):
                t = u if before else points - reach + u
                taps = [(h, h - u) for h in range(u, reach)] if before else [(h, reach - 1 + h - u) for h in range(u + 1)]
                around = None
                for h, w in taps:
                    term = weights[w] * side[h]
                    around = term if around is None else around + term
                n_ref[c, t, :, lanes] = n_in_ref[c, t, :, lanes] + v_ref[1, t, :, lanes] * inv_r * around


def core_kernel(me_ref, tap_ref, v_ref, core_ref, n_in_ref, n_ref):
    even = me_ref[0] % 2 == 0
    add = functools.partial(add_side, tap_ref, v_ref, core_ref, n_in_ref, n_ref)
    pl.when(even)(lambda: add(False))
    pl.when(jnp.logical_not(even))(lambda: add(True))


def late_kernel(me_ref, tap_ref, v_ref, chip_ref, n_in_ref, n_ref):
    even = me_ref[0] % 2 == 0
    add = functools.partial(add_side, tap_ref, v_ref, chip_ref, n_in_ref, n_ref)
    pl.when(even)(lambda: add(True))
    pl.when(jnp.logical_not(even))(lambda: add(False))


def side_terms(kernel, name, me, taps, v, side, n):
    return pl.pallas_call(
        kernel,
        name=name,
        out_shape=held(*v.shape),
        in_specs=[SMEM, VMEM, VMEM, VMEM, VMEM],
        out_specs=VMEM,
        input_output_aliases={4: 0},
        compiler_params=params(v.size * 4, 5),
        cost_estimate=pl.CostEstimate(flops=20 * v.size, bytes_accessed=12 * v.size, transcendentals=0),
    )(me, taps, v, side, n)


def planes_kernel(me_ref, v_ref, y_ref, power_ref, n_in_ref, n_ref, keep_ref, send_ref, tile_ref, ends_ref):
    comps, points, planes, radial = v_ref.shape
    carriers = y_ref.shape[1]
    lo, hi = AXIAL_REACH, planes - AXIAL_REACH
    weights = axial_weights(planes, False)
    for c in range(comps):
        for j in range(points - carriers):
            tile_ref[c, j, 0:2] = y_ref[c, 3 * j, lo:hi]
            tile_ref[c, j, 2:3] = y_ref[c, 3 * j + 1, lo : lo + 1]
            tile_ref[c, j, lo:hi] = jnp.zeros((hi - lo, radial), jnp.float32)
            tile_ref[c, j, hi : hi + 1] = y_ref[c, 3 * j + 1, lo + 1 : hi]
            tile_ref[c, j, hi + 1 :] = y_ref[c, 3 * j + 2, lo:hi]

    decay = power_ref[1:2]
    ends_ref[...] = jnp.zeros_like(ends_ref)
    for t in range(points):
        for c in range(comps):
            tile = y_ref[c, t] if t < carriers else tile_ref[c, t - carriers]
            n = n_in_ref[c, t] + v_ref[2, t] * axial_part(tile, weights)
            n_ref[c, t] = n
            right_side = v_ref[c, t] - STEP_WEIGHT * n
            ends_ref[0, c] = decay * ends_ref[0, c] + right_side
            ends_ref[1, c] = ends_ref[1, c] + power_ref[t : t + 1] * right_side

    half = radial // 2
    core = me_ref[0] % 2
    keep_ref[...] = ends_ref[:, :, :, pl.ds(pl.multiple_of(core * half, half), half)]
    send_ref[...] = ends_ref[:, :, :, pl.ds(pl.multiple_of((1 - core) * half, half), half)]


def planes_terms(me, v, y, power, n):
    comps, points, planes, radial = v.shape
    part = held(2, comps, planes, radial // 2)
    return pl.pallas_call(
        planes_kernel,
        name="planes_terms",
        out_shape=(held(*v.shape), part, part),
        in_specs=[SMEM] + [VMEM] * 4,
        out_specs=(VMEM, VMEM, VMEM),
        scratch_shapes=[
            pltpu.VMEM((comps, points - y.shape[1], planes, radial), jnp.float32),
            pltpu.VMEM((2, comps, planes, radial), jnp.float32),
        ],
        input_output_aliases={4: 0},
        compiler_params=params(v.size * 4, 6),
        cost_estimate=pl.CostEstimate(flops=20 * v.size, bytes_accessed=16 * v.size, transcendentals=0),
    )(me, v, y, power, n)


def table_kernel(me_ref, factor_ref, stencil_ref, row_ref, tap_ref, *, points, sectors):
    radial = row_ref.shape[1]
    one = jnp.ones((1, radial), jnp.float32)
    half = (0.5 * lax.rsqrt(factor_ref[0] * one)) / inverse_radius(radial)
    root = jnp.sqrt(1.0 + half * half)
    loss = 2.0 * half * (root - half)
    rows = [one]
    for _ in range(points):
        rows.append(rows[-1] * (1.0 - loss))
    total = loss
    left, result = points * sectors, None
    while left:
        if left & 1:
            result = total if result is None else result + total - result * total
        total = total * (2.0 - total)
        left >>= 1
    across = rows[points] * rows[points]
    rows += [half / root, 1.0 / result]
    before = after = one
    for bit in range(1, sectors.bit_length() - 1):
        upper = (me_ref[0] >> bit) % 2 == 1
        rows += [across, before, after]
        before, after = jnp.where(upper, before * across, before), jnp.where(upper, after, after * across)
        across = across * across
    for k, row in enumerate(rows + [before, after]):
        row_ref[k : k + 1] = row
    for k in range(tap_ref.shape[0]):
        tap_ref[k] = jnp.full(tap_ref.shape[1:], stencil_ref[k], jnp.float32)


def table(me, viscous_factor, stencil, points, sectors, planes, radial):
    count = points + 5 + 3 * (sectors.bit_length() - 2)
    return pl.pallas_call(
        functools.partial(table_kernel, points=points, sectors=sectors),
        name="table",
        out_shape=(held(count, radial), held(stencil.shape[0], planes, LANES)),
        in_specs=[SMEM, SMEM, SMEM],
        out_specs=(VMEM, VMEM),
        compiler_params=params(1 << 20, 1),
        cost_estimate=pl.CostEstimate(flops=1000 * radial, bytes_accessed=400 * radial, transcendentals=0),
    )(me, viscous_factor, stencil)


def sweep_kernel(v_ref, n_ref, power_ref, s_ref, nonlinear_ref, sem):
    leave = pltpu.make_async_copy(n_ref, nonlinear_ref, sem)
    leave.start()
    comps, points, planes, radial = v_ref.shape
    decay = power_ref[1:2]
    height = power_ref[points + 1 : points + 2]
    for c in range(comps):
        s_ref[c, 0] = height * (v_ref[c, 0] - STEP_WEIGHT * n_ref[c, 0])

        def forward(i):
            t = i + 1
            s_ref[c, t] = decay * s_ref[c, t - 1] + height * (v_ref[c, t] - STEP_WEIGHT * n_ref[c, t])

        each(points - 1, forward)

    def backward(i, carry):
        t = points - 1 - i
        after = []
        for c in range(comps):
            s_ref[c, t] = s_ref[c, t] + carry[c]
            after.append(decay * (carry[c] + height * (v_ref[c, t] - STEP_WEIGHT * n_ref[c, t])))
        return tuple(after)

    start = (jnp.zeros((planes, radial), jnp.float32),) * comps
    lax.fori_loop(0, points, backward, start, unroll=points <= UNROLL)
    leave.wait()


def sweep(v, n, power):
    return pl.pallas_call(
        sweep_kernel,
        name="sweep",
        out_shape=(held(*v.shape), jax.ShapeDtypeStruct(v.shape, v.dtype)),
        in_specs=[VMEM] * 3,
        out_specs=(VMEM, ANY),
        scratch_shapes=[pltpu.SemaphoreType.DMA],
        compiler_params=params(v.size * 4, 4),
        cost_estimate=pl.CostEstimate(flops=10 * v.size, bytes_accessed=12 * v.size, transcendentals=0),
    )(v, n, power)


def my_lanes(me_ref, radial, half):
    core = me_ref[0] % 2
    return pl.ds(pl.multiple_of(core * half, half), half)


def pair_kernel(me_ref, power_ref, own_ref, other_ref, block_ref, *, points):
    half = own_ref.shape[3]
    hop = power_ref[points : points + 1, my_lanes(me_ref, power_ref.shape[1], half)]
    odd = me_ref[0] % 2 == 1
    for c in range(own_ref.shape[1]):
        for side in range(2):
            own, other = own_ref[side, c], other_ref[side, c]
            far, near = (own, other) if side == 0 else (other, own)
            block_ref[side, c] = jnp.where(odd, hop * near + far, hop * far + near)


def pair(me, power, own, other, points):
    return pl.pallas_call(
        functools.partial(pair_kernel, points=points),
        name="pair",
        out_shape=held(*own.shape),
        in_specs=[SMEM, VMEM, VMEM, VMEM],
        out_specs=VMEM,
        compiler_params=params(own.size * 4, 8),
    )(me, power, own, other)


def merge_kernel(me_ref, power_ref, block_ref, other_ref, *refs, points, bit):
    *entry_refs, block_out_ref, entry_out_ref = refs
    comps, half = block_ref.shape[1], block_ref.shape[3]
    lanes = my_lanes(me_ref, power_ref.shape[1], half)
    first = points + 3 * bit
    across, before, after = [power_ref[first + k : first + k + 1, lanes] for k in range(3)]
    upper = (me_ref[0] >> bit) % 2 == 1
    before = jnp.where(upper, before, 0.0)
    after = jnp.where(upper, 0.0, after)
    for c in range(comps):
        low, high = block_ref[0, c], block_ref[1, c]
        other_low, other_high = other_ref[0, c], other_ref[1, c]
        block_out_ref[0, c] = jnp.where(upper, across * other_low + low, across * low + other_low)
        block_out_ref[1, c] = jnp.where(upper, other_high + across * high, high + across * other_high)
        for side, enters in enumerate((before * other_low, after * other_high)):
            entry_out_ref[side, c] = entry_refs[0][side, c] + enters if entry_refs else enters


def merge(me, power, block, other, entries, points, bit):
    return pl.pallas_call(
        functools.partial(merge_kernel, points=points, bit=bit),
        name="merge",
        out_shape=(held(*block.shape), held(*block.shape)),
        in_specs=[SMEM] + [VMEM] * (3 + len(entries)),
        out_specs=(VMEM, VMEM),
        compiler_params=params(block.size * 4, 8),
    )(me, power, block, other, *entries)


def enter_kernel(me_ref, power_ref, block_ref, entry_ref, own_ref, other_ref, ready_ref, mine_ref, send_ref, *, points):
    comps, half = block_ref.shape[1], block_ref.shape[3]
    lanes = my_lanes(me_ref, power_ref.shape[1], half)
    row = lambda k: power_ref[k : k + 1, lanes]
    hop, height, wrap = row(points), row(points + 1), row(points + 2)
    last = power_ref.shape[0]
    before, after = row(last - 2) * wrap, row(last - 1) * wrap
    odd = me_ref[0] % 2 == 1
    for c in range(comps):
        low = height * (entry_ref[0, c] + before * block_ref[0, c])
        high = height * (entry_ref[1, c] + after * block_ref[1, c])
        even_low = height * jnp.where(odd, other_ref[0, c], own_ref[0, c])
        odd_high = height * jnp.where(odd, own_ref[1, c], other_ref[1, c])
        even_in = (low, odd_high + hop * high)
        odd_in = (even_low + hop * low, high)
        for side in range(2):
            mine_ref[side, c] = jnp.where(odd, odd_in[side], even_in[side])
            send_ref[side, c] = jnp.where(odd, even_in[side], odd_in[side])


def enter(me, power, block, entry, own, other, ready, points):
    return pl.pallas_call(
        functools.partial(enter_kernel, points=points),
        name="enter",
        out_shape=(held(*block.shape), held(*block.shape)),
        in_specs=[SMEM] + [VMEM] * 5 + [ANY],
        out_specs=(VMEM, VMEM),
        compiler_params=params(block.size * 4, 12),
    )(me, power, block, entry, own, other, ready)


def close_kernel(me_ref, s_ref, power_ref, mine_ref, got_ref, out_ref, x_ref, both_ref, sems):
    comps, points, planes, radial = s_ref.shape
    half = mine_ref.shape[3]
    core = me_ref[0] % 2
    both_ref[:, :, :, pl.ds(pl.multiple_of(core * half, half), half)] = mine_ref[...]
    both_ref[:, :, :, pl.ds(pl.multiple_of((1 - core) * half, half), half)] = got_ref[...]
    leaves = []
    for c in range(comps):
        before, after = both_ref[0, c], both_ref[1, c]

        def point(t):
            x_ref[c, t] = s_ref[c, t] + power_ref[pl.ds(t + 1, 1)] * before + power_ref[pl.ds(points - t, 1)] * after

        each(points, point)
        leaves.append(pltpu.make_async_copy(x_ref.at[c], out_ref.at[c], sems.at[c]))
        leaves[c].start()
    for leave in leaves:
        leave.wait()


def close(me, s, power, mine, got):
    return pl.pallas_call(
        close_kernel,
        name="close",
        out_shape=jax.ShapeDtypeStruct(s.shape, s.dtype),
        in_specs=[SMEM] + [VMEM] * 4,
        out_specs=ANY,
        scratch_shapes=[
            pltpu.VMEM(s.shape, jnp.float32),
            pltpu.VMEM((2,) + s.shape[:1] + s.shape[2:], jnp.float32),
            pltpu.SemaphoreType.DMA((s.shape[0],)),
        ],
        compiler_params=params(s.size * 4, 5),
    )(me, s, power, mine, got)


def local(velocity, radial_op, azimuth_stencil, viscous_factor):
    sectors = lax.axis_size("theta")
    comps, points, planes, radial = velocity.shape
    reach = (azimuth_stencil.shape[0] - 1) // 2
    width = radial_op.shape[1] - radial
    me = lax.axis_index("theta").astype(jnp.int32).reshape(1)
    op = radial_op.T

    velocity, planes_out = load(pltpu.with_memory_space_constraint(velocity, pltpu.HBM))
    planes_in = swap(planes_out, "gz", 1)
    mirror_out = pack_mirror(velocity, planes_out, width)
    mirror_in = swap(mirror_out, "theta", sectors // 2)
    chip_out = pack_side(me, velocity, mirror_out, reach, False)
    chip_in = swap_across(chip_out, "theta")
    core_out = pack_side(me, velocity, chip_out, reach, True)
    core_in = swap(core_out, "theta", 1)
    power, taps = table(me, viscous_factor, azimuth_stencil, points, sectors, planes, radial)
    n = mirror_terms(velocity, op, mirror_in)
    n = inner_terms(taps, velocity, op, n)
    n = side_terms(core_kernel, "core_terms", me, taps, velocity, core_in, n)
    n = side_terms(late_kernel, "late_terms", me, taps, velocity, chip_in, n)
    n, own, send = planes_terms(me, velocity, planes_in, power, n)
    other = swap(send, "theta", 1)
    s, nonlinear = sweep(velocity, n, power)
    block = pair(me, power, own, other, points)
    entries = ()
    for bit in range(1, sectors.bit_length() - 1):
        block, entry = merge(me, power, block, swap(block, "theta", 1 << bit), entries, points, bit)
        entries = (entry,)
    mine, send = enter(me, power, block, entry, own, other, s, points)
    new_velocity = close(me, s, power, mine, swap(send, "theta", 1))
    return (new_velocity, nonlinear)


def solution(mesh):
    in_specs = (P(None, "theta", "gz", None), P(), P(), P())
    out_specs = (P(None, "theta", "gz", None), P(None, "theta", "gz", None))
    return jax.shard_map(local, mesh=mesh, in_specs=in_specs, out_specs=out_specs, check_vma=False)
```

```python
import functools

import jax
import jax.numpy as jnp
from jax import lax
from jax.experimental import pallas as pl
from jax.experimental.pallas import tpu as pltpu
from jax.sharding import PartitionSpec as P

AXIAL_WEIGHTS = (0.75, -0.15, 1.0 / 60.0)
AXIAL_REACH = len(AXIAL_WEIGHTS)
STEP_WEIGHT = 0.2
MIRROR_SIGNS = (-1.0, -1.0, 1.0)
LANES = 128
UNROLL = 16
INNER = 10 << 29
MIRROR = 1 << 26
SIDE = 1 << 26

VMEM = pl.BlockSpec(memory_space=pltpu.VMEM)
SMEM = pl.BlockSpec(memory_space=pltpu.SMEM)
ANY = pl.BlockSpec(memory_space=pl.ANY)
HBM = pl.BlockSpec(memory_space=pltpu.HBM)


def params(block_bytes, blocks):
    return pltpu.CompilerParams(vmem_limit_bytes=(2 << 20) + blocks * block_bytes)


def held(*shape):
    return pltpu.VMEM(shape, jnp.float32)


def each(count, body):
    if count <= UNROLL:
        for i in range(count):
            body(i)
    else:
        pl.loop(0, count)(body)


def swap(block, axis, bit):
    size = lax.axis_size(axis)
    return lax.ppermute(block, axis, [(i, i ^ bit) for i in range(size)])


def swap_across(block, axis):
    size = lax.axis_size(axis)
    route = []
    for odd in range(1, size, 2):
        route += [(odd, (odd + 1) % size), ((odd + 1) % size, odd)]
    return lax.ppermute(block, axis, route)


def split(x):
    high = x.astype(jnp.bfloat16)
    return high, (x - high.astype(jnp.float32)).astype(jnp.bfloat16)


def product(left, right):
    dot = functools.partial(jnp.dot, preferred_element_type=jnp.float32)
    return dot(left[0], right[0]) + (dot(left[0], right[1]) + dot(left[1], right[0]))


def load_kernel(hbm_ref, v_ref, y_ref, sems):
    comps, points, planes, _ = v_ref.shape
    carriers = y_ref.shape[1]
    lo, hi = AXIAL_REACH, planes - AXIAL_REACH
    loads = [pltpu.make_async_copy(hbm_ref.at[c], v_ref.at[c], sems.at[c]) for c in range(comps)]
    for load in loads:
        load.start()
    for c in range(comps):
        loads[c].wait()

        def carry(t):
            y_ref[c, t] = v_ref[c, t]

        def ride(j):
            t = carriers + j
            y_ref[c, 3 * j, lo:hi] = v_ref[c, t, 0:2]
            y_ref[c, 3 * j + 1, lo : lo + 1] = v_ref[c, t, 2:3]
            y_ref[c, 3 * j + 1, lo + 1 : hi] = v_ref[c, t, hi : hi + 1]
            y_ref[c, 3 * j + 2, lo:hi] = v_ref[c, t, hi + 1 :]

        each(carriers, carry)
        each(points - carriers, ride)


def load(v):
    comps, points, planes, radial = v.shape
    return pl.pallas_call(
        load_kernel,
        name="load",
        out_shape=(held(*v.shape), held(comps, points - points // 4, planes, radial)),
        in_specs=[HBM],
        out_specs=(VMEM, VMEM),
        scratch_shapes=[pltpu.SemaphoreType.DMA((comps,))],
        compiler_params=params(v.size * 4, 2),
    )(v)


def pack_side_kernel(me_ref, v_ref, first_ref, side_ref, *, after):
    points, reach = v_ref.shape[1], side_ref.shape[1]

    def put(start):
        for c in range(v_ref.shape[0]):
            for h in range(reach):
                side_ref[c, h] = v_ref[c, start + h]

    even = me_ref[0] % 2 == 0
    last = even if after else jnp.logical_not(even)
    pl.when(last)(lambda: put(points - reach))
    pl.when(jnp.logical_not(last))(lambda: put(0))


def pack_side(me, v, first, reach, after):
    comps, _, planes, radial = v.shape
    return pl.pallas_call(
        functools.partial(pack_side_kernel, after=after),
        name="pack_core" if after else "pack_chip",
        out_shape=held(comps, reach, planes, radial),
        in_specs=[SMEM, VMEM, ANY],
        out_specs=VMEM,
        compiler_params=params(v.size * 4, 3),
    )(me, v, first)


def pack_mirror_kernel(v_ref, first_ref, mirror_ref):
    points, tiles = v_ref.shape[1], mirror_ref.shape[1]
    width = LANES // (points // tiles)
    lane = lax.broadcasted_iota(jnp.int32, mirror_ref.shape[2:], 1)

    def put(p):
        for c in range(v_ref.shape[0]):
            tile = v_ref[c, p, :, :LANES]
            for q in range(1, points // tiles):
                part = pltpu.roll(v_ref[c, q * tiles + p, :, :LANES], q * width, 1)
                tile = jnp.where(lane < q * width, tile, part)
            mirror_ref[c, p] = tile

    each(tiles, put)


def pack_mirror(v, first, width):
    comps, points, planes, _ = v.shape
    return pl.pallas_call(
        pack_mirror_kernel,
        name="pack_mirror",
        out_shape=held(comps, points // (LANES // width), planes, LANES),
        in_specs=[VMEM, ANY],
        out_specs=VMEM,
        compiler_params=params(v.size * 4, 2),
    )(v, first)


def inverse_radius(radial, start=0):
    return 1.0 / ((lax.broadcasted_iota(jnp.int32, (1, radial), 1) + start).astype(jnp.float32) + 0.5)


def axial_weights(planes, inside):
    row = lax.broadcasted_iota(jnp.int32, (planes, LANES), 0)
    weights = []
    for m, w in enumerate(AXIAL_WEIGHTS, 1):
        for shift, own, sign in ((m, row < planes - m, 1.0), (planes - m, row >= m, -1.0)):
            keep = own if inside else jnp.logical_not(own)
            weights.append((shift, jnp.where(keep, sign * w, 0.0)))
    return weights


def axial_part(tile, weights):
    planes, width = tile.shape
    weights = [(shift, jnp.concatenate([weight] * (width // LANES), axis=1)) for shift, weight in weights]
    total = None
    for shift, weight in weights:
        term = weight * pltpu.roll(tile, planes - shift, 0)
        total = term if total is None else total + term
    return total


def mirror_kernel(v_ref, op_ref, mirror_ref, n_in_ref, n_ref, grad_ref):
    comps, points, planes, radial = v_ref.shape
    tiles = mirror_ref.shape[1]
    count = points // tiles
    width = LANES // count
    rows = tiles * planes
    right = split(jnp.concatenate([op_ref[radial:]] * count, axis=0))
    lane = lax.broadcasted_iota(jnp.int32, (rows, LANES), 1)
    for c in range(comps):
        high, low = split(MIRROR_SIGNS[c] * mirror_ref[c].reshape(rows, LANES))
        zero = jnp.zeros_like(high)
        parts = [
            [jnp.where((lane >= q * width) & (lane < (q + 1) * width), x, zero) for q in range(count)]
            for x in (high, low)
        ]
        left = [jnp.concatenate(x, axis=0) for x in parts]
        grad_ref[c * points * planes : (c + 1) * points * planes] = product(left, right)

    def finish(t):
        for c in range(comps):
            start = pl.multiple_of((c * points + t) * planes, planes)
            n_ref[c, t] = n_in_ref[c, t] + v_ref[0, t] * grad_ref[pl.ds(start, planes)]

    each(points, finish)


def mirror_terms(v, op, mirror, n):
    return pl.pallas_call(
        mirror_kernel,
        name="mirror_terms",
        out_shape=held(*v.shape),
        in_specs=[VMEM] * 4,
        out_specs=VMEM,
        scratch_shapes=[pltpu.VMEM((v.size // v.shape[3], v.shape[3]), jnp.float32)],
        input_output_aliases={3: 0},
        compiler_params=params(v.size * 4, 8),
        cost_estimate=pl.CostEstimate(flops=MIRROR, bytes_accessed=16 * v.size, transcendentals=0),
    )(v, op, mirror, n)


def inner_kernel(tap_ref, v_ref, op_ref, n_ref, grad_ref):
    comps, points, planes, radial = v_ref.shape
    reach = (tap_ref.shape[0] - 1) // 2
    rows = points * planes
    right = split(op_ref[:radial])
    for c in range(comps):
        grad_ref[c * rows : (c + 1) * rows] = product(split(v_ref[c].reshape(rows, radial)), right)
    weights = axial_weights(planes, True)

    @pl.loop(0, radial // LANES)
    def column(k):
        lanes = pl.ds(pl.multiple_of(k * LANES, LANES), LANES)
        inv_r = inverse_radius(LANES, k * LANES)
        for c in range(comps):
            for t in range(points):
                a, b, e = [v_ref[i, t, :, lanes] for i in range(3)]
                b_inv = b * inv_r
                around = None
                for m in range(max(-reach, -t), min(reach, points - 1 - t) + 1):
                    term = tap_ref[m + reach] * v_ref[c, t + m, :, lanes]
                    around = term if around is None else around + term
                start = c * rows + t * planes
                n = a * grad_ref[start : start + planes, lanes] + b_inv * around
                n = n + e * axial_part(v_ref[c, t, :, lanes], weights)
                if c == 0:
                    n = n - b_inv * b
                elif c == 1:
                    n = n + a * b_inv
                n_ref[c, t, :, lanes] = n


def inner_terms(taps, v, op):
    return pl.pallas_call(
        inner_kernel,
        name="inner_terms",
        out_shape=held(*v.shape),
        in_specs=[VMEM] * 3,
        out_specs=VMEM,
        scratch_shapes=[pltpu.VMEM((v.size // v.shape[3], v.shape[3]), jnp.float32)],
        compiler_params=params(v.size * 4, 7),
        cost_estimate=pl.CostEstimate(flops=INNER, bytes_accessed=16 * v.size, transcendentals=0),
    )(taps, v, op)


def add_side(tap_ref, v_ref, side_ref, n_in_ref, n_ref, before):
    comps, points, _, radial = v_ref.shape
    reach = side_ref.shape[1]
    first = 0 if before else reach + 1

    @pl.loop(0, radial // LANES)
    def column(k):
        lanes = pl.ds(pl.multiple_of(k * LANES, LANES), LANES)
        inv_r = inverse_radius(LANES, k * LANES)
        weights = [tap_ref[first + i] for i in range(reach)]
        for c in range(comps):
            side = [side_ref[c, h, :, lanes] for h in range(reach)]
            for u in range(reach):
                t = u if before else points - reach + u
                taps = [(h, h - u) for h in range(u, reach)] if before else [(h, reach - 1 + h - u) for h in range(u + 1)]
                around = None
                for h, w in taps:
                    term = weights[w] * side[h]
                    around = term if around is None else around + term
                n_ref[c, t, :, lanes] = n_in_ref[c, t, :, lanes] + v_ref[1, t, :, lanes] * inv_r * around


def core_kernel(me_ref, tap_ref, v_ref, core_ref, n_in_ref, n_ref):
    even = me_ref[0] % 2 == 0
    add = functools.partial(add_side, tap_ref, v_ref, core_ref, n_in_ref, n_ref)
    pl.when(even)(lambda: add(False))
    pl.when(jnp.logical_not(even))(lambda: add(True))


def late_kernel(me_ref, tap_ref, v_ref, chip_ref, n_in_ref, n_ref):
    even = me_ref[0] % 2 == 0
    add = functools.partial(add_side, tap_ref, v_ref, chip_ref, n_in_ref, n_ref)
    pl.when(even)(lambda: add(True))
    pl.when(jnp.logical_not(even))(lambda: add(False))


def side_terms(kernel, name, me, taps, v, side, n):
    return pl.pallas_call(
        kernel,
        name=name,
        out_shape=held(*v.shape),
        in_specs=[SMEM, VMEM, VMEM, VMEM, VMEM],
        out_specs=VMEM,
        input_output_aliases={4: 0},
        compiler_params=params(v.size * 4, 5),
        cost_estimate=pl.CostEstimate(flops=SIDE, bytes_accessed=12 * v.size, transcendentals=0),
    )(me, taps, v, side, n)


def planes_kernel(me_ref, v_ref, y_ref, power_ref, n_in_ref, n_ref, keep_ref, send_ref, tile_ref, ends_ref):
    comps, points, planes, radial = v_ref.shape
    carriers = y_ref.shape[1]
    lo, hi = AXIAL_REACH, planes - AXIAL_REACH
    weights = axial_weights(planes, False)
    for c in range(comps):
        for j in range(points - carriers):
            tile_ref[c, j, 0:2] = y_ref[c, 3 * j, lo:hi]
            tile_ref[c, j, 2:3] = y_ref[c, 3 * j + 1, lo : lo + 1]
            tile_ref[c, j, lo:hi] = jnp.zeros((hi - lo, radial), jnp.float32)
            tile_ref[c, j, hi : hi + 1] = y_ref[c, 3 * j + 1, lo + 1 : hi]
            tile_ref[c, j, hi + 1 :] = y_ref[c, 3 * j + 2, lo:hi]

    decay = power_ref[1:2]
    ends_ref[...] = jnp.zeros_like(ends_ref)
    for t in range(points):
        for c in range(comps):
            tile = y_ref[c, t] if t < carriers else tile_ref[c, t - carriers]
            n = n_in_ref[c, t] + v_ref[2, t] * axial_part(tile, weights)
            n_ref[c, t] = n
            right_side = v_ref[c, t] - STEP_WEIGHT * n
            ends_ref[0, c] = decay * ends_ref[0, c] + right_side
            ends_ref[1, c] = ends_ref[1, c] + power_ref[t : t + 1] * right_side

    half = radial // 2
    core = me_ref[0] % 2
    keep_ref[...] = ends_ref[:, :, :, pl.ds(pl.multiple_of(core * half, half), half)]
    send_ref[...] = ends_ref[:, :, :, pl.ds(pl.multiple_of((1 - core) * half, half), half)]


def planes_terms(me, v, y, power, n):
    comps, points, planes, radial = v.shape
    part = held(2, comps, planes, radial // 2)
    return pl.pallas_call(
        planes_kernel,
        name="planes_terms",
        out_shape=(held(*v.shape), part, part),
        in_specs=[SMEM] + [VMEM] * 4,
        out_specs=(VMEM, VMEM, VMEM),
        scratch_shapes=[
            pltpu.VMEM((comps, points - y.shape[1], planes, radial), jnp.float32),
            pltpu.VMEM((2, comps, planes, radial), jnp.float32),
        ],
        input_output_aliases={4: 0},
        compiler_params=params(v.size * 4, 6),
        cost_estimate=pl.CostEstimate(flops=20 * v.size, bytes_accessed=16 * v.size, transcendentals=0),
    )(me, v, y, power, n)


def table_kernel(me_ref, factor_ref, stencil_ref, row_ref, tap_ref, *, points, sectors):
    radial = row_ref.shape[1]
    one = jnp.ones((1, radial), jnp.float32)
    half = (0.5 * lax.rsqrt(factor_ref[0] * one)) / inverse_radius(radial)
    root = jnp.sqrt(1.0 + half * half)
    loss = 2.0 * half * (root - half)
    rows = [one]
    for _ in range(points):
        rows.append(rows[-1] * (1.0 - loss))
    total = loss
    left, result = points * sectors, None
    while left:
        if left & 1:
            result = total if result is None else result + total - result * total
        total = total * (2.0 - total)
        left >>= 1
    across = rows[points] * rows[points]
    rows += [half / root, 1.0 / result]
    before = after = one
    for bit in range(1, sectors.bit_length() - 1):
        upper = (me_ref[0] >> bit) % 2 == 1
        rows += [across, before, after]
        before, after = jnp.where(upper, before * across, before), jnp.where(upper, after, after * across)
        across = across * across
    for k, row in enumerate(rows + [before, after]):
        row_ref[k : k + 1] = row
    for k in range(tap_ref.shape[0]):
        tap_ref[k] = jnp.full(tap_ref.shape[1:], stencil_ref[k], jnp.float32)


def table(me, viscous_factor, stencil, points, sectors, planes, radial):
    count = points + 5 + 3 * (sectors.bit_length() - 2)
    return pl.pallas_call(
        functools.partial(table_kernel, points=points, sectors=sectors),
        name="table",
        out_shape=(held(count, radial), held(stencil.shape[0], planes, LANES)),
        in_specs=[SMEM, SMEM, SMEM],
        out_specs=(VMEM, VMEM),
        compiler_params=params(1 << 20, 1),
        cost_estimate=pl.CostEstimate(flops=1000 * radial, bytes_accessed=400 * radial, transcendentals=0),
    )(me, viscous_factor, stencil)


def sweep_kernel(v_ref, n_ref, power_ref, s_ref, nonlinear_ref, sem):
    leave = pltpu.make_async_copy(n_ref, nonlinear_ref, sem)
    leave.start()
    comps, points, planes, radial = v_ref.shape
    decay = power_ref[1:2]
    height = power_ref[points + 1 : points + 2]
    for c in range(comps):
        s_ref[c, 0] = height * (v_ref[c, 0] - STEP_WEIGHT * n_ref[c, 0])

        def forward(i):
            t = i + 1
            s_ref[c, t] = decay * s_ref[c, t - 1] + height * (v_ref[c, t] - STEP_WEIGHT * n_ref[c, t])

        each(points - 1, forward)

    def backward(i, carry):
        t = points - 1 - i
        after = []
        for c in range(comps):
            s_ref[c, t] = s_ref[c, t] + carry[c]
            after.append(decay * (carry[c] + height * (v_ref[c, t] - STEP_WEIGHT * n_ref[c, t])))
        return tuple(after)

    start = (jnp.zeros((planes, radial), jnp.float32),) * comps
    lax.fori_loop(0, points, backward, start, unroll=points <= UNROLL)
    leave.wait()


def sweep(v, n, power):
    return pl.pallas_call(
        sweep_kernel,
        name="sweep",
        out_shape=(held(*v.shape), jax.ShapeDtypeStruct(v.shape, v.dtype)),
        in_specs=[VMEM] * 3,
        out_specs=(VMEM, ANY),
        scratch_shapes=[pltpu.SemaphoreType.DMA],
        compiler_params=params(v.size * 4, 4),
        cost_estimate=pl.CostEstimate(flops=10 * v.size, bytes_accessed=12 * v.size, transcendentals=0),
    )(v, n, power)


def my_lanes(me_ref, radial, half):
    core = me_ref[0] % 2
    return pl.ds(pl.multiple_of(core * half, half), half)


def pair_kernel(me_ref, power_ref, own_ref, other_ref, block_ref, *, points):
    half = own_ref.shape[3]
    hop = power_ref[points : points + 1, my_lanes(me_ref, power_ref.shape[1], half)]
    odd = me_ref[0] % 2 == 1
    for c in range(own_ref.shape[1]):
        for side in range(2):
            own, other = own_ref[side, c], other_ref[side, c]
            far, near = (own, other) if side == 0 else (other, own)
            block_ref[side, c] = jnp.where(odd, hop * near + far, hop * far + near)


def pair(me, power, own, other, points):
    return pl.pallas_call(
        functools.partial(pair_kernel, points=points),
        name="pair",
        out_shape=held(*own.shape),
        in_specs=[SMEM, VMEM, VMEM, VMEM],
        out_specs=VMEM,
        compiler_params=params(own.size * 4, 8),
    )(me, power, own, other)


def merge_kernel(me_ref, power_ref, block_ref, other_ref, *refs, points, bit):
    *entry_refs, block_out_ref, entry_out_ref = refs
    comps, half = block_ref.shape[1], block_ref.shape[3]
    lanes = my_lanes(me_ref, power_ref.shape[1], half)
    first = points + 3 * bit
    across, before, after = [power_ref[first + k : first + k + 1, lanes] for k in range(3)]
    upper = (me_ref[0] >> bit) % 2 == 1
    before = jnp.where(upper, before, 0.0)
    after = jnp.where(upper, 0.0, after)
    for c in range(comps):
        low, high = block_ref[0, c], block_ref[1, c]
        other_low, other_high = other_ref[0, c], other_ref[1, c]
        block_out_ref[0, c] = jnp.where(upper, across * other_low + low, across * low + other_low)
        block_out_ref[1, c] = jnp.where(upper, other_high + across * high, high + across * other_high)
        for side, enters in enumerate((before * other_low, after * other_high)):
            entry_out_ref[side, c] = entry_refs[0][side, c] + enters if entry_refs else enters


def merge(me, power, block, other, entries, points, bit):
    return pl.pallas_call(
        functools.partial(merge_kernel, points=points, bit=bit),
        name="merge",
        out_shape=(held(*block.shape), held(*block.shape)),
        in_specs=[SMEM] + [VMEM] * (3 + len(entries)),
        out_specs=(VMEM, VMEM),
        compiler_params=params(block.size * 4, 8),
    )(me, power, block, other, *entries)


def enter_kernel(me_ref, power_ref, block_ref, entry_ref, own_ref, other_ref, ready_ref, mine_ref, send_ref, *, points):
    comps, half = block_ref.shape[1], block_ref.shape[3]
    lanes = my_lanes(me_ref, power_ref.shape[1], half)
    row = lambda k: power_ref[k : k + 1, lanes]
    hop, height, wrap = row(points), row(points + 1), row(points + 2)
    last = power_ref.shape[0]
    before, after = row(last - 2) * wrap, row(last - 1) * wrap
    odd = me_ref[0] % 2 == 1
    for c in range(comps):
        low = height * (entry_ref[0, c] + before * block_ref[0, c])
        high = height * (entry_ref[1, c] + after * block_ref[1, c])
        even_low = height * jnp.where(odd, other_ref[0, c], own_ref[0, c])
        odd_high = height * jnp.where(odd, own_ref[1, c], other_ref[1, c])
        even_in = (low, odd_high + hop * high)
        odd_in = (even_low + hop * low, high)
        for side in range(2):
            mine_ref[side, c] = jnp.where(odd, odd_in[side], even_in[side])
            send_ref[side, c] = jnp.where(odd, even_in[side], odd_in[side])


def enter(me, power, block, entry, own, other, ready, points):
    return pl.pallas_call(
        functools.partial(enter_kernel, points=points),
        name="enter",
        out_shape=(held(*block.shape), held(*block.shape)),
        in_specs=[SMEM] + [VMEM] * 5 + [ANY],
        out_specs=(VMEM, VMEM),
        compiler_params=params(block.size * 4, 12),
    )(me, power, block, entry, own, other, ready)


def close_kernel(me_ref, s_ref, power_ref, mine_ref, got_ref, out_ref, x_ref, both_ref, sems):
    comps, points, planes, radial = s_ref.shape
    half = mine_ref.shape[3]
    core = me_ref[0] % 2
    both_ref[:, :, :, pl.ds(pl.multiple_of(core * half, half), half)] = mine_ref[...]
    both_ref[:, :, :, pl.ds(pl.multiple_of((1 - core) * half, half), half)] = got_ref[...]
    leaves = []
    for c in range(comps):
        before, after = both_ref[0, c], both_ref[1, c]

        def point(t):
            x_ref[c, t] = s_ref[c, t] + power_ref[pl.ds(t + 1, 1)] * before + power_ref[pl.ds(points - t, 1)] * after

        each(points, point)
        leaves.append(pltpu.make_async_copy(x_ref.at[c], out_ref.at[c], sems.at[c]))
        leaves[c].start()
    for leave in leaves:
        leave.wait()


def close(me, s, power, mine, got):
    return pl.pallas_call(
        close_kernel,
        name="close",
        out_shape=jax.ShapeDtypeStruct(s.shape, s.dtype),
        in_specs=[SMEM] + [VMEM] * 4,
        out_specs=ANY,
        scratch_shapes=[
            pltpu.VMEM(s.shape, jnp.float32),
            pltpu.VMEM((2,) + s.shape[:1] + s.shape[2:], jnp.float32),
            pltpu.SemaphoreType.DMA((s.shape[0],)),
        ],
        compiler_params=params(s.size * 4, 5),
    )(me, s, power, mine, got)


def local(velocity, radial_op, azimuth_stencil, viscous_factor):
    sectors = lax.axis_size("theta")
    comps, points, planes, radial = velocity.shape
    reach = (azimuth_stencil.shape[0] - 1) // 2
    width = radial_op.shape[1] - radial
    me = lax.axis_index("theta").astype(jnp.int32).reshape(1)
    op = radial_op.T

    velocity, planes_out = load(pltpu.with_memory_space_constraint(velocity, pltpu.HBM))
    planes_in = swap(planes_out, "gz", 1)
    chip_out = pack_side(me, velocity, planes_out, reach, False)
    chip_in = swap_across(chip_out, "theta")
    mirror_out = pack_mirror(velocity, chip_out, width)
    mirror_in = swap(mirror_out, "theta", sectors // 2)
    core_out = pack_side(me, velocity, mirror_out, reach, True)
    core_in = swap(core_out, "theta", 1)
    power, taps = table(me, viscous_factor, azimuth_stencil, points, sectors, planes, radial)
    n = inner_terms(taps, velocity, op)
    n = side_terms(core_kernel, "core_terms", me, taps, velocity, core_in, n)
    n = side_terms(late_kernel, "late_terms", me, taps, velocity, chip_in, n)
    n = mirror_terms(velocity, op, mirror_in, n)
    n, own, send = planes_terms(me, velocity, planes_in, power, n)
    other = swap(send, "theta", 1)
    s, nonlinear = sweep(velocity, n, power)
    block = pair(me, power, own, other, points)
    entries = ()
    for bit in range(1, sectors.bit_length() - 1):
        block, entry = merge(me, power, block, swap(block, "theta", 1 << bit), entries, points, bit)
        entries = (entry,)
    mine, send = enter(me, power, block, entry, own, other, s, points)
    new_velocity = close(me, s, power, mine, swap(send, "theta", 1))
    return (new_velocity, nonlinear)


def solution(mesh):
    in_specs = (P(None, "theta", "gz", None), P(), P(), P())
    out_specs = (P(None, "theta", "gz", None), P(None, "theta", "gz", None))
    return jax.shard_map(local, mesh=mesh, in_specs=in_specs, out_specs=out_specs, check_vma=False)
```

```python
import functools

import jax
import jax.numpy as jnp
from jax import lax
from jax.experimental import pallas as pl
from jax.experimental.pallas import tpu as pltpu
from jax.sharding import PartitionSpec as P

AXIAL_WEIGHTS = (0.75, -0.15, 1.0 / 60.0)
AXIAL_REACH = len(AXIAL_WEIGHTS)
STEP_WEIGHT = 0.2
MIRROR_SIGNS = (-1.0, -1.0, 1.0)
LANES = 128
UNROLL = 16
INNER = 10 << 29
MIRROR = 1 << 26
SIDE = 1 << 26

VMEM = pl.BlockSpec(memory_space=pltpu.VMEM)
SMEM = pl.BlockSpec(memory_space=pltpu.SMEM)
ANY = pl.BlockSpec(memory_space=pl.ANY)
HBM = pl.BlockSpec(memory_space=pltpu.HBM)


def params(block_bytes, blocks):
    return pltpu.CompilerParams(vmem_limit_bytes=(2 << 20) + blocks * block_bytes)


def held(*shape):
    return pltpu.VMEM(shape, jnp.float32)


def each(count, body):
    if count <= UNROLL:
        for i in range(count):
            body(i)
    else:
        pl.loop(0, count)(body)


def swap(block, axis, bit):
    size = lax.axis_size(axis)
    return lax.ppermute(block, axis, [(i, i ^ bit) for i in range(size)])


def swap_across(block, axis):
    size = lax.axis_size(axis)
    route = []
    for odd in range(1, size, 2):
        route += [(odd, (odd + 1) % size), ((odd + 1) % size, odd)]
    return lax.ppermute(block, axis, route)


def split(x):
    high = x.astype(jnp.bfloat16)
    return high, (x - high.astype(jnp.float32)).astype(jnp.bfloat16)


def product(left, right):
    dot = functools.partial(jnp.dot, preferred_element_type=jnp.float32)
    return dot(left[0], right[0]) + (dot(left[0], right[1]) + dot(left[1], right[0]))


def load_kernel(hbm_ref, v_ref, y_ref, sems):
    comps, points, planes, _ = v_ref.shape
    carriers = y_ref.shape[1]
    lo, hi = AXIAL_REACH, planes - AXIAL_REACH
    loads = []
    for c in range(comps):
        ways = ((hbm_ref.at[c], v_ref.at[c]), (hbm_ref.at[c, pl.ds(0, carriers)], y_ref.at[c]))
        loads.append([pltpu.make_async_copy(*way, sems.at[k, c]) for k, way in enumerate(ways)])
    for c in range(comps):
        for way in loads[c]:
            way.start()
    for c in range(comps):
        for way in loads[c]:
            way.wait()

        def ride(j):
            t = carriers + j
            y_ref[c, 3 * j, lo:hi] = v_ref[c, t, 0:2]
            y_ref[c, 3 * j + 1, lo : lo + 1] = v_ref[c, t, 2:3]
            y_ref[c, 3 * j + 1, lo + 1 : hi] = v_ref[c, t, hi : hi + 1]
            y_ref[c, 3 * j + 2, lo:hi] = v_ref[c, t, hi + 1 :]

        each(points - carriers, ride)


def load(v):
    comps, points, planes, radial = v.shape
    return pl.pallas_call(
        load_kernel,
        name="load",
        out_shape=(held(*v.shape), held(comps, points - points // 4, planes, radial)),
        in_specs=[HBM],
        out_specs=(VMEM, VMEM),
        scratch_shapes=[pltpu.SemaphoreType.DMA((2, comps))],
        compiler_params=params(v.size * 4, 2),
    )(v)


def pack_side_kernel(me_ref, v_ref, first_ref, side_ref, *, after):
    points, reach = v_ref.shape[1], side_ref.shape[1]

    def put(start):
        for c in range(v_ref.shape[0]):
            for h in range(reach):
                side_ref[c, h] = v_ref[c, start + h]

    even = me_ref[0] % 2 == 0
    last = even if after else jnp.logical_not(even)
    pl.when(last)(lambda: put(points - reach))
    pl.when(jnp.logical_not(last))(lambda: put(0))


def pack_side(me, v, first, reach, after):
    comps, _, planes, radial = v.shape
    return pl.pallas_call(
        functools.partial(pack_side_kernel, after=after),
        name="pack_core" if after else "pack_chip",
        out_shape=held(comps, reach, planes, radial),
        in_specs=[SMEM, VMEM, ANY],
        out_specs=VMEM,
        compiler_params=params(v.size * 4, 3),
    )(me, v, first)


def pack_mirror_kernel(v_ref, first_ref, mirror_ref):
    points, tiles = v_ref.shape[1], mirror_ref.shape[1]
    width = LANES // (points // tiles)
    lane = lax.broadcasted_iota(jnp.int32, mirror_ref.shape[2:], 1)

    def put(p):
        for c in range(v_ref.shape[0]):
            tile = v_ref[c, p, :, :LANES]
            for q in range(1, points // tiles):
                part = pltpu.roll(v_ref[c, q * tiles + p, :, :LANES], q * width, 1)
                tile = jnp.where(lane < q * width, tile, part)
            mirror_ref[c, p] = tile

    each(tiles, put)


def pack_mirror(v, first, width):
    comps, points, planes, _ = v.shape
    return pl.pallas_call(
        pack_mirror_kernel,
        name="pack_mirror",
        out_shape=held(comps, points // (LANES // width), planes, LANES),
        in_specs=[VMEM, ANY],
        out_specs=VMEM,
        compiler_params=params(v.size * 4, 2),
    )(v, first)


def inverse_radius(radial, start=0):
    return 1.0 / ((lax.broadcasted_iota(jnp.int32, (1, radial), 1) + start).astype(jnp.float32) + 0.5)


def axial_weights(planes, inside):
    row = lax.broadcasted_iota(jnp.int32, (planes, LANES), 0)
    weights = []
    for m, w in enumerate(AXIAL_WEIGHTS, 1):
        for shift, own, sign in ((m, row < planes - m, 1.0), (planes - m, row >= m, -1.0)):
            keep = own if inside else jnp.logical_not(own)
            weights.append((shift, jnp.where(keep, sign * w, 0.0)))
    return weights


def axial_part(tile, weights):
    planes, width = tile.shape
    weights = [(shift, jnp.concatenate([weight] * (width // LANES), axis=1)) for shift, weight in weights]
    total = None
    for shift, weight in weights:
        term = weight * pltpu.roll(tile, planes - shift, 0)
        total = term if total is None else total + term
    return total


def mirror_kernel(v_ref, op_ref, mirror_ref, n_in_ref, n_ref, grad_ref):
    comps, points, planes, radial = v_ref.shape
    tiles = mirror_ref.shape[1]
    count = points // tiles
    width = LANES // count
    rows = tiles * planes
    right = split(jnp.concatenate([op_ref[radial:]] * count, axis=0))
    lane = lax.broadcasted_iota(jnp.int32, (rows, LANES), 1)
    for c in range(comps):
        high, low = split(MIRROR_SIGNS[c] * mirror_ref[c].reshape(rows, LANES))
        zero = jnp.zeros_like(high)
        parts = [
            [jnp.where((lane >= q * width) & (lane < (q + 1) * width), x, zero) for q in range(count)]
            for x in (high, low)
        ]
        left = [jnp.concatenate(x, axis=0) for x in parts]
        grad_ref[c * points * planes : (c + 1) * points * planes] = product(left, right)

    def finish(t):
        for c in range(comps):
            start = pl.multiple_of((c * points + t) * planes, planes)
            n_ref[c, t] = n_in_ref[c, t] + v_ref[0, t] * grad_ref[pl.ds(start, planes)]

    each(points, finish)


def mirror_terms(v, op, mirror, n):
    return pl.pallas_call(
        mirror_kernel,
        name="mirror_terms",
        out_shape=held(*v.shape),
        in_specs=[VMEM] * 4,
        out_specs=VMEM,
        scratch_shapes=[pltpu.VMEM((v.size // v.shape[3], v.shape[3]), jnp.float32)],
        input_output_aliases={3: 0},
        compiler_params=params(v.size * 4, 8),
        cost_estimate=pl.CostEstimate(flops=MIRROR, bytes_accessed=16 * v.size, transcendentals=0),
    )(v, op, mirror, n)


def inner_kernel(tap_ref, v_ref, op_ref, n_ref, grad_ref):
    comps, points, planes, radial = v_ref.shape
    reach = (tap_ref.shape[0] - 1) // 2
    rows = points * planes
    right = split(op_ref[:radial])
    for c in range(comps):
        grad_ref[c * rows : (c + 1) * rows] = product(split(v_ref[c].reshape(rows, radial)), right)
    weights = axial_weights(planes, True)

    @pl.loop(0, radial // LANES)
    def column(k):
        lanes = pl.ds(pl.multiple_of(k * LANES, LANES), LANES)
        inv_r = inverse_radius(LANES, k * LANES)
        for c in range(comps):
            for t in range(points):
                a, b, e = [v_ref[i, t, :, lanes] for i in range(3)]
                b_inv = b * inv_r
                around = None
                for m in range(max(-reach, -t), min(reach, points - 1 - t) + 1):
                    term = tap_ref[m + reach] * v_ref[c, t + m, :, lanes]
                    around = term if around is None else around + term
                start = c * rows + t * planes
                n = a * grad_ref[start : start + planes, lanes] + b_inv * around
                n = n + e * axial_part(v_ref[c, t, :, lanes], weights)
                if c == 0:
                    n = n - b_inv * b
                elif c == 1:
                    n = n + a * b_inv
                n_ref[c, t, :, lanes] = n


def inner_terms(taps, v, op):
    return pl.pallas_call(
        inner_kernel,
        name="inner_terms",
        out_shape=held(*v.shape),
        in_specs=[VMEM] * 3,
        out_specs=VMEM,
        scratch_shapes=[pltpu.VMEM((v.size // v.shape[3], v.shape[3]), jnp.float32)],
        compiler_params=params(v.size * 4, 7),
        cost_estimate=pl.CostEstimate(flops=INNER, bytes_accessed=16 * v.size, transcendentals=0),
    )(taps, v, op)


def add_side(tap_ref, v_ref, side_ref, n_in_ref, n_ref, before):
    comps, points, _, radial = v_ref.shape
    reach = side_ref.shape[1]
    first = 0 if before else reach + 1

    @pl.loop(0, radial // LANES)
    def column(k):
        lanes = pl.ds(pl.multiple_of(k * LANES, LANES), LANES)
        inv_r = inverse_radius(LANES, k * LANES)
        weights = [tap_ref[first + i] for i in range(reach)]
        for c in range(comps):
            side = [side_ref[c, h, :, lanes] for h in range(reach)]
            for u in range(reach):
                t = u if before else points - reach + u
                taps = [(h, h - u) for h in range(u, reach)] if before else [(h, reach - 1 + h - u) for h in range(u + 1)]
                around = None
                for h, w in taps:
                    term = weights[w] * side[h]
                    around = term if around is None else around + term
                n_ref[c, t, :, lanes] = n_in_ref[c, t, :, lanes] + v_ref[1, t, :, lanes] * inv_r * around


def core_kernel(me_ref, tap_ref, v_ref, core_ref, n_in_ref, n_ref):
    even = me_ref[0] % 2 == 0
    add = functools.partial(add_side, tap_ref, v_ref, core_ref, n_in_ref, n_ref)
    pl.when(even)(lambda: add(False))
    pl.when(jnp.logical_not(even))(lambda: add(True))


def late_kernel(me_ref, tap_ref, v_ref, chip_ref, n_in_ref, n_ref):
    even = me_ref[0] % 2 == 0
    add = functools.partial(add_side, tap_ref, v_ref, chip_ref, n_in_ref, n_ref)
    pl.when(even)(lambda: add(True))
    pl.when(jnp.logical_not(even))(lambda: add(False))


def side_terms(kernel, name, me, taps, v, side, n):
    return pl.pallas_call(
        kernel,
        name=name,
        out_shape=held(*v.shape),
        in_specs=[SMEM, VMEM, VMEM, VMEM, VMEM],
        out_specs=VMEM,
        input_output_aliases={4: 0},
        compiler_params=params(v.size * 4, 5),
        cost_estimate=pl.CostEstimate(flops=SIDE, bytes_accessed=12 * v.size, transcendentals=0),
    )(me, taps, v, side, n)


def planes_kernel(me_ref, v_ref, y_ref, power_ref, n_in_ref, n_ref, ends_ref, tile_ref, *, own):
    comps, points, planes, radial = v_ref.shape
    half = radial // 2
    carriers = y_ref.shape[1]
    lo, hi = AXIAL_REACH, planes - AXIAL_REACH
    weights = axial_weights(planes, False)
    lanes = half_lanes(me_ref, half, own)
    for c in range(comps):
        for j in range(points - carriers):
            tile_ref[c, j, 0:2] = y_ref[c, 3 * j, lo:hi, lanes]
            tile_ref[c, j, 2:3] = y_ref[c, 3 * j + 1, lo : lo + 1, lanes]
            tile_ref[c, j, lo:hi] = jnp.zeros((hi - lo, half), jnp.float32)
            tile_ref[c, j, hi : hi + 1] = y_ref[c, 3 * j + 1, lo + 1 : hi, lanes]
            tile_ref[c, j, hi + 1 :] = y_ref[c, 3 * j + 2, lo:hi, lanes]
    decay = power_ref[1:2, lanes]
    ends_ref[...] = jnp.zeros_like(ends_ref)
    for t in range(points):
        for c in range(comps):
            tile = y_ref[c, t, :, lanes] if t < carriers else tile_ref[c, t - carriers]
            n = n_in_ref[c, t, :, lanes] + v_ref[2, t, :, lanes] * axial_part(tile, weights)
            n_ref[c, t, :, lanes] = n
            right_side = v_ref[c, t, :, lanes] - STEP_WEIGHT * n
            ends_ref[0, c] = decay * ends_ref[0, c] + right_side
            ends_ref[1, c] = ends_ref[1, c] + power_ref[t : t + 1, lanes] * right_side


def planes_terms(me, v, y, power, n, own):
    comps, points, planes, radial = v.shape
    return pl.pallas_call(
        functools.partial(planes_kernel, own=own),
        name="planes_own" if own else "planes_other",
        out_shape=(held(*v.shape), held(2, comps, planes, radial // 2)),
        in_specs=[SMEM] + [VMEM] * 4,
        out_specs=(VMEM, VMEM),
        scratch_shapes=[pltpu.VMEM((comps, points - y.shape[1], planes, radial // 2), jnp.float32)],
        input_output_aliases={4: 0},
        compiler_params=params(v.size * 4, 6),
        cost_estimate=pl.CostEstimate(flops=20 * v.size, bytes_accessed=16 * v.size, transcendentals=0),
    )(me, v, y, power, n)


def table_kernel(me_ref, factor_ref, stencil_ref, row_ref, tap_ref, *, points, sectors):
    radial = row_ref.shape[1]
    one = jnp.ones((1, radial), jnp.float32)
    half = (0.5 * lax.rsqrt(factor_ref[0] * one)) / inverse_radius(radial)
    root = jnp.sqrt(1.0 + half * half)
    loss = 2.0 * half * (root - half)
    rows = [one]
    for _ in range(points):
        rows.append(rows[-1] * (1.0 - loss))
    total = loss
    left, result = points * sectors, None
    while left:
        if left & 1:
            result = total if result is None else result + total - result * total
        total = total * (2.0 - total)
        left >>= 1
    across = rows[points] * rows[points]
    rows += [half / root, 1.0 / result]
    before = after = one
    for bit in range(1, sectors.bit_length() - 1):
        upper = (me_ref[0] >> bit) % 2 == 1
        rows += [across, before, after]
        before, after = jnp.where(upper, before * across, before), jnp.where(upper, after, after * across)
        across = across * across
    for k, row in enumerate(rows + [before, after]):
        row_ref[k : k + 1] = row
    for k in range(tap_ref.shape[0]):
        tap_ref[k] = jnp.full(tap_ref.shape[1:], stencil_ref[k], jnp.float32)


def table(me, viscous_factor, stencil, points, sectors, planes, radial):
    count = points + 5 + 3 * (sectors.bit_length() - 2)
    return pl.pallas_call(
        functools.partial(table_kernel, points=points, sectors=sectors),
        name="table",
        out_shape=(held(count, radial), held(stencil.shape[0], planes, LANES)),
        in_specs=[SMEM, SMEM, SMEM],
        out_specs=(VMEM, VMEM),
        compiler_params=params(1 << 20, 1),
        cost_estimate=pl.CostEstimate(flops=1000 * radial, bytes_accessed=400 * radial, transcendentals=0),
    )(me, viscous_factor, stencil)


def sweep_kernel(v_ref, n_ref, power_ref, s_ref, nonlinear_ref, sem):
    leave = pltpu.make_async_copy(n_ref, nonlinear_ref, sem)
    leave.start()
    comps, points, planes, radial = v_ref.shape
    decay = power_ref[1:2]
    height = power_ref[points + 1 : points + 2]
    for c in range(comps):
        s_ref[c, 0] = height * (v_ref[c, 0] - STEP_WEIGHT * n_ref[c, 0])

        def forward(i):
            t = i + 1
            s_ref[c, t] = decay * s_ref[c, t - 1] + height * (v_ref[c, t] - STEP_WEIGHT * n_ref[c, t])

        each(points - 1, forward)

    def backward(i, carry):
        t = points - 1 - i
        after = []
        for c in range(comps):
            s_ref[c, t] = s_ref[c, t] + carry[c]
            after.append(decay * (carry[c] + height * (v_ref[c, t] - STEP_WEIGHT * n_ref[c, t])))
        return tuple(after)

    start = (jnp.zeros((planes, radial), jnp.float32),) * comps
    lax.fori_loop(0, points, backward, start, unroll=points <= UNROLL)
    leave.wait()


def sweep(v, n, power):
    return pl.pallas_call(
        sweep_kernel,
        name="sweep",
        out_shape=(held(*v.shape), jax.ShapeDtypeStruct(v.shape, v.dtype)),
        in_specs=[VMEM] * 3,
        out_specs=(VMEM, ANY),
        scratch_shapes=[pltpu.SemaphoreType.DMA],
        compiler_params=params(v.size * 4, 4),
        cost_estimate=pl.CostEstimate(flops=10 * v.size, bytes_accessed=12 * v.size, transcendentals=0),
    )(v, n, power)


def half_lanes(me_ref, half, own=True):
    core = me_ref[0] % 2
    return pl.ds(pl.multiple_of((core if own else 1 - core) * half, half), half)


def pair_kernel(me_ref, power_ref, own_ref, other_ref, block_ref, *, points):
    half = own_ref.shape[3]
    hop = power_ref[points : points + 1, half_lanes(me_ref, half)]
    odd = me_ref[0] % 2 == 1
    for c in range(own_ref.shape[1]):
        for side in range(2):
            own, other = own_ref[side, c], other_ref[side, c]
            far, near = (own, other) if side == 0 else (other, own)
            block_ref[side, c] = jnp.where(odd, hop * near + far, hop * far + near)


def pair(me, power, own, other, points):
    return pl.pallas_call(
        functools.partial(pair_kernel, points=points),
        name="pair",
        out_shape=held(*own.shape),
        in_specs=[SMEM, VMEM, VMEM, VMEM],
        out_specs=VMEM,
        compiler_params=params(own.size * 4, 8),
    )(me, power, own, other)


def merge_kernel(me_ref, power_ref, block_ref, other_ref, *refs, points, bit):
    *entry_refs, block_out_ref, entry_out_ref = refs
    comps, half = block_ref.shape[1], block_ref.shape[3]
    lanes = half_lanes(me_ref, half)
    first = points + 3 * bit
    across, before, after = [power_ref[first + k : first + k + 1, lanes] for k in range(3)]
    upper = (me_ref[0] >> bit) % 2 == 1
    before = jnp.where(upper, before, 0.0)
    after = jnp.where(upper, 0.0, after)
    for c in range(comps):
        low, high = block_ref[0, c], block_ref[1, c]
        other_low, other_high = other_ref[0, c], other_ref[1, c]
        block_out_ref[0, c] = jnp.where(upper, across * other_low + low, across * low + other_low)
        block_out_ref[1, c] = jnp.where(upper, other_high + across * high, high + across * other_high)
        for side, enters in enumerate((before * other_low, after * other_high)):
            entry_out_ref[side, c] = entry_refs[0][side, c] + enters if entry_refs else enters


def merge(me, power, block, other, entries, points, bit):
    return pl.pallas_call(
        functools.partial(merge_kernel, points=points, bit=bit),
        name="merge",
        out_shape=(held(*block.shape), held(*block.shape)),
        in_specs=[SMEM] + [VMEM] * (3 + len(entries)),
        out_specs=(VMEM, VMEM),
        compiler_params=params(block.size * 4, 8),
    )(me, power, block, other, *entries)


def enter_kernel(me_ref, power_ref, block_ref, entry_ref, own_ref, other_ref, ready_ref, mine_ref, send_ref, *, points):
    comps, half = block_ref.shape[1], block_ref.shape[3]
    lanes = half_lanes(me_ref, half)
    row = lambda k: power_ref[k : k + 1, lanes]
    hop, height, wrap = row(points), row(points + 1), row(points + 2)
    last = power_ref.shape[0]
    before, after = row(last - 2) * wrap, row(last - 1) * wrap
    odd = me_ref[0] % 2 == 1
    for c in range(comps):
        low = height * (entry_ref[0, c] + before * block_ref[0, c])
        high = height * (entry_ref[1, c] + after * block_ref[1, c])
        even_low = height * jnp.where(odd, other_ref[0, c], own_ref[0, c])
        odd_high = height * jnp.where(odd, own_ref[1, c], other_ref[1, c])
        even_in = (low, odd_high + hop * high)
        odd_in = (even_low + hop * low, high)
        for side in range(2):
            mine_ref[side, c] = jnp.where(odd, odd_in[side], even_in[side])
            send_ref[side, c] = jnp.where(odd, even_in[side], odd_in[side])


def enter(me, power, block, entry, own, other, ready, points):
    return pl.pallas_call(
        functools.partial(enter_kernel, points=points),
        name="enter",
        out_shape=(held(*block.shape), held(*block.shape)),
        in_specs=[SMEM] + [VMEM] * 5 + [ANY],
        out_specs=(VMEM, VMEM),
        compiler_params=params(block.size * 4, 12),
    )(me, power, block, entry, own, other, ready)


def close_kernel(me_ref, s_ref, power_ref, entry_ref, *refs, own):
    out_ref, x_ref, sems = refs[-3:]
    comps, points, _, _ = s_ref.shape
    lanes = half_lanes(me_ref, entry_ref.shape[3], own)
    leaves = []
    for c in range(comps):
        before, after = entry_ref[0, c], entry_ref[1, c]

        def point(t):
            decayed = power_ref[pl.ds(t + 1, 1), lanes] * before + power_ref[pl.ds(points - t, 1), lanes] * after
            x_ref[c, t] = s_ref[c, t, :, lanes] + decayed

        each(points, point)
        leaves.append(pltpu.make_async_copy(x_ref.at[c], out_ref.at[c, :, :, lanes], sems.at[c]))
        leaves[c].start()
    for leave in leaves:
        leave.wait()


def close(me, s, power, entry, out, own):
    comps, points, planes, radial = s.shape
    return pl.pallas_call(
        functools.partial(close_kernel, own=own),
        name="close_own" if own else "close_other",
        out_shape=jax.ShapeDtypeStruct(s.shape, s.dtype),
        in_specs=[SMEM] + [VMEM] * 3 + [ANY] * len(out),
        out_specs=ANY,
        scratch_shapes=[
            pltpu.VMEM((comps, points, planes, radial // 2), jnp.float32),
            pltpu.SemaphoreType.DMA((comps,)),
        ],
        input_output_aliases={4: 0} if out else {},
        compiler_params=params(s.size * 4, 5),
        cost_estimate=pl.CostEstimate(flops=4 * s.size, bytes_accessed=8 * s.size, transcendentals=0),
    )(me, s, power, entry, *out)


def local(velocity, radial_op, azimuth_stencil, viscous_factor):
    sectors = lax.axis_size("theta")
    comps, points, planes, radial = velocity.shape
    reach = (azimuth_stencil.shape[0] - 1) // 2
    width = radial_op.shape[1] - radial
    me = lax.axis_index("theta").astype(jnp.int32).reshape(1)
    op = radial_op.T

    velocity, planes_out = load(pltpu.with_memory_space_constraint(velocity, pltpu.HBM))
    planes_in = swap(planes_out, "gz", 1)
    chip_out = pack_side(me, velocity, planes_out, reach, False)
    chip_in = swap_across(chip_out, "theta")
    mirror_out = pack_mirror(velocity, chip_out, width)
    mirror_in = swap(mirror_out, "theta", sectors // 2)
    core_out = pack_side(me, velocity, mirror_out, reach, True)
    core_in = swap(core_out, "theta", 1)
    power, taps = table(me, viscous_factor, azimuth_stencil, points, sectors, planes, radial)
    n = inner_terms(taps, velocity, op)
    n = side_terms(core_kernel, "core_terms", me, taps, velocity, core_in, n)
    n = mirror_terms(velocity, op, mirror_in, n)
    n = side_terms(late_kernel, "late_terms", me, taps, velocity, chip_in, n)
    n, send = planes_terms(me, velocity, planes_in, power, n, False)
    other = swap(send, "theta", 1)
    n, own = planes_terms(me, velocity, planes_in, power, n, True)
    s, nonlinear = sweep(velocity, n, power)
    block = pair(me, power, own, other, points)
    entries = ()
    for bit in range(1, sectors.bit_length() - 1):
        block, entry = merge(me, power, block, swap(block, "theta", 1 << bit), entries, points, bit)
        entries = (entry,)
    mine, send = enter(me, power, block, entry, own, other, s, points)
    got = swap(send, "theta", 1)
    new_velocity = close(me, s, power, mine, (), True)
    new_velocity = close(me, s, power, got, (new_velocity,), False)
    return (new_velocity, nonlinear)


def solution(mesh):
    in_specs = (P(None, "theta", "gz", None), P(), P(), P())
    out_specs = (P(None, "theta", "gz", None), P(None, "theta", "gz", None))
    return jax.shard_map(local, mesh=mesh, in_specs=in_specs, out_specs=out_specs, check_vma=False)
```

```python
import functools

import jax
import jax.numpy as jnp
from jax import lax
from jax.experimental import pallas as pl
from jax.experimental.pallas import tpu as pltpu
from jax.sharding import PartitionSpec as P

AXIAL_WEIGHTS = (0.75, -0.15, 1.0 / 60.0)
AXIAL_REACH = len(AXIAL_WEIGHTS)
STEP_WEIGHT = 0.2
MIRROR_SIGNS = (-1.0, -1.0, 1.0)
LANES = 128
UNROLL = 16
INNER = 10 << 29
MIRROR = 1 << 26
SIDE = 1 << 26

VMEM = pl.BlockSpec(memory_space=pltpu.VMEM)
SMEM = pl.BlockSpec(memory_space=pltpu.SMEM)
ANY = pl.BlockSpec(memory_space=pl.ANY)
HBM = pl.BlockSpec(memory_space=pltpu.HBM)


def params(block_bytes, blocks):
    return pltpu.CompilerParams(vmem_limit_bytes=(2 << 20) + blocks * block_bytes)


def held(*shape):
    return pltpu.VMEM(shape, jnp.float32)


def each(count, body):
    if count <= UNROLL:
        for i in range(count):
            body(i)
    else:
        pl.loop(0, count)(body)


def swap(block, axis, bit):
    size = lax.axis_size(axis)
    return lax.ppermute(block, axis, [(i, i ^ bit) for i in range(size)])


def swap_across(block, axis):
    size = lax.axis_size(axis)
    route = []
    for odd in range(1, size, 2):
        route += [(odd, (odd + 1) % size), ((odd + 1) % size, odd)]
    return lax.ppermute(block, axis, route)


def split(x):
    high = x.astype(jnp.bfloat16)
    return high, (x - high.astype(jnp.float32)).astype(jnp.bfloat16)


def product(left, right):
    dot = functools.partial(jnp.dot, preferred_element_type=jnp.float32)
    return dot(left[0], right[0]) + (dot(left[0], right[1]) + dot(left[1], right[0]))


def pack_tiles(v_ref, y_ref, comps):
    points, planes = v_ref.shape[1:3]
    carriers = y_ref.shape[1]
    lo, hi = AXIAL_REACH, planes - AXIAL_REACH
    for i, c in enumerate(comps):

        def carry(t):
            y_ref[i, t] = v_ref[c, t]

        def ride(j):
            t = carriers + j
            y_ref[i, 3 * j, lo:hi] = v_ref[c, t, 0:2]
            y_ref[i, 3 * j + 1, lo : lo + 1] = v_ref[c, t, 2:3]
            y_ref[i, 3 * j + 1, lo + 1 : hi] = v_ref[c, t, hi : hi + 1]
            y_ref[i, 3 * j + 2, lo:hi] = v_ref[c, t, hi + 1 :]

        each(carriers, carry)
        each(points - carriers, ride)


def rebuild_tiles(y_ref, tile_ref):
    carriers = y_ref.shape[1]
    comps, riders, planes, radial = tile_ref.shape
    lo, hi = AXIAL_REACH, planes - AXIAL_REACH
    for c in range(comps):
        for j in range(riders):
            tile_ref[c, j, 0:2] = y_ref[c, 3 * j, lo:hi]
            tile_ref[c, j, 2:3] = y_ref[c, 3 * j + 1, lo : lo + 1]
            tile_ref[c, j, lo:hi] = jnp.zeros((hi - lo, radial), jnp.float32)
            tile_ref[c, j, hi : hi + 1] = y_ref[c, 3 * j + 1, lo + 1 : hi]
            tile_ref[c, j, hi + 1 :] = y_ref[c, 3 * j + 2, lo:hi]


def load_kernel(hbm_ref, v_ref, y_ref, sems):
    order = list(range(v_ref.shape[0]))
    loads = [pltpu.make_async_copy(hbm_ref.at[c], v_ref.at[c], sems.at[c]) for c in order]
    for c in reversed(order):
        loads[c].start()
    loads[-1].wait()
    pack_tiles(v_ref, y_ref, order[-1:])
    for c in order[:-1]:
        loads[c].wait()


def load(v):
    comps, points, planes, radial = v.shape
    return pl.pallas_call(
        load_kernel,
        name="load",
        out_shape=(held(*v.shape), held(1, points - points // 4, planes, radial)),
        in_specs=[HBM],
        out_specs=(VMEM, VMEM),
        scratch_shapes=[pltpu.SemaphoreType.DMA((comps,))],
        compiler_params=params(v.size * 4, 2),
    )(v)


def pack_planes_kernel(v_ref, first_ref, y_ref):
    pack_tiles(v_ref, y_ref, range(y_ref.shape[0]))


def pack_planes(v, first):
    comps, points, planes, radial = v.shape
    return pl.pallas_call(
        pack_planes_kernel,
        name="pack_planes",
        out_shape=held(comps - 1, points - points // 4, planes, radial),
        in_specs=[VMEM, ANY],
        out_specs=VMEM,
        compiler_params=params(v.size * 4, 2),
    )(v, first)


def pack_side_kernel(me_ref, v_ref, first_ref, side_ref, *, after):
    points, reach = v_ref.shape[1], side_ref.shape[1]

    def put(start):
        for c in range(v_ref.shape[0]):
            for h in range(reach):
                side_ref[c, h] = v_ref[c, start + h]

    even = me_ref[0] % 2 == 0
    last = even if after else jnp.logical_not(even)
    pl.when(last)(lambda: put(points - reach))
    pl.when(jnp.logical_not(last))(lambda: put(0))


def pack_side(me, v, first, reach, after):
    comps, _, planes, radial = v.shape
    return pl.pallas_call(
        functools.partial(pack_side_kernel, after=after),
        name="pack_core" if after else "pack_chip",
        out_shape=held(comps, reach, planes, radial),
        in_specs=[SMEM, VMEM, ANY],
        out_specs=VMEM,
        compiler_params=params(v.size * 4, 3),
    )(me, v, first)


def pack_mirror_kernel(v_ref, first_ref, mirror_ref):
    points, tiles = v_ref.shape[1], mirror_ref.shape[1]
    width = LANES // (points // tiles)
    lane = lax.broadcasted_iota(jnp.int32, mirror_ref.shape[2:], 1)

    def put(p):
        for c in range(v_ref.shape[0]):
            tile = v_ref[c, p, :, :LANES]
            for q in range(1, points // tiles):
                part = pltpu.roll(v_ref[c, q * tiles + p, :, :LANES], q * width, 1)
                tile = jnp.where(lane < q * width, tile, part)
            mirror_ref[c, p] = tile

    each(tiles, put)


def pack_mirror(v, first, width):
    comps, points, planes, _ = v.shape
    return pl.pallas_call(
        pack_mirror_kernel,
        name="pack_mirror",
        out_shape=held(comps, points // (LANES // width), planes, LANES),
        in_specs=[VMEM, ANY],
        out_specs=VMEM,
        compiler_params=params(v.size * 4, 2),
    )(v, first)


def inverse_radius(radial, start=0):
    return 1.0 / ((lax.broadcasted_iota(jnp.int32, (1, radial), 1) + start).astype(jnp.float32) + 0.5)


def axial_weights(planes, inside):
    row = lax.broadcasted_iota(jnp.int32, (planes, LANES), 0)
    weights = []
    for m, w in enumerate(AXIAL_WEIGHTS, 1):
        for shift, own, sign in ((m, row < planes - m, 1.0), (planes - m, row >= m, -1.0)):
            keep = own if inside else jnp.logical_not(own)
            weights.append((shift, jnp.where(keep, sign * w, 0.0)))
    return weights


def axial_part(tile, weights):
    planes, width = tile.shape
    weights = [(shift, jnp.concatenate([weight] * (width // LANES), axis=1)) for shift, weight in weights]
    total = None
    for shift, weight in weights:
        term = weight * pltpu.roll(tile, planes - shift, 0)
        total = term if total is None else total + term
    return total


def mirror_kernel(v_ref, op_ref, mirror_ref, n_in_ref, n_ref, grad_ref):
    comps, points, planes, radial = v_ref.shape
    tiles = mirror_ref.shape[1]
    count = points // tiles
    width = LANES // count
    rows = tiles * planes
    right = split(jnp.concatenate([op_ref[radial:]] * count, axis=0))
    lane = lax.broadcasted_iota(jnp.int32, (rows, LANES), 1)
    for c in range(comps):
        high, low = split(MIRROR_SIGNS[c] * mirror_ref[c].reshape(rows, LANES))
        zero = jnp.zeros_like(high)
        parts = [
            [jnp.where((lane >= q * width) & (lane < (q + 1) * width), x, zero) for q in range(count)]
            for x in (high, low)
        ]
        left = [jnp.concatenate(x, axis=0) for x in parts]
        grad_ref[c * points * planes : (c + 1) * points * planes] = product(left, right)

    def finish(t):
        for c in range(comps):
            start = pl.multiple_of((c * points + t) * planes, planes)
            n_ref[c, t] = n_in_ref[c, t] + v_ref[0, t] * grad_ref[pl.ds(start, planes)]

    each(points, finish)


def mirror_terms(v, op, mirror, n):
    return pl.pallas_call(
        mirror_kernel,
        name="mirror_terms",
        out_shape=held(*v.shape),
        in_specs=[VMEM] * 4,
        out_specs=VMEM,
        scratch_shapes=[pltpu.VMEM((v.size // v.shape[3], v.shape[3]), jnp.float32)],
        input_output_aliases={3: 0},
        compiler_params=params(v.size * 4, 8),
        cost_estimate=pl.CostEstimate(flops=MIRROR, bytes_accessed=16 * v.size, transcendentals=0),
    )(v, op, mirror, n)


def inner_kernel(tap_ref, v_ref, op_ref, n_ref, grad_ref):
    comps, points, planes, radial = v_ref.shape
    reach = (tap_ref.shape[0] - 1) // 2
    rows = points * planes
    right = split(op_ref[:radial])
    for c in range(comps):
        grad_ref[c * rows : (c + 1) * rows] = product(split(v_ref[c].reshape(rows, radial)), right)
    weights = axial_weights(planes, True)

    @pl.loop(0, radial // LANES)
    def column(k):
        lanes = pl.ds(pl.multiple_of(k * LANES, LANES), LANES)
        inv_r = inverse_radius(LANES, k * LANES)
        for c in range(comps):
            for t in range(points):
                a, b, e = [v_ref[i, t, :, lanes] for i in range(3)]
                b_inv = b * inv_r
                around = None
                for m in range(max(-reach, -t), min(reach, points - 1 - t) + 1):
                    term = tap_ref[m + reach] * v_ref[c, t + m, :, lanes]
                    around = term if around is None else around + term
                start = c * rows + t * planes
                n = a * grad_ref[start : start + planes, lanes] + b_inv * around
                n = n + e * axial_part(v_ref[c, t, :, lanes], weights)
                if c == 0:
                    n = n - b_inv * b
                elif c == 1:
                    n = n + a * b_inv
                n_ref[c, t, :, lanes] = n


def inner_terms(taps, v, op):
    return pl.pallas_call(
        inner_kernel,
        name="inner_terms",
        out_shape=held(*v.shape),
        in_specs=[VMEM] * 3,
        out_specs=VMEM,
        scratch_shapes=[pltpu.VMEM((v.size // v.shape[3], v.shape[3]), jnp.float32)],
        compiler_params=params(v.size * 4, 7),
        cost_estimate=pl.CostEstimate(flops=INNER, bytes_accessed=16 * v.size, transcendentals=0),
    )(taps, v, op)


def add_side(tap_ref, v_ref, side_ref, n_in_ref, n_ref, before):
    comps, points, _, radial = v_ref.shape
    reach = side_ref.shape[1]
    first = 0 if before else reach + 1

    @pl.loop(0, radial // LANES)
    def column(k):
        lanes = pl.ds(pl.multiple_of(k * LANES, LANES), LANES)
        inv_r = inverse_radius(LANES, k * LANES)
        weights = [tap_ref[first + i] for i in range(reach)]
        for c in range(comps):
            side = [side_ref[c, h, :, lanes] for h in range(reach)]
            for u in range(reach):
                t = u if before else points - reach + u
                taps = [(h, h - u) for h in range(u, reach)] if before else [(h, reach - 1 + h - u) for h in range(u + 1)]
                around = None
                for h, w in taps:
                    term = weights[w] * side[h]
                    around = term if around is None else around + term
                n_ref[c, t, :, lanes] = n_in_ref[c, t, :, lanes] + v_ref[1, t, :, lanes] * inv_r * around


def core_kernel(me_ref, tap_ref, v_ref, core_ref, n_in_ref, n_ref):
    even = me_ref[0] % 2 == 0
    add = functools.partial(add_side, tap_ref, v_ref, core_ref, n_in_ref, n_ref)
    pl.when(even)(lambda: add(False))
    pl.when(jnp.logical_not(even))(lambda: add(True))


def late_kernel(me_ref, tap_ref, v_ref, chip_ref, n_in_ref, n_ref):
    even = me_ref[0] % 2 == 0
    add = functools.partial(add_side, tap_ref, v_ref, chip_ref, n_in_ref, n_ref)
    pl.when(even)(lambda: add(True))
    pl.when(jnp.logical_not(even))(lambda: add(False))


def side_terms(kernel, name, me, taps, v, side, n):
    return pl.pallas_call(
        kernel,
        name=name,
        out_shape=held(*v.shape),
        in_specs=[SMEM, VMEM, VMEM, VMEM, VMEM],
        out_specs=VMEM,
        input_output_aliases={4: 0},
        compiler_params=params(v.size * 4, 5),
        cost_estimate=pl.CostEstimate(flops=SIDE, bytes_accessed=12 * v.size, transcendentals=0),
    )(me, taps, v, side, n)


def share_kernel(v_ref, e_ref, power_ref, ends_ref, tile_ref):
    comps, points, planes, radial = v_ref.shape
    carriers = e_ref.shape[1]
    weights = axial_weights(planes, False)
    rebuild_tiles(e_ref, tile_ref)
    decay = power_ref[1:2]
    ends_ref[...] = jnp.zeros_like(ends_ref)
    for t in range(points):
        e = STEP_WEIGHT * (e_ref[0, t] if t < carriers else tile_ref[0, t - carriers])
        for c in range(comps):
            right_side = e * axial_part(v_ref[c, t], weights)
            ends_ref[0, c] = decay * ends_ref[0, c] - right_side
            ends_ref[1, c] = ends_ref[1, c] - power_ref[t : t + 1] * right_side


def share_terms(v, e, power):
    comps, points, planes, radial = v.shape
    return pl.pallas_call(
        share_kernel,
        name="share_terms",
        out_shape=held(2, comps, planes, radial),
        in_specs=[VMEM] * 3,
        out_specs=VMEM,
        scratch_shapes=[pltpu.VMEM((1, points - e.shape[1], planes, radial), jnp.float32)],
        compiler_params=params(v.size * 4, 4),
        cost_estimate=pl.CostEstimate(flops=20 * v.size, bytes_accessed=8 * v.size, transcendentals=0),
    )(v, e, power)


def ends_kernel(me_ref, v_ref, share_ref, power_ref, n_ref, ends_ref, *, own):
    comps, points, _, radial = v_ref.shape
    lanes = half_lanes(me_ref, radial // 2, own)
    decay = power_ref[1:2, lanes]
    for c in range(comps):
        low = high = None
        for t in range(points):
            right_side = v_ref[c, t, :, lanes] - STEP_WEIGHT * n_ref[c, t, :, lanes]
            low = right_side if t == 0 else decay * low + right_side
            high = right_side if t == 0 else high + power_ref[t : t + 1, lanes] * right_side
        ends_ref[0, c] = low + share_ref[0, c, :, lanes]
        ends_ref[1, c] = high + share_ref[1, c, :, lanes]


def ends_terms(me, v, share, power, n, own):
    comps, _, planes, radial = v.shape
    return pl.pallas_call(
        functools.partial(ends_kernel, own=own),
        name="ends_own" if own else "ends_other",
        out_shape=held(2, comps, planes, radial // 2),
        in_specs=[SMEM] + [VMEM] * 4,
        out_specs=VMEM,
        compiler_params=params(v.size * 4, 4),
        cost_estimate=pl.CostEstimate(flops=20 * v.size, bytes_accessed=8 * v.size, transcendentals=0),
    )(me, v, share, power, n)


def planes_kernel(v_ref, y_ref, e_ref, ready_ref, n_in_ref, n_ref, y_tile_ref, e_tile_ref):
    comps, points, planes, _ = v_ref.shape
    carriers = y_ref.shape[1]
    weights = axial_weights(planes, False)
    rebuild_tiles(y_ref, y_tile_ref)
    rebuild_tiles(e_ref, e_tile_ref)
    for t in range(points):
        for c in range(comps):
            ref, tile_ref, i = (y_ref, y_tile_ref, c) if c < comps - 1 else (e_ref, e_tile_ref, 0)
            tile = ref[i, t] if t < carriers else tile_ref[i, t - carriers]
            n_ref[c, t] = n_in_ref[c, t] + v_ref[2, t] * axial_part(tile, weights)


def planes_terms(v, y, e, ready, n):
    comps, points, planes, radial = v.shape
    riders = points - y.shape[1]
    return pl.pallas_call(
        planes_kernel,
        name="planes_terms",
        out_shape=held(*v.shape),
        in_specs=[VMEM] * 3 + [ANY, VMEM],
        out_specs=VMEM,
        scratch_shapes=[pltpu.VMEM((k, riders, planes, radial), jnp.float32) for k in (comps - 1, 1)],
        input_output_aliases={4: 0},
        compiler_params=params(v.size * 4, 6),
        cost_estimate=pl.CostEstimate(flops=20 * v.size, bytes_accessed=16 * v.size, transcendentals=0),
    )(v, y, e, ready, n)


def table_kernel(me_ref, factor_ref, stencil_ref, row_ref, tap_ref, *, points, sectors):
    radial = row_ref.shape[1]
    one = jnp.ones((1, radial), jnp.float32)
    half = (0.5 * lax.rsqrt(factor_ref[0] * one)) / inverse_radius(radial)
    root = jnp.sqrt(1.0 + half * half)
    loss = 2.0 * half * (root - half)
    rows = [one]
    for _ in range(points):
        rows.append(rows[-1] * (1.0 - loss))
    total = loss
    left, result = points * sectors, None
    while left:
        if left & 1:
            result = total if result is None else result + total - result * total
        total = total * (2.0 - total)
        left >>= 1
    across = rows[points] * rows[points]
    rows += [half / root, 1.0 / result]
    before = after = one
    for bit in range(1, sectors.bit_length() - 1):
        upper = (me_ref[0] >> bit) % 2 == 1
        rows += [across, before, after]
        before, after = jnp.where(upper, before * across, before), jnp.where(upper, after, after * across)
        across = across * across
    for k, row in enumerate(rows + [before, after]):
        row_ref[k : k + 1] = row
    for k in range(tap_ref.shape[0]):
        tap_ref[k] = jnp.full(tap_ref.shape[1:], stencil_ref[k], jnp.float32)


def table(me, viscous_factor, stencil, points, sectors, planes, radial):
    count = points + 5 + 3 * (sectors.bit_length() - 2)
    return pl.pallas_call(
        functools.partial(table_kernel, points=points, sectors=sectors),
        name="table",
        out_shape=(held(count, radial), held(stencil.shape[0], planes, LANES)),
        in_specs=[SMEM, SMEM, SMEM],
        out_specs=(VMEM, VMEM),
        compiler_params=params(1 << 20, 1),
        cost_estimate=pl.CostEstimate(flops=1000 * radial, bytes_accessed=400 * radial, transcendentals=0),
    )(me, viscous_factor, stencil)


def sweep_kernel(v_ref, n_ref, power_ref, s_ref, nonlinear_ref, sem):
    leave = pltpu.make_async_copy(n_ref, nonlinear_ref, sem)
    leave.start()
    comps, points, planes, radial = v_ref.shape
    decay = power_ref[1:2]
    height = power_ref[points + 1 : points + 2]
    for c in range(comps):
        s_ref[c, 0] = height * (v_ref[c, 0] - STEP_WEIGHT * n_ref[c, 0])

        def forward(i):
            t = i + 1
            s_ref[c, t] = decay * s_ref[c, t - 1] + height * (v_ref[c, t] - STEP_WEIGHT * n_ref[c, t])

        each(points - 1, forward)

    def backward(i, carry):
        t = points - 1 - i
        after = []
        for c in range(comps):
            s_ref[c, t] = s_ref[c, t] + carry[c]
            after.append(decay * (carry[c] + height * (v_ref[c, t] - STEP_WEIGHT * n_ref[c, t])))
        return tuple(after)

    start = (jnp.zeros((planes, radial), jnp.float32),) * comps
    lax.fori_loop(0, points, backward, start, unroll=points <= UNROLL)
    leave.wait()


def sweep(v, n, power):
    return pl.pallas_call(
        sweep_kernel,
        name="sweep",
        out_shape=(held(*v.shape), jax.ShapeDtypeStruct(v.shape, v.dtype)),
        in_specs=[VMEM] * 3,
        out_specs=(VMEM, ANY),
        scratch_shapes=[pltpu.SemaphoreType.DMA],
        compiler_params=params(v.size * 4, 4),
        cost_estimate=pl.CostEstimate(flops=10 * v.size, bytes_accessed=12 * v.size, transcendentals=0),
    )(v, n, power)


def half_lanes(me_ref, half, own=True):
    core = me_ref[0] % 2
    return pl.ds(pl.multiple_of((core if own else 1 - core) * half, half), half)


def pair_kernel(me_ref, power_ref, own_ref, other_ref, block_ref, *, points):
    half = own_ref.shape[3]
    hop = power_ref[points : points + 1, half_lanes(me_ref, half)]
    odd = me_ref[0] % 2 == 1
    for c in range(own_ref.shape[1]):
        for side in range(2):
            own, other = own_ref[side, c], other_ref[side, c]
            far, near = (own, other) if side == 0 else (other, own)
            block_ref[side, c] = jnp.where(odd, hop * near + far, hop * far + near)


def pair(me, power, own, other, points):
    return pl.pallas_call(
        functools.partial(pair_kernel, points=points),
        name="pair",
        out_shape=held(*own.shape),
        in_specs=[SMEM, VMEM, VMEM, VMEM],
        out_specs=VMEM,
        compiler_params=params(own.size * 4, 8),
    )(me, power, own, other)


def merge_kernel(me_ref, power_ref, block_ref, other_ref, *refs, points, bit):
    *entry_refs, block_out_ref, entry_out_ref = refs
    comps, half = block_ref.shape[1], block_ref.shape[3]
    lanes = half_lanes(me_ref, half)
    first = points + 3 * bit
    across, before, after = [power_ref[first + k : first + k + 1, lanes] for k in range(3)]
    upper = (me_ref[0] >> bit) % 2 == 1
    before = jnp.where(upper, before, 0.0)
    after = jnp.where(upper, 0.0, after)
    for c in range(comps):
        low, high = block_ref[0, c], block_ref[1, c]
        other_low, other_high = other_ref[0, c], other_ref[1, c]
        block_out_ref[0, c] = jnp.where(upper, across * other_low + low, across * low + other_low)
        block_out_ref[1, c] = jnp.where(upper, other_high + across * high, high + across * other_high)
        for side, enters in enumerate((before * other_low, after * other_high)):
            entry_out_ref[side, c] = entry_refs[0][side, c] + enters if entry_refs else enters


def merge(me, power, block, other, entries, points, bit):
    return pl.pallas_call(
        functools.partial(merge_kernel, points=points, bit=bit),
        name="merge",
        out_shape=(held(*block.shape), held(*block.shape)),
        in_specs=[SMEM] + [VMEM] * (3 + len(entries)),
        out_specs=(VMEM, VMEM),
        compiler_params=params(block.size * 4, 8),
    )(me, power, block, other, *entries)


def enter_kernel(me_ref, power_ref, block_ref, entry_ref, own_ref, other_ref, ready_ref, mine_ref, send_ref, *, points):
    comps, half = block_ref.shape[1], block_ref.shape[3]
    lanes = half_lanes(me_ref, half)
    row = lambda k: power_ref[k : k + 1, lanes]
    hop, height, wrap = row(points), row(points + 1), row(points + 2)
    last = power_ref.shape[0]
    before, after = row(last - 2) * wrap, row(last - 1) * wrap
    odd = me_ref[0] % 2 == 1
    for c in range(comps):
        low = height * (entry_ref[0, c] + before * block_ref[0, c])
        high = height * (entry_ref[1, c] + after * block_ref[1, c])
        even_low = height * jnp.where(odd, other_ref[0, c], own_ref[0, c])
        odd_high = height * jnp.where(odd, own_ref[1, c], other_ref[1, c])
        even_in = (low, odd_high + hop * high)
        odd_in = (even_low + hop * low, high)
        for side in range(2):
            mine_ref[side, c] = jnp.where(odd, odd_in[side], even_in[side])
            send_ref[side, c] = jnp.where(odd, even_in[side], odd_in[side])


def enter(me, power, block, entry, own, other, ready, points):
    return pl.pallas_call(
        functools.partial(enter_kernel, points=points),
        name="enter",
        out_shape=(held(*block.shape), held(*block.shape)),
        in_specs=[SMEM] + [VMEM] * 5 + [ANY],
        out_specs=(VMEM, VMEM),
        compiler_params=params(block.size * 4, 12),
    )(me, power, block, entry, own, other, ready)


def close_kernel(me_ref, s_ref, power_ref, entry_ref, *refs, own):
    out_ref, x_ref, sems = refs[-3:]
    comps, points, _, _ = s_ref.shape
    lanes = half_lanes(me_ref, entry_ref.shape[3], own)
    leaves = []
    for c in range(comps):
        before, after = entry_ref[0, c], entry_ref[1, c]

        def point(t):
            decayed = power_ref[pl.ds(t + 1, 1), lanes] * before + power_ref[pl.ds(points - t, 1), lanes] * after
            x_ref[c, t] = s_ref[c, t, :, lanes] + decayed

        each(points, point)
        leaves.append(pltpu.make_async_copy(x_ref.at[c], out_ref.at[c, :, :, lanes], sems.at[c]))
        leaves[c].start()
    for leave in leaves:
        leave.wait()


def close(me, s, power, entry, out, own):
    comps, points, planes, radial = s.shape
    return pl.pallas_call(
        functools.partial(close_kernel, own=own),
        name="close_own" if own else "close_other",
        out_shape=jax.ShapeDtypeStruct(s.shape, s.dtype),
        in_specs=[SMEM] + [VMEM] * 3 + [ANY] * len(out),
        out_specs=ANY,
        scratch_shapes=[
            pltpu.VMEM((comps, points, planes, radial // 2), jnp.float32),
            pltpu.SemaphoreType.DMA((comps,)),
        ],
        input_output_aliases={4: 0} if out else {},
        compiler_params=params(s.size * 4, 5),
        cost_estimate=pl.CostEstimate(flops=4 * s.size, bytes_accessed=8 * s.size, transcendentals=0),
    )(me, s, power, entry, *out)


def local(velocity, radial_op, azimuth_stencil, viscous_factor):
    sectors = lax.axis_size("theta")
    comps, points, planes, radial = velocity.shape
    reach = (azimuth_stencil.shape[0] - 1) // 2
    width = radial_op.shape[1] - radial
    me = lax.axis_index("theta").astype(jnp.int32).reshape(1)
    op = radial_op.T

    velocity, axial_out = load(pltpu.with_memory_space_constraint(velocity, pltpu.HBM))
    axial_in = swap(axial_out, "gz", 1)
    chip_out = pack_side(me, velocity, axial_out, reach, False)
    chip_in = swap_across(chip_out, "theta")
    mirror_out = pack_mirror(velocity, chip_out, width)
    mirror_in = swap(mirror_out, "theta", sectors // 2)
    core_out = pack_side(me, velocity, mirror_out, reach, True)
    core_in = swap(core_out, "theta", 1)
    power, taps = table(me, viscous_factor, azimuth_stencil, points, sectors, planes, radial)
    n = inner_terms(taps, velocity, op)
    share_out = share_terms(velocity, axial_in, power)
    share_in = swap(share_out, "gz", 1)
    planes_in = swap(pack_planes(velocity, share_out), "gz", 1)
    n = side_terms(core_kernel, "core_terms", me, taps, velocity, core_in, n)
    n = mirror_terms(velocity, op, mirror_in, n)
    n = side_terms(late_kernel, "late_terms", me, taps, velocity, chip_in, n)
    send = ends_terms(me, velocity, share_in, power, n, False)
    other = swap(send, "theta", 1)
    own = ends_terms(me, velocity, share_in, power, n, True)
    block = pair(me, power, own, other, points)
    entries = ()
    last = sectors.bit_length() - 2
    for bit in range(1, last + 1):
        if bit == last:
            n = planes_terms(velocity, planes_in, axial_in, block, n)
            s, nonlinear = sweep(velocity, n, power)
        block, entry = merge(me, power, block, swap(block, "theta", 1 << bit), entries, points, bit)
        entries = (entry,)
    mine, send = enter(me, power, block, entry, own, other, s, points)
    got = swap(send, "theta", 1)
    new_velocity = close(me, s, power, mine, (), True)
    new_velocity = close(me, s, power, got, (new_velocity,), False)
    return (new_velocity, nonlinear)


def solution(mesh):
    in_specs = (P(None, "theta", "gz", None), P(), P(), P())
    out_specs = (P(None, "theta", "gz", None), P(None, "theta", "gz", None))
    return jax.shard_map(local, mesh=mesh, in_specs=in_specs, out_specs=out_specs, check_vma=False)
```

```python
import functools

import jax
import jax.numpy as jnp
from jax import lax
from jax.experimental import pallas as pl
from jax.experimental.pallas import tpu as pltpu
from jax.sharding import PartitionSpec as P

AXIAL_WEIGHTS = (0.75, -0.15, 1.0 / 60.0)
AXIAL_REACH = len(AXIAL_WEIGHTS)
STEP_WEIGHT = 0.2
MIRROR_SIGNS = (-1.0, -1.0, 1.0)
CORE_PARTS = ((0, 1), (2,))
LANES = 128
UNROLL = 16
INNER = 1 << 31
MIRROR = 1 << 26
SIDE = 1 << 26

VMEM = pl.BlockSpec(memory_space=pltpu.VMEM)
SMEM = pl.BlockSpec(memory_space=pltpu.SMEM)
ANY = pl.BlockSpec(memory_space=pl.ANY)
HBM = pl.BlockSpec(memory_space=pltpu.HBM)


def params(block_bytes, blocks):
    return pltpu.CompilerParams(vmem_limit_bytes=(2 << 20) + blocks * block_bytes)


def held(*shape):
    return pltpu.VMEM(shape, jnp.float32)


def each(count, body):
    if count <= UNROLL:
        for i in range(count):
            body(i)
    else:
        pl.loop(0, count)(body)


def swap(block, axis, bit):
    size = lax.axis_size(axis)
    return lax.ppermute(block, axis, [(i, i ^ bit) for i in range(size)])


def swap_across(block, axis):
    size = lax.axis_size(axis)
    route = []
    for odd in range(1, size, 2):
        route += [(odd, (odd + 1) % size), ((odd + 1) % size, odd)]
    return lax.ppermute(block, axis, route)


def split(x):
    high = x.astype(jnp.bfloat16)
    return high, (x - high.astype(jnp.float32)).astype(jnp.bfloat16)


def product(left, right):
    dot = functools.partial(jnp.dot, preferred_element_type=jnp.float32)
    return dot(left[0], right[0]) + (dot(left[0], right[1]) + dot(left[1], right[0]))


def pack_tiles(v_ref, y_ref, comps):
    points, planes = v_ref.shape[1:3]
    carriers = y_ref.shape[1]
    lo, hi = AXIAL_REACH, planes - AXIAL_REACH
    for i, c in enumerate(comps):

        def carry(t):
            y_ref[i, t] = v_ref[c, t]

        def ride(j):
            t = carriers + j
            y_ref[i, 3 * j, lo:hi] = v_ref[c, t, 0:2]
            y_ref[i, 3 * j + 1, lo : lo + 1] = v_ref[c, t, 2:3]
            y_ref[i, 3 * j + 1, lo + 1 : hi] = v_ref[c, t, hi : hi + 1]
            y_ref[i, 3 * j + 2, lo:hi] = v_ref[c, t, hi + 1 :]

        each(carriers, carry)
        each(points - carriers, ride)


def rebuild_tiles(y_ref, tile_ref):
    carriers = y_ref.shape[1]
    comps, riders, planes, radial = tile_ref.shape
    lo, hi = AXIAL_REACH, planes - AXIAL_REACH
    for c in range(comps):
        for j in range(riders):
            tile_ref[c, j, 0:2] = y_ref[c, 3 * j, lo:hi]
            tile_ref[c, j, 2:3] = y_ref[c, 3 * j + 1, lo : lo + 1]
            tile_ref[c, j, lo:hi] = jnp.zeros((hi - lo, radial), jnp.float32)
            tile_ref[c, j, hi : hi + 1] = y_ref[c, 3 * j + 1, lo + 1 : hi]
            tile_ref[c, j, hi + 1 :] = y_ref[c, 3 * j + 2, lo:hi]


def load_kernel(hbm_ref, v_ref, y_ref, sems):
    order = list(range(v_ref.shape[0]))
    loads = [pltpu.make_async_copy(hbm_ref.at[c], v_ref.at[c], sems.at[c]) for c in order]
    for c in reversed(order):
        loads[c].start()
    loads[-1].wait()
    pack_tiles(v_ref, y_ref, order[-1:])
    for c in order[:-1]:
        loads[c].wait()


def load(v):
    comps, points, planes, radial = v.shape
    return pl.pallas_call(
        load_kernel,
        name="load",
        out_shape=(held(*v.shape), held(1, points - points // 4, planes, radial)),
        in_specs=[HBM],
        out_specs=(VMEM, VMEM),
        scratch_shapes=[pltpu.SemaphoreType.DMA((comps,))],
        compiler_params=params(v.size * 4, 2),
    )(v)


def pack_planes_kernel(v_ref, first_ref, y_ref):
    pack_tiles(v_ref, y_ref, range(y_ref.shape[0]))


def pack_planes(v, first):
    comps, points, planes, radial = v.shape
    return pl.pallas_call(
        pack_planes_kernel,
        name="pack_planes",
        out_shape=held(comps - 1, points - points // 4, planes, radial),
        in_specs=[VMEM, ANY],
        out_specs=VMEM,
        compiler_params=params(v.size * 4, 2),
    )(v, first)


def pack_side_kernel(me_ref, v_ref, first_ref, *side_refs, after, parts):
    points, reach = v_ref.shape[1], side_refs[0].shape[1]

    def put(start):
        for side_ref, part in zip(side_refs, parts):
            for i, c in enumerate(part):
                for h in range(reach):
                    side_ref[i, h] = v_ref[c, start + h]

    even = me_ref[0] % 2 == 0
    last = even if after else jnp.logical_not(even)
    pl.when(last)(lambda: put(points - reach))
    pl.when(jnp.logical_not(last))(lambda: put(0))


def pack_side(me, v, first, reach, after, parts):
    _, _, planes, radial = v.shape
    return pl.pallas_call(
        functools.partial(pack_side_kernel, after=after, parts=parts),
        name="pack_core" if after else "pack_chip",
        out_shape=tuple(held(len(part), reach, planes, radial) for part in parts),
        in_specs=[SMEM, VMEM, ANY],
        out_specs=(VMEM,) * len(parts),
        compiler_params=params(v.size * 4, 3),
    )(me, v, first)


def pack_mirror_kernel(v_ref, first_ref, mirror_ref):
    points, tiles = v_ref.shape[1], mirror_ref.shape[1]
    width = LANES // (points // tiles)
    lane = lax.broadcasted_iota(jnp.int32, mirror_ref.shape[2:], 1)

    def put(p):
        for c in range(v_ref.shape[0]):
            tile = v_ref[c, p, :, :LANES]
            for q in range(1, points // tiles):
                part = pltpu.roll(v_ref[c, q * tiles + p, :, :LANES], q * width, 1)
                tile = jnp.where(lane < q * width, tile, part)
            mirror_ref[c, p] = tile

    each(tiles, put)


def pack_mirror(v, first, width):
    comps, points, planes, _ = v.shape
    return pl.pallas_call(
        pack_mirror_kernel,
        name="pack_mirror",
        out_shape=held(comps, points // (LANES // width), planes, LANES),
        in_specs=[VMEM, ANY],
        out_specs=VMEM,
        compiler_params=params(v.size * 4, 2),
    )(v, first)


def inverse_radius(radial, start=0):
    return 1.0 / ((lax.broadcasted_iota(jnp.int32, (1, radial), 1) + start).astype(jnp.float32) + 0.5)


def axial_weights(planes, inside):
    row = lax.broadcasted_iota(jnp.int32, (planes, LANES), 0)
    weights = []
    for m, w in enumerate(AXIAL_WEIGHTS, 1):
        for shift, own, sign in ((m, row < planes - m, 1.0), (planes - m, row >= m, -1.0)):
            keep = own if inside else jnp.logical_not(own)
            weights.append((shift, jnp.where(keep, sign * w, 0.0)))
    return weights


def axial_part(tile, weights):
    planes, width = tile.shape
    weights = [(shift, jnp.concatenate([weight] * (width // LANES), axis=1)) for shift, weight in weights]
    total = None
    for shift, weight in weights:
        term = weight * pltpu.roll(tile, planes - shift, 0)
        total = term if total is None else total + term
    return total


def mirror_kernel(v_ref, op_ref, mirror_ref, n_in_ref, n_ref, grad_ref):
    comps, points, planes, radial = v_ref.shape
    tiles = mirror_ref.shape[1]
    count = points // tiles
    width = LANES // count
    rows = tiles * planes
    right = split(jnp.concatenate([op_ref[radial:]] * count, axis=0))
    lane = lax.broadcasted_iota(jnp.int32, (rows, LANES), 1)
    for c in range(comps):
        high, low = split(MIRROR_SIGNS[c] * mirror_ref[c].reshape(rows, LANES))
        zero = jnp.zeros_like(high)
        parts = [
            [jnp.where((lane >= q * width) & (lane < (q + 1) * width), x, zero) for q in range(count)]
            for x in (high, low)
        ]
        left = [jnp.concatenate(x, axis=0) for x in parts]
        grad_ref[c * points * planes : (c + 1) * points * planes] = product(left, right)

    def finish(t):
        for c in range(comps):
            start = pl.multiple_of((c * points + t) * planes, planes)
            n_ref[c, t] = n_in_ref[c, t] + v_ref[0, t] * grad_ref[pl.ds(start, planes)]

    each(points, finish)


def mirror_terms(v, op, mirror, n):
    return pl.pallas_call(
        mirror_kernel,
        name="mirror_terms",
        out_shape=held(*v.shape),
        in_specs=[VMEM] * 4,
        out_specs=VMEM,
        scratch_shapes=[pltpu.VMEM((v.size // v.shape[3], v.shape[3]), jnp.float32)],
        input_output_aliases={3: 0},
        compiler_params=params(v.size * 4, 8),
        cost_estimate=pl.CostEstimate(flops=MIRROR, bytes_accessed=16 * v.size, transcendentals=0),
    )(v, op, mirror, n)


def inner_kernel(tap_ref, v_ref, op_ref, n_ref, grad_ref):
    comps, points, planes, radial = v_ref.shape
    reach = (tap_ref.shape[0] - 1) // 2
    rows = points * planes
    right = split(op_ref[:radial])
    for c in range(comps):
        grad_ref[c * rows : (c + 1) * rows] = product(split(v_ref[c].reshape(rows, radial)), right)
    weights = axial_weights(planes, True)

    @pl.loop(0, radial // LANES)
    def column(k):
        lanes = pl.ds(pl.multiple_of(k * LANES, LANES), LANES)
        inv_r = inverse_radius(LANES, k * LANES)
        for c in range(comps):
            for t in range(points):
                a, b, e = [v_ref[i, t, :, lanes] for i in range(3)]
                b_inv = b * inv_r
                around = None
                for m in range(max(-reach, -t), min(reach, points - 1 - t) + 1):
                    term = tap_ref[m + reach] * v_ref[c, t + m, :, lanes]
                    around = term if around is None else around + term
                start = c * rows + t * planes
                n = a * grad_ref[start : start + planes, lanes] + b_inv * around
                n = n + e * axial_part(v_ref[c, t, :, lanes], weights)
                if c == 0:
                    n = n - b_inv * b
                elif c == 1:
                    n = n + a * b_inv
                n_ref[c, t, :, lanes] = n


def inner_terms(taps, v, op):
    return pl.pallas_call(
        inner_kernel,
        name="inner_terms",
        out_shape=held(*v.shape),
        in_specs=[VMEM] * 3,
        out_specs=VMEM,
        scratch_shapes=[pltpu.VMEM((v.size // v.shape[3], v.shape[3]), jnp.float32)],
        compiler_params=params(v.size * 4, 7),
        cost_estimate=pl.CostEstimate(flops=INNER, bytes_accessed=16 * v.size, transcendentals=0),
    )(taps, v, op)


def add_side(tap_ref, v_ref, side_refs, n_in_ref, n_ref, before):
    comps, points, _, radial = v_ref.shape
    reach = side_refs[0].shape[1]
    sides = [(ref, i) for ref in side_refs for i in range(ref.shape[0])]
    first = 0 if before else reach + 1

    @pl.loop(0, radial // LANES)
    def column(k):
        lanes = pl.ds(pl.multiple_of(k * LANES, LANES), LANES)
        inv_r = inverse_radius(LANES, k * LANES)
        weights = [tap_ref[first + i] for i in range(reach)]
        for c in range(comps):
            ref, i = sides[c]
            side = [ref[i, h, :, lanes] for h in range(reach)]
            for u in range(reach):
                t = u if before else points - reach + u
                taps = [(h, h - u) for h in range(u, reach)] if before else [(h, reach - 1 + h - u) for h in range(u + 1)]
                around = None
                for h, w in taps:
                    term = weights[w] * side[h]
                    around = term if around is None else around + term
                n_ref[c, t, :, lanes] = n_in_ref[c, t, :, lanes] + v_ref[1, t, :, lanes] * inv_r * around


def core_kernel(me_ref, tap_ref, v_ref, *refs):
    *core_refs, n_in_ref, n_ref = refs
    even = me_ref[0] % 2 == 0
    add = functools.partial(add_side, tap_ref, v_ref, core_refs, n_in_ref, n_ref)
    pl.when(even)(lambda: add(False))
    pl.when(jnp.logical_not(even))(lambda: add(True))


def late_kernel(me_ref, tap_ref, v_ref, *refs):
    *chip_refs, n_in_ref, n_ref = refs
    even = me_ref[0] % 2 == 0
    add = functools.partial(add_side, tap_ref, v_ref, chip_refs, n_in_ref, n_ref)
    pl.when(even)(lambda: add(True))
    pl.when(jnp.logical_not(even))(lambda: add(False))


def side_terms(kernel, name, me, taps, v, sides, n):
    return pl.pallas_call(
        kernel,
        name=name,
        out_shape=held(*v.shape),
        in_specs=[SMEM] + [VMEM] * (3 + len(sides)),
        out_specs=VMEM,
        input_output_aliases={3 + len(sides): 0},
        compiler_params=params(v.size * 4, 5),
        cost_estimate=pl.CostEstimate(flops=SIDE, bytes_accessed=12 * v.size, transcendentals=0),
    )(me, taps, v, *sides, n)


def share_kernel(v_ref, e_ref, power_ref, ends_ref, tile_ref):
    comps, points, planes, radial = v_ref.shape
    carriers = e_ref.shape[1]
    weights = axial_weights(planes, False)
    rebuild_tiles(e_ref, tile_ref)
    decay = power_ref[1:2]
    ends_ref[...] = jnp.zeros_like(ends_ref)
    for t in range(points):
        e = STEP_WEIGHT * (e_ref[0, t] if t < carriers else tile_ref[0, t - carriers])
        for c in range(comps):
            right_side = e * axial_part(v_ref[c, t], weights)
            ends_ref[0, c] = decay * ends_ref[0, c] - right_side
            ends_ref[1, c] = ends_ref[1, c] - power_ref[t : t + 1] * right_side


def share_terms(v, e, power):
    comps, points, planes, radial = v.shape
    return pl.pallas_call(
        share_kernel,
        name="share_terms",
        out_shape=held(2, comps, planes, radial),
        in_specs=[VMEM] * 3,
        out_specs=VMEM,
        scratch_shapes=[pltpu.VMEM((1, points - e.shape[1], planes, radial), jnp.float32)],
        compiler_params=params(v.size * 4, 4),
        cost_estimate=pl.CostEstimate(flops=20 * v.size, bytes_accessed=8 * v.size, transcendentals=0),
    )(v, e, power)


def ends_kernel(me_ref, v_ref, share_ref, power_ref, n_ref, ends_ref, *, own):
    comps, points, _, radial = v_ref.shape
    lanes = half_lanes(me_ref, radial // 2, own)
    decay = power_ref[1:2, lanes]
    for c in range(comps):
        low = high = None
        for t in range(points):
            right_side = v_ref[c, t, :, lanes] - STEP_WEIGHT * n_ref[c, t, :, lanes]
            low = right_side if t == 0 else decay * low + right_side
            high = right_side if t == 0 else high + power_ref[t : t + 1, lanes] * right_side
        ends_ref[0, c] = low + share_ref[0, c, :, lanes]
        ends_ref[1, c] = high + share_ref[1, c, :, lanes]


def ends_terms(me, v, share, power, n, own):
    comps, _, planes, radial = v.shape
    return pl.pallas_call(
        functools.partial(ends_kernel, own=own),
        name="ends_own" if own else "ends_other",
        out_shape=held(2, comps, planes, radial // 2),
        in_specs=[SMEM] + [VMEM] * 4,
        out_specs=VMEM,
        compiler_params=params(v.size * 4, 4),
        cost_estimate=pl.CostEstimate(flops=20 * v.size, bytes_accessed=8 * v.size, transcendentals=0),
    )(me, v, share, power, n)


def planes_kernel(v_ref, y_ref, e_ref, ready_ref, n_in_ref, n_ref, y_tile_ref, e_tile_ref):
    comps, points, planes, _ = v_ref.shape
    carriers = y_ref.shape[1]
    weights = axial_weights(planes, False)
    rebuild_tiles(y_ref, y_tile_ref)
    rebuild_tiles(e_ref, e_tile_ref)
    for t in range(points):
        for c in range(comps):
            ref, tile_ref, i = (y_ref, y_tile_ref, c) if c < comps - 1 else (e_ref, e_tile_ref, 0)
            tile = ref[i, t] if t < carriers else tile_ref[i, t - carriers]
            n_ref[c, t] = n_in_ref[c, t] + v_ref[2, t] * axial_part(tile, weights)


def planes_terms(v, y, e, ready, n):
    comps, points, planes, radial = v.shape
    riders = points - y.shape[1]
    return pl.pallas_call(
        planes_kernel,
        name="planes_terms",
        out_shape=held(*v.shape),
        in_specs=[VMEM] * 3 + [ANY, VMEM],
        out_specs=VMEM,
        scratch_shapes=[pltpu.VMEM((k, riders, planes, radial), jnp.float32) for k in (comps - 1, 1)],
        input_output_aliases={4: 0},
        compiler_params=params(v.size * 4, 6),
        cost_estimate=pl.CostEstimate(flops=20 * v.size, bytes_accessed=16 * v.size, transcendentals=0),
    )(v, y, e, ready, n)


def table_kernel(me_ref, factor_ref, stencil_ref, row_ref, tap_ref, *, points, sectors):
    radial = row_ref.shape[1]
    one = jnp.ones((1, radial), jnp.float32)
    half = (0.5 * lax.rsqrt(factor_ref[0] * one)) / inverse_radius(radial)
    root = jnp.sqrt(1.0 + half * half)
    loss = 2.0 * half * (root - half)
    rows = [one]
    for _ in range(points):
        rows.append(rows[-1] * (1.0 - loss))
    total = loss
    left, result = points * sectors, None
    while left:
        if left & 1:
            result = total if result is None else result + total - result * total
        total = total * (2.0 - total)
        left >>= 1
    across = rows[points] * rows[points]
    rows += [half / root, 1.0 / result]
    before = after = one
    for bit in range(1, sectors.bit_length() - 1):
        upper = (me_ref[0] >> bit) % 2 == 1
        rows += [across, before, after]
        before, after = jnp.where(upper, before * across, before), jnp.where(upper, after, after * across)
        across = across * across
    for k, row in enumerate(rows + [before, after]):
        row_ref[k : k + 1] = row
    for k in range(tap_ref.shape[0]):
        tap_ref[k] = jnp.full(tap_ref.shape[1:], stencil_ref[k], jnp.float32)


def table(me, viscous_factor, stencil, points, sectors, planes, radial):
    count = points + 5 + 3 * (sectors.bit_length() - 2)
    return pl.pallas_call(
        functools.partial(table_kernel, points=points, sectors=sectors),
        name="table",
        out_shape=(held(count, radial), held(stencil.shape[0], planes, LANES)),
        in_specs=[SMEM, SMEM, SMEM],
        out_specs=(VMEM, VMEM),
        compiler_params=params(1 << 20, 1),
        cost_estimate=pl.CostEstimate(flops=1000 * radial, bytes_accessed=400 * radial, transcendentals=0),
    )(me, viscous_factor, stencil)


def sweep_kernel(v_ref, n_ref, power_ref, s_ref, nonlinear_ref, sem):
    leave = pltpu.make_async_copy(n_ref, nonlinear_ref, sem)
    leave.start()
    comps, points, planes, radial = v_ref.shape
    decay = power_ref[1:2]
    height = power_ref[points + 1 : points + 2]
    for c in range(comps):
        s_ref[c, 0] = height * (v_ref[c, 0] - STEP_WEIGHT * n_ref[c, 0])

        def forward(i):
            t = i + 1
            s_ref[c, t] = decay * s_ref[c, t - 1] + height * (v_ref[c, t] - STEP_WEIGHT * n_ref[c, t])

        each(points - 1, forward)

    def backward(i, carry):
        t = points - 1 - i
        after = []
        for c in range(comps):
            s_ref[c, t] = s_ref[c, t] + carry[c]
            after.append(decay * (carry[c] + height * (v_ref[c, t] - STEP_WEIGHT * n_ref[c, t])))
        return tuple(after)

    start = (jnp.zeros((planes, radial), jnp.float32),) * comps
    lax.fori_loop(0, points, backward, start, unroll=points <= UNROLL)
    leave.wait()


def sweep(v, n, power):
    return pl.pallas_call(
        sweep_kernel,
        name="sweep",
        out_shape=(held(*v.shape), jax.ShapeDtypeStruct(v.shape, v.dtype)),
        in_specs=[VMEM] * 3,
        out_specs=(VMEM, ANY),
        scratch_shapes=[pltpu.SemaphoreType.DMA],
        compiler_params=params(v.size * 4, 4),
        cost_estimate=pl.CostEstimate(flops=10 * v.size, bytes_accessed=12 * v.size, transcendentals=0),
    )(v, n, power)


def half_lanes(me_ref, half, own=True):
    core = me_ref[0] % 2
    return pl.ds(pl.multiple_of((core if own else 1 - core) * half, half), half)


def pair_kernel(me_ref, power_ref, own_ref, other_ref, block_ref, *, points):
    half = own_ref.shape[3]
    hop = power_ref[points : points + 1, half_lanes(me_ref, half)]
    odd = me_ref[0] % 2 == 1
    for c in range(own_ref.shape[1]):
        for side in range(2):
            own, other = own_ref[side, c], other_ref[side, c]
            far, near = (own, other) if side == 0 else (other, own)
            block_ref[side, c] = jnp.where(odd, hop * near + far, hop * far + near)


def pair(me, power, own, other, points):
    return pl.pallas_call(
        functools.partial(pair_kernel, points=points),
        name="pair",
        out_shape=held(*own.shape),
        in_specs=[SMEM, VMEM, VMEM, VMEM],
        out_specs=VMEM,
        compiler_params=params(own.size * 4, 8),
    )(me, power, own, other)


def merge_kernel(me_ref, power_ref, block_ref, other_ref, *refs, points, bit):
    *entry_refs, block_out_ref, entry_out_ref = refs
    comps, half = block_ref.shape[1], block_ref.shape[3]
    lanes = half_lanes(me_ref, half)
    first = points + 3 * bit
    across, before, after = [power_ref[first + k : first + k + 1, lanes] for k in range(3)]
    upper = (me_ref[0] >> bit) % 2 == 1
    before = jnp.where(upper, before, 0.0)
    after = jnp.where(upper, 0.0, after)
    for c in range(comps):
        low, high = block_ref[0, c], block_ref[1, c]
        other_low, other_high = other_ref[0, c], other_ref[1, c]
        block_out_ref[0, c] = jnp.where(upper, across * other_low + low, across * low + other_low)
        block_out_ref[1, c] = jnp.where(upper, other_high + across * high, high + across * other_high)
        for side, enters in enumerate((before * other_low, after * other_high)):
            entry_out_ref[side, c] = entry_refs[0][side, c] + enters if entry_refs else enters


def merge(me, power, block, other, entries, points, bit):
    return pl.pallas_call(
        functools.partial(merge_kernel, points=points, bit=bit),
        name="merge",
        out_shape=(held(*block.shape), held(*block.shape)),
        in_specs=[SMEM] + [VMEM] * (3 + len(entries)),
        out_specs=(VMEM, VMEM),
        compiler_params=params(block.size * 4, 8),
    )(me, power, block, other, *entries)


def enter_kernel(me_ref, power_ref, block_ref, entry_ref, own_ref, other_ref, ready_ref, mine_ref, send_ref, *, points):
    comps, half = block_ref.shape[1], block_ref.shape[3]
    lanes = half_lanes(me_ref, half)
    row = lambda k: power_ref[k : k + 1, lanes]
    hop, height, wrap = row(points), row(points + 1), row(points + 2)
    last = power_ref.shape[0]
    before, after = row(last - 2) * wrap, row(last - 1) * wrap
    odd = me_ref[0] % 2 == 1
    for c in range(comps):
        low = height * (entry_ref[0, c] + before * block_ref[0, c])
        high = height * (entry_ref[1, c] + after * block_ref[1, c])
        even_low = height * jnp.where(odd, other_ref[0, c], own_ref[0, c])
        odd_high = height * jnp.where(odd, own_ref[1, c], other_ref[1, c])
        even_in = (low, odd_high + hop * high)
        odd_in = (even_low + hop * low, high)
        for side in range(2):
            mine_ref[side, c] = jnp.where(odd, odd_in[side], even_in[side])
            send_ref[side, c] = jnp.where(odd, even_in[side], odd_in[side])


def enter(me, power, block, entry, own, other, ready, points):
    return pl.pallas_call(
        functools.partial(enter_kernel, points=points),
        name="enter",
        out_shape=(held(*block.shape), held(*block.shape)),
        in_specs=[SMEM] + [VMEM] * 5 + [ANY],
        out_specs=(VMEM, VMEM),
        compiler_params=params(block.size * 4, 12),
    )(me, power, block, entry, own, other, ready)


def close_kernel(me_ref, s_ref, power_ref, entry_ref, *refs, own):
    out_ref, x_ref, sems = refs[-3:]
    comps, points, _, _ = s_ref.shape
    lanes = half_lanes(me_ref, entry_ref.shape[3], own)
    leaves = []
    for c in range(comps):
        before, after = entry_ref[0, c], entry_ref[1, c]

        def point(t):
            decayed = power_ref[pl.ds(t + 1, 1), lanes] * before + power_ref[pl.ds(points - t, 1), lanes] * after
            x_ref[c, t] = s_ref[c, t, :, lanes] + decayed

        each(points, point)
        leaves.append(pltpu.make_async_copy(x_ref.at[c], out_ref.at[c, :, :, lanes], sems.at[c]))
        leaves[c].start()
    for leave in leaves:
        leave.wait()


def close(me, s, power, entry, out, own):
    comps, points, planes, radial = s.shape
    return pl.pallas_call(
        functools.partial(close_kernel, own=own),
        name="close_own" if own else "close_other",
        out_shape=jax.ShapeDtypeStruct(s.shape, s.dtype),
        in_specs=[SMEM] + [VMEM] * 3 + [ANY] * len(out),
        out_specs=ANY,
        scratch_shapes=[
            pltpu.VMEM((comps, points, planes, radial // 2), jnp.float32),
            pltpu.SemaphoreType.DMA((comps,)),
        ],
        input_output_aliases={4: 0} if out else {},
        compiler_params=params(s.size * 4, 5),
        cost_estimate=pl.CostEstimate(flops=4 * s.size, bytes_accessed=8 * s.size, transcendentals=0),
    )(me, s, power, entry, *out)


def local(velocity, radial_op, azimuth_stencil, viscous_factor):
    sectors = lax.axis_size("theta")
    comps, points, planes, radial = velocity.shape
    reach = (azimuth_stencil.shape[0] - 1) // 2
    width = radial_op.shape[1] - radial
    me = lax.axis_index("theta").astype(jnp.int32).reshape(1)
    op = radial_op.T

    velocity, axial_out = load(pltpu.with_memory_space_constraint(velocity, pltpu.HBM))
    axial_in = swap(axial_out, "gz", 1)
    everything = (tuple(range(comps)),)
    chip_out = pack_side(me, velocity, axial_out, reach, False, everything)
    chip_in = [swap_across(part, "theta") for part in chip_out]
    mirror_out = pack_mirror(velocity, chip_out[0], width)
    mirror_in = swap(mirror_out, "theta", sectors // 2)
    core_out = pack_side(me, velocity, mirror_out, reach, True, CORE_PARTS)
    core_in = [swap(part, "theta", 1) for part in core_out]
    power, taps = table(me, viscous_factor, azimuth_stencil, points, sectors, planes, radial)
    n = inner_terms(taps, velocity, op)
    share_out = share_terms(velocity, axial_in, power)
    share_in = swap(share_out, "gz", 1)
    planes_in = swap(pack_planes(velocity, share_out), "gz", 1)
    n = side_terms(core_kernel, "core_terms", me, taps, velocity, core_in, n)
    n = mirror_terms(velocity, op, mirror_in, n)
    n = side_terms(late_kernel, "late_terms", me, taps, velocity, chip_in, n)
    send = ends_terms(me, velocity, share_in, power, n, False)
    other = swap(send, "theta", 1)
    own = ends_terms(me, velocity, share_in, power, n, True)
    block = pair(me, power, own, other, points)
    entries = ()
    last = sectors.bit_length() - 2
    for bit in range(1, last + 1):
        if bit == last:
            n = planes_terms(velocity, planes_in, axial_in, block, n)
            s, nonlinear = sweep(velocity, n, power)
        block, entry = merge(me, power, block, swap(block, "theta", 1 << bit), entries, points, bit)
        entries = (entry,)
    mine, send = enter(me, power, block, entry, own, other, s, points)
    got = swap(send, "theta", 1)
    new_velocity = close(me, s, power, mine, (), True)
    new_velocity = close(me, s, power, got, (new_velocity,), False)
    return (new_velocity, nonlinear)


def solution(mesh):
    in_specs = (P(None, "theta", "gz", None), P(), P(), P())
    out_specs = (P(None, "theta", "gz", None), P(None, "theta", "gz", None))
    return jax.shard_map(local, mesh=mesh, in_specs=in_specs, out_specs=out_specs, check_vma=False)
```

```python
import functools

import jax
import jax.numpy as jnp
from jax import lax
from jax.experimental import pallas as pl
from jax.experimental.pallas import tpu as pltpu
from jax.sharding import PartitionSpec as P

AXIAL_WEIGHTS = (0.75, -0.15, 1.0 / 60.0)
AXIAL_REACH = len(AXIAL_WEIGHTS)
STEP_WEIGHT = 0.2
MIRROR_SIGNS = (-1.0, -1.0, 1.0)
CORE_PARTS = ((0, 1), (2,))
LANES = 128
UNROLL = 16
INNER = 1 << 20
MIRROR = 25 << 26
SIDE = 1 << 20
LATE = 1 << 30

VMEM = pl.BlockSpec(memory_space=pltpu.VMEM)
SMEM = pl.BlockSpec(memory_space=pltpu.SMEM)
ANY = pl.BlockSpec(memory_space=pl.ANY)
HBM = pl.BlockSpec(memory_space=pltpu.HBM)


def params(block_bytes, blocks):
    return pltpu.CompilerParams(vmem_limit_bytes=(2 << 20) + blocks * block_bytes)


def held(*shape):
    return pltpu.VMEM(shape, jnp.float32)


def each(count, body):
    if count <= UNROLL:
        for i in range(count):
            body(i)
    else:
        pl.loop(0, count)(body)


def swap(block, axis, bit):
    size = lax.axis_size(axis)
    return lax.ppermute(block, axis, [(i, i ^ bit) for i in range(size)])


def swap_across(block, axis):
    size = lax.axis_size(axis)
    route = []
    for odd in range(1, size, 2):
        route += [(odd, (odd + 1) % size), ((odd + 1) % size, odd)]
    return lax.ppermute(block, axis, route)


def split(x):
    high = x.astype(jnp.bfloat16)
    return high, (x - high.astype(jnp.float32)).astype(jnp.bfloat16)


def product(left, right):
    dot = functools.partial(jnp.dot, preferred_element_type=jnp.float32)
    return dot(left[0], right[0]) + (dot(left[0], right[1]) + dot(left[1], right[0]))


def pack_tiles(v_ref, y_ref, comps):
    points, planes = v_ref.shape[1:3]
    carriers = y_ref.shape[1]
    lo, hi = AXIAL_REACH, planes - AXIAL_REACH
    for i, c in enumerate(comps):

        def carry(t):
            y_ref[i, t] = v_ref[c, t]

        def ride(j):
            t = carriers + j
            y_ref[i, 3 * j, lo:hi] = v_ref[c, t, 0:2]
            y_ref[i, 3 * j + 1, lo : lo + 1] = v_ref[c, t, 2:3]
            y_ref[i, 3 * j + 1, lo + 1 : hi] = v_ref[c, t, hi : hi + 1]
            y_ref[i, 3 * j + 2, lo:hi] = v_ref[c, t, hi + 1 :]

        each(carriers, carry)
        each(points - carriers, ride)


def rebuild_tiles(y_ref, tile_ref):
    carriers = y_ref.shape[1]
    comps, riders, planes, radial = tile_ref.shape
    lo, hi = AXIAL_REACH, planes - AXIAL_REACH
    for c in range(comps):
        for j in range(riders):
            tile_ref[c, j, 0:2] = y_ref[c, 3 * j, lo:hi]
            tile_ref[c, j, 2:3] = y_ref[c, 3 * j + 1, lo : lo + 1]
            tile_ref[c, j, lo:hi] = jnp.zeros((hi - lo, radial), jnp.float32)
            tile_ref[c, j, hi : hi + 1] = y_ref[c, 3 * j + 1, lo + 1 : hi]
            tile_ref[c, j, hi + 1 :] = y_ref[c, 3 * j + 2, lo:hi]


def load_kernel(hbm_ref, v_ref, y_ref, sems):
    order = list(range(v_ref.shape[0]))
    loads = [pltpu.make_async_copy(hbm_ref.at[c], v_ref.at[c], sems.at[c]) for c in order]
    for c in reversed(order):
        loads[c].start()
    loads[-1].wait()
    pack_tiles(v_ref, y_ref, order[-1:])
    for c in order[:-1]:
        loads[c].wait()


def load(v):
    comps, points, planes, radial = v.shape
    return pl.pallas_call(
        load_kernel,
        name="load",
        out_shape=(held(*v.shape), held(1, points - points // 4, planes, radial)),
        in_specs=[HBM],
        out_specs=(VMEM, VMEM),
        scratch_shapes=[pltpu.SemaphoreType.DMA((comps,))],
        compiler_params=params(v.size * 4, 2),
    )(v)


def pack_planes_kernel(v_ref, first_ref, y_ref):
    pack_tiles(v_ref, y_ref, range(y_ref.shape[0]))


def pack_planes(v, first):
    comps, points, planes, radial = v.shape
    return pl.pallas_call(
        pack_planes_kernel,
        name="pack_planes",
        out_shape=held(comps - 1, points - points // 4, planes, radial),
        in_specs=[VMEM, ANY],
        out_specs=VMEM,
        compiler_params=params(v.size * 4, 2),
    )(v, first)


def pack_side_kernel(me_ref, v_ref, first_ref, *side_refs, after, parts):
    points, reach = v_ref.shape[1], side_refs[0].shape[1]

    def put(start):
        for side_ref, part in zip(side_refs, parts):
            for i, c in enumerate(part):
                for h in range(reach):
                    side_ref[i, h] = v_ref[c, start + h]

    even = me_ref[0] % 2 == 0
    last = even if after else jnp.logical_not(even)
    pl.when(last)(lambda: put(points - reach))
    pl.when(jnp.logical_not(last))(lambda: put(0))


def pack_side(me, v, first, reach, after, parts):
    _, _, planes, radial = v.shape
    return pl.pallas_call(
        functools.partial(pack_side_kernel, after=after, parts=parts),
        name="pack_core" if after else "pack_chip",
        out_shape=tuple(held(len(part), reach, planes, radial) for part in parts),
        in_specs=[SMEM, VMEM, ANY],
        out_specs=(VMEM,) * len(parts),
        compiler_params=params(v.size * 4, 3),
    )(me, v, first)


def pack_mirror_kernel(v_ref, first_ref, mirror_ref):
    points, tiles = v_ref.shape[1], mirror_ref.shape[1]
    width = LANES // (points // tiles)
    lane = lax.broadcasted_iota(jnp.int32, mirror_ref.shape[2:], 1)

    def put(p):
        for c in range(v_ref.shape[0]):
            tile = v_ref[c, p, :, :LANES]
            for q in range(1, points // tiles):
                part = pltpu.roll(v_ref[c, q * tiles + p, :, :LANES], q * width, 1)
                tile = jnp.where(lane < q * width, tile, part)
            mirror_ref[c, p] = tile

    each(tiles, put)


def pack_mirror(v, first, width):
    comps, points, planes, _ = v.shape
    return pl.pallas_call(
        pack_mirror_kernel,
        name="pack_mirror",
        out_shape=held(comps, points // (LANES // width), planes, LANES),
        in_specs=[VMEM, ANY],
        out_specs=VMEM,
        compiler_params=params(v.size * 4, 2),
    )(v, first)


def inverse_radius(radial, start=0):
    return 1.0 / ((lax.broadcasted_iota(jnp.int32, (1, radial), 1) + start).astype(jnp.float32) + 0.5)


def axial_weights(planes, inside):
    row = lax.broadcasted_iota(jnp.int32, (planes, LANES), 0)
    weights = []
    for m, w in enumerate(AXIAL_WEIGHTS, 1):
        for shift, own, sign in ((m, row < planes - m, 1.0), (planes - m, row >= m, -1.0)):
            keep = own if inside else jnp.logical_not(own)
            weights.append((shift, jnp.where(keep, sign * w, 0.0)))
    return weights


def axial_part(tile, weights):
    planes, width = tile.shape
    weights = [(shift, jnp.concatenate([weight] * (width // LANES), axis=1)) for shift, weight in weights]
    total = None
    for shift, weight in weights:
        term = weight * pltpu.roll(tile, planes - shift, 0)
        total = term if total is None else total + term
    return total


def mirror_kernel(v_ref, op_ref, mirror_ref, n_in_ref, n_ref, grad_ref):
    comps, points, planes, radial = v_ref.shape
    tiles = mirror_ref.shape[1]
    count = points // tiles
    width = LANES // count
    rows = tiles * planes
    right = split(jnp.concatenate([op_ref[radial:]] * count, axis=0))
    lane = lax.broadcasted_iota(jnp.int32, (rows, LANES), 1)
    for c in range(comps):
        high, low = split(MIRROR_SIGNS[c] * mirror_ref[c].reshape(rows, LANES))
        zero = jnp.zeros_like(high)
        parts = [
            [jnp.where((lane >= q * width) & (lane < (q + 1) * width), x, zero) for q in range(count)]
            for x in (high, low)
        ]
        left = [jnp.concatenate(x, axis=0) for x in parts]
        grad_ref[c * points * planes : (c + 1) * points * planes] = product(left, right)

    def finish(t):
        for c in range(comps):
            start = pl.multiple_of((c * points + t) * planes, planes)
            n_ref[c, t] = n_in_ref[c, t] + v_ref[0, t] * grad_ref[pl.ds(start, planes)]

    each(points, finish)


def mirror_terms(v, op, mirror, n):
    return pl.pallas_call(
        mirror_kernel,
        name="mirror_terms",
        out_shape=held(*v.shape),
        in_specs=[VMEM] * 4,
        out_specs=VMEM,
        scratch_shapes=[pltpu.VMEM((v.size // v.shape[3], v.shape[3]), jnp.float32)],
        input_output_aliases={3: 0},
        compiler_params=params(v.size * 4, 8),
        cost_estimate=pl.CostEstimate(flops=MIRROR, bytes_accessed=16 * v.size, transcendentals=0),
    )(v, op, mirror, n)


def inner_kernel(tap_ref, v_ref, op_ref, n_ref, grad_ref):
    comps, points, planes, radial = v_ref.shape
    reach = (tap_ref.shape[0] - 1) // 2
    rows = points * planes
    right = split(op_ref[:radial])
    for c in range(comps):
        grad_ref[c * rows : (c + 1) * rows] = product(split(v_ref[c].reshape(rows, radial)), right)
    weights = axial_weights(planes, True)

    @pl.loop(0, radial // LANES)
    def column(k):
        lanes = pl.ds(pl.multiple_of(k * LANES, LANES), LANES)
        inv_r = inverse_radius(LANES, k * LANES)
        for c in range(comps):
            for t in range(points):
                a, b, e = [v_ref[i, t, :, lanes] for i in range(3)]
                b_inv = b * inv_r
                around = None
                for m in range(max(-reach, -t), min(reach, points - 1 - t) + 1):
                    term = tap_ref[m + reach] * v_ref[c, t + m, :, lanes]
                    around = term if around is None else around + term
                start = c * rows + t * planes
                n = a * grad_ref[start : start + planes, lanes] + b_inv * around
                n = n + e * axial_part(v_ref[c, t, :, lanes], weights)
                if c == 0:
                    n = n - b_inv * b
                elif c == 1:
                    n = n + a * b_inv
                n_ref[c, t, :, lanes] = n


def inner_terms(taps, v, op):
    return pl.pallas_call(
        inner_kernel,
        name="inner_terms",
        out_shape=held(*v.shape),
        in_specs=[VMEM] * 3,
        out_specs=VMEM,
        scratch_shapes=[pltpu.VMEM((v.size // v.shape[3], v.shape[3]), jnp.float32)],
        compiler_params=params(v.size * 4, 7),
        cost_estimate=pl.CostEstimate(flops=INNER, bytes_accessed=16 * v.size, transcendentals=0),
    )(taps, v, op)


def add_side(tap_ref, v_ref, side_refs, n_in_ref, n_ref, before):
    comps, points, _, radial = v_ref.shape
    reach = side_refs[0].shape[1]
    sides = [(ref, i) for ref in side_refs for i in range(ref.shape[0])]
    first = 0 if before else reach + 1

    @pl.loop(0, radial // LANES)
    def column(k):
        lanes = pl.ds(pl.multiple_of(k * LANES, LANES), LANES)
        inv_r = inverse_radius(LANES, k * LANES)
        weights = [tap_ref[first + i] for i in range(reach)]
        for c in range(comps):
            ref, i = sides[c]
            side = [ref[i, h, :, lanes] for h in range(reach)]
            for u in range(reach):
                t = u if before else points - reach + u
                taps = [(h, h - u) for h in range(u, reach)] if before else [(h, reach - 1 + h - u) for h in range(u + 1)]
                around = None
                for h, w in taps:
                    term = weights[w] * side[h]
                    around = term if around is None else around + term
                n_ref[c, t, :, lanes] = n_in_ref[c, t, :, lanes] + v_ref[1, t, :, lanes] * inv_r * around


def core_kernel(me_ref, tap_ref, v_ref, *refs):
    *core_refs, n_in_ref, n_ref = refs
    even = me_ref[0] % 2 == 0
    add = functools.partial(add_side, tap_ref, v_ref, core_refs, n_in_ref, n_ref)
    pl.when(even)(lambda: add(False))
    pl.when(jnp.logical_not(even))(lambda: add(True))


def late_kernel(me_ref, tap_ref, v_ref, *refs):
    *chip_refs, n_in_ref, _, n_ref = refs
    even = me_ref[0] % 2 == 0
    add = functools.partial(add_side, tap_ref, v_ref, chip_refs, n_in_ref, n_ref)
    pl.when(even)(lambda: add(True))
    pl.when(jnp.logical_not(even))(lambda: add(False))


def side_terms(kernel, name, me, taps, v, sides, n, ready=(), flops=SIDE):
    return pl.pallas_call(
        kernel,
        name=name,
        out_shape=held(*v.shape),
        in_specs=[SMEM] + [VMEM] * (3 + len(sides)) + [ANY] * len(ready),
        out_specs=VMEM,
        input_output_aliases={3 + len(sides): 0},
        compiler_params=params(v.size * 4, 5),
        cost_estimate=pl.CostEstimate(flops=flops, bytes_accessed=12 * v.size, transcendentals=0),
    )(me, taps, v, *sides, n, *ready)


def share_kernel(v_ref, e_ref, power_ref, ready_ref, ends_ref, tile_ref):
    comps, points, planes, radial = v_ref.shape
    carriers = e_ref.shape[1]
    weights = axial_weights(planes, False)
    rebuild_tiles(e_ref, tile_ref)
    decay = power_ref[1:2]
    ends_ref[...] = jnp.zeros_like(ends_ref)
    for t in range(points):
        e = STEP_WEIGHT * (e_ref[0, t] if t < carriers else tile_ref[0, t - carriers])
        for c in range(comps):
            right_side = e * axial_part(v_ref[c, t], weights)
            ends_ref[0, c] = decay * ends_ref[0, c] - right_side
            ends_ref[1, c] = ends_ref[1, c] - power_ref[t : t + 1] * right_side


def share_terms(v, e, power, ready):
    comps, points, planes, radial = v.shape
    return pl.pallas_call(
        share_kernel,
        name="share_terms",
        out_shape=held(2, comps, planes, radial),
        in_specs=[VMEM] * 3 + [ANY],
        out_specs=VMEM,
        scratch_shapes=[pltpu.VMEM((1, points - e.shape[1], planes, radial), jnp.float32)],
        compiler_params=params(v.size * 4, 4),
        cost_estimate=pl.CostEstimate(flops=20 * v.size, bytes_accessed=8 * v.size, transcendentals=0),
    )(v, e, power, ready)


def ends_kernel(me_ref, v_ref, share_ref, power_ref, n_ref, ends_ref, *, own):
    comps, points, _, radial = v_ref.shape
    lanes = half_lanes(me_ref, radial // 2, own)
    decay = power_ref[1:2, lanes]
    for c in range(comps):
        low = high = None
        for t in range(points):
            right_side = v_ref[c, t, :, lanes] - STEP_WEIGHT * n_ref[c, t, :, lanes]
            low = right_side if t == 0 else decay * low + right_side
            high = right_side if t == 0 else high + power_ref[t : t + 1, lanes] * right_side
        ends_ref[0, c] = low + share_ref[0, c, :, lanes]
        ends_ref[1, c] = high + share_ref[1, c, :, lanes]


def ends_terms(me, v, share, power, n, own):
    comps, _, planes, radial = v.shape
    return pl.pallas_call(
        functools.partial(ends_kernel, own=own),
        name="ends_own" if own else "ends_other",
        out_shape=held(2, comps, planes, radial // 2),
        in_specs=[SMEM] + [VMEM] * 4,
        out_specs=VMEM,
        compiler_params=params(v.size * 4, 4),
        cost_estimate=pl.CostEstimate(flops=20 * v.size, bytes_accessed=8 * v.size, transcendentals=0),
    )(me, v, share, power, n)


def planes_kernel(v_ref, y_ref, e_ref, ready_ref, n_in_ref, n_ref, y_tile_ref, e_tile_ref):
    comps, points, planes, _ = v_ref.shape
    carriers = y_ref.shape[1]
    weights = axial_weights(planes, False)
    rebuild_tiles(y_ref, y_tile_ref)
    rebuild_tiles(e_ref, e_tile_ref)
    for t in range(points):
        for c in range(comps):
            ref, tile_ref, i = (y_ref, y_tile_ref, c) if c < comps - 1 else (e_ref, e_tile_ref, 0)
            tile = ref[i, t] if t < carriers else tile_ref[i, t - carriers]
            n_ref[c, t] = n_in_ref[c, t] + v_ref[2, t] * axial_part(tile, weights)


def planes_terms(v, y, e, ready, n):
    comps, points, planes, radial = v.shape
    riders = points - y.shape[1]
    return pl.pallas_call(
        planes_kernel,
        name="planes_terms",
        out_shape=held(*v.shape),
        in_specs=[VMEM] * 3 + [ANY, VMEM],
        out_specs=VMEM,
        scratch_shapes=[pltpu.VMEM((k, riders, planes, radial), jnp.float32) for k in (comps - 1, 1)],
        input_output_aliases={4: 0},
        compiler_params=params(v.size * 4, 6),
        cost_estimate=pl.CostEstimate(flops=20 * v.size, bytes_accessed=16 * v.size, transcendentals=0),
    )(v, y, e, ready, n)


def table_kernel(me_ref, factor_ref, stencil_ref, row_ref, tap_ref, *, points, sectors):
    radial = row_ref.shape[1]
    one = jnp.ones((1, radial), jnp.float32)
    half = (0.5 * lax.rsqrt(factor_ref[0] * one)) / inverse_radius(radial)
    root = jnp.sqrt(1.0 + half * half)
    loss = 2.0 * half * (root - half)
    rows = [one]
    for _ in range(points):
        rows.append(rows[-1] * (1.0 - loss))
    total = loss
    left, result = points * sectors, None
    while left:
        if left & 1:
            result = total if result is None else result + total - result * total
        total = total * (2.0 - total)
        left >>= 1
    across = rows[points] * rows[points]
    rows += [half / root, 1.0 / result]
    before = after = one
    for bit in range(1, sectors.bit_length() - 1):
        upper = (me_ref[0] >> bit) % 2 == 1
        rows += [across, before, after]
        before, after = jnp.where(upper, before * across, before), jnp.where(upper, after, after * across)
        across = across * across
    for k, row in enumerate(rows + [before, after]):
        row_ref[k : k + 1] = row
    for k in range(tap_ref.shape[0]):
        tap_ref[k] = jnp.full(tap_ref.shape[1:], stencil_ref[k], jnp.float32)


def table(me, viscous_factor, stencil, points, sectors, planes, radial):
    count = points + 5 + 3 * (sectors.bit_length() - 2)
    return pl.pallas_call(
        functools.partial(table_kernel, points=points, sectors=sectors),
        name="table",
        out_shape=(held(count, radial), held(stencil.shape[0], planes, LANES)),
        in_specs=[SMEM, SMEM, SMEM],
        out_specs=(VMEM, VMEM),
        compiler_params=params(1 << 20, 1),
        cost_estimate=pl.CostEstimate(flops=1000 * radial, bytes_accessed=400 * radial, transcendentals=0),
    )(me, viscous_factor, stencil)


def sweep_kernel(v_ref, n_ref, power_ref, s_ref, nonlinear_ref, sem):
    leave = pltpu.make_async_copy(n_ref, nonlinear_ref, sem)
    leave.start()
    comps, points, planes, radial = v_ref.shape
    decay = power_ref[1:2]
    height = power_ref[points + 1 : points + 2]
    for c in range(comps):
        s_ref[c, 0] = height * (v_ref[c, 0] - STEP_WEIGHT * n_ref[c, 0])

        def forward(i):
            t = i + 1
            s_ref[c, t] = decay * s_ref[c, t - 1] + height * (v_ref[c, t] - STEP_WEIGHT * n_ref[c, t])

        each(points - 1, forward)

    def backward(i, carry):
        t = points - 1 - i
        after = []
        for c in range(comps):
            s_ref[c, t] = s_ref[c, t] + carry[c]
            after.append(decay * (carry[c] + height * (v_ref[c, t] - STEP_WEIGHT * n_ref[c, t])))
        return tuple(after)

    start = (jnp.zeros((planes, radial), jnp.float32),) * comps
    lax.fori_loop(0, points, backward, start, unroll=points <= UNROLL)
    leave.wait()


def sweep(v, n, power):
    return pl.pallas_call(
        sweep_kernel,
        name="sweep",
        out_shape=(held(*v.shape), jax.ShapeDtypeStruct(v.shape, v.dtype)),
        in_specs=[VMEM] * 3,
        out_specs=(VMEM, ANY),
        scratch_shapes=[pltpu.SemaphoreType.DMA],
        compiler_params=params(v.size * 4, 4),
        cost_estimate=pl.CostEstimate(flops=10 * v.size, bytes_accessed=12 * v.size, transcendentals=0),
    )(v, n, power)


def half_lanes(me_ref, half, own=True):
    core = me_ref[0] % 2
    return pl.ds(pl.multiple_of((core if own else 1 - core) * half, half), half)


def pair_kernel(me_ref, power_ref, own_ref, other_ref, block_ref, *, points):
    half = own_ref.shape[3]
    hop = power_ref[points : points + 1, half_lanes(me_ref, half)]
    odd = me_ref[0] % 2 == 1
    for c in range(own_ref.shape[1]):
        for side in range(2):
            own, other = own_ref[side, c], other_ref[side, c]
            far, near = (own, other) if side == 0 else (other, own)
            block_ref[side, c] = jnp.where(odd, hop * near + far, hop * far + near)


def pair(me, power, own, other, points):
    return pl.pallas_call(
        functools.partial(pair_kernel, points=points),
        name="pair",
        out_shape=held(*own.shape),
        in_specs=[SMEM, VMEM, VMEM, VMEM],
        out_specs=VMEM,
        compiler_params=params(own.size * 4, 8),
    )(me, power, own, other)


def merge_kernel(me_ref, power_ref, block_ref, other_ref, *refs, points, bit):
    *entry_refs, block_out_ref, entry_out_ref = refs
    comps, half = block_ref.shape[1], block_ref.shape[3]
    lanes = half_lanes(me_ref, half)
    first = points + 3 * bit
    across, before, after = [power_ref[first + k : first + k + 1, lanes] for k in range(3)]
    upper = (me_ref[0] >> bit) % 2 == 1
    before = jnp.where(upper, before, 0.0)
    after = jnp.where(upper, 0.0, after)
    for c in range(comps):
        low, high = block_ref[0, c], block_ref[1, c]
        other_low, other_high = other_ref[0, c], other_ref[1, c]
        block_out_ref[0, c] = jnp.where(upper, across * other_low + low, across * low + other_low)
        block_out_ref[1, c] = jnp.where(upper, other_high + across * high, high + across * other_high)
        for side, enters in enumerate((before * other_low, after * other_high)):
            entry_out_ref[side, c] = entry_refs[0][side, c] + enters if entry_refs else enters


def merge(me, power, block, other, entries, points, bit):
    return pl.pallas_call(
        functools.partial(merge_kernel, points=points, bit=bit),
        name="merge",
        out_shape=(held(*block.shape), held(*block.shape)),
        in_specs=[SMEM] + [VMEM] * (3 + len(entries)),
        out_specs=(VMEM, VMEM),
        compiler_params=params(block.size * 4, 8),
    )(me, power, block, other, *entries)


def enter_kernel(me_ref, power_ref, block_ref, entry_ref, own_ref, other_ref, ready_ref, mine_ref, send_ref, *, points):
    comps, half = block_ref.shape[1], block_ref.shape[3]
    lanes = half_lanes(me_ref, half)
    row = lambda k: power_ref[k : k + 1, lanes]
    hop, height, wrap = row(points), row(points + 1), row(points + 2)
    last = power_ref.shape[0]
    before, after = row(last - 2) * wrap, row(last - 1) * wrap
    odd = me_ref[0] % 2 == 1
    for c in range(comps):
        low = height * (entry_ref[0, c] + before * block_ref[0, c])
        high = height * (entry_ref[1, c] + after * block_ref[1, c])
        even_low = height * jnp.where(odd, other_ref[0, c], own_ref[0, c])
        odd_high = height * jnp.where(odd, own_ref[1, c], other_ref[1, c])
        even_in = (low, odd_high + hop * high)
        odd_in = (even_low + hop * low, high)
        for side in range(2):
            mine_ref[side, c] = jnp.where(odd, odd_in[side], even_in[side])
            send_ref[side, c] = jnp.where(odd, even_in[side], odd_in[side])


def enter(me, power, block, entry, own, other, ready, points):
    return pl.pallas_call(
        functools.partial(enter_kernel, points=points),
        name="enter",
        out_shape=(held(*block.shape), held(*block.shape)),
        in_specs=[SMEM] + [VMEM] * 5 + [ANY],
        out_specs=(VMEM, VMEM),
        compiler_params=params(block.size * 4, 12),
    )(me, power, block, entry, own, other, ready)


def close_kernel(me_ref, s_ref, power_ref, entry_ref, *refs, own):
    out_ref, x_ref, sems = refs[-3:]
    comps, points, _, _ = s_ref.shape
    lanes = half_lanes(me_ref, entry_ref.shape[3], own)
    leaves = []
    for c in range(comps):
        before, after = entry_ref[0, c], entry_ref[1, c]

        def point(t):
            decayed = power_ref[pl.ds(t + 1, 1), lanes] * before + power_ref[pl.ds(points - t, 1), lanes] * after
            x_ref[c, t] = s_ref[c, t, :, lanes] + decayed

        each(points, point)
        leaves.append(pltpu.make_async_copy(x_ref.at[c], out_ref.at[c, :, :, lanes], sems.at[c]))
        leaves[c].start()
    for leave in leaves:
        leave.wait()


def close(me, s, power, entry, out, own):
    comps, points, planes, radial = s.shape
    return pl.pallas_call(
        functools.partial(close_kernel, own=own),
        name="close_own" if own else "close_other",
        out_shape=jax.ShapeDtypeStruct(s.shape, s.dtype),
        in_specs=[SMEM] + [VMEM] * 3 + [ANY] * len(out),
        out_specs=ANY,
        scratch_shapes=[
            pltpu.VMEM((comps, points, planes, radial // 2), jnp.float32),
            pltpu.SemaphoreType.DMA((comps,)),
        ],
        input_output_aliases={4: 0} if out else {},
        compiler_params=params(s.size * 4, 5),
        cost_estimate=pl.CostEstimate(flops=4 * s.size, bytes_accessed=8 * s.size, transcendentals=0),
    )(me, s, power, entry, *out)


def local(velocity, radial_op, azimuth_stencil, viscous_factor):
    sectors = lax.axis_size("theta")
    comps, points, planes, radial = velocity.shape
    reach = (azimuth_stencil.shape[0] - 1) // 2
    width = radial_op.shape[1] - radial
    me = lax.axis_index("theta").astype(jnp.int32).reshape(1)
    op = radial_op.T

    velocity, axial_out = load(pltpu.with_memory_space_constraint(velocity, pltpu.HBM))
    axial_in = swap(axial_out, "gz", 1)
    everything = (tuple(range(comps)),)
    chip_out = pack_side(me, velocity, axial_out, reach, False, everything)
    chip_in = [swap_across(part, "theta") for part in chip_out]
    mirror_out = pack_mirror(velocity, chip_out[0], width)
    mirror_in = swap(mirror_out, "theta", sectors // 2)
    core_out = pack_side(me, velocity, mirror_out, reach, True, CORE_PARTS)
    core_in = [swap(part, "theta", 1) for part in core_out]
    power, taps = table(me, viscous_factor, azimuth_stencil, points, sectors, planes, radial)
    n = inner_terms(taps, velocity, op)
    share_out = share_terms(velocity, axial_in, power, n)
    share_in = swap(share_out, "gz", 1)
    planes_in = swap(pack_planes(velocity, share_out), "gz", 1)
    n = side_terms(core_kernel, "core_terms", me, taps, velocity, core_in, n)
    n = mirror_terms(velocity, op, mirror_in, n)
    n = side_terms(late_kernel, "late_terms", me, taps, velocity, chip_in, n, (share_in,), LATE)
    send = ends_terms(me, velocity, share_in, power, n, False)
    other = swap(send, "theta", 1)
    own = ends_terms(me, velocity, share_in, power, n, True)
    block = pair(me, power, own, other, points)
    entries = ()
    last = sectors.bit_length() - 2
    for bit in range(1, last + 1):
        if bit == last:
            n = planes_terms(velocity, planes_in, axial_in, block, n)
            s, nonlinear = sweep(velocity, n, power)
        block, entry = merge(me, power, block, swap(block, "theta", 1 << bit), entries, points, bit)
        entries = (entry,)
    mine, send = enter(me, power, block, entry, own, other, s, points)
    got = swap(send, "theta", 1)
    new_velocity = close(me, s, power, mine, (), True)
    new_velocity = close(me, s, power, got, (new_velocity,), False)
    return (new_velocity, nonlinear)


def solution(mesh):
    in_specs = (P(None, "theta", "gz", None), P(), P(), P())
    out_specs = (P(None, "theta", "gz", None), P(None, "theta", "gz", None))
    return jax.shard_map(local, mesh=mesh, in_specs=in_specs, out_specs=out_specs, check_vma=False)
```

```python
import functools

import jax
import jax.numpy as jnp
from jax import lax
from jax.experimental import pallas as pl
from jax.experimental.pallas import tpu as pltpu
from jax.sharding import PartitionSpec as P

AXIAL_WEIGHTS = (0.75, -0.15, 1.0 / 60.0)
AXIAL_REACH = len(AXIAL_WEIGHTS)
STEP_WEIGHT = 0.2
MIRROR_SIGNS = (-1.0, -1.0, 1.0)
CORE_PARTS = ((0, 1), (2,))
LANES = 128
UNROLL = 16
INNER = 1 << 20
MIRROR = 25 << 26
SIDE = 1 << 20
LATE = 1 << 30

VMEM = pl.BlockSpec(memory_space=pltpu.VMEM)
SMEM = pl.BlockSpec(memory_space=pltpu.SMEM)
ANY = pl.BlockSpec(memory_space=pl.ANY)
HBM = pl.BlockSpec(memory_space=pltpu.HBM)


def params(block_bytes, blocks):
    return pltpu.CompilerParams(vmem_limit_bytes=(2 << 20) + blocks * block_bytes)


def held(*shape):
    return pltpu.VMEM(shape, jnp.float32)


def each(count, body):
    if count <= UNROLL:
        for i in range(count):
            body(i)
    else:
        pl.loop(0, count)(body)


def swap(block, axis, bit):
    size = lax.axis_size(axis)
    return lax.ppermute(block, axis, [(i, i ^ bit) for i in range(size)])


def swap_across(block, axis):
    size = lax.axis_size(axis)
    route = []
    for odd in range(1, size, 2):
        route += [(odd, (odd + 1) % size), ((odd + 1) % size, odd)]
    return lax.ppermute(block, axis, route)


def split(x):
    high = x.astype(jnp.bfloat16)
    return high, (x - high.astype(jnp.float32)).astype(jnp.bfloat16)


def product(left, right):
    dot = functools.partial(jnp.dot, preferred_element_type=jnp.float32)
    return dot(left[0], right[0]) + (dot(left[0], right[1]) + dot(left[1], right[0]))


def pack_tiles(v_ref, y_ref, comps):
    points, planes = v_ref.shape[1:3]
    carriers = y_ref.shape[1]
    lo, hi = AXIAL_REACH, planes - AXIAL_REACH
    for i, c in enumerate(comps):

        def carry(t):
            y_ref[i, t] = v_ref[c, t]

        def ride(j):
            t = carriers + j
            y_ref[i, 3 * j, lo:hi] = v_ref[c, t, 0:2]
            y_ref[i, 3 * j + 1, lo : lo + 1] = v_ref[c, t, 2:3]
            y_ref[i, 3 * j + 1, lo + 1 : hi] = v_ref[c, t, hi : hi + 1]
            y_ref[i, 3 * j + 2, lo:hi] = v_ref[c, t, hi + 1 :]

        each(carriers, carry)
        each(points - carriers, ride)


def rebuild_tiles(y_ref, tile_ref):
    carriers = y_ref.shape[1]
    comps, riders, planes, radial = tile_ref.shape
    lo, hi = AXIAL_REACH, planes - AXIAL_REACH
    for c in range(comps):
        for j in range(riders):
            tile_ref[c, j, 0:2] = y_ref[c, 3 * j, lo:hi]
            tile_ref[c, j, 2:3] = y_ref[c, 3 * j + 1, lo : lo + 1]
            tile_ref[c, j, lo:hi] = jnp.zeros((hi - lo, radial), jnp.float32)
            tile_ref[c, j, hi : hi + 1] = y_ref[c, 3 * j + 1, lo + 1 : hi]
            tile_ref[c, j, hi + 1 :] = y_ref[c, 3 * j + 2, lo:hi]


def load_kernel(hbm_ref, v_ref, y_ref, sems):
    order = list(range(v_ref.shape[0]))
    loads = [pltpu.make_async_copy(hbm_ref.at[c], v_ref.at[c], sems.at[c]) for c in order]
    for c in reversed(order):
        loads[c].start()
    loads[-1].wait()
    pack_tiles(v_ref, y_ref, order[-1:])
    for c in order[:-1]:
        loads[c].wait()


def load(v):
    comps, points, planes, radial = v.shape
    return pl.pallas_call(
        load_kernel,
        name="load",
        out_shape=(held(*v.shape), held(1, points - points // 4, planes, radial)),
        in_specs=[HBM],
        out_specs=(VMEM, VMEM),
        scratch_shapes=[pltpu.SemaphoreType.DMA((comps,))],
        compiler_params=params(v.size * 4, 2),
    )(v)


def pack_planes_kernel(v_ref, first_ref, y_ref):
    pack_tiles(v_ref, y_ref, range(y_ref.shape[0]))


def pack_planes(v, first):
    comps, points, planes, radial = v.shape
    return pl.pallas_call(
        pack_planes_kernel,
        name="pack_planes",
        out_shape=held(comps - 1, points - points // 4, planes, radial),
        in_specs=[VMEM, ANY],
        out_specs=VMEM,
        compiler_params=params(v.size * 4, 2),
    )(v, first)


def pack_side_kernel(me_ref, v_ref, first_ref, *side_refs, after, parts):
    points, reach = v_ref.shape[1], side_refs[0].shape[1]

    def put(start):
        for side_ref, part in zip(side_refs, parts):
            for i, c in enumerate(part):
                for h in range(reach):
                    side_ref[i, h] = v_ref[c, start + h]

    even = me_ref[0] % 2 == 0
    last = even if after else jnp.logical_not(even)
    pl.when(last)(lambda: put(points - reach))
    pl.when(jnp.logical_not(last))(lambda: put(0))


def pack_side(me, v, first, reach, after, parts):
    _, _, planes, radial = v.shape
    return pl.pallas_call(
        functools.partial(pack_side_kernel, after=after, parts=parts),
        name="pack_core" if after else "pack_chip",
        out_shape=tuple(held(len(part), reach, planes, radial) for part in parts),
        in_specs=[SMEM, VMEM, ANY],
        out_specs=(VMEM,) * len(parts),
        compiler_params=params(v.size * 4, 3),
    )(me, v, first)


def pack_mirror_kernel(v_ref, first_ref, mirror_ref):
    points, tiles = v_ref.shape[1], mirror_ref.shape[1]
    width = LANES // (points // tiles)
    lane = lax.broadcasted_iota(jnp.int32, mirror_ref.shape[2:], 1)

    def put(p):
        for c in range(v_ref.shape[0]):
            tile = v_ref[c, p, :, :LANES]
            for q in range(1, points // tiles):
                part = pltpu.roll(v_ref[c, q * tiles + p, :, :LANES], q * width, 1)
                tile = jnp.where(lane < q * width, tile, part)
            mirror_ref[c, p] = tile

    each(tiles, put)


def pack_mirror(v, first, width):
    comps, points, planes, _ = v.shape
    return pl.pallas_call(
        pack_mirror_kernel,
        name="pack_mirror",
        out_shape=held(comps, points // (LANES // width), planes, LANES),
        in_specs=[VMEM, ANY],
        out_specs=VMEM,
        compiler_params=params(v.size * 4, 2),
    )(v, first)


def inverse_radius(radial, start=0):
    return 1.0 / ((lax.broadcasted_iota(jnp.int32, (1, radial), 1) + start).astype(jnp.float32) + 0.5)


def axial_weights(planes, inside):
    row = lax.broadcasted_iota(jnp.int32, (planes, LANES), 0)
    weights = []
    for m, w in enumerate(AXIAL_WEIGHTS, 1):
        for shift, own, sign in ((m, row < planes - m, 1.0), (planes - m, row >= m, -1.0)):
            keep = own if inside else jnp.logical_not(own)
            weights.append((shift, jnp.where(keep, sign * w, 0.0)))
    return weights


def axial_part(tile, weights):
    planes, width = tile.shape
    weights = [(shift, jnp.concatenate([weight] * (width // LANES), axis=1)) for shift, weight in weights]
    total = None
    for shift, weight in weights:
        term = weight * pltpu.roll(tile, planes - shift, 0)
        total = term if total is None else total + term
    return total


def mirror_kernel(v_ref, op_ref, mirror_ref, n_in_ref, n_ref, grad_ref):
    comps, points, planes, radial = v_ref.shape
    tiles = mirror_ref.shape[1]
    count = points // tiles
    width = LANES // count
    rows = tiles * planes
    right = split(jnp.concatenate([op_ref[radial:]] * count, axis=0))
    lane = lax.broadcasted_iota(jnp.int32, (rows, LANES), 1)
    for c in range(comps):
        high, low = split(MIRROR_SIGNS[c] * mirror_ref[c].reshape(rows, LANES))
        zero = jnp.zeros_like(high)
        parts = [
            [jnp.where((lane >= q * width) & (lane < (q + 1) * width), x, zero) for q in range(count)]
            for x in (high, low)
        ]
        left = [jnp.concatenate(x, axis=0) for x in parts]
        grad_ref[c * points * planes : (c + 1) * points * planes] = product(left, right)

    def finish(t):
        for c in range(comps):
            start = pl.multiple_of((c * points + t) * planes, planes)
            n_ref[c, t] = n_in_ref[c, t] + v_ref[0, t] * grad_ref[pl.ds(start, planes)]

    each(points, finish)


def mirror_terms(v, op, mirror, n):
    return pl.pallas_call(
        mirror_kernel,
        name="mirror_terms",
        out_shape=held(*v.shape),
        in_specs=[VMEM] * 4,
        out_specs=VMEM,
        scratch_shapes=[pltpu.VMEM((v.size // v.shape[3], v.shape[3]), jnp.float32)],
        input_output_aliases={3: 0},
        compiler_params=params(v.size * 4, 8),
        cost_estimate=pl.CostEstimate(flops=MIRROR, bytes_accessed=16 * v.size, transcendentals=0),
    )(v, op, mirror, n)


def inner_kernel(tap_ref, v_ref, op_ref, n_ref, grad_ref):
    comps, points, planes, radial = v_ref.shape
    reach = (tap_ref.shape[0] - 1) // 2
    rows = points * planes
    right = split(op_ref[:radial])
    for c in range(comps):
        grad_ref[c * rows : (c + 1) * rows] = product(split(v_ref[c].reshape(rows, radial)), right)
    weights = axial_weights(planes, True)

    @pl.loop(0, radial // LANES)
    def column(k):
        lanes = pl.ds(pl.multiple_of(k * LANES, LANES), LANES)
        inv_r = inverse_radius(LANES, k * LANES)
        for c in range(comps):
            for t in range(points):
                a, b, e = [v_ref[i, t, :, lanes] for i in range(3)]
                b_inv = b * inv_r
                around = None
                for m in range(max(-reach, -t), min(reach, points - 1 - t) + 1):
                    term = tap_ref[m + reach] * v_ref[c, t + m, :, lanes]
                    around = term if around is None else around + term
                start = c * rows + t * planes
                n = a * grad_ref[start : start + planes, lanes] + b_inv * around
                n = n + e * axial_part(v_ref[c, t, :, lanes], weights)
                if c == 0:
                    n = n - b_inv * b
                elif c == 1:
                    n = n + a * b_inv
                n_ref[c, t, :, lanes] = n


def inner_terms(taps, v, op):
    return pl.pallas_call(
        inner_kernel,
        name="inner_terms",
        out_shape=held(*v.shape),
        in_specs=[VMEM] * 3,
        out_specs=VMEM,
        scratch_shapes=[pltpu.VMEM((v.size // v.shape[3], v.shape[3]), jnp.float32)],
        compiler_params=params(v.size * 4, 7),
        cost_estimate=pl.CostEstimate(flops=INNER, bytes_accessed=16 * v.size, transcendentals=0),
    )(taps, v, op)


def add_side(tap_ref, v_ref, side_refs, n_in_ref, n_ref, before, columns):
    comps, points, _, radial = v_ref.shape
    reach = side_refs[0].shape[1]
    sides = [(ref, i) for ref in side_refs for i in range(ref.shape[0])]
    first = 0 if before else reach + 1

    start, count = columns

    @pl.loop(0, count)
    def column(i):
        k = start + i
        lanes = pl.ds(pl.multiple_of(k * LANES, LANES), LANES)
        inv_r = inverse_radius(LANES, k * LANES)
        weights = [tap_ref[first + i] for i in range(reach)]
        for c in range(comps):
            ref, part = sides[c]
            side = [ref[part, h, :, lanes] for h in range(reach)]
            for u in range(reach):
                t = u if before else points - reach + u
                taps = [(h, h - u) for h in range(u, reach)] if before else [(h, reach - 1 + h - u) for h in range(u + 1)]
                around = None
                for h, w in taps:
                    term = weights[w] * side[h]
                    around = term if around is None else around + term
                n_ref[c, t, :, lanes] = n_in_ref[c, t, :, lanes] + v_ref[1, t, :, lanes] * inv_r * around


def core_kernel(me_ref, tap_ref, v_ref, *refs):
    *core_refs, n_in_ref, n_ref = refs
    even = me_ref[0] % 2 == 0
    columns = (0, v_ref.shape[3] // LANES)
    add = functools.partial(add_side, tap_ref, v_ref, core_refs, n_in_ref, n_ref, columns=columns)
    pl.when(even)(lambda: add(before=False))
    pl.when(jnp.logical_not(even))(lambda: add(before=True))


def late_kernel(me_ref, tap_ref, v_ref, *refs, own):
    *chip_refs, n_in_ref, _, n_ref = refs
    core = me_ref[0] % 2
    count = v_ref.shape[3] // (2 * LANES)
    columns = ((core if own else 1 - core) * count, count)
    add = functools.partial(add_side, tap_ref, v_ref, chip_refs, n_in_ref, n_ref, columns=columns)
    pl.when(core == 0)(lambda: add(before=True))
    pl.when(core == 1)(lambda: add(before=False))


def side_terms(kernel, name, me, taps, v, sides, n, ready=(), flops=SIDE):
    return pl.pallas_call(
        kernel,
        name=name,
        out_shape=held(*v.shape),
        in_specs=[SMEM] + [VMEM] * (3 + len(sides)) + [ANY] * len(ready),
        out_specs=VMEM,
        input_output_aliases={3 + len(sides): 0},
        compiler_params=params(v.size * 4, 5),
        cost_estimate=pl.CostEstimate(flops=flops, bytes_accessed=12 * v.size, transcendentals=0),
    )(me, taps, v, *sides, n, *ready)


def share_kernel(v_ref, e_ref, power_ref, ready_ref, ends_ref, tile_ref):
    comps, points, planes, radial = v_ref.shape
    carriers = e_ref.shape[1]
    weights = axial_weights(planes, False)
    rebuild_tiles(e_ref, tile_ref)
    decay = power_ref[1:2]
    ends_ref[...] = jnp.zeros_like(ends_ref)
    for t in range(points):
        e = STEP_WEIGHT * (e_ref[0, t] if t < carriers else tile_ref[0, t - carriers])
        for c in range(comps):
            right_side = e * axial_part(v_ref[c, t], weights)
            ends_ref[0, c] = decay * ends_ref[0, c] - right_side
            ends_ref[1, c] = ends_ref[1, c] - power_ref[t : t + 1] * right_side


def share_terms(v, e, power, ready):
    comps, points, planes, radial = v.shape
    return pl.pallas_call(
        share_kernel,
        name="share_terms",
        out_shape=held(2, comps, planes, radial),
        in_specs=[VMEM] * 3 + [ANY],
        out_specs=VMEM,
        scratch_shapes=[pltpu.VMEM((1, points - e.shape[1], planes, radial), jnp.float32)],
        compiler_params=params(v.size * 4, 4),
        cost_estimate=pl.CostEstimate(flops=20 * v.size, bytes_accessed=8 * v.size, transcendentals=0),
    )(v, e, power, ready)


def ends_kernel(me_ref, v_ref, share_ref, power_ref, n_ref, ends_ref, *, own):
    comps, points, _, radial = v_ref.shape
    lanes = half_lanes(me_ref, radial // 2, own)
    decay = power_ref[1:2, lanes]
    for c in range(comps):
        low = high = None
        for t in range(points):
            right_side = v_ref[c, t, :, lanes] - STEP_WEIGHT * n_ref[c, t, :, lanes]
            low = right_side if t == 0 else decay * low + right_side
            high = right_side if t == 0 else high + power_ref[t : t + 1, lanes] * right_side
        ends_ref[0, c] = low + share_ref[0, c, :, lanes]
        ends_ref[1, c] = high + share_ref[1, c, :, lanes]


def ends_terms(me, v, share, power, n, own):
    comps, _, planes, radial = v.shape
    return pl.pallas_call(
        functools.partial(ends_kernel, own=own),
        name="ends_own" if own else "ends_other",
        out_shape=held(2, comps, planes, radial // 2),
        in_specs=[SMEM] + [VMEM] * 4,
        out_specs=VMEM,
        compiler_params=params(v.size * 4, 4),
        cost_estimate=pl.CostEstimate(flops=20 * v.size, bytes_accessed=8 * v.size, transcendentals=0),
    )(me, v, share, power, n)


def planes_kernel(v_ref, y_ref, e_ref, ready_ref, n_in_ref, n_ref, y_tile_ref, e_tile_ref):
    comps, points, planes, _ = v_ref.shape
    carriers = y_ref.shape[1]
    weights = axial_weights(planes, False)
    rebuild_tiles(y_ref, y_tile_ref)
    rebuild_tiles(e_ref, e_tile_ref)
    for t in range(points):
        for c in range(comps):
            ref, tile_ref, i = (y_ref, y_tile_ref, c) if c < comps - 1 else (e_ref, e_tile_ref, 0)
            tile = ref[i, t] if t < carriers else tile_ref[i, t - carriers]
            n_ref[c, t] = n_in_ref[c, t] + v_ref[2, t] * axial_part(tile, weights)


def planes_terms(v, y, e, ready, n):
    comps, points, planes, radial = v.shape
    riders = points - y.shape[1]
    return pl.pallas_call(
        planes_kernel,
        name="planes_terms",
        out_shape=held(*v.shape),
        in_specs=[VMEM] * 3 + [ANY, VMEM],
        out_specs=VMEM,
        scratch_shapes=[pltpu.VMEM((k, riders, planes, radial), jnp.float32) for k in (comps - 1, 1)],
        input_output_aliases={4: 0},
        compiler_params=params(v.size * 4, 6),
        cost_estimate=pl.CostEstimate(flops=20 * v.size, bytes_accessed=16 * v.size, transcendentals=0),
    )(v, y, e, ready, n)


def table_kernel(me_ref, factor_ref, stencil_ref, row_ref, tap_ref, *, points, sectors):
    radial = row_ref.shape[1]
    one = jnp.ones((1, radial), jnp.float32)
    half = (0.5 * lax.rsqrt(factor_ref[0] * one)) / inverse_radius(radial)
    root = jnp.sqrt(1.0 + half * half)
    loss = 2.0 * half * (root - half)
    rows = [one]
    for _ in range(points):
        rows.append(rows[-1] * (1.0 - loss))
    total = loss
    left, result = points * sectors, None
    while left:
        if left & 1:
            result = total if result is None else result + total - result * total
        total = total * (2.0 - total)
        left >>= 1
    across = rows[points] * rows[points]
    rows += [half / root, 1.0 / result]
    before = after = one
    for bit in range(1, sectors.bit_length() - 1):
        upper = (me_ref[0] >> bit) % 2 == 1
        rows += [across, before, after]
        before, after = jnp.where(upper, before * across, before), jnp.where(upper, after, after * across)
        across = across * across
    for k, row in enumerate(rows + [before, after]):
        row_ref[k : k + 1] = row
    for k in range(tap_ref.shape[0]):
        tap_ref[k] = jnp.full(tap_ref.shape[1:], stencil_ref[k], jnp.float32)


def table(me, viscous_factor, stencil, points, sectors, planes, radial):
    count = points + 5 + 3 * (sectors.bit_length() - 2)
    return pl.pallas_call(
        functools.partial(table_kernel, points=points, sectors=sectors),
        name="table",
        out_shape=(held(count, radial), held(stencil.shape[0], planes, LANES)),
        in_specs=[SMEM, SMEM, SMEM],
        out_specs=(VMEM, VMEM),
        compiler_params=params(1 << 20, 1),
        cost_estimate=pl.CostEstimate(flops=1000 * radial, bytes_accessed=400 * radial, transcendentals=0),
    )(me, viscous_factor, stencil)


def sweep_kernel(v_ref, n_ref, power_ref, s_ref, nonlinear_ref, sem):
    leave = pltpu.make_async_copy(n_ref, nonlinear_ref, sem)
    leave.start()
    comps, points, planes, radial = v_ref.shape
    decay = power_ref[1:2]
    height = power_ref[points + 1 : points + 2]
    for c in range(comps):
        s_ref[c, 0] = height * (v_ref[c, 0] - STEP_WEIGHT * n_ref[c, 0])

        def forward(i):
            t = i + 1
            s_ref[c, t] = decay * s_ref[c, t - 1] + height * (v_ref[c, t] - STEP_WEIGHT * n_ref[c, t])

        each(points - 1, forward)

    def backward(i, carry):
        t = points - 1 - i
        after = []
        for c in range(comps):
            s_ref[c, t] = s_ref[c, t] + carry[c]
            after.append(decay * (carry[c] + height * (v_ref[c, t] - STEP_WEIGHT * n_ref[c, t])))
        return tuple(after)

    start = (jnp.zeros((planes, radial), jnp.float32),) * comps
    lax.fori_loop(0, points, backward, start, unroll=points <= UNROLL)
    leave.wait()


def sweep(v, n, power):
    return pl.pallas_call(
        sweep_kernel,
        name="sweep",
        out_shape=(held(*v.shape), jax.ShapeDtypeStruct(v.shape, v.dtype)),
        in_specs=[VMEM] * 3,
        out_specs=(VMEM, ANY),
        scratch_shapes=[pltpu.SemaphoreType.DMA],
        compiler_params=params(v.size * 4, 4),
        cost_estimate=pl.CostEstimate(flops=10 * v.size, bytes_accessed=12 * v.size, transcendentals=0),
    )(v, n, power)


def half_lanes(me_ref, half, own=True):
    core = me_ref[0] % 2
    return pl.ds(pl.multiple_of((core if own else 1 - core) * half, half), half)


def pair_kernel(me_ref, power_ref, own_ref, other_ref, block_ref, *, points):
    half = own_ref.shape[3]
    hop = power_ref[points : points + 1, half_lanes(me_ref, half)]
    odd = me_ref[0] % 2 == 1
    for c in range(own_ref.shape[1]):
        for side in range(2):
            own, other = own_ref[side, c], other_ref[side, c]
            far, near = (own, other) if side == 0 else (other, own)
            block_ref[side, c] = jnp.where(odd, hop * near + far, hop * far + near)


def pair(me, power, own, other, points):
    return pl.pallas_call(
        functools.partial(pair_kernel, points=points),
        name="pair",
        out_shape=held(*own.shape),
        in_specs=[SMEM, VMEM, VMEM, VMEM],
        out_specs=VMEM,
        compiler_params=params(own.size * 4, 8),
    )(me, power, own, other)


def merge_kernel(me_ref, power_ref, block_ref, other_ref, *refs, points, bit, entries):
    entry_refs, (block_out_ref, entry_out_ref) = refs[:entries], refs[-2:]
    comps, half = block_ref.shape[1], block_ref.shape[3]
    lanes = half_lanes(me_ref, half)
    first = points + 3 * bit
    across, before, after = [power_ref[first + k : first + k + 1, lanes] for k in range(3)]
    upper = (me_ref[0] >> bit) % 2 == 1
    before = jnp.where(upper, before, 0.0)
    after = jnp.where(upper, 0.0, after)
    for c in range(comps):
        low, high = block_ref[0, c], block_ref[1, c]
        other_low, other_high = other_ref[0, c], other_ref[1, c]
        block_out_ref[0, c] = jnp.where(upper, across * other_low + low, across * low + other_low)
        block_out_ref[1, c] = jnp.where(upper, other_high + across * high, high + across * other_high)
        for side, enters in enumerate((before * other_low, after * other_high)):
            entry_out_ref[side, c] = entry_refs[0][side, c] + enters if entry_refs else enters


def merge(me, power, block, other, entries, ready, points, bit):
    return pl.pallas_call(
        functools.partial(merge_kernel, points=points, bit=bit, entries=len(entries)),
        name="merge",
        out_shape=(held(*block.shape), held(*block.shape)),
        in_specs=[SMEM] + [VMEM] * (3 + len(entries)) + [ANY] * len(ready),
        out_specs=(VMEM, VMEM),
        compiler_params=params(block.size * 4, 8),
    )(me, power, block, other, *entries, *ready)


def enter_kernel(me_ref, power_ref, block_ref, entry_ref, own_ref, other_ref, ready_ref, mine_ref, send_ref, *, points):
    comps, half = block_ref.shape[1], block_ref.shape[3]
    lanes = half_lanes(me_ref, half)
    row = lambda k: power_ref[k : k + 1, lanes]
    hop, height, wrap = row(points), row(points + 1), row(points + 2)
    last = power_ref.shape[0]
    before, after = row(last - 2) * wrap, row(last - 1) * wrap
    odd = me_ref[0] % 2 == 1
    for c in range(comps):
        low = height * (entry_ref[0, c] + before * block_ref[0, c])
        high = height * (entry_ref[1, c] + after * block_ref[1, c])
        even_low = height * jnp.where(odd, other_ref[0, c], own_ref[0, c])
        odd_high = height * jnp.where(odd, own_ref[1, c], other_ref[1, c])
        even_in = (low, odd_high + hop * high)
        odd_in = (even_low + hop * low, high)
        for side in range(2):
            mine_ref[side, c] = jnp.where(odd, odd_in[side], even_in[side])
            send_ref[side, c] = jnp.where(odd, even_in[side], odd_in[side])


def enter(me, power, block, entry, own, other, ready, points):
    return pl.pallas_call(
        functools.partial(enter_kernel, points=points),
        name="enter",
        out_shape=(held(*block.shape), held(*block.shape)),
        in_specs=[SMEM] + [VMEM] * 5 + [ANY],
        out_specs=(VMEM, VMEM),
        compiler_params=params(block.size * 4, 12),
    )(me, power, block, entry, own, other, ready)


def close_kernel(me_ref, s_ref, power_ref, entry_ref, *refs, own):
    out_ref, x_ref, sems = refs[-3:]
    comps, points, _, _ = s_ref.shape
    lanes = half_lanes(me_ref, entry_ref.shape[3], own)
    leaves = []
    for c in range(comps):
        before, after = entry_ref[0, c], entry_ref[1, c]

        def point(t):
            decayed = power_ref[pl.ds(t + 1, 1), lanes] * before + power_ref[pl.ds(points - t, 1), lanes] * after
            x_ref[c, t] = s_ref[c, t, :, lanes] + decayed

        each(points, point)
        leaves.append(pltpu.make_async_copy(x_ref.at[c], out_ref.at[c, :, :, lanes], sems.at[c]))
        leaves[c].start()
    for leave in leaves:
        leave.wait()


def close(me, s, power, entry, out, own):
    comps, points, planes, radial = s.shape
    return pl.pallas_call(
        functools.partial(close_kernel, own=own),
        name="close_own" if own else "close_other",
        out_shape=jax.ShapeDtypeStruct(s.shape, s.dtype),
        in_specs=[SMEM] + [VMEM] * 3 + [ANY] * len(out),
        out_specs=ANY,
        scratch_shapes=[
            pltpu.VMEM((comps, points, planes, radial // 2), jnp.float32),
            pltpu.SemaphoreType.DMA((comps,)),
        ],
        input_output_aliases={4: 0} if out else {},
        compiler_params=params(s.size * 4, 5),
        cost_estimate=pl.CostEstimate(flops=4 * s.size, bytes_accessed=8 * s.size, transcendentals=0),
    )(me, s, power, entry, *out)


def local(velocity, radial_op, azimuth_stencil, viscous_factor):
    sectors = lax.axis_size("theta")
    comps, points, planes, radial = velocity.shape
    reach = (azimuth_stencil.shape[0] - 1) // 2
    width = radial_op.shape[1] - radial
    me = lax.axis_index("theta").astype(jnp.int32).reshape(1)
    op = radial_op.T

    velocity, axial_out = load(pltpu.with_memory_space_constraint(velocity, pltpu.HBM))
    axial_in = swap(axial_out, "gz", 1)
    everything = (tuple(range(comps)),)
    chip_out = pack_side(me, velocity, axial_out, reach, False, everything)
    chip_in = [swap_across(part, "theta") for part in chip_out]
    mirror_out = pack_mirror(velocity, chip_out[0], width)
    mirror_in = swap(mirror_out, "theta", sectors // 2)
    core_out = pack_side(me, velocity, mirror_out, reach, True, CORE_PARTS)
    core_in = [swap(part, "theta", 1) for part in core_out]
    power, taps = table(me, viscous_factor, azimuth_stencil, points, sectors, planes, radial)
    n = inner_terms(taps, velocity, op)
    share_out = share_terms(velocity, axial_in, power, n)
    share_in = swap(share_out, "gz", 1)
    n = side_terms(core_kernel, "core_terms", me, taps, velocity, core_in, n)
    n = mirror_terms(velocity, op, mirror_in, n)
    late = functools.partial(late_kernel, own=False)
    n = side_terms(late, "late_other", me, taps, velocity, chip_in, n, (share_in,), LATE)
    send = ends_terms(me, velocity, share_in, power, n, False)
    other = swap(send, "theta", 1)
    late = functools.partial(late_kernel, own=True)
    n = side_terms(late, "late_own", me, taps, velocity, chip_in, n, (send,))
    own = ends_terms(me, velocity, share_in, power, n, True)
    block = pair(me, power, own, other, points)
    planes_in = swap(pack_planes(velocity, block), "gz", 1)
    entries, ready = (), ()
    last = sectors.bit_length() - 2
    for bit in range(1, last + 1):
        if bit == last:
            n = planes_terms(velocity, planes_in, axial_in, block, n)
            s, nonlinear = sweep(velocity, n, power)
            ready = (s,)
        block, entry = merge(me, power, block, swap(block, "theta", 1 << bit), entries, ready, points, bit)
        entries = (entry,)
    mine, send = enter(me, power, block, entry, own, other, s, points)
    got = swap(send, "theta", 1)
    new_velocity = close(me, s, power, mine, (), True)
    new_velocity = close(me, s, power, got, (new_velocity,), False)
    return (new_velocity, nonlinear)


def solution(mesh):
    in_specs = (P(None, "theta", "gz", None), P(), P(), P())
    out_specs = (P(None, "theta", "gz", None), P(None, "theta", "gz", None))
    return jax.shard_map(local, mesh=mesh, in_specs=in_specs, out_specs=out_specs, check_vma=False)
```

```python
import functools

import jax
import jax.numpy as jnp
from jax import lax
from jax.experimental import pallas as pl
from jax.experimental.pallas import tpu as pltpu
from jax.sharding import PartitionSpec as P

AXIAL_WEIGHTS = (0.75, -0.15, 1.0 / 60.0)
AXIAL_REACH = len(AXIAL_WEIGHTS)
STEP_WEIGHT = 0.2
MIRROR_SIGNS = (-1.0, -1.0, 1.0)
LANES = 128
UNROLL = 16
INNER = 10 << 29
MIRROR = 1 << 26
SIDE = 1 << 26

VMEM = pl.BlockSpec(memory_space=pltpu.VMEM)
SMEM = pl.BlockSpec(memory_space=pltpu.SMEM)
ANY = pl.BlockSpec(memory_space=pl.ANY)
HBM = pl.BlockSpec(memory_space=pltpu.HBM)


def params(block_bytes, blocks):
    return pltpu.CompilerParams(vmem_limit_bytes=(2 << 20) + blocks * block_bytes)


def held(*shape):
    return pltpu.VMEM(shape, jnp.float32)


def each(count, body):
    if count <= UNROLL:
        for i in range(count):
            body(i)
    else:
        pl.loop(0, count)(body)


def swap(block, axis, bit):
    size = lax.axis_size(axis)
    return lax.ppermute(block, axis, [(i, i ^ bit) for i in range(size)])


def swap_across(block, axis):
    size = lax.axis_size(axis)
    route = []
    for odd in range(1, size, 2):
        route += [(odd, (odd + 1) % size), ((odd + 1) % size, odd)]
    return lax.ppermute(block, axis, route)


def split(x):
    high = x.astype(jnp.bfloat16)
    return high, (x - high.astype(jnp.float32)).astype(jnp.bfloat16)


def product(left, right):
    dot = functools.partial(jnp.dot, preferred_element_type=jnp.float32)
    return dot(left[0], right[0]) + (dot(left[0], right[1]) + dot(left[1], right[0]))


def pack_tiles(v_ref, y_ref, comps):
    points, planes = v_ref.shape[1:3]
    carriers = y_ref.shape[1]
    lo, hi = AXIAL_REACH, planes - AXIAL_REACH
    for i, c in enumerate(comps):

        def carry(t):
            y_ref[i, t] = v_ref[c, t]

        def ride(j):
            t = carriers + j
            y_ref[i, 3 * j, lo:hi] = v_ref[c, t, 0:2]
            y_ref[i, 3 * j + 1, lo : lo + 1] = v_ref[c, t, 2:3]
            y_ref[i, 3 * j + 1, lo + 1 : hi] = v_ref[c, t, hi : hi + 1]
            y_ref[i, 3 * j + 2, lo:hi] = v_ref[c, t, hi + 1 :]

        each(carriers, carry)
        each(points - carriers, ride)


def rebuild_tiles(y_ref, tile_ref):
    carriers = y_ref.shape[1]
    comps, riders, planes, radial = tile_ref.shape
    lo, hi = AXIAL_REACH, planes - AXIAL_REACH
    for c in range(comps):
        for j in range(riders):
            tile_ref[c, j, 0:2] = y_ref[c, 3 * j, lo:hi]
            tile_ref[c, j, 2:3] = y_ref[c, 3 * j + 1, lo : lo + 1]
            tile_ref[c, j, lo:hi] = jnp.zeros((hi - lo, radial), jnp.float32)
            tile_ref[c, j, hi : hi + 1] = y_ref[c, 3 * j + 1, lo + 1 : hi]
            tile_ref[c, j, hi + 1 :] = y_ref[c, 3 * j + 2, lo:hi]


def load_kernel(hbm_ref, v_ref, y_ref, sems):
    order = list(range(v_ref.shape[0]))
    loads = [pltpu.make_async_copy(hbm_ref.at[c], v_ref.at[c], sems.at[c]) for c in order]
    for c in reversed(order):
        loads[c].start()
    loads[-1].wait()
    pack_tiles(v_ref, y_ref, order[-1:])
    for c in order[:-1]:
        loads[c].wait()


def load(v):
    comps, points, planes, radial = v.shape
    return pl.pallas_call(
        load_kernel,
        name="load",
        out_shape=(held(*v.shape), held(1, points - points // 4, planes, radial)),
        in_specs=[HBM],
        out_specs=(VMEM, VMEM),
        scratch_shapes=[pltpu.SemaphoreType.DMA((comps,))],
        compiler_params=params(v.size * 4, 2),
    )(v)


def pack_planes_kernel(v_ref, first_ref, y_ref):
    pack_tiles(v_ref, y_ref, range(y_ref.shape[0]))


def pack_planes(v, first):
    comps, points, planes, radial = v.shape
    return pl.pallas_call(
        pack_planes_kernel,
        name="pack_planes",
        out_shape=held(comps - 1, points - points // 4, planes, radial),
        in_specs=[VMEM, ANY],
        out_specs=VMEM,
        compiler_params=params(v.size * 4, 2),
    )(v, first)


def pack_side_kernel(me_ref, v_ref, first_ref, side_ref, *, after):
    points, reach = v_ref.shape[1], side_ref.shape[1]

    def put(start):
        for c in range(v_ref.shape[0]):
            for h in range(reach):
                side_ref[c, h] = v_ref[c, start + h]

    even = me_ref[0] % 2 == 0
    last = even if after else jnp.logical_not(even)
    pl.when(last)(lambda: put(points - reach))
    pl.when(jnp.logical_not(last))(lambda: put(0))


def pack_side(me, v, first, reach, after):
    comps, _, planes, radial = v.shape
    return pl.pallas_call(
        functools.partial(pack_side_kernel, after=after),
        name="pack_core" if after else "pack_chip",
        out_shape=held(comps, reach, planes, radial),
        in_specs=[SMEM, VMEM, ANY],
        out_specs=VMEM,
        compiler_params=params(v.size * 4, 3),
    )(me, v, first)


def pack_mirror_kernel(v_ref, first_ref, mirror_ref):
    points, tiles = v_ref.shape[1], mirror_ref.shape[1]
    width = LANES // (points // tiles)
    lane = lax.broadcasted_iota(jnp.int32, mirror_ref.shape[2:], 1)

    def put(p):
        for c in range(v_ref.shape[0]):
            tile = v_ref[c, p, :, :LANES]
            for q in range(1, points // tiles):
                part = pltpu.roll(v_ref[c, q * tiles + p, :, :LANES], q * width, 1)
                tile = jnp.where(lane < q * width, tile, part)
            mirror_ref[c, p] = tile

    each(tiles, put)


def pack_mirror(v, first, width):
    comps, points, planes, _ = v.shape
    return pl.pallas_call(
        pack_mirror_kernel,
        name="pack_mirror",
        out_shape=held(comps, points // (LANES // width), planes, LANES),
        in_specs=[VMEM, ANY],
        out_specs=VMEM,
        compiler_params=params(v.size * 4, 2),
    )(v, first)


def inverse_radius(radial, start=0):
    return 1.0 / ((lax.broadcasted_iota(jnp.int32, (1, radial), 1) + start).astype(jnp.float32) + 0.5)


def axial_weights(planes, inside):
    row = lax.broadcasted_iota(jnp.int32, (planes, LANES), 0)
    weights = []
    for m, w in enumerate(AXIAL_WEIGHTS, 1):
        for shift, own, sign in ((m, row < planes - m, 1.0), (planes - m, row >= m, -1.0)):
            keep = own if inside else jnp.logical_not(own)
            weights.append((shift, jnp.where(keep, sign * w, 0.0)))
    return weights


def axial_part(tile, weights):
    planes, width = tile.shape
    weights = [(shift, jnp.concatenate([weight] * (width // LANES), axis=1)) for shift, weight in weights]
    total = None
    for shift, weight in weights:
        term = weight * pltpu.roll(tile, planes - shift, 0)
        total = term if total is None else total + term
    return total


def mirror_kernel(v_ref, op_ref, mirror_ref, n_in_ref, n_ref, grad_ref):
    comps, points, planes, radial = v_ref.shape
    tiles = mirror_ref.shape[1]
    count = points // tiles
    width = LANES // count
    rows = tiles * planes
    right = split(jnp.concatenate([op_ref[radial:]] * count, axis=0))
    lane = lax.broadcasted_iota(jnp.int32, (rows, LANES), 1)
    for c in range(comps):
        high, low = split(MIRROR_SIGNS[c] * mirror_ref[c].reshape(rows, LANES))
        zero = jnp.zeros_like(high)
        parts = [
            [jnp.where((lane >= q * width) & (lane < (q + 1) * width), x, zero) for q in range(count)]
            for x in (high, low)
        ]
        left = [jnp.concatenate(x, axis=0) for x in parts]
        grad_ref[c * points * planes : (c + 1) * points * planes] = product(left, right)

    def finish(t):
        for c in range(comps):
            start = pl.multiple_of((c * points + t) * planes, planes)
            n_ref[c, t] = n_in_ref[c, t] + v_ref[0, t] * grad_ref[pl.ds(start, planes)]

    each(points, finish)


def mirror_terms(v, op, mirror, n):
    return pl.pallas_call(
        mirror_kernel,
        name="mirror_terms",
        out_shape=held(*v.shape),
        in_specs=[VMEM] * 4,
        out_specs=VMEM,
        scratch_shapes=[pltpu.VMEM((v.size // v.shape[3], v.shape[3]), jnp.float32)],
        input_output_aliases={3: 0},
        compiler_params=params(v.size * 4, 8),
        cost_estimate=pl.CostEstimate(flops=MIRROR, bytes_accessed=16 * v.size, transcendentals=0),
    )(v, op, mirror, n)


def inner_kernel(tap_ref, v_ref, op_ref, n_ref, grad_ref):
    comps, points, planes, radial = v_ref.shape
    reach = (tap_ref.shape[0] - 1) // 2
    rows = points * planes
    right = split(op_ref[:radial])
    for c in range(comps):
        grad_ref[c * rows : (c + 1) * rows] = product(split(v_ref[c].reshape(rows, radial)), right)
    weights = axial_weights(planes, True)

    @pl.loop(0, radial // LANES)
    def column(k):
        lanes = pl.ds(pl.multiple_of(k * LANES, LANES), LANES)
        inv_r = inverse_radius(LANES, k * LANES)
        for c in range(comps):
            for t in range(points):
                a, b, e = [v_ref[i, t, :, lanes] for i in range(3)]
                b_inv = b * inv_r
                around = None
                for m in range(max(-reach, -t), min(reach, points - 1 - t) + 1):
                    term = tap_ref[m + reach] * v_ref[c, t + m, :, lanes]
                    around = term if around is None else around + term
                start = c * rows + t * planes
                n = a * grad_ref[start : start + planes, lanes] + b_inv * around
                n = n + e * axial_part(v_ref[c, t, :, lanes], weights)
                if c == 0:
                    n = n - b_inv * b
                elif c == 1:
                    n = n + a * b_inv
                n_ref[c, t, :, lanes] = n


def inner_terms(taps, v, op):
    return pl.pallas_call(
        inner_kernel,
        name="inner_terms",
        out_shape=held(*v.shape),
        in_specs=[VMEM] * 3,
        out_specs=VMEM,
        scratch_shapes=[pltpu.VMEM((v.size // v.shape[3], v.shape[3]), jnp.float32)],
        compiler_params=params(v.size * 4, 7),
        cost_estimate=pl.CostEstimate(flops=INNER, bytes_accessed=16 * v.size, transcendentals=0),
    )(taps, v, op)


def add_side(tap_ref, v_ref, side_ref, n_in_ref, n_ref, before, columns):
    comps, points, _, radial = v_ref.shape
    reach = side_ref.shape[1]
    first = 0 if before else reach + 1

    start, count = columns

    @pl.loop(0, count)
    def column(i):
        k = start + i
        lanes = pl.ds(pl.multiple_of(k * LANES, LANES), LANES)
        inv_r = inverse_radius(LANES, k * LANES)
        weights = [tap_ref[first + i] for i in range(reach)]
        for c in range(comps):
            side = [side_ref[c, h, :, lanes] for h in range(reach)]
            for u in range(reach):
                t = u if before else points - reach + u
                taps = [(h, h - u) for h in range(u, reach)] if before else [(h, reach - 1 + h - u) for h in range(u + 1)]
                around = None
                for h, w in taps:
                    term = weights[w] * side[h]
                    around = term if around is None else around + term
                n_ref[c, t, :, lanes] = n_in_ref[c, t, :, lanes] + v_ref[1, t, :, lanes] * inv_r * around


def core_kernel(me_ref, tap_ref, v_ref, core_ref, n_in_ref, n_ref):
    even = me_ref[0] % 2 == 0
    columns = (0, v_ref.shape[3] // LANES)
    add = functools.partial(add_side, tap_ref, v_ref, core_ref, n_in_ref, n_ref, columns=columns)
    pl.when(even)(lambda: add(before=False))
    pl.when(jnp.logical_not(even))(lambda: add(before=True))


def late_kernel(me_ref, tap_ref, v_ref, chip_ref, n_in_ref, ready_ref, n_ref, *, own):
    core = me_ref[0] % 2
    count = v_ref.shape[3] // (2 * LANES)
    columns = ((core if own else 1 - core) * count, count)
    add = functools.partial(add_side, tap_ref, v_ref, chip_ref, n_in_ref, n_ref, columns=columns)
    pl.when(core == 0)(lambda: add(before=True))
    pl.when(core == 1)(lambda: add(before=False))


def side_terms(kernel, name, me, taps, v, side, n, ready=()):
    return pl.pallas_call(
        kernel,
        name=name,
        out_shape=held(*v.shape),
        in_specs=[SMEM] + [VMEM] * 4 + [ANY] * len(ready),
        out_specs=VMEM,
        input_output_aliases={4: 0},
        compiler_params=params(v.size * 4, 5),
        cost_estimate=pl.CostEstimate(flops=SIDE, bytes_accessed=12 * v.size, transcendentals=0),
    )(me, taps, v, side, n, *ready)


def share_kernel(v_ref, e_ref, power_ref, ends_ref, tile_ref):
    comps, points, planes, radial = v_ref.shape
    carriers = e_ref.shape[1]
    weights = axial_weights(planes, False)
    rebuild_tiles(e_ref, tile_ref)
    decay = power_ref[1:2]
    ends_ref[...] = jnp.zeros_like(ends_ref)
    for t in range(points):
        e = STEP_WEIGHT * (e_ref[0, t] if t < carriers else tile_ref[0, t - carriers])
        for c in range(comps):
            right_side = e * axial_part(v_ref[c, t], weights)
            ends_ref[0, c] = decay * ends_ref[0, c] - right_side
            ends_ref[1, c] = ends_ref[1, c] - power_ref[t : t + 1] * right_side


def share_terms(v, e, power):
    comps, points, planes, radial = v.shape
    return pl.pallas_call(
        share_kernel,
        name="share_terms",
        out_shape=held(2, comps, planes, radial),
        in_specs=[VMEM] * 3,
        out_specs=VMEM,
        scratch_shapes=[pltpu.VMEM((1, points - e.shape[1], planes, radial), jnp.float32)],
        compiler_params=params(v.size * 4, 4),
        cost_estimate=pl.CostEstimate(flops=20 * v.size, bytes_accessed=8 * v.size, transcendentals=0),
    )(v, e, power)


def ends_kernel(me_ref, v_ref, share_ref, power_ref, n_ref, ends_ref, *, own):
    comps, points, _, radial = v_ref.shape
    lanes = half_lanes(me_ref, radial // 2, own)
    decay = power_ref[1:2, lanes]
    for c in range(comps):
        low = high = None
        for t in range(points):
            right_side = v_ref[c, t, :, lanes] - STEP_WEIGHT * n_ref[c, t, :, lanes]
            low = right_side if t == 0 else decay * low + right_side
            high = right_side if t == 0 else high + power_ref[t : t + 1, lanes] * right_side
        ends_ref[0, c] = low + share_ref[0, c, :, lanes]
        ends_ref[1, c] = high + share_ref[1, c, :, lanes]


def ends_terms(me, v, share, power, n, own):
    comps, _, planes, radial = v.shape
    return pl.pallas_call(
        functools.partial(ends_kernel, own=own),
        name="ends_own" if own else "ends_other",
        out_shape=held(2, comps, planes, radial // 2),
        in_specs=[SMEM] + [VMEM] * 4,
        out_specs=VMEM,
        compiler_params=params(v.size * 4, 4),
        cost_estimate=pl.CostEstimate(flops=20 * v.size, bytes_accessed=8 * v.size, transcendentals=0),
    )(me, v, share, power, n)


def planes_kernel(v_ref, y_ref, e_ref, ready_ref, n_in_ref, n_ref, y_tile_ref, e_tile_ref):
    comps, points, planes, _ = v_ref.shape
    carriers = y_ref.shape[1]
    weights = axial_weights(planes, False)
    rebuild_tiles(y_ref, y_tile_ref)
    rebuild_tiles(e_ref, e_tile_ref)
    for t in range(points):
        for c in range(comps):
            ref, tile_ref, i = (y_ref, y_tile_ref, c) if c < comps - 1 else (e_ref, e_tile_ref, 0)
            tile = ref[i, t] if t < carriers else tile_ref[i, t - carriers]
            n_ref[c, t] = n_in_ref[c, t] + v_ref[2, t] * axial_part(tile, weights)


def planes_terms(v, y, e, ready, n):
    comps, points, planes, radial = v.shape
    riders = points - y.shape[1]
    return pl.pallas_call(
        planes_kernel,
        name="planes_terms",
        out_shape=held(*v.shape),
        in_specs=[VMEM] * 3 + [ANY, VMEM],
        out_specs=VMEM,
        scratch_shapes=[pltpu.VMEM((k, riders, planes, radial), jnp.float32) for k in (comps - 1, 1)],
        input_output_aliases={4: 0},
        compiler_params=params(v.size * 4, 6),
        cost_estimate=pl.CostEstimate(flops=20 * v.size, bytes_accessed=16 * v.size, transcendentals=0),
    )(v, y, e, ready, n)


def table_kernel(me_ref, factor_ref, stencil_ref, row_ref, tap_ref, *, points, sectors):
    radial = row_ref.shape[1]
    one = jnp.ones((1, radial), jnp.float32)
    half = (0.5 * lax.rsqrt(factor_ref[0] * one)) / inverse_radius(radial)
    root = jnp.sqrt(1.0 + half * half)
    loss = 2.0 * half * (root - half)
    rows = [one]
    for _ in range(points):
        rows.append(rows[-1] * (1.0 - loss))
    total = loss
    left, result = points * sectors, None
    while left:
        if left & 1:
            result = total if result is None else result + total - result * total
        total = total * (2.0 - total)
        left >>= 1
    across = rows[points] * rows[points]
    rows += [half / root, 1.0 / result]
    before = after = one
    for bit in range(1, sectors.bit_length() - 1):
        upper = (me_ref[0] >> bit) % 2 == 1
        rows += [across, before, after]
        before, after = jnp.where(upper, before * across, before), jnp.where(upper, after, after * across)
        across = across * across
    for k, row in enumerate(rows + [before, after]):
        row_ref[k : k + 1] = row
    for k in range(tap_ref.shape[0]):
        tap_ref[k] = jnp.full(tap_ref.shape[1:], stencil_ref[k], jnp.float32)


def table(me, viscous_factor, stencil, points, sectors, planes, radial):
    count = points + 5 + 3 * (sectors.bit_length() - 2)
    return pl.pallas_call(
        functools.partial(table_kernel, points=points, sectors=sectors),
        name="table",
        out_shape=(held(count, radial), held(stencil.shape[0], planes, LANES)),
        in_specs=[SMEM, SMEM, SMEM],
        out_specs=(VMEM, VMEM),
        compiler_params=params(1 << 20, 1),
        cost_estimate=pl.CostEstimate(flops=1000 * radial, bytes_accessed=400 * radial, transcendentals=0),
    )(me, viscous_factor, stencil)


def sweep_kernel(v_ref, n_ref, power_ref, s_ref, nonlinear_ref, sem):
    leave = pltpu.make_async_copy(n_ref, nonlinear_ref, sem)
    leave.start()
    comps, points, planes, radial = v_ref.shape
    decay = power_ref[1:2]
    height = power_ref[points + 1 : points + 2]
    for c in range(comps):
        s_ref[c, 0] = height * (v_ref[c, 0] - STEP_WEIGHT * n_ref[c, 0])

        def forward(i):
            t = i + 1
            s_ref[c, t] = decay * s_ref[c, t - 1] + height * (v_ref[c, t] - STEP_WEIGHT * n_ref[c, t])

        each(points - 1, forward)

    def backward(i, carry):
        t = points - 1 - i
        after = []
        for c in range(comps):
            s_ref[c, t] = s_ref[c, t] + carry[c]
            after.append(decay * (carry[c] + height * (v_ref[c, t] - STEP_WEIGHT * n_ref[c, t])))
        return tuple(after)

    start = (jnp.zeros((planes, radial), jnp.float32),) * comps
    lax.fori_loop(0, points, backward, start, unroll=points <= UNROLL)
    leave.wait()


def sweep(v, n, power):
    return pl.pallas_call(
        sweep_kernel,
        name="sweep",
        out_shape=(held(*v.shape), jax.ShapeDtypeStruct(v.shape, v.dtype)),
        in_specs=[VMEM] * 3,
        out_specs=(VMEM, ANY),
        scratch_shapes=[pltpu.SemaphoreType.DMA],
        compiler_params=params(v.size * 4, 4),
        cost_estimate=pl.CostEstimate(flops=10 * v.size, bytes_accessed=12 * v.size, transcendentals=0),
    )(v, n, power)


def half_lanes(me_ref, half, own=True):
    core = me_ref[0] % 2
    return pl.ds(pl.multiple_of((core if own else 1 - core) * half, half), half)


def pair_kernel(me_ref, power_ref, own_ref, other_ref, block_ref, *, points):
    half = own_ref.shape[3]
    hop = power_ref[points : points + 1, half_lanes(me_ref, half)]
    odd = me_ref[0] % 2 == 1
    for c in range(own_ref.shape[1]):
        for side in range(2):
            own, other = own_ref[side, c], other_ref[side, c]
            far, near = (own, other) if side == 0 else (other, own)
            block_ref[side, c] = jnp.where(odd, hop * near + far, hop * far + near)


def pair(me, power, own, other, points):
    return pl.pallas_call(
        functools.partial(pair_kernel, points=points),
        name="pair",
        out_shape=held(*own.shape),
        in_specs=[SMEM, VMEM, VMEM, VMEM],
        out_specs=VMEM,
        compiler_params=params(own.size * 4, 8),
    )(me, power, own, other)


def merge_kernel(me_ref, power_ref, block_ref, other_ref, *refs, points, bit):
    *entry_refs, block_out_ref, entry_out_ref = refs
    comps, half = block_ref.shape[1], block_ref.shape[3]
    lanes = half_lanes(me_ref, half)
    first = points + 3 * bit
    across, before, after = [power_ref[first + k : first + k + 1, lanes] for k in range(3)]
    upper = (me_ref[0] >> bit) % 2 == 1
    before = jnp.where(upper, before, 0.0)
    after = jnp.where(upper, 0.0, after)
    for c in range(comps):
        low, high = block_ref[0, c], block_ref[1, c]
        other_low, other_high = other_ref[0, c], other_ref[1, c]
        block_out_ref[0, c] = jnp.where(upper, across * other_low + low, across * low + other_low)
        block_out_ref[1, c] = jnp.where(upper, other_high + across * high, high + across * other_high)
        for side, enters in enumerate((before * other_low, after * other_high)):
            entry_out_ref[side, c] = entry_refs[0][side, c] + enters if entry_refs else enters


def merge(me, power, block, other, entries, points, bit):
    return pl.pallas_call(
        functools.partial(merge_kernel, points=points, bit=bit),
        name="merge",
        out_shape=(held(*block.shape), held(*block.shape)),
        in_specs=[SMEM] + [VMEM] * (3 + len(entries)),
        out_specs=(VMEM, VMEM),
        compiler_params=params(block.size * 4, 8),
    )(me, power, block, other, *entries)


def enter_kernel(me_ref, power_ref, block_ref, entry_ref, own_ref, other_ref, ready_ref, mine_ref, send_ref, *, points):
    comps, half = block_ref.shape[1], block_ref.shape[3]
    lanes = half_lanes(me_ref, half)
    row = lambda k: power_ref[k : k + 1, lanes]
    hop, height, wrap = row(points), row(points + 1), row(points + 2)
    last = power_ref.shape[0]
    before, after = row(last - 2) * wrap, row(last - 1) * wrap
    odd = me_ref[0] % 2 == 1
    for c in range(comps):
        low = height * (entry_ref[0, c] + before * block_ref[0, c])
        high = height * (entry_ref[1, c] + after * block_ref[1, c])
        even_low = height * jnp.where(odd, other_ref[0, c], own_ref[0, c])
        odd_high = height * jnp.where(odd, own_ref[1, c], other_ref[1, c])
        even_in = (low, odd_high + hop * high)
        odd_in = (even_low + hop * low, high)
        for side in range(2):
            mine_ref[side, c] = jnp.where(odd, odd_in[side], even_in[side])
            send_ref[side, c] = jnp.where(odd, even_in[side], odd_in[side])


def enter(me, power, block, entry, own, other, ready, points):
    return pl.pallas_call(
        functools.partial(enter_kernel, points=points),
        name="enter",
        out_shape=(held(*block.shape), held(*block.shape)),
        in_specs=[SMEM] + [VMEM] * 5 + [ANY],
        out_specs=(VMEM, VMEM),
        compiler_params=params(block.size * 4, 12),
    )(me, power, block, entry, own, other, ready)


def close_kernel(me_ref, s_ref, power_ref, entry_ref, *refs, own):
    out_ref, x_ref, sems = refs[-3:]
    comps, points, _, _ = s_ref.shape
    lanes = half_lanes(me_ref, entry_ref.shape[3], own)
    leaves = []
    for c in range(comps):
        before, after = entry_ref[0, c], entry_ref[1, c]

        def point(t):
            decayed = power_ref[pl.ds(t + 1, 1), lanes] * before + power_ref[pl.ds(points - t, 1), lanes] * after
            x_ref[c, t] = s_ref[c, t, :, lanes] + decayed

        each(points, point)
        leaves.append(pltpu.make_async_copy(x_ref.at[c], out_ref.at[c, :, :, lanes], sems.at[c]))
        leaves[c].start()
    for leave in leaves:
        leave.wait()


def close(me, s, power, entry, out, own):
    comps, points, planes, radial = s.shape
    return pl.pallas_call(
        functools.partial(close_kernel, own=own),
        name="close_own" if own else "close_other",
        out_shape=jax.ShapeDtypeStruct(s.shape, s.dtype),
        in_specs=[SMEM] + [VMEM] * 3 + [ANY] * len(out),
        out_specs=ANY,
        scratch_shapes=[
            pltpu.VMEM((comps, points, planes, radial // 2), jnp.float32),
            pltpu.SemaphoreType.DMA((comps,)),
        ],
        input_output_aliases={4: 0} if out else {},
        compiler_params=params(s.size * 4, 5),
        cost_estimate=pl.CostEstimate(flops=4 * s.size, bytes_accessed=8 * s.size, transcendentals=0),
    )(me, s, power, entry, *out)


def local(velocity, radial_op, azimuth_stencil, viscous_factor):
    sectors = lax.axis_size("theta")
    comps, points, planes, radial = velocity.shape
    reach = (azimuth_stencil.shape[0] - 1) // 2
    width = radial_op.shape[1] - radial
    me = lax.axis_index("theta").astype(jnp.int32).reshape(1)
    op = radial_op.T

    velocity, axial_out = load(pltpu.with_memory_space_constraint(velocity, pltpu.HBM))
    axial_in = swap(axial_out, "gz", 1)
    chip_out = pack_side(me, velocity, axial_out, reach, False)
    chip_in = swap_across(chip_out, "theta")
    mirror_out = pack_mirror(velocity, chip_out, width)
    mirror_in = swap(mirror_out, "theta", sectors // 2)
    core_out = pack_side(me, velocity, axial_in, reach, True)
    core_in = swap(core_out, "theta", 1)
    power, taps = table(me, viscous_factor, azimuth_stencil, points, sectors, planes, radial)
    n = inner_terms(taps, velocity, op)
    share_out = share_terms(velocity, axial_in, power)
    share_in = swap(share_out, "gz", 1)
    planes_in = swap(pack_planes(velocity, share_out), "gz", 1)
    n = side_terms(core_kernel, "core_terms", me, taps, velocity, core_in, n)
    n = mirror_terms(velocity, op, mirror_in, n)
    late = functools.partial(late_kernel, own=False)
    n = side_terms(late, "late_other", me, taps, velocity, chip_in, n, (share_in,))
    send = ends_terms(me, velocity, share_in, power, n, False)
    other = swap(send, "theta", 1)
    late = functools.partial(late_kernel, own=True)
    n = side_terms(late, "late_own", me, taps, velocity, chip_in, n, (send,))
    own = ends_terms(me, velocity, share_in, power, n, True)
    block = pair(me, power, own, other, points)
    entries = ()
    last = sectors.bit_length() - 2
    for bit in range(1, last + 1):
        if bit == last:
            n = planes_terms(velocity, planes_in, axial_in, block, n)
            s, nonlinear = sweep(velocity, n, power)
        block, entry = merge(me, power, block, swap(block, "theta", 1 << bit), entries, points, bit)
        entries = (entry,)
    mine, send = enter(me, power, block, entry, own, other, s, points)
    got = swap(send, "theta", 1)
    new_velocity = close(me, s, power, mine, (), True)
    new_velocity = close(me, s, power, got, (new_velocity,), False)
    return (new_velocity, nonlinear)


def solution(mesh):
    in_specs = (P(None, "theta", "gz", None), P(), P(), P())
    out_specs = (P(None, "theta", "gz", None), P(None, "theta", "gz", None))
    return jax.shard_map(local, mesh=mesh, in_specs=in_specs, out_specs=out_specs, check_vma=False)
```

```python
import functools

import jax
import jax.numpy as jnp
from jax import lax
from jax.experimental import pallas as pl
from jax.experimental.pallas import tpu as pltpu
from jax.sharding import PartitionSpec as P

AXIAL_WEIGHTS = (0.75, -0.15, 1.0 / 60.0)
AXIAL_REACH = len(AXIAL_WEIGHTS)
STEP_WEIGHT = 0.2
MIRROR_SIGNS = (-1.0, -1.0, 1.0)
LANES = 128
UNROLL = 16
INNER = 10 << 29
MIRROR = 1 << 31
SIDE = 1 << 26

VMEM = pl.BlockSpec(memory_space=pltpu.VMEM)
SMEM = pl.BlockSpec(memory_space=pltpu.SMEM)
ANY = pl.BlockSpec(memory_space=pl.ANY)
HBM = pl.BlockSpec(memory_space=pltpu.HBM)


def params(block_bytes, blocks):
    return pltpu.CompilerParams(vmem_limit_bytes=(2 << 20) + blocks * block_bytes)


def held(*shape):
    return pltpu.VMEM(shape, jnp.float32)


def each(count, body):
    if count <= UNROLL:
        for i in range(count):
            body(i)
    else:
        pl.loop(0, count)(body)


def swap(block, axis, bit):
    size = lax.axis_size(axis)
    return lax.ppermute(block, axis, [(i, i ^ bit) for i in range(size)])


def swap_across(block, axis):
    size = lax.axis_size(axis)
    route = []
    for odd in range(1, size, 2):
        route += [(odd, (odd + 1) % size), ((odd + 1) % size, odd)]
    return lax.ppermute(block, axis, route)


def split(x):
    high = x.astype(jnp.bfloat16)
    return high, (x - high.astype(jnp.float32)).astype(jnp.bfloat16)


def product(left, right):
    dot = functools.partial(jnp.dot, preferred_element_type=jnp.float32)
    return dot(left[0], right[0]) + (dot(left[0], right[1]) + dot(left[1], right[0]))


def pack_tiles(v_ref, y_ref, comps):
    points, planes = v_ref.shape[1:3]
    carriers = y_ref.shape[1]
    lo, hi = AXIAL_REACH, planes - AXIAL_REACH
    for i, c in enumerate(comps):

        def carry(t):
            y_ref[i, t] = v_ref[c, t]

        def ride(j):
            t = carriers + j
            y_ref[i, 3 * j, lo:hi] = v_ref[c, t, 0:2]
            y_ref[i, 3 * j + 1, lo : lo + 1] = v_ref[c, t, 2:3]
            y_ref[i, 3 * j + 1, lo + 1 : hi] = v_ref[c, t, hi : hi + 1]
            y_ref[i, 3 * j + 2, lo:hi] = v_ref[c, t, hi + 1 :]

        each(carriers, carry)
        each(points - carriers, ride)


def rebuild_tiles(y_ref, tile_ref):
    carriers = y_ref.shape[1]
    comps, riders, planes, radial = tile_ref.shape
    lo, hi = AXIAL_REACH, planes - AXIAL_REACH
    for c in range(comps):
        for j in range(riders):
            tile_ref[c, j, 0:2] = y_ref[c, 3 * j, lo:hi]
            tile_ref[c, j, 2:3] = y_ref[c, 3 * j + 1, lo : lo + 1]
            tile_ref[c, j, lo:hi] = jnp.zeros((hi - lo, radial), jnp.float32)
            tile_ref[c, j, hi : hi + 1] = y_ref[c, 3 * j + 1, lo + 1 : hi]
            tile_ref[c, j, hi + 1 :] = y_ref[c, 3 * j + 2, lo:hi]


def load_kernel(hbm_ref, v_ref, y_ref, sems):
    order = list(range(v_ref.shape[0]))
    loads = [pltpu.make_async_copy(hbm_ref.at[c], v_ref.at[c], sems.at[c]) for c in order]
    for c in reversed(order):
        loads[c].start()
    loads[-1].wait()
    pack_tiles(v_ref, y_ref, order[-1:])
    for c in order[:-1]:
        loads[c].wait()


def load(v):
    comps, points, planes, radial = v.shape
    return pl.pallas_call(
        load_kernel,
        name="load",
        out_shape=(held(*v.shape), held(1, points - points // 4, planes, radial)),
        in_specs=[HBM],
        out_specs=(VMEM, VMEM),
        scratch_shapes=[pltpu.SemaphoreType.DMA((comps,))],
        compiler_params=params(v.size * 4, 2),
    )(v)


def pack_planes_kernel(v_ref, *refs):
    y_ref = refs[-1]
    pack_tiles(v_ref, y_ref, range(y_ref.shape[0]))


def pack_planes(v, *first):
    comps, points, planes, radial = v.shape
    return pl.pallas_call(
        pack_planes_kernel,
        name="pack_planes",
        out_shape=held(comps - 1, points - points // 4, planes, radial),
        in_specs=[VMEM] + [ANY] * len(first),
        out_specs=VMEM,
        compiler_params=params(v.size * 4, 2),
    )(v, *first)


def pack_side_kernel(me_ref, v_ref, first_ref, side_ref, *, after):
    points, reach = v_ref.shape[1], side_ref.shape[1]

    def put(start):
        for c in range(v_ref.shape[0]):
            for h in range(reach):
                side_ref[c, h] = v_ref[c, start + h]

    even = me_ref[0] % 2 == 0
    last = even if after else jnp.logical_not(even)
    pl.when(last)(lambda: put(points - reach))
    pl.when(jnp.logical_not(last))(lambda: put(0))


def pack_side(me, v, first, reach, after):
    comps, _, planes, radial = v.shape
    return pl.pallas_call(
        functools.partial(pack_side_kernel, after=after),
        name="pack_core" if after else "pack_chip",
        out_shape=held(comps, reach, planes, radial),
        in_specs=[SMEM, VMEM, ANY],
        out_specs=VMEM,
        compiler_params=params(v.size * 4, 3),
    )(me, v, first)


def pack_mirror_kernel(v_ref, first_ref, mirror_ref):
    points, tiles = v_ref.shape[1], mirror_ref.shape[1]
    width = LANES // (points // tiles)
    lane = lax.broadcasted_iota(jnp.int32, mirror_ref.shape[2:], 1)

    def put(p):
        for c in range(v_ref.shape[0]):
            tile = v_ref[c, p, :, :LANES]
            for q in range(1, points // tiles):
                part = pltpu.roll(v_ref[c, q * tiles + p, :, :LANES], q * width, 1)
                tile = jnp.where(lane < q * width, tile, part)
            mirror_ref[c, p] = tile

    each(tiles, put)


def pack_mirror(v, first, width):
    comps, points, planes, _ = v.shape
    return pl.pallas_call(
        pack_mirror_kernel,
        name="pack_mirror",
        out_shape=held(comps, points // (LANES // width), planes, LANES),
        in_specs=[VMEM, ANY],
        out_specs=VMEM,
        compiler_params=params(v.size * 4, 2),
    )(v, first)


def inverse_radius(radial, start=0):
    return 1.0 / ((lax.broadcasted_iota(jnp.int32, (1, radial), 1) + start).astype(jnp.float32) + 0.5)


def axial_weights(planes, inside):
    row = lax.broadcasted_iota(jnp.int32, (planes, LANES), 0)
    weights = []
    for m, w in enumerate(AXIAL_WEIGHTS, 1):
        for shift, own, sign in ((m, row < planes - m, 1.0), (planes - m, row >= m, -1.0)):
            keep = own if inside else jnp.logical_not(own)
            weights.append((shift, jnp.where(keep, sign * w, 0.0)))
    return weights


def axial_part(tile, weights):
    planes, width = tile.shape
    weights = [(shift, jnp.concatenate([weight] * (width // LANES), axis=1)) for shift, weight in weights]
    total = None
    for shift, weight in weights:
        term = weight * pltpu.roll(tile, planes - shift, 0)
        total = term if total is None else total + term
    return total


def mirror_kernel(v_ref, op_ref, mirror_ref, n_in_ref, n_ref, grad_ref):
    comps, points, planes, radial = v_ref.shape
    tiles = mirror_ref.shape[1]
    count = points // tiles
    width = LANES // count
    rows = tiles * planes
    right = split(jnp.concatenate([op_ref[radial:]] * count, axis=0))
    lane = lax.broadcasted_iota(jnp.int32, (rows, LANES), 1)
    for c in range(comps):
        high, low = split(MIRROR_SIGNS[c] * mirror_ref[c].reshape(rows, LANES))
        zero = jnp.zeros_like(high)
        parts = [
            [jnp.where((lane >= q * width) & (lane < (q + 1) * width), x, zero) for q in range(count)]
            for x in (high, low)
        ]
        left = [jnp.concatenate(x, axis=0) for x in parts]
        grad_ref[c * points * planes : (c + 1) * points * planes] = product(left, right)

    def finish(t):
        for c in range(comps):
            start = pl.multiple_of((c * points + t) * planes, planes)
            n_ref[c, t] = n_in_ref[c, t] + v_ref[0, t] * grad_ref[pl.ds(start, planes)]

    each(points, finish)


def mirror_terms(v, op, mirror, n):
    return pl.pallas_call(
        mirror_kernel,
        name="mirror_terms",
        out_shape=held(*v.shape),
        in_specs=[VMEM] * 4,
        out_specs=VMEM,
        scratch_shapes=[pltpu.VMEM((v.size // v.shape[3], v.shape[3]), jnp.float32)],
        input_output_aliases={3: 0},
        compiler_params=params(v.size * 4, 8),
        cost_estimate=pl.CostEstimate(flops=MIRROR, bytes_accessed=16 * v.size, transcendentals=0),
    )(v, op, mirror, n)


def inner_kernel(tap_ref, v_ref, op_ref, ready_ref, n_ref, grad_ref):
    comps, points, planes, radial = v_ref.shape
    reach = (tap_ref.shape[0] - 1) // 2
    rows = points * planes
    right = split(op_ref[:radial])
    for c in range(comps):
        grad_ref[c * rows : (c + 1) * rows] = product(split(v_ref[c].reshape(rows, radial)), right)
    weights = axial_weights(planes, True)

    @pl.loop(0, radial // LANES)
    def column(k):
        lanes = pl.ds(pl.multiple_of(k * LANES, LANES), LANES)
        inv_r = inverse_radius(LANES, k * LANES)
        for c in range(comps):
            for t in range(points):
                a, b, e = [v_ref[i, t, :, lanes] for i in range(3)]
                b_inv = b * inv_r
                around = None
                for m in range(max(-reach, -t), min(reach, points - 1 - t) + 1):
                    term = tap_ref[m + reach] * v_ref[c, t + m, :, lanes]
                    around = term if around is None else around + term
                start = c * rows + t * planes
                n = a * grad_ref[start : start + planes, lanes] + b_inv * around
                n = n + e * axial_part(v_ref[c, t, :, lanes], weights)
                if c == 0:
                    n = n - b_inv * b
                elif c == 1:
                    n = n + a * b_inv
                n_ref[c, t, :, lanes] = n


def inner_terms(taps, v, op, ready):
    return pl.pallas_call(
        inner_kernel,
        name="inner_terms",
        out_shape=held(*v.shape),
        in_specs=[VMEM] * 3 + [ANY],
        out_specs=VMEM,
        scratch_shapes=[pltpu.VMEM((v.size // v.shape[3], v.shape[3]), jnp.float32)],
        compiler_params=params(v.size * 4, 7),
        cost_estimate=pl.CostEstimate(flops=INNER, bytes_accessed=16 * v.size, transcendentals=0),
    )(taps, v, op, ready)


def add_side(tap_ref, v_ref, side_ref, n_in_ref, n_ref, before, columns):
    comps, points, _, radial = v_ref.shape
    reach = side_ref.shape[1]
    first = 0 if before else reach + 1

    start, count = columns

    @pl.loop(0, count)
    def column(i):
        k = start + i
        lanes = pl.ds(pl.multiple_of(k * LANES, LANES), LANES)
        inv_r = inverse_radius(LANES, k * LANES)
        weights = [tap_ref[first + i] for i in range(reach)]
        for c in range(comps):
            side = [side_ref[c, h, :, lanes] for h in range(reach)]
            for u in range(reach):
                t = u if before else points - reach + u
                taps = [(h, h - u) for h in range(u, reach)] if before else [(h, reach - 1 + h - u) for h in range(u + 1)]
                around = None
                for h, w in taps:
                    term = weights[w] * side[h]
                    around = term if around is None else around + term
                n_ref[c, t, :, lanes] = n_in_ref[c, t, :, lanes] + v_ref[1, t, :, lanes] * inv_r * around


def core_kernel(me_ref, tap_ref, v_ref, core_ref, n_in_ref, n_ref, done_ref):
    even = me_ref[0] % 2 == 0
    columns = (0, v_ref.shape[3] // LANES)
    add = functools.partial(add_side, tap_ref, v_ref, core_ref, n_in_ref, n_ref, columns=columns)
    pl.when(even)(lambda: add(before=False))
    pl.when(jnp.logical_not(even))(lambda: add(before=True))
    done_ref[...] = jnp.zeros_like(done_ref)


def late_kernel(me_ref, tap_ref, v_ref, chip_ref, n_in_ref, ready_ref, n_ref, done_ref, *, own):
    core = me_ref[0] % 2
    count = v_ref.shape[3] // (2 * LANES)
    columns = ((core if own else 1 - core) * count, count)
    add = functools.partial(add_side, tap_ref, v_ref, chip_ref, n_in_ref, n_ref, columns=columns)
    pl.when(core == 0)(lambda: add(before=True))
    pl.when(core == 1)(lambda: add(before=False))
    done_ref[...] = jnp.zeros_like(done_ref)


def side_terms(kernel, name, me, taps, v, side, n, ready=()):
    return pl.pallas_call(
        kernel,
        name=name,
        out_shape=(held(*v.shape), held(8, LANES)),
        in_specs=[SMEM] + [VMEM] * 4 + [ANY] * len(ready),
        out_specs=(VMEM, VMEM),
        input_output_aliases={4: 0},
        compiler_params=params(v.size * 4, 5),
        cost_estimate=pl.CostEstimate(flops=SIDE, bytes_accessed=12 * v.size, transcendentals=0),
    )(me, taps, v, side, n, *ready)


def share_kernel(v_ref, e_ref, power_ref, ends_ref, tile_ref):
    comps, points, planes, radial = v_ref.shape
    carriers = e_ref.shape[1]
    weights = axial_weights(planes, False)
    rebuild_tiles(e_ref, tile_ref)
    decay = power_ref[1:2]
    ends_ref[...] = jnp.zeros_like(ends_ref)
    for t in range(points):
        e = STEP_WEIGHT * (e_ref[0, t] if t < carriers else tile_ref[0, t - carriers])
        for c in range(comps):
            right_side = e * axial_part(v_ref[c, t], weights)
            ends_ref[0, c] = decay * ends_ref[0, c] - right_side
            ends_ref[1, c] = ends_ref[1, c] - power_ref[t : t + 1] * right_side


def share_terms(v, e, power):
    comps, points, planes, radial = v.shape
    return pl.pallas_call(
        share_kernel,
        name="share_terms",
        out_shape=held(2, comps, planes, radial),
        in_specs=[VMEM] * 3,
        out_specs=VMEM,
        scratch_shapes=[pltpu.VMEM((1, points - e.shape[1], planes, radial), jnp.float32)],
        compiler_params=params(v.size * 4, 4),
        cost_estimate=pl.CostEstimate(flops=20 * v.size, bytes_accessed=8 * v.size, transcendentals=0),
    )(v, e, power)


def ends_kernel(me_ref, v_ref, share_ref, power_ref, n_ref, ends_ref, *, own):
    comps, points, _, radial = v_ref.shape
    lanes = half_lanes(me_ref, radial // 2, own)
    decay = power_ref[1:2, lanes]
    for c in range(comps):
        low = high = None
        for t in range(points):
            right_side = v_ref[c, t, :, lanes] - STEP_WEIGHT * n_ref[c, t, :, lanes]
            low = right_side if t == 0 else decay * low + right_side
            high = right_side if t == 0 else high + power_ref[t : t + 1, lanes] * right_side
        ends_ref[0, c] = low + share_ref[0, c, :, lanes]
        ends_ref[1, c] = high + share_ref[1, c, :, lanes]


def ends_terms(me, v, share, power, n, own):
    comps, _, planes, radial = v.shape
    return pl.pallas_call(
        functools.partial(ends_kernel, own=own),
        name="ends_own" if own else "ends_other",
        out_shape=held(2, comps, planes, radial // 2),
        in_specs=[SMEM] + [VMEM] * 4,
        out_specs=VMEM,
        compiler_params=params(v.size * 4, 4),
        cost_estimate=pl.CostEstimate(flops=20 * v.size, bytes_accessed=8 * v.size, transcendentals=0),
    )(me, v, share, power, n)


def planes_kernel(v_ref, y_ref, e_ref, ready_ref, n_in_ref, n_ref, y_tile_ref, e_tile_ref):
    comps, points, planes, _ = v_ref.shape
    carriers = y_ref.shape[1]
    weights = axial_weights(planes, False)
    rebuild_tiles(y_ref, y_tile_ref)
    rebuild_tiles(e_ref, e_tile_ref)
    for t in range(points):
        for c in range(comps):
            ref, tile_ref, i = (y_ref, y_tile_ref, c) if c < comps - 1 else (e_ref, e_tile_ref, 0)
            tile = ref[i, t] if t < carriers else tile_ref[i, t - carriers]
            n_ref[c, t] = n_in_ref[c, t] + v_ref[2, t] * axial_part(tile, weights)


def planes_terms(v, y, e, ready, n):
    comps, points, planes, radial = v.shape
    riders = points - y.shape[1]
    return pl.pallas_call(
        planes_kernel,
        name="planes_terms",
        out_shape=held(*v.shape),
        in_specs=[VMEM] * 3 + [ANY, VMEM],
        out_specs=VMEM,
        scratch_shapes=[pltpu.VMEM((k, riders, planes, radial), jnp.float32) for k in (comps - 1, 1)],
        input_output_aliases={4: 0},
        compiler_params=params(v.size * 4, 6),
        cost_estimate=pl.CostEstimate(flops=20 * v.size, bytes_accessed=16 * v.size, transcendentals=0),
    )(v, y, e, ready, n)


def table_kernel(me_ref, factor_ref, stencil_ref, row_ref, tap_ref, *, points, sectors):
    radial = row_ref.shape[1]
    one = jnp.ones((1, radial), jnp.float32)
    half = (0.5 * lax.rsqrt(factor_ref[0] * one)) / inverse_radius(radial)
    root = jnp.sqrt(1.0 + half * half)
    loss = 2.0 * half * (root - half)
    rows = [one]
    for _ in range(points):
        rows.append(rows[-1] * (1.0 - loss))
    total = loss
    left, result = points * sectors, None
    while left:
        if left & 1:
            result = total if result is None else result + total - result * total
        total = total * (2.0 - total)
        left >>= 1
    across = rows[points] * rows[points]
    rows += [half / root, 1.0 / result]
    before = after = one
    for bit in range(1, sectors.bit_length() - 1):
        upper = (me_ref[0] >> bit) % 2 == 1
        rows += [across, before, after]
        before, after = jnp.where(upper, before * across, before), jnp.where(upper, after, after * across)
        across = across * across
    for k, row in enumerate(rows + [before, after]):
        row_ref[k : k + 1] = row
    for k in range(tap_ref.shape[0]):
        tap_ref[k] = jnp.full(tap_ref.shape[1:], stencil_ref[k], jnp.float32)


def table(me, viscous_factor, stencil, points, sectors, planes, radial):
    count = points + 5 + 3 * (sectors.bit_length() - 2)
    return pl.pallas_call(
        functools.partial(table_kernel, points=points, sectors=sectors),
        name="table",
        out_shape=(held(count, radial), held(stencil.shape[0], planes, LANES)),
        in_specs=[SMEM, SMEM, SMEM],
        out_specs=(VMEM, VMEM),
        compiler_params=params(1 << 20, 1),
        cost_estimate=pl.CostEstimate(flops=1000 * radial, bytes_accessed=400 * radial, transcendentals=0),
    )(me, viscous_factor, stencil)


def sweep_kernel(v_ref, n_ref, power_ref, s_ref, nonlinear_ref, sem):
    leave = pltpu.make_async_copy(n_ref, nonlinear_ref, sem)
    leave.start()
    comps, points, planes, radial = v_ref.shape
    decay = power_ref[1:2]
    height = power_ref[points + 1 : points + 2]
    for c in range(comps):
        s_ref[c, 0] = height * (v_ref[c, 0] - STEP_WEIGHT * n_ref[c, 0])

        def forward(i):
            t = i + 1
            s_ref[c, t] = decay * s_ref[c, t - 1] + height * (v_ref[c, t] - STEP_WEIGHT * n_ref[c, t])

        each(points - 1, forward)

    def backward(i, carry):
        t = points - 1 - i
        after = []
        for c in range(comps):
            s_ref[c, t] = s_ref[c, t] + carry[c]
            after.append(decay * (carry[c] + height * (v_ref[c, t] - STEP_WEIGHT * n_ref[c, t])))
        return tuple(after)

    start = (jnp.zeros((planes, radial), jnp.float32),) * comps
    lax.fori_loop(0, points, backward, start, unroll=points <= UNROLL)
    leave.wait()


def sweep(v, n, power):
    return pl.pallas_call(
        sweep_kernel,
        name="sweep",
        out_shape=(held(*v.shape), jax.ShapeDtypeStruct(v.shape, v.dtype)),
        in_specs=[VMEM] * 3,
        out_specs=(VMEM, ANY),
        scratch_shapes=[pltpu.SemaphoreType.DMA],
        compiler_params=params(v.size * 4, 4),
        cost_estimate=pl.CostEstimate(flops=10 * v.size, bytes_accessed=12 * v.size, transcendentals=0),
    )(v, n, power)


def half_lanes(me_ref, half, own=True):
    core = me_ref[0] % 2
    return pl.ds(pl.multiple_of((core if own else 1 - core) * half, half), half)


def pair_kernel(me_ref, power_ref, own_ref, other_ref, block_ref, *, points):
    half = own_ref.shape[3]
    hop = power_ref[points : points + 1, half_lanes(me_ref, half)]
    odd = me_ref[0] % 2 == 1
    for c in range(own_ref.shape[1]):
        for side in range(2):
            own, other = own_ref[side, c], other_ref[side, c]
            far, near = (own, other) if side == 0 else (other, own)
            block_ref[side, c] = jnp.where(odd, hop * near + far, hop * far + near)


def pair(me, power, own, other, points):
    return pl.pallas_call(
        functools.partial(pair_kernel, points=points),
        name="pair",
        out_shape=held(*own.shape),
        in_specs=[SMEM, VMEM, VMEM, VMEM],
        out_specs=VMEM,
        compiler_params=params(own.size * 4, 8),
    )(me, power, own, other)


def merge_kernel(me_ref, power_ref, block_ref, other_ref, *refs, points, bit):
    *entry_refs, block_out_ref, entry_out_ref = refs
    comps, half = block_ref.shape[1], block_ref.shape[3]
    lanes = half_lanes(me_ref, half)
    first = points + 3 * bit
    across, before, after = [power_ref[first + k : first + k + 1, lanes] for k in range(3)]
    upper = (me_ref[0] >> bit) % 2 == 1
    before = jnp.where(upper, before, 0.0)
    after = jnp.where(upper, 0.0, after)
    for c in range(comps):
        low, high = block_ref[0, c], block_ref[1, c]
        other_low, other_high = other_ref[0, c], other_ref[1, c]
        block_out_ref[0, c] = jnp.where(upper, across * other_low + low, across * low + other_low)
        block_out_ref[1, c] = jnp.where(upper, other_high + across * high, high + across * other_high)
        for side, enters in enumerate((before * other_low, after * other_high)):
            entry_out_ref[side, c] = entry_refs[0][side, c] + enters if entry_refs else enters


def merge(me, power, block, other, entries, points, bit):
    return pl.pallas_call(
        functools.partial(merge_kernel, points=points, bit=bit),
        name="merge",
        out_shape=(held(*block.shape), held(*block.shape)),
        in_specs=[SMEM] + [VMEM] * (3 + len(entries)),
        out_specs=(VMEM, VMEM),
        compiler_params=params(block.size * 4, 8),
    )(me, power, block, other, *entries)


def enter_kernel(me_ref, power_ref, block_ref, entry_ref, own_ref, other_ref, ready_ref, mine_ref, send_ref, *, points):
    comps, half = block_ref.shape[1], block_ref.shape[3]
    lanes = half_lanes(me_ref, half)
    row = lambda k: power_ref[k : k + 1, lanes]
    hop, height, wrap = row(points), row(points + 1), row(points + 2)
    last = power_ref.shape[0]
    before, after = row(last - 2) * wrap, row(last - 1) * wrap
    odd = me_ref[0] % 2 == 1
    for c in range(comps):
        low = height * (entry_ref[0, c] + before * block_ref[0, c])
        high = height * (entry_ref[1, c] + after * block_ref[1, c])
        even_low = height * jnp.where(odd, other_ref[0, c], own_ref[0, c])
        odd_high = height * jnp.where(odd, own_ref[1, c], other_ref[1, c])
        even_in = (low, odd_high + hop * high)
        odd_in = (even_low + hop * low, high)
        for side in range(2):
            mine_ref[side, c] = jnp.where(odd, odd_in[side], even_in[side])
            send_ref[side, c] = jnp.where(odd, even_in[side], odd_in[side])


def enter(me, power, block, entry, own, other, ready, points):
    return pl.pallas_call(
        functools.partial(enter_kernel, points=points),
        name="enter",
        out_shape=(held(*block.shape), held(*block.shape)),
        in_specs=[SMEM] + [VMEM] * 5 + [ANY],
        out_specs=(VMEM, VMEM),
        compiler_params=params(block.size * 4, 12),
    )(me, power, block, entry, own, other, ready)


def close_kernel(me_ref, s_ref, power_ref, entry_ref, *refs, own):
    out_ref, x_ref, sems = refs[-3:]
    comps, points, _, _ = s_ref.shape
    lanes = half_lanes(me_ref, entry_ref.shape[3], own)
    leaves = []
    for c in range(comps):
        before, after = entry_ref[0, c], entry_ref[1, c]

        def point(t):
            decayed = power_ref[pl.ds(t + 1, 1), lanes] * before + power_ref[pl.ds(points - t, 1), lanes] * after
            x_ref[c, t] = s_ref[c, t, :, lanes] + decayed

        each(points, point)
        leaves.append(pltpu.make_async_copy(x_ref.at[c], out_ref.at[c, :, :, lanes], sems.at[c]))
        leaves[c].start()
    for leave in leaves:
        leave.wait()


def close(me, s, power, entry, out, own):
    comps, points, planes, radial = s.shape
    return pl.pallas_call(
        functools.partial(close_kernel, own=own),
        name="close_own" if own else "close_other",
        out_shape=jax.ShapeDtypeStruct(s.shape, s.dtype),
        in_specs=[SMEM] + [VMEM] * 3 + [ANY] * len(out),
        out_specs=ANY,
        scratch_shapes=[
            pltpu.VMEM((comps, points, planes, radial // 2), jnp.float32),
            pltpu.SemaphoreType.DMA((comps,)),
        ],
        input_output_aliases={4: 0} if out else {},
        compiler_params=params(s.size * 4, 5),
        cost_estimate=pl.CostEstimate(flops=4 * s.size, bytes_accessed=8 * s.size, transcendentals=0),
    )(me, s, power, entry, *out)


def local(velocity, radial_op, azimuth_stencil, viscous_factor):
    sectors = lax.axis_size("theta")
    comps, points, planes, radial = velocity.shape
    reach = (azimuth_stencil.shape[0] - 1) // 2
    width = radial_op.shape[1] - radial
    me = lax.axis_index("theta").astype(jnp.int32).reshape(1)
    op = radial_op.T

    velocity, axial_out = load(pltpu.with_memory_space_constraint(velocity, pltpu.HBM))
    axial_in = swap(axial_out, "gz", 1)
    chip_out = pack_side(me, velocity, axial_out, reach, False)
    chip_in = swap_across(chip_out, "theta")
    mirror_out = pack_mirror(velocity, chip_out, width)
    mirror_in = swap(mirror_out, "theta", sectors // 2)
    core_out = pack_side(me, velocity, axial_in, reach, True)
    core_in = swap(core_out, "theta", 1)
    power, taps = table(me, viscous_factor, azimuth_stencil, points, sectors, planes, radial)
    share_out = share_terms(velocity, axial_in, power)
    share_in = swap(share_out, "gz", 1)
    n = inner_terms(taps, velocity, op, share_out)
    n, done = side_terms(core_kernel, "core_terms", me, taps, velocity, core_in, n)
    planes_in = swap(pack_planes(velocity, done), "gz", 1)
    n = mirror_terms(velocity, op, mirror_in, n)
    late = functools.partial(late_kernel, own=False)
    n, _ = side_terms(late, "late_other", me, taps, velocity, chip_in, n, (share_in,))
    send = ends_terms(me, velocity, share_in, power, n, False)
    other = swap(send, "theta", 1)
    late = functools.partial(late_kernel, own=True)
    n, _ = side_terms(late, "late_own", me, taps, velocity, chip_in, n, (send,))
    own = ends_terms(me, velocity, share_in, power, n, True)
    block = pair(me, power, own, other, points)
    entries = ()
    last = sectors.bit_length() - 2
    for bit in range(1, last + 1):
        if bit == last:
            n = planes_terms(velocity, planes_in, axial_in, block, n)
            s, nonlinear = sweep(velocity, n, power)
        block, entry = merge(me, power, block, swap(block, "theta", 1 << bit), entries, points, bit)
        entries = (entry,)
    mine, send = enter(me, power, block, entry, own, other, s, points)
    got = swap(send, "theta", 1)
    new_velocity = close(me, s, power, mine, (), True)
    new_velocity = close(me, s, power, got, (new_velocity,), False)
    return (new_velocity, nonlinear)


def solution(mesh):
    in_specs = (P(None, "theta", "gz", None), P(), P(), P())
    out_specs = (P(None, "theta", "gz", None), P(None, "theta", "gz", None))
    return jax.shard_map(local, mesh=mesh, in_specs=in_specs, out_specs=out_specs, check_vma=False)
```

```python
import functools

import jax
import jax.numpy as jnp
from jax import lax
from jax.experimental import pallas as pl
from jax.experimental.pallas import tpu as pltpu
from jax.sharding import PartitionSpec as P

AXIAL_WEIGHTS = (0.75, -0.15, 1.0 / 60.0)
AXIAL_REACH = len(AXIAL_WEIGHTS)
STEP_WEIGHT = 0.2
MIRROR_SIGNS = (-1.0, -1.0, 1.0)
LANES = 128
UNROLL = 16
INNER = 1 << 20
MIRROR = 25 << 26
SIDE = 1 << 20
LATE = 1 << 30

VMEM = pl.BlockSpec(memory_space=pltpu.VMEM)
SMEM = pl.BlockSpec(memory_space=pltpu.SMEM)
ANY = pl.BlockSpec(memory_space=pl.ANY)
HBM = pl.BlockSpec(memory_space=pltpu.HBM)


def params(block_bytes, blocks):
    return pltpu.CompilerParams(vmem_limit_bytes=(2 << 20) + blocks * block_bytes)


def held(*shape):
    return pltpu.VMEM(shape, jnp.float32)


def each(count, body):
    if count <= UNROLL:
        for i in range(count):
            body(i)
    else:
        pl.loop(0, count)(body)


def swap(block, axis, bit):
    size = lax.axis_size(axis)
    return lax.ppermute(block, axis, [(i, i ^ bit) for i in range(size)])


def swap_across(block, axis):
    size = lax.axis_size(axis)
    route = []
    for odd in range(1, size, 2):
        route += [(odd, (odd + 1) % size), ((odd + 1) % size, odd)]
    return lax.ppermute(block, axis, route)


def split(x):
    high = x.astype(jnp.bfloat16)
    return high, (x - high.astype(jnp.float32)).astype(jnp.bfloat16)


def product(left, right):
    dot = functools.partial(jnp.dot, preferred_element_type=jnp.float32)
    return dot(left[0], right[0]) + (dot(left[0], right[1]) + dot(left[1], right[0]))


def pack_tiles(v_ref, y_ref, comps, lanes=slice(None)):
    points, planes = v_ref.shape[1:3]
    carriers = y_ref.shape[1]
    lo, hi = AXIAL_REACH, planes - AXIAL_REACH
    for i, c in enumerate(comps):

        def carry(t):
            y_ref[i, t] = v_ref[c, t, :, lanes]

        def ride(j):
            t = carriers + j
            y_ref[i, 3 * j, lo:hi] = v_ref[c, t, 0:2, lanes]
            y_ref[i, 3 * j + 1, lo : lo + 1] = v_ref[c, t, 2:3, lanes]
            y_ref[i, 3 * j + 1, lo + 1 : hi] = v_ref[c, t, hi : hi + 1, lanes]
            y_ref[i, 3 * j + 2, lo:hi] = v_ref[c, t, hi + 1 :, lanes]

        each(carriers, carry)
        each(points - carriers, ride)


def rebuild_tiles(y_ref, tile_ref):
    carriers = y_ref.shape[1]
    comps, riders, planes, radial = tile_ref.shape
    lo, hi = AXIAL_REACH, planes - AXIAL_REACH
    for c in range(comps):
        for j in range(riders):
            tile_ref[c, j, 0:2] = y_ref[c, 3 * j, lo:hi]
            tile_ref[c, j, 2:3] = y_ref[c, 3 * j + 1, lo : lo + 1]
            tile_ref[c, j, lo:hi] = jnp.zeros((hi - lo, radial), jnp.float32)
            tile_ref[c, j, hi : hi + 1] = y_ref[c, 3 * j + 1, lo + 1 : hi]
            tile_ref[c, j, hi + 1 :] = y_ref[c, 3 * j + 2, lo:hi]


def load_kernel(me_ref, hbm_ref, v_ref, other_ref, own_ref, sems):
    order = list(range(v_ref.shape[0]))
    loads = [pltpu.make_async_copy(hbm_ref.at[c], v_ref.at[c], sems.at[c]) for c in order]
    for c in reversed(order):
        loads[c].start()
    loads[-1].wait()
    half = other_ref.shape[3]
    pack_tiles(v_ref, other_ref, order[-1:], half_lanes(me_ref, half, False))
    pack_tiles(v_ref, own_ref, order[-1:], half_lanes(me_ref, half, True))
    for c in order[:-1]:
        loads[c].wait()


def load(me, v):
    comps, points, planes, radial = v.shape
    part = held(1, points - points // 4, planes, radial // 2)
    return pl.pallas_call(
        load_kernel,
        name="load",
        out_shape=(held(*v.shape), part, part),
        in_specs=[SMEM, HBM],
        out_specs=(VMEM, VMEM, VMEM),
        scratch_shapes=[pltpu.SemaphoreType.DMA((comps,))],
        compiler_params=params(v.size * 4, 2),
    )(me, v)


def pack_planes_kernel(v_ref, first_ref, y_ref):
    pack_tiles(v_ref, y_ref, range(y_ref.shape[0]))


def pack_planes(v, first):
    comps, points, planes, radial = v.shape
    return pl.pallas_call(
        pack_planes_kernel,
        name="pack_planes",
        out_shape=held(comps - 1, points - points // 4, planes, radial),
        in_specs=[VMEM, ANY],
        out_specs=VMEM,
        compiler_params=params(v.size * 4, 2),
    )(v, first)


def pack_side_kernel(me_ref, v_ref, first_ref, side_ref, *, after):
    points, reach = v_ref.shape[1], side_ref.shape[1]

    def put(start):
        for c in range(v_ref.shape[0]):
            for h in range(reach):
                side_ref[c, h] = v_ref[c, start + h]

    even = me_ref[0] % 2 == 0
    last = even if after else jnp.logical_not(even)
    pl.when(last)(lambda: put(points - reach))
    pl.when(jnp.logical_not(last))(lambda: put(0))


def pack_side(me, v, first, reach, after):
    comps, _, planes, radial = v.shape
    return pl.pallas_call(
        functools.partial(pack_side_kernel, after=after),
        name="pack_core" if after else "pack_chip",
        out_shape=held(comps, reach, planes, radial),
        in_specs=[SMEM, VMEM, ANY],
        out_specs=VMEM,
        compiler_params=params(v.size * 4, 3),
    )(me, v, first)


def pack_mirror_kernel(v_ref, first_ref, mirror_ref):
    points, tiles = v_ref.shape[1], mirror_ref.shape[1]
    width = LANES // (points // tiles)
    lane = lax.broadcasted_iota(jnp.int32, mirror_ref.shape[2:], 1)

    def put(p):
        for c in range(v_ref.shape[0]):
            tile = v_ref[c, p, :, :LANES]
            for q in range(1, points // tiles):
                part = pltpu.roll(v_ref[c, q * tiles + p, :, :LANES], q * width, 1)
                tile = jnp.where(lane < q * width, tile, part)
            mirror_ref[c, p] = tile

    each(tiles, put)


def pack_mirror(v, first, width):
    comps, points, planes, _ = v.shape
    return pl.pallas_call(
        pack_mirror_kernel,
        name="pack_mirror",
        out_shape=held(comps, points // (LANES // width), planes, LANES),
        in_specs=[VMEM, ANY],
        out_specs=VMEM,
        compiler_params=params(v.size * 4, 2),
    )(v, first)


def inverse_radius(radial, start=0):
    return 1.0 / ((lax.broadcasted_iota(jnp.int32, (1, radial), 1) + start).astype(jnp.float32) + 0.5)


def axial_weights(planes, inside):
    row = lax.broadcasted_iota(jnp.int32, (planes, LANES), 0)
    weights = []
    for m, w in enumerate(AXIAL_WEIGHTS, 1):
        for shift, own, sign in ((m, row < planes - m, 1.0), (planes - m, row >= m, -1.0)):
            keep = own if inside else jnp.logical_not(own)
            weights.append((shift, jnp.where(keep, sign * w, 0.0)))
    return weights


def axial_part(tile, weights):
    planes, width = tile.shape
    weights = [(shift, jnp.concatenate([weight] * (width // LANES), axis=1)) for shift, weight in weights]
    total = None
    for shift, weight in weights:
        term = weight * pltpu.roll(tile, planes - shift, 0)
        total = term if total is None else total + term
    return total


def mirror_kernel(v_ref, op_ref, mirror_ref, n_in_ref, n_ref, grad_ref):
    comps, points, planes, radial = v_ref.shape
    tiles = mirror_ref.shape[1]
    count = points // tiles
    width = LANES // count
    rows = tiles * planes
    right = split(jnp.concatenate([op_ref[radial:]] * count, axis=0))
    lane = lax.broadcasted_iota(jnp.int32, (rows, LANES), 1)
    for c in range(comps):
        high, low = split(MIRROR_SIGNS[c] * mirror_ref[c].reshape(rows, LANES))
        zero = jnp.zeros_like(high)
        parts = [
            [jnp.where((lane >= q * width) & (lane < (q + 1) * width), x, zero) for q in range(count)]
            for x in (high, low)
        ]
        left = [jnp.concatenate(x, axis=0) for x in parts]
        grad_ref[c * points * planes : (c + 1) * points * planes] = product(left, right)

    def finish(t):
        for c in range(comps):
            start = pl.multiple_of((c * points + t) * planes, planes)
            n_ref[c, t] = n_in_ref[c, t] + v_ref[0, t] * grad_ref[pl.ds(start, planes)]

    each(points, finish)


def mirror_terms(v, op, mirror, n):
    return pl.pallas_call(
        mirror_kernel,
        name="mirror_terms",
        out_shape=held(*v.shape),
        in_specs=[VMEM] * 4,
        out_specs=VMEM,
        scratch_shapes=[pltpu.VMEM((v.size // v.shape[3], v.shape[3]), jnp.float32)],
        input_output_aliases={3: 0},
        compiler_params=params(v.size * 4, 8),
        cost_estimate=pl.CostEstimate(flops=MIRROR, bytes_accessed=16 * v.size, transcendentals=0),
    )(v, op, mirror, n)


def inner_kernel(tap_ref, v_ref, op_ref, n_ref, grad_ref):
    comps, points, planes, radial = v_ref.shape
    reach = (tap_ref.shape[0] - 1) // 2
    rows = points * planes
    right = split(op_ref[:radial])
    for c in range(comps):
        grad_ref[c * rows : (c + 1) * rows] = product(split(v_ref[c].reshape(rows, radial)), right)
    weights = axial_weights(planes, True)

    @pl.loop(0, radial // LANES)
    def column(k):
        lanes = pl.ds(pl.multiple_of(k * LANES, LANES), LANES)
        inv_r = inverse_radius(LANES, k * LANES)
        for c in range(comps):
            for t in range(points):
                a, b, e = [v_ref[i, t, :, lanes] for i in range(3)]
                b_inv = b * inv_r
                around = None
                for m in range(max(-reach, -t), min(reach, points - 1 - t) + 1):
                    term = tap_ref[m + reach] * v_ref[c, t + m, :, lanes]
                    around = term if around is None else around + term
                start = c * rows + t * planes
                n = a * grad_ref[start : start + planes, lanes] + b_inv * around
                n = n + e * axial_part(v_ref[c, t, :, lanes], weights)
                if c == 0:
                    n = n - b_inv * b
                elif c == 1:
                    n = n + a * b_inv
                n_ref[c, t, :, lanes] = n


def inner_terms(taps, v, op):
    return pl.pallas_call(
        inner_kernel,
        name="inner_terms",
        out_shape=held(*v.shape),
        in_specs=[VMEM] * 3,
        out_specs=VMEM,
        scratch_shapes=[pltpu.VMEM((v.size // v.shape[3], v.shape[3]), jnp.float32)],
        compiler_params=params(v.size * 4, 7),
        cost_estimate=pl.CostEstimate(flops=INNER, bytes_accessed=16 * v.size, transcendentals=0),
    )(taps, v, op)


def add_side(tap_ref, v_ref, side_ref, n_in_ref, n_ref, before, columns):
    comps, points, _, radial = v_ref.shape
    reach = side_ref.shape[1]
    first = 0 if before else reach + 1

    start, count = columns

    @pl.loop(0, count)
    def column(i):
        k = start + i
        lanes = pl.ds(pl.multiple_of(k * LANES, LANES), LANES)
        inv_r = inverse_radius(LANES, k * LANES)
        weights = [tap_ref[first + i] for i in range(reach)]
        for c in range(comps):
            side = [side_ref[c, h, :, lanes] for h in range(reach)]
            for u in range(reach):
                t = u if before else points - reach + u
                taps = [(h, h - u) for h in range(u, reach)] if before else [(h, reach - 1 + h - u) for h in range(u + 1)]
                around = None
                for h, w in taps:
                    term = weights[w] * side[h]
                    around = term if around is None else around + term
                n_ref[c, t, :, lanes] = n_in_ref[c, t, :, lanes] + v_ref[1, t, :, lanes] * inv_r * around


def core_kernel(me_ref, tap_ref, v_ref, core_ref, n_in_ref, n_ref):
    even = me_ref[0] % 2 == 0
    columns = (0, v_ref.shape[3] // LANES)
    add = functools.partial(add_side, tap_ref, v_ref, core_ref, n_in_ref, n_ref, columns=columns)
    pl.when(even)(lambda: add(before=False))
    pl.when(jnp.logical_not(even))(lambda: add(before=True))


def late_kernel(me_ref, tap_ref, v_ref, chip_ref, n_in_ref, ready_ref, n_ref, *, own):
    core = me_ref[0] % 2
    count = v_ref.shape[3] // (2 * LANES)
    columns = ((core if own else 1 - core) * count, count)
    add = functools.partial(add_side, tap_ref, v_ref, chip_ref, n_in_ref, n_ref, columns=columns)
    pl.when(core == 0)(lambda: add(before=True))
    pl.when(core == 1)(lambda: add(before=False))


def side_terms(kernel, name, me, taps, v, side, n, ready=(), flops=SIDE):
    return pl.pallas_call(
        kernel,
        name=name,
        out_shape=held(*v.shape),
        in_specs=[SMEM] + [VMEM] * 4 + [ANY] * len(ready),
        out_specs=VMEM,
        input_output_aliases={4: 0},
        compiler_params=params(v.size * 4, 5),
        cost_estimate=pl.CostEstimate(flops=flops, bytes_accessed=12 * v.size, transcendentals=0),
    )(me, taps, v, side, n, *ready)


def share_kernel(me_ref, v_ref, e_ref, power_ref, ready_ref, ends_ref, tile_ref, *, own):
    comps, points, planes, radial = v_ref.shape
    lanes = half_lanes(me_ref, radial // 2, own)
    carriers = e_ref.shape[1]
    weights = axial_weights(planes, False)
    rebuild_tiles(e_ref, tile_ref)
    decay = power_ref[1:2, lanes]
    ends_ref[...] = jnp.zeros_like(ends_ref)
    for t in range(points):
        e = STEP_WEIGHT * (e_ref[0, t] if t < carriers else tile_ref[0, t - carriers])
        for c in range(comps):
            right_side = e * axial_part(v_ref[c, t, :, lanes], weights)
            ends_ref[0, c] = decay * ends_ref[0, c] - right_side
            ends_ref[1, c] = ends_ref[1, c] - power_ref[t : t + 1, lanes] * right_side


def share_terms(me, v, e, power, ready, own):
    comps, points, planes, radial = v.shape
    return pl.pallas_call(
        functools.partial(share_kernel, own=own),
        name="share_own" if own else "share_other",
        out_shape=held(2, comps, planes, radial // 2),
        in_specs=[SMEM] + [VMEM] * 3 + [ANY],
        out_specs=VMEM,
        scratch_shapes=[pltpu.VMEM((1, points - e.shape[1], planes, radial // 2), jnp.float32)],
        compiler_params=params(v.size * 4, 4),
        cost_estimate=pl.CostEstimate(flops=20 * v.size, bytes_accessed=8 * v.size, transcendentals=0),
    )(me, v, e, power, ready)


def ends_kernel(me_ref, v_ref, share_ref, power_ref, n_ref, ends_ref, *, own):
    comps, points, _, radial = v_ref.shape
    lanes = half_lanes(me_ref, radial // 2, own)
    decay = power_ref[1:2, lanes]
    for c in range(comps):
        low = high = None
        for t in range(points):
            right_side = v_ref[c, t, :, lanes] - STEP_WEIGHT * n_ref[c, t, :, lanes]
            low = right_side if t == 0 else decay * low + right_side
            high = right_side if t == 0 else high + power_ref[t : t + 1, lanes] * right_side
        ends_ref[0, c] = low + share_ref[0, c]
        ends_ref[1, c] = high + share_ref[1, c]


def ends_terms(me, v, share, power, n, own):
    comps, _, planes, radial = v.shape
    return pl.pallas_call(
        functools.partial(ends_kernel, own=own),
        name="ends_own" if own else "ends_other",
        out_shape=held(2, comps, planes, radial // 2),
        in_specs=[SMEM] + [VMEM] * 4,
        out_specs=VMEM,
        compiler_params=params(v.size * 4, 4),
        cost_estimate=pl.CostEstimate(flops=20 * v.size, bytes_accessed=8 * v.size, transcendentals=0),
    )(me, v, share, power, n)


def planes_kernel(me_ref, v_ref, y_ref, other_ref, own_ref, ready_ref, n_in_ref, n_ref, y_tile_ref, half_ref, e_ref):
    comps, points, planes, radial = v_ref.shape
    carriers = y_ref.shape[1]
    weights = axial_weights(planes, False)
    rebuild_tiles(y_ref, y_tile_ref)
    for own, part_ref in ((False, other_ref), (True, own_ref)):
        lanes = half_lanes(me_ref, radial // 2, own)
        rebuild_tiles(part_ref, half_ref)
        for t in range(points):
            e_ref[t, :, lanes] = part_ref[0, t] if t < carriers else half_ref[0, t - carriers]
    for t in range(points):
        for c in range(comps):
            if c == comps - 1:
                tile = e_ref[t]
            else:
                tile = y_ref[c, t] if t < carriers else y_tile_ref[c, t - carriers]
            n_ref[c, t] = n_in_ref[c, t] + v_ref[2, t] * axial_part(tile, weights)


def planes_terms(me, v, y, other, own, ready, n):
    comps, points, planes, radial = v.shape
    riders = points - y.shape[1]
    return pl.pallas_call(
        planes_kernel,
        name="planes_terms",
        out_shape=held(*v.shape),
        in_specs=[SMEM] + [VMEM] * 4 + [ANY, VMEM],
        out_specs=VMEM,
        scratch_shapes=[
            pltpu.VMEM((comps - 1, riders, planes, radial), jnp.float32),
            pltpu.VMEM((1, riders, planes, radial // 2), jnp.float32),
            pltpu.VMEM((points, planes, radial), jnp.float32),
        ],
        input_output_aliases={6: 0},
        compiler_params=params(v.size * 4, 8),
        cost_estimate=pl.CostEstimate(flops=20 * v.size, bytes_accessed=16 * v.size, transcendentals=0),
    )(me, v, y, other, own, ready, n)


def table_kernel(me_ref, factor_ref, stencil_ref, row_ref, tap_ref, *, points, sectors):
    radial = row_ref.shape[1]
    one = jnp.ones((1, radial), jnp.float32)
    half = (0.5 * lax.rsqrt(factor_ref[0] * one)) / inverse_radius(radial)
    root = jnp.sqrt(1.0 + half * half)
    loss = 2.0 * half * (root - half)
    rows = [one]
    for _ in range(points):
        rows.append(rows[-1] * (1.0 - loss))
    total = loss
    left, result = points * sectors, None
    while left:
        if left & 1:
            result = total if result is None else result + total - result * total
        total = total * (2.0 - total)
        left >>= 1
    across = rows[points] * rows[points]
    rows += [half / root, 1.0 / result]
    before = after = one
    for bit in range(1, sectors.bit_length() - 1):
        upper = (me_ref[0] >> bit) % 2 == 1
        rows += [across, before, after]
        before, after = jnp.where(upper, before * across, before), jnp.where(upper, after, after * across)
        across = across * across
    for k, row in enumerate(rows + [before, after]):
        row_ref[k : k + 1] = row
    for k in range(tap_ref.shape[0]):
        tap_ref[k] = jnp.full(tap_ref.shape[1:], stencil_ref[k], jnp.float32)


def table(me, viscous_factor, stencil, points, sectors, planes, radial):
    count = points + 5 + 3 * (sectors.bit_length() - 2)
    return pl.pallas_call(
        functools.partial(table_kernel, points=points, sectors=sectors),
        name="table",
        out_shape=(held(count, radial), held(stencil.shape[0], planes, LANES)),
        in_specs=[SMEM, SMEM, SMEM],
        out_specs=(VMEM, VMEM),
        compiler_params=params(1 << 20, 1),
        cost_estimate=pl.CostEstimate(flops=1000 * radial, bytes_accessed=400 * radial, transcendentals=0),
    )(me, viscous_factor, stencil)


def sweep_kernel(v_ref, n_ref, power_ref, s_ref, nonlinear_ref, sem):
    leave = pltpu.make_async_copy(n_ref, nonlinear_ref, sem)
    leave.start()
    comps, points, planes, radial = v_ref.shape
    decay = power_ref[1:2]
    height = power_ref[points + 1 : points + 2]
    for c in range(comps):
        s_ref[c, 0] = height * (v_ref[c, 0] - STEP_WEIGHT * n_ref[c, 0])

        def forward(i):
            t = i + 1
            s_ref[c, t] = decay * s_ref[c, t - 1] + height * (v_ref[c, t] - STEP_WEIGHT * n_ref[c, t])

        each(points - 1, forward)

    def backward(i, carry):
        t = points - 1 - i
        after = []
        for c in range(comps):
            s_ref[c, t] = s_ref[c, t] + carry[c]
            after.append(decay * (carry[c] + height * (v_ref[c, t] - STEP_WEIGHT * n_ref[c, t])))
        return tuple(after)

    start = (jnp.zeros((planes, radial), jnp.float32),) * comps
    lax.fori_loop(0, points, backward, start, unroll=points <= UNROLL)
    leave.wait()


def sweep(v, n, power):
    return pl.pallas_call(
        sweep_kernel,
        name="sweep",
        out_shape=(held(*v.shape), jax.ShapeDtypeStruct(v.shape, v.dtype)),
        in_specs=[VMEM] * 3,
        out_specs=(VMEM, ANY),
        scratch_shapes=[pltpu.SemaphoreType.DMA],
        compiler_params=params(v.size * 4, 4),
        cost_estimate=pl.CostEstimate(flops=10 * v.size, bytes_accessed=12 * v.size, transcendentals=0),
    )(v, n, power)


def half_lanes(me_ref, half, own=True):
    core = me_ref[0] % 2
    return pl.ds(pl.multiple_of((core if own else 1 - core) * half, half), half)


def pair_kernel(me_ref, power_ref, own_ref, other_ref, block_ref, *, points):
    half = own_ref.shape[3]
    hop = power_ref[points : points + 1, half_lanes(me_ref, half)]
    odd = me_ref[0] % 2 == 1
    for c in range(own_ref.shape[1]):
        for side in range(2):
            own, other = own_ref[side, c], other_ref[side, c]
            far, near = (own, other) if side == 0 else (other, own)
            block_ref[side, c] = jnp.where(odd, hop * near + far, hop * far + near)


def pair(me, power, own, other, points):
    return pl.pallas_call(
        functools.partial(pair_kernel, points=points),
        name="pair",
        out_shape=held(*own.shape),
        in_specs=[SMEM, VMEM, VMEM, VMEM],
        out_specs=VMEM,
        compiler_params=params(own.size * 4, 8),
    )(me, power, own, other)


def merge_kernel(me_ref, power_ref, block_ref, other_ref, *refs, points, bit):
    *entry_refs, block_out_ref, entry_out_ref = refs
    comps, half = block_ref.shape[1], block_ref.shape[3]
    lanes = half_lanes(me_ref, half)
    first = points + 3 * bit
    across, before, after = [power_ref[first + k : first + k + 1, lanes] for k in range(3)]
    upper = (me_ref[0] >> bit) % 2 == 1
    before = jnp.where(upper, before, 0.0)
    after = jnp.where(upper, 0.0, after)
    for c in range(comps):
        low, high = block_ref[0, c], block_ref[1, c]
        other_low, other_high = other_ref[0, c], other_ref[1, c]
        block_out_ref[0, c] = jnp.where(upper, across * other_low + low, across * low + other_low)
        block_out_ref[1, c] = jnp.where(upper, other_high + across * high, high + across * other_high)
        for side, enters in enumerate((before * other_low, after * other_high)):
            entry_out_ref[side, c] = entry_refs[0][side, c] + enters if entry_refs else enters


def merge(me, power, block, other, entries, points, bit):
    return pl.pallas_call(
        functools.partial(merge_kernel, points=points, bit=bit),
        name="merge",
        out_shape=(held(*block.shape), held(*block.shape)),
        in_specs=[SMEM] + [VMEM] * (3 + len(entries)),
        out_specs=(VMEM, VMEM),
        compiler_params=params(block.size * 4, 8),
    )(me, power, block, other, *entries)


def enter_kernel(me_ref, power_ref, block_ref, entry_ref, own_ref, other_ref, ready_ref, mine_ref, send_ref, *, points):
    comps, half = block_ref.shape[1], block_ref.shape[3]
    lanes = half_lanes(me_ref, half)
    row = lambda k: power_ref[k : k + 1, lanes]
    hop, height, wrap = row(points), row(points + 1), row(points + 2)
    last = power_ref.shape[0]
    before, after = row(last - 2) * wrap, row(last - 1) * wrap
    odd = me_ref[0] % 2 == 1
    for c in range(comps):
        low = height * (entry_ref[0, c] + before * block_ref[0, c])
        high = height * (entry_ref[1, c] + after * block_ref[1, c])
        even_low = height * jnp.where(odd, other_ref[0, c], own_ref[0, c])
        odd_high = height * jnp.where(odd, own_ref[1, c], other_ref[1, c])
        even_in = (low, odd_high + hop * high)
        odd_in = (even_low + hop * low, high)
        for side in range(2):
            mine_ref[side, c] = jnp.where(odd, odd_in[side], even_in[side])
            send_ref[side, c] = jnp.where(odd, even_in[side], odd_in[side])


def enter(me, power, block, entry, own, other, ready, points):
    return pl.pallas_call(
        functools.partial(enter_kernel, points=points),
        name="enter",
        out_shape=(held(*block.shape), held(*block.shape)),
        in_specs=[SMEM] + [VMEM] * 5 + [ANY],
        out_specs=(VMEM, VMEM),
        compiler_params=params(block.size * 4, 12),
    )(me, power, block, entry, own, other, ready)


def close_kernel(me_ref, s_ref, power_ref, entry_ref, *refs, own):
    out_ref, x_ref, sems = refs[-3:]
    comps, points, _, _ = s_ref.shape
    lanes = half_lanes(me_ref, entry_ref.shape[3], own)
    leaves = []
    for c in range(comps):
        before, after = entry_ref[0, c], entry_ref[1, c]

        def point(t):
            decayed = power_ref[pl.ds(t + 1, 1), lanes] * before + power_ref[pl.ds(points - t, 1), lanes] * after
            x_ref[c, t] = s_ref[c, t, :, lanes] + decayed

        each(points, point)
        leaves.append(pltpu.make_async_copy(x_ref.at[c], out_ref.at[c, :, :, lanes], sems.at[c]))
        leaves[c].start()
    for leave in leaves:
        leave.wait()


def close(me, s, power, entry, out, own):
    comps, points, planes, radial = s.shape
    return pl.pallas_call(
        functools.partial(close_kernel, own=own),
        name="close_own" if own else "close_other",
        out_shape=jax.ShapeDtypeStruct(s.shape, s.dtype),
        in_specs=[SMEM] + [VMEM] * 3 + [ANY] * len(out),
        out_specs=ANY,
        scratch_shapes=[
            pltpu.VMEM((comps, points, planes, radial // 2), jnp.float32),
            pltpu.SemaphoreType.DMA((comps,)),
        ],
        input_output_aliases={4: 0} if out else {},
        compiler_params=params(s.size * 4, 5),
        cost_estimate=pl.CostEstimate(flops=4 * s.size, bytes_accessed=8 * s.size, transcendentals=0),
    )(me, s, power, entry, *out)


def local(velocity, radial_op, azimuth_stencil, viscous_factor):
    sectors = lax.axis_size("theta")
    comps, points, planes, radial = velocity.shape
    reach = (azimuth_stencil.shape[0] - 1) // 2
    width = radial_op.shape[1] - radial
    me = lax.axis_index("theta").astype(jnp.int32).reshape(1)
    op = radial_op.T

    velocity, other_out, own_out = load(me, pltpu.with_memory_space_constraint(velocity, pltpu.HBM))
    chip_out = pack_side(me, velocity, other_out, reach, False)
    chip_in = swap_across(chip_out, "theta")
    other_in = swap(other_out, "gz", 1)
    own_in = swap(own_out, "gz", 1)
    mirror_out = pack_mirror(velocity, chip_out, width)
    mirror_in = swap(mirror_out, "theta", sectors // 2)
    core_out = pack_side(me, velocity, mirror_out, reach, True)
    core_in = swap(core_out, "theta", 1)
    power, taps = table(me, viscous_factor, azimuth_stencil, points, sectors, planes, radial)
    n = inner_terms(taps, velocity, op)
    share_other_out = share_terms(me, velocity, other_in, power, n, False)
    share_other = swap(share_other_out, "gz", 1)
    share_own_out = share_terms(me, velocity, own_in, power, share_other_out, True)
    share_own = swap(share_own_out, "gz", 1)
    planes_in = swap(pack_planes(velocity, share_own_out), "gz", 1)
    n = side_terms(core_kernel, "core_terms", me, taps, velocity, core_in, n)
    n = mirror_terms(velocity, op, mirror_in, n)
    late = functools.partial(late_kernel, own=False)
    n = side_terms(late, "late_other", me, taps, velocity, chip_in, n, (share_other,), LATE)
    send = ends_terms(me, velocity, share_other, power, n, False)
    other = swap(send, "theta", 1)
    late = functools.partial(late_kernel, own=True)
    n = side_terms(late, "late_own", me, taps, velocity, chip_in, n, (send,))
    own = ends_terms(me, velocity, share_own, power, n, True)
    block = pair(me, power, own, other, points)
    entries = ()
    last = sectors.bit_length() - 2
    for bit in range(1, last + 1):
        if bit == last:
            n = planes_terms(me, velocity, planes_in, other_in, own_in, block, n)
            s, nonlinear = sweep(velocity, n, power)
        block, entry = merge(me, power, block, swap(block, "theta", 1 << bit), entries, points, bit)
        entries = (entry,)
    mine, send = enter(me, power, block, entry, own, other, s, points)
    got = swap(send, "theta", 1)
    new_velocity = close(me, s, power, mine, (), True)
    new_velocity = close(me, s, power, got, (new_velocity,), False)
    return (new_velocity, nonlinear)


def solution(mesh):
    in_specs = (P(None, "theta", "gz", None), P(), P(), P())
    out_specs = (P(None, "theta", "gz", None), P(None, "theta", "gz", None))
    return jax.shard_map(local, mesh=mesh, in_specs=in_specs, out_specs=out_specs, check_vma=False)
```

```python
import functools

import jax
import jax.numpy as jnp
from jax import lax
from jax.experimental import pallas as pl
from jax.experimental.pallas import tpu as pltpu
from jax.sharding import PartitionSpec as P

AXIAL_WEIGHTS = (0.75, -0.15, 1.0 / 60.0)
AXIAL_REACH = len(AXIAL_WEIGHTS)
STEP_WEIGHT = 0.2
MIRROR_SIGNS = (-1.0, -1.0, 1.0)
CHIP_PARTS = 2
LANES = 128
UNROLL = 16
INNER = 1 << 31
MIRROR = 1 << 26
SIDE = 1 << 26

VMEM = pl.BlockSpec(memory_space=pltpu.VMEM)
SMEM = pl.BlockSpec(memory_space=pltpu.SMEM)
ANY = pl.BlockSpec(memory_space=pl.ANY)
HBM = pl.BlockSpec(memory_space=pltpu.HBM)


def params(block_bytes, blocks):
    return pltpu.CompilerParams(vmem_limit_bytes=(2 << 20) + blocks * block_bytes)


def held(*shape):
    return pltpu.VMEM(shape, jnp.float32)


def each(count, body):
    if count <= UNROLL:
        for i in range(count):
            body(i)
    else:
        pl.loop(0, count)(body)


def swap(block, axis, bit):
    size = lax.axis_size(axis)
    return lax.ppermute(block, axis, [(i, i ^ bit) for i in range(size)])


def swap_across(block, axis):
    size = lax.axis_size(axis)
    route = []
    for odd in range(1, size, 2):
        route += [(odd, (odd + 1) % size), ((odd + 1) % size, odd)]
    return lax.ppermute(block, axis, route)


def split(x):
    high = x.astype(jnp.bfloat16)
    return high, (x - high.astype(jnp.float32)).astype(jnp.bfloat16)


def product(left, right):
    dot = functools.partial(jnp.dot, preferred_element_type=jnp.float32)
    return dot(left[0], right[0]) + (dot(left[0], right[1]) + dot(left[1], right[0]))


def pack_tiles(v_ref, y_ref, comps):
    points, planes = v_ref.shape[1:3]
    carriers = y_ref.shape[1]
    lo, hi = AXIAL_REACH, planes - AXIAL_REACH
    for i, c in enumerate(comps):

        def carry(t):
            y_ref[i, t] = v_ref[c, t]

        def ride(j):
            t = carriers + j
            y_ref[i, 3 * j, lo:hi] = v_ref[c, t, 0:2]
            y_ref[i, 3 * j + 1, lo : lo + 1] = v_ref[c, t, 2:3]
            y_ref[i, 3 * j + 1, lo + 1 : hi] = v_ref[c, t, hi : hi + 1]
            y_ref[i, 3 * j + 2, lo:hi] = v_ref[c, t, hi + 1 :]

        each(carriers, carry)
        each(points - carriers, ride)


def rebuild_tiles(y_ref, tile_ref):
    carriers = y_ref.shape[1]
    comps, riders, planes, radial = tile_ref.shape
    lo, hi = AXIAL_REACH, planes - AXIAL_REACH
    for c in range(comps):
        for j in range(riders):
            tile_ref[c, j, 0:2] = y_ref[c, 3 * j, lo:hi]
            tile_ref[c, j, 2:3] = y_ref[c, 3 * j + 1, lo : lo + 1]
            tile_ref[c, j, lo:hi] = jnp.zeros((hi - lo, radial), jnp.float32)
            tile_ref[c, j, hi : hi + 1] = y_ref[c, 3 * j + 1, lo + 1 : hi]
            tile_ref[c, j, hi + 1 :] = y_ref[c, 3 * j + 2, lo:hi]


def load_kernel(hbm_ref, v_ref, y_ref, sems):
    order = list(range(v_ref.shape[0]))
    loads = [pltpu.make_async_copy(hbm_ref.at[c], v_ref.at[c], sems.at[c]) for c in order]
    for c in reversed(order):
        loads[c].start()
    loads[-1].wait()
    pack_tiles(v_ref, y_ref, order[-1:])
    for c in order[:-1]:
        loads[c].wait()


def load(v):
    comps, points, planes, radial = v.shape
    return pl.pallas_call(
        load_kernel,
        name="load",
        out_shape=(held(*v.shape), held(1, points - points // 4, planes, radial)),
        in_specs=[HBM],
        out_specs=(VMEM, VMEM),
        scratch_shapes=[pltpu.SemaphoreType.DMA((comps,))],
        compiler_params=params(v.size * 4, 2),
    )(v)


def pack_planes_kernel(v_ref, first_ref, y_ref):
    pack_tiles(v_ref, y_ref, range(y_ref.shape[0]))


def pack_planes(v, first):
    comps, points, planes, radial = v.shape
    return pl.pallas_call(
        pack_planes_kernel,
        name="pack_planes",
        out_shape=held(comps - 1, points - points // 4, planes, radial),
        in_specs=[VMEM, ANY],
        out_specs=VMEM,
        compiler_params=params(v.size * 4, 2),
    )(v, first)


def pack_side_kernel(me_ref, v_ref, first_ref, *side_refs, after):
    points = v_ref.shape[1]
    each_part = side_refs[0].shape[1]
    reach = each_part * len(side_refs)

    def put(start):
        for k, side_ref in enumerate(side_refs):
            for c in range(v_ref.shape[0]):
                for h in range(each_part):
                    side_ref[c, h] = v_ref[c, start + k * each_part + h]

    even = me_ref[0] % 2 == 0
    last = even if after else jnp.logical_not(even)
    pl.when(last)(lambda: put(points - reach))
    pl.when(jnp.logical_not(last))(lambda: put(0))


def pack_side(me, v, first, reach, after, parts):
    comps, _, planes, radial = v.shape
    parts = parts if reach % parts == 0 else 1
    return pl.pallas_call(
        functools.partial(pack_side_kernel, after=after),
        name="pack_core" if after else "pack_chip",
        out_shape=(held(comps, reach // parts, planes, radial),) * parts,
        in_specs=[SMEM, VMEM, ANY],
        out_specs=(VMEM,) * parts,
        compiler_params=params(v.size * 4, 3),
    )(me, v, first)


def pack_mirror_kernel(v_ref, first_ref, mirror_ref):
    points, tiles = v_ref.shape[1], mirror_ref.shape[1]
    width = LANES // (points // tiles)
    lane = lax.broadcasted_iota(jnp.int32, mirror_ref.shape[2:], 1)

    def put(p):
        for c in range(v_ref.shape[0]):
            tile = v_ref[c, p, :, :LANES]
            for q in range(1, points // tiles):
                part = pltpu.roll(v_ref[c, q * tiles + p, :, :LANES], q * width, 1)
                tile = jnp.where(lane < q * width, tile, part)
            mirror_ref[c, p] = tile

    each(tiles, put)


def pack_mirror(v, first, width):
    comps, points, planes, _ = v.shape
    return pl.pallas_call(
        pack_mirror_kernel,
        name="pack_mirror",
        out_shape=held(comps, points // (LANES // width), planes, LANES),
        in_specs=[VMEM, ANY],
        out_specs=VMEM,
        compiler_params=params(v.size * 4, 2),
    )(v, first)


def inverse_radius(radial, start=0):
    return 1.0 / ((lax.broadcasted_iota(jnp.int32, (1, radial), 1) + start).astype(jnp.float32) + 0.5)


def axial_weights(planes, inside):
    row = lax.broadcasted_iota(jnp.int32, (planes, LANES), 0)
    weights = []
    for m, w in enumerate(AXIAL_WEIGHTS, 1):
        for shift, own, sign in ((m, row < planes - m, 1.0), (planes - m, row >= m, -1.0)):
            keep = own if inside else jnp.logical_not(own)
            weights.append((shift, jnp.where(keep, sign * w, 0.0)))
    return weights


def axial_part(tile, weights):
    planes, width = tile.shape
    weights = [(shift, jnp.concatenate([weight] * (width // LANES), axis=1)) for shift, weight in weights]
    total = None
    for shift, weight in weights:
        term = weight * pltpu.roll(tile, planes - shift, 0)
        total = term if total is None else total + term
    return total


def mirror_kernel(v_ref, op_ref, mirror_ref, n_in_ref, n_ref, grad_ref):
    comps, points, planes, radial = v_ref.shape
    tiles = mirror_ref.shape[1]
    count = points // tiles
    width = LANES // count
    rows = tiles * planes
    right = split(jnp.concatenate([op_ref[radial:]] * count, axis=0))
    lane = lax.broadcasted_iota(jnp.int32, (rows, LANES), 1)
    for c in range(comps):
        high, low = split(MIRROR_SIGNS[c] * mirror_ref[c].reshape(rows, LANES))
        zero = jnp.zeros_like(high)
        parts = [
            [jnp.where((lane >= q * width) & (lane < (q + 1) * width), x, zero) for q in range(count)]
            for x in (high, low)
        ]
        left = [jnp.concatenate(x, axis=0) for x in parts]
        grad_ref[c * points * planes : (c + 1) * points * planes] = product(left, right)

    def finish(t):
        for c in range(comps):
            start = pl.multiple_of((c * points + t) * planes, planes)
            n_ref[c, t] = n_in_ref[c, t] + v_ref[0, t] * grad_ref[pl.ds(start, planes)]

    each(points, finish)


def mirror_terms(v, op, mirror, n):
    return pl.pallas_call(
        mirror_kernel,
        name="mirror_terms",
        out_shape=held(*v.shape),
        in_specs=[VMEM] * 4,
        out_specs=VMEM,
        scratch_shapes=[pltpu.VMEM((v.size // v.shape[3], v.shape[3]), jnp.float32)],
        input_output_aliases={3: 0},
        compiler_params=params(v.size * 4, 8),
        cost_estimate=pl.CostEstimate(flops=MIRROR, bytes_accessed=16 * v.size, transcendentals=0),
    )(v, op, mirror, n)


def inner_kernel(tap_ref, v_ref, op_ref, n_ref, grad_ref):
    comps, points, planes, radial = v_ref.shape
    reach = (tap_ref.shape[0] - 1) // 2
    rows = points * planes
    right = split(op_ref[:radial])
    for c in range(comps):
        grad_ref[c * rows : (c + 1) * rows] = product(split(v_ref[c].reshape(rows, radial)), right)
    weights = axial_weights(planes, True)

    @pl.loop(0, radial // LANES)
    def column(k):
        lanes = pl.ds(pl.multiple_of(k * LANES, LANES), LANES)
        inv_r = inverse_radius(LANES, k * LANES)
        for c in range(comps):
            for t in range(points):
                a, b, e = [v_ref[i, t, :, lanes] for i in range(3)]
                b_inv = b * inv_r
                around = None
                for m in range(max(-reach, -t), min(reach, points - 1 - t) + 1):
                    term = tap_ref[m + reach] * v_ref[c, t + m, :, lanes]
                    around = term if around is None else around + term
                start = c * rows + t * planes
                n = a * grad_ref[start : start + planes, lanes] + b_inv * around
                n = n + e * axial_part(v_ref[c, t, :, lanes], weights)
                if c == 0:
                    n = n - b_inv * b
                elif c == 1:
                    n = n + a * b_inv
                n_ref[c, t, :, lanes] = n


def inner_terms(taps, v, op):
    return pl.pallas_call(
        inner_kernel,
        name="inner_terms",
        out_shape=held(*v.shape),
        in_specs=[VMEM] * 3,
        out_specs=VMEM,
        scratch_shapes=[pltpu.VMEM((v.size // v.shape[3], v.shape[3]), jnp.float32)],
        compiler_params=params(v.size * 4, 7),
        cost_estimate=pl.CostEstimate(flops=INNER, bytes_accessed=16 * v.size, transcendentals=0),
    )(taps, v, op)


def add_side(tap_ref, v_ref, side_refs, n_in_ref, n_ref, before, columns):
    comps, points, _, radial = v_ref.shape
    each_part = side_refs[0].shape[1]
    reach = each_part * len(side_refs)
    first = 0 if before else reach + 1

    start, count = columns

    @pl.loop(0, count)
    def column(i):
        k = start + i
        lanes = pl.ds(pl.multiple_of(k * LANES, LANES), LANES)
        inv_r = inverse_radius(LANES, k * LANES)
        weights = [tap_ref[first + i] for i in range(reach)]
        for c in range(comps):
            side = [side_refs[h // each_part][c, h % each_part, :, lanes] for h in range(reach)]
            for u in range(reach):
                t = u if before else points - reach + u
                taps = [(h, h - u) for h in range(u, reach)] if before else [(h, reach - 1 + h - u) for h in range(u + 1)]
                around = None
                for h, w in taps:
                    term = weights[w] * side[h]
                    around = term if around is None else around + term
                n_ref[c, t, :, lanes] = n_in_ref[c, t, :, lanes] + v_ref[1, t, :, lanes] * inv_r * around


def core_kernel(me_ref, tap_ref, v_ref, *refs):
    *core_refs, n_in_ref, n_ref = refs
    even = me_ref[0] % 2 == 0
    columns = (0, v_ref.shape[3] // LANES)
    add = functools.partial(add_side, tap_ref, v_ref, core_refs, n_in_ref, n_ref, columns=columns)
    pl.when(even)(lambda: add(before=False))
    pl.when(jnp.logical_not(even))(lambda: add(before=True))


def late_kernel(me_ref, tap_ref, v_ref, *refs, own):
    *chip_refs, n_in_ref, _, n_ref = refs
    core = me_ref[0] % 2
    count = v_ref.shape[3] // (2 * LANES)
    columns = ((core if own else 1 - core) * count, count)
    add = functools.partial(add_side, tap_ref, v_ref, chip_refs, n_in_ref, n_ref, columns=columns)
    pl.when(core == 0)(lambda: add(before=True))
    pl.when(core == 1)(lambda: add(before=False))


def side_terms(kernel, name, me, taps, v, sides, n, ready=()):
    return pl.pallas_call(
        kernel,
        name=name,
        out_shape=held(*v.shape),
        in_specs=[SMEM] + [VMEM] * (3 + len(sides)) + [ANY] * len(ready),
        out_specs=VMEM,
        input_output_aliases={3 + len(sides): 0},
        compiler_params=params(v.size * 4, 5),
        cost_estimate=pl.CostEstimate(flops=SIDE, bytes_accessed=12 * v.size, transcendentals=0),
    )(me, taps, v, *sides, n, *ready)


def share_kernel(v_ref, e_ref, power_ref, ends_ref, tile_ref):
    comps, points, planes, radial = v_ref.shape
    carriers = e_ref.shape[1]
    weights = axial_weights(planes, False)
    rebuild_tiles(e_ref, tile_ref)
    decay = power_ref[1:2]
    ends_ref[...] = jnp.zeros_like(ends_ref)
    for t in range(points):
        e = STEP_WEIGHT * (e_ref[0, t] if t < carriers else tile_ref[0, t - carriers])
        for c in range(comps):
            right_side = e * axial_part(v_ref[c, t], weights)
            ends_ref[0, c] = decay * ends_ref[0, c] - right_side
            ends_ref[1, c] = ends_ref[1, c] - power_ref[t : t + 1] * right_side


def share_terms(v, e, power):
    comps, points, planes, radial = v.shape
    return pl.pallas_call(
        share_kernel,
        name="share_terms",
        out_shape=held(2, comps, planes, radial),
        in_specs=[VMEM] * 3,
        out_specs=VMEM,
        scratch_shapes=[pltpu.VMEM((1, points - e.shape[1], planes, radial), jnp.float32)],
        compiler_params=params(v.size * 4, 4),
        cost_estimate=pl.CostEstimate(flops=20 * v.size, bytes_accessed=8 * v.size, transcendentals=0),
    )(v, e, power)


def ends_kernel(me_ref, v_ref, share_ref, power_ref, n_ref, ends_ref, *, own):
    comps, points, _, radial = v_ref.shape
    lanes = half_lanes(me_ref, radial // 2, own)
    decay = power_ref[1:2, lanes]
    for c in range(comps):
        low = high = None
        for t in range(points):
            right_side = v_ref[c, t, :, lanes] - STEP_WEIGHT * n_ref[c, t, :, lanes]
            low = right_side if t == 0 else decay * low + right_side
            high = right_side if t == 0 else high + power_ref[t : t + 1, lanes] * right_side
        ends_ref[0, c] = low + share_ref[0, c, :, lanes]
        ends_ref[1, c] = high + share_ref[1, c, :, lanes]


def ends_terms(me, v, share, power, n, own):
    comps, _, planes, radial = v.shape
    return pl.pallas_call(
        functools.partial(ends_kernel, own=own),
        name="ends_own" if own else "ends_other",
        out_shape=held(2, comps, planes, radial // 2),
        in_specs=[SMEM] + [VMEM] * 4,
        out_specs=VMEM,
        compiler_params=params(v.size * 4, 4),
        cost_estimate=pl.CostEstimate(flops=20 * v.size, bytes_accessed=8 * v.size, transcendentals=0),
    )(me, v, share, power, n)


def planes_kernel(v_ref, y_ref, e_ref, ready_ref, n_in_ref, n_ref, y_tile_ref, e_tile_ref):
    comps, points, planes, _ = v_ref.shape
    carriers = y_ref.shape[1]
    weights = axial_weights(planes, False)
    rebuild_tiles(y_ref, y_tile_ref)
    rebuild_tiles(e_ref, e_tile_ref)
    for t in range(points):
        for c in range(comps):
            ref, tile_ref, i = (y_ref, y_tile_ref, c) if c < comps - 1 else (e_ref, e_tile_ref, 0)
            tile = ref[i, t] if t < carriers else tile_ref[i, t - carriers]
            n_ref[c, t] = n_in_ref[c, t] + v_ref[2, t] * axial_part(tile, weights)


def planes_terms(v, y, e, ready, n):
    comps, points, planes, radial = v.shape
    riders = points - y.shape[1]
    return pl.pallas_call(
        planes_kernel,
        name="planes_terms",
        out_shape=held(*v.shape),
        in_specs=[VMEM] * 3 + [ANY, VMEM],
        out_specs=VMEM,
        scratch_shapes=[pltpu.VMEM((k, riders, planes, radial), jnp.float32) for k in (comps - 1, 1)],
        input_output_aliases={4: 0},
        compiler_params=params(v.size * 4, 6),
        cost_estimate=pl.CostEstimate(flops=20 * v.size, bytes_accessed=16 * v.size, transcendentals=0),
    )(v, y, e, ready, n)


def table_kernel(me_ref, factor_ref, stencil_ref, row_ref, tap_ref, *, points, sectors):
    radial = row_ref.shape[1]
    one = jnp.ones((1, radial), jnp.float32)
    half = (0.5 * lax.rsqrt(factor_ref[0] * one)) / inverse_radius(radial)
    root = jnp.sqrt(1.0 + half * half)
    loss = 2.0 * half * (root - half)
    rows = [one]
    for _ in range(points):
        rows.append(rows[-1] * (1.0 - loss))
    total = loss
    left, result = points * sectors, None
    while left:
        if left & 1:
            result = total if result is None else result + total - result * total
        total = total * (2.0 - total)
        left >>= 1
    across = rows[points] * rows[points]
    rows += [half / root, 1.0 / result]
    before = after = one
    for bit in range(1, sectors.bit_length() - 1):
        upper = (me_ref[0] >> bit) % 2 == 1
        rows += [across, before, after]
        before, after = jnp.where(upper, before * across, before), jnp.where(upper, after, after * across)
        across = across * across
    for k, row in enumerate(rows + [before, after]):
        row_ref[k : k + 1] = row
    for k in range(tap_ref.shape[0]):
        tap_ref[k] = jnp.full(tap_ref.shape[1:], stencil_ref[k], jnp.float32)


def table(me, viscous_factor, stencil, points, sectors, planes, radial):
    count = points + 5 + 3 * (sectors.bit_length() - 2)
    return pl.pallas_call(
        functools.partial(table_kernel, points=points, sectors=sectors),
        name="table",
        out_shape=(held(count, radial), held(stencil.shape[0], planes, LANES)),
        in_specs=[SMEM, SMEM, SMEM],
        out_specs=(VMEM, VMEM),
        compiler_params=params(1 << 20, 1),
        cost_estimate=pl.CostEstimate(flops=1000 * radial, bytes_accessed=400 * radial, transcendentals=0),
    )(me, viscous_factor, stencil)


def sweep_kernel(v_ref, n_ref, power_ref, s_ref, nonlinear_ref, sem):
    leave = pltpu.make_async_copy(n_ref, nonlinear_ref, sem)
    leave.start()
    comps, points, planes, radial = v_ref.shape
    decay = power_ref[1:2]
    height = power_ref[points + 1 : points + 2]
    for c in range(comps):
        s_ref[c, 0] = height * (v_ref[c, 0] - STEP_WEIGHT * n_ref[c, 0])

        def forward(i):
            t = i + 1
            s_ref[c, t] = decay * s_ref[c, t - 1] + height * (v_ref[c, t] - STEP_WEIGHT * n_ref[c, t])

        each(points - 1, forward)

    def backward(i, carry):
        t = points - 1 - i
        after = []
        for c in range(comps):
            s_ref[c, t] = s_ref[c, t] + carry[c]
            after.append(decay * (carry[c] + height * (v_ref[c, t] - STEP_WEIGHT * n_ref[c, t])))
        return tuple(after)

    start = (jnp.zeros((planes, radial), jnp.float32),) * comps
    lax.fori_loop(0, points, backward, start, unroll=points <= UNROLL)
    leave.wait()


def sweep(v, n, power):
    return pl.pallas_call(
        sweep_kernel,
        name="sweep",
        out_shape=(held(*v.shape), jax.ShapeDtypeStruct(v.shape, v.dtype)),
        in_specs=[VMEM] * 3,
        out_specs=(VMEM, ANY),
        scratch_shapes=[pltpu.SemaphoreType.DMA],
        compiler_params=params(v.size * 4, 4),
        cost_estimate=pl.CostEstimate(flops=10 * v.size, bytes_accessed=12 * v.size, transcendentals=0),
    )(v, n, power)


def half_lanes(me_ref, half, own=True):
    core = me_ref[0] % 2
    return pl.ds(pl.multiple_of((core if own else 1 - core) * half, half), half)


def pair_kernel(me_ref, power_ref, own_ref, other_ref, block_ref, *, points):
    half = own_ref.shape[3]
    hop = power_ref[points : points + 1, half_lanes(me_ref, half)]
    odd = me_ref[0] % 2 == 1
    for c in range(own_ref.shape[1]):
        for side in range(2):
            own, other = own_ref[side, c], other_ref[side, c]
            far, near = (own, other) if side == 0 else (other, own)
            block_ref[side, c] = jnp.where(odd, hop * near + far, hop * far + near)


def pair(me, power, own, other, points):
    return pl.pallas_call(
        functools.partial(pair_kernel, points=points),
        name="pair",
        out_shape=held(*own.shape),
        in_specs=[SMEM, VMEM, VMEM, VMEM],
        out_specs=VMEM,
        compiler_params=params(own.size * 4, 8),
    )(me, power, own, other)


def merge_kernel(me_ref, power_ref, block_ref, other_ref, *refs, points, bit):
    *entry_refs, block_out_ref, entry_out_ref = refs
    comps, half = block_ref.shape[1], block_ref.shape[3]
    lanes = half_lanes(me_ref, half)
    first = points + 3 * bit
    across, before, after = [power_ref[first + k : first + k + 1, lanes] for k in range(3)]
    upper = (me_ref[0] >> bit) % 2 == 1
    before = jnp.where(upper, before, 0.0)
    after = jnp.where(upper, 0.0, after)
    for c in range(comps):
        low, high = block_ref[0, c], block_ref[1, c]
        other_low, other_high = other_ref[0, c], other_ref[1, c]
        block_out_ref[0, c] = jnp.where(upper, across * other_low + low, across * low + other_low)
        block_out_ref[1, c] = jnp.where(upper, other_high + across * high, high + across * other_high)
        for side, enters in enumerate((before * other_low, after * other_high)):
            entry_out_ref[side, c] = entry_refs[0][side, c] + enters if entry_refs else enters


def merge(me, power, block, other, entries, points, bit):
    return pl.pallas_call(
        functools.partial(merge_kernel, points=points, bit=bit),
        name="merge",
        out_shape=(held(*block.shape), held(*block.shape)),
        in_specs=[SMEM] + [VMEM] * (3 + len(entries)),
        out_specs=(VMEM, VMEM),
        compiler_params=params(block.size * 4, 8),
    )(me, power, block, other, *entries)


def enter_kernel(me_ref, power_ref, block_ref, entry_ref, own_ref, other_ref, ready_ref, mine_ref, send_ref, *, points):
    comps, half = block_ref.shape[1], block_ref.shape[3]
    lanes = half_lanes(me_ref, half)
    row = lambda k: power_ref[k : k + 1, lanes]
    hop, height, wrap = row(points), row(points + 1), row(points + 2)
    last = power_ref.shape[0]
    before, after = row(last - 2) * wrap, row(last - 1) * wrap
    odd = me_ref[0] % 2 == 1
    for c in range(comps):
        low = height * (entry_ref[0, c] + before * block_ref[0, c])
        high = height * (entry_ref[1, c] + after * block_ref[1, c])
        even_low = height * jnp.where(odd, other_ref[0, c], own_ref[0, c])
        odd_high = height * jnp.where(odd, own_ref[1, c], other_ref[1, c])
        even_in = (low, odd_high + hop * high)
        odd_in = (even_low + hop * low, high)
        for side in range(2):
            mine_ref[side, c] = jnp.where(odd, odd_in[side], even_in[side])
            send_ref[side, c] = jnp.where(odd, even_in[side], odd_in[side])


def enter(me, power, block, entry, own, other, ready, points):
    return pl.pallas_call(
        functools.partial(enter_kernel, points=points),
        name="enter",
        out_shape=(held(*block.shape), held(*block.shape)),
        in_specs=[SMEM] + [VMEM] * 5 + [ANY],
        out_specs=(VMEM, VMEM),
        compiler_params=params(block.size * 4, 12),
    )(me, power, block, entry, own, other, ready)


def close_kernel(me_ref, s_ref, power_ref, entry_ref, *refs, own):
    out_ref, x_ref, sems = refs[-3:]
    comps, points, _, _ = s_ref.shape
    lanes = half_lanes(me_ref, entry_ref.shape[3], own)
    leaves = []
    for c in range(comps):
        before, after = entry_ref[0, c], entry_ref[1, c]

        def point(t):
            decayed = power_ref[pl.ds(t + 1, 1), lanes] * before + power_ref[pl.ds(points - t, 1), lanes] * after
            x_ref[c, t] = s_ref[c, t, :, lanes] + decayed

        each(points, point)
        leaves.append(pltpu.make_async_copy(x_ref.at[c], out_ref.at[c, :, :, lanes], sems.at[c]))
        leaves[c].start()
    for leave in leaves:
        leave.wait()


def close(me, s, power, entry, out, own):
    comps, points, planes, radial = s.shape
    return pl.pallas_call(
        functools.partial(close_kernel, own=own),
        name="close_own" if own else "close_other",
        out_shape=jax.ShapeDtypeStruct(s.shape, s.dtype),
        in_specs=[SMEM] + [VMEM] * 3 + [ANY] * len(out),
        out_specs=ANY,
        scratch_shapes=[
            pltpu.VMEM((comps, points, planes, radial // 2), jnp.float32),
            pltpu.SemaphoreType.DMA((comps,)),
        ],
        input_output_aliases={4: 0} if out else {},
        compiler_params=params(s.size * 4, 5),
        cost_estimate=pl.CostEstimate(flops=4 * s.size, bytes_accessed=8 * s.size, transcendentals=0),
    )(me, s, power, entry, *out)


def local(velocity, radial_op, azimuth_stencil, viscous_factor):
    sectors = lax.axis_size("theta")
    comps, points, planes, radial = velocity.shape
    reach = (azimuth_stencil.shape[0] - 1) // 2
    width = radial_op.shape[1] - radial
    me = lax.axis_index("theta").astype(jnp.int32).reshape(1)
    op = radial_op.T

    velocity, axial_out = load(pltpu.with_memory_space_constraint(velocity, pltpu.HBM))
    axial_in = swap(axial_out, "gz", 1)
    chip_out = pack_side(me, velocity, axial_out, reach, False, CHIP_PARTS)
    chip_in = [swap_across(part, "theta") for part in chip_out]
    mirror_out = pack_mirror(velocity, chip_out[0], width)
    mirror_in = swap(mirror_out, "theta", sectors // 2)
    core_out = pack_side(me, velocity, mirror_out, reach, True, 1)
    core_in = [swap(part, "theta", 1) for part in core_out]
    power, taps = table(me, viscous_factor, azimuth_stencil, points, sectors, planes, radial)
    n = inner_terms(taps, velocity, op)
    share_out = share_terms(velocity, axial_in, power)
    share_in = swap(share_out, "gz", 1)
    planes_in = swap(pack_planes(velocity, share_out), "gz", 1)
    n = side_terms(core_kernel, "core_terms", me, taps, velocity, core_in, n)
    n = mirror_terms(velocity, op, mirror_in, n)
    late = functools.partial(late_kernel, own=False)
    n = side_terms(late, "late_other", me, taps, velocity, chip_in, n, (share_in,))
    send = ends_terms(me, velocity, share_in, power, n, False)
    other = swap(send, "theta", 1)
    late = functools.partial(late_kernel, own=True)
    n = side_terms(late, "late_own", me, taps, velocity, chip_in, n, (send,))
    own = ends_terms(me, velocity, share_in, power, n, True)
    block = pair(me, power, own, other, points)
    entries = ()
    last = sectors.bit_length() - 2
    for bit in range(1, last + 1):
        if bit == last:
            n = planes_terms(velocity, planes_in, axial_in, block, n)
            s, nonlinear = sweep(velocity, n, power)
        block, entry = merge(me, power, block, swap(block, "theta", 1 << bit), entries, points, bit)
        entries = (entry,)
    mine, send = enter(me, power, block, entry, own, other, s, points)
    got = swap(send, "theta", 1)
    new_velocity = close(me, s, power, mine, (), True)
    new_velocity = close(me, s, power, got, (new_velocity,), False)
    return (new_velocity, nonlinear)


def solution(mesh):
    in_specs = (P(None, "theta", "gz", None), P(), P(), P())
    out_specs = (P(None, "theta", "gz", None), P(None, "theta", "gz", None))
    return jax.shard_map(local, mesh=mesh, in_specs=in_specs, out_specs=out_specs, check_vma=False)
```

```python
import functools

import jax
import jax.numpy as jnp
from jax import lax
from jax.experimental import pallas as pl
from jax.experimental.pallas import tpu as pltpu
from jax.sharding import PartitionSpec as P

AXIAL_WEIGHTS = (0.75, -0.15, 1.0 / 60.0)
AXIAL_REACH = len(AXIAL_WEIGHTS)
STEP_WEIGHT = 0.2
MIRROR_SIGNS = (-1.0, -1.0, 1.0)
LANES = 128
UNROLL = 16
INNER = 10 << 29
MIRROR = 1 << 26
SIDE = 1 << 26

VMEM = pl.BlockSpec(memory_space=pltpu.VMEM)
SMEM = pl.BlockSpec(memory_space=pltpu.SMEM)
ANY = pl.BlockSpec(memory_space=pl.ANY)
HBM = pl.BlockSpec(memory_space=pltpu.HBM)


def params(block_bytes, blocks):
    return pltpu.CompilerParams(vmem_limit_bytes=(2 << 20) + blocks * block_bytes)


def held(*shape):
    return pltpu.VMEM(shape, jnp.float32)


def each(count, body):
    if count <= UNROLL:
        for i in range(count):
            body(i)
    else:
        pl.loop(0, count)(body)


def swap(block, axis, bit):
    size = lax.axis_size(axis)
    return lax.ppermute(block, axis, [(i, i ^ bit) for i in range(size)])


def swap_across(block, axis):
    size = lax.axis_size(axis)
    route = []
    for odd in range(1, size, 2):
        route += [(odd, (odd + 1) % size), ((odd + 1) % size, odd)]
    return lax.ppermute(block, axis, route)


def split(x):
    high = x.astype(jnp.bfloat16)
    return high, (x - high.astype(jnp.float32)).astype(jnp.bfloat16)


def product(left, right):
    dot = functools.partial(jnp.dot, preferred_element_type=jnp.float32)
    return dot(left[0], right[0]) + (dot(left[0], right[1]) + dot(left[1], right[0]))


def pack_tiles(v_ref, y_ref, comps):
    points, planes = v_ref.shape[1:3]
    carriers = y_ref.shape[1]
    lo, hi = AXIAL_REACH, planes - AXIAL_REACH
    for i, c in enumerate(comps):

        def carry(t):
            y_ref[i, t] = v_ref[c, t]

        def ride(j):
            t = carriers + j
            y_ref[i, 3 * j, lo:hi] = v_ref[c, t, 0:2]
            y_ref[i, 3 * j + 1, lo : lo + 1] = v_ref[c, t, 2:3]
            y_ref[i, 3 * j + 1, lo + 1 : hi] = v_ref[c, t, hi : hi + 1]
            y_ref[i, 3 * j + 2, lo:hi] = v_ref[c, t, hi + 1 :]

        each(carriers, carry)
        each(points - carriers, ride)


def rebuild_tiles(y_ref, tile_ref):
    carriers = y_ref.shape[1]
    comps, riders, planes, radial = tile_ref.shape
    lo, hi = AXIAL_REACH, planes - AXIAL_REACH
    for c in range(comps):
        for j in range(riders):
            tile_ref[c, j, 0:2] = y_ref[c, 3 * j, lo:hi]
            tile_ref[c, j, 2:3] = y_ref[c, 3 * j + 1, lo : lo + 1]
            tile_ref[c, j, lo:hi] = jnp.zeros((hi - lo, radial), jnp.float32)
            tile_ref[c, j, hi : hi + 1] = y_ref[c, 3 * j + 1, lo + 1 : hi]
            tile_ref[c, j, hi + 1 :] = y_ref[c, 3 * j + 2, lo:hi]


def load_axial_kernel(hbm_ref, y_ref, e_ref, sem):
    load = pltpu.make_async_copy(hbm_ref.at[pl.ds(hbm_ref.shape[0] - 1, 1)], e_ref, sem)
    load.start()
    load.wait()
    pack_tiles(e_ref, y_ref, (0,))


def load_axial(v):
    comps, points, planes, radial = v.shape
    return pl.pallas_call(
        load_axial_kernel,
        name="load_axial",
        out_shape=held(1, points - points // 4, planes, radial),
        in_specs=[HBM],
        out_specs=VMEM,
        scratch_shapes=[pltpu.VMEM((1, points, planes, radial), jnp.float32), pltpu.SemaphoreType.DMA],
        compiler_params=params(v.size * 4, 2),
    )(v)


def pack_planes_kernel(v_ref, first_ref, y_ref):
    pack_tiles(v_ref, y_ref, range(y_ref.shape[0]))


def pack_planes(v, first):
    comps, points, planes, radial = v.shape
    return pl.pallas_call(
        pack_planes_kernel,
        name="pack_planes",
        out_shape=held(comps - 1, points - points // 4, planes, radial),
        in_specs=[VMEM, ANY],
        out_specs=VMEM,
        compiler_params=params(v.size * 4, 2),
    )(v, first)


def pack_side_kernel(me_ref, v_ref, first_ref, side_ref, *, after):
    points, reach = v_ref.shape[1], side_ref.shape[1]

    def put(start):
        for c in range(v_ref.shape[0]):
            for h in range(reach):
                side_ref[c, h] = v_ref[c, start + h]

    even = me_ref[0] % 2 == 0
    last = even if after else jnp.logical_not(even)
    pl.when(last)(lambda: put(points - reach))
    pl.when(jnp.logical_not(last))(lambda: put(0))


def pack_side(me, v, first, reach, after):
    comps, _, planes, radial = v.shape
    return pl.pallas_call(
        functools.partial(pack_side_kernel, after=after),
        name="pack_core" if after else "pack_chip",
        out_shape=held(comps, reach, planes, radial),
        in_specs=[SMEM, VMEM, ANY],
        out_specs=VMEM,
        compiler_params=params(v.size * 4, 3),
    )(me, v, first)


def pack_mirror_kernel(v_ref, first_ref, mirror_ref):
    points, tiles = v_ref.shape[1], mirror_ref.shape[1]
    width = LANES // (points // tiles)
    lane = lax.broadcasted_iota(jnp.int32, mirror_ref.shape[2:], 1)

    def put(p):
        for c in range(v_ref.shape[0]):
            tile = v_ref[c, p, :, :LANES]
            for q in range(1, points // tiles):
                part = pltpu.roll(v_ref[c, q * tiles + p, :, :LANES], q * width, 1)
                tile = jnp.where(lane < q * width, tile, part)
            mirror_ref[c, p] = tile

    each(tiles, put)


def pack_mirror(v, first, width):
    comps, points, planes, _ = v.shape
    return pl.pallas_call(
        pack_mirror_kernel,
        name="pack_mirror",
        out_shape=held(comps, points // (LANES // width), planes, LANES),
        in_specs=[VMEM, ANY],
        out_specs=VMEM,
        compiler_params=params(v.size * 4, 2),
    )(v, first)


def inverse_radius(radial, start=0):
    return 1.0 / ((lax.broadcasted_iota(jnp.int32, (1, radial), 1) + start).astype(jnp.float32) + 0.5)


def axial_weights(planes, inside):
    row = lax.broadcasted_iota(jnp.int32, (planes, LANES), 0)
    weights = []
    for m, w in enumerate(AXIAL_WEIGHTS, 1):
        for shift, own, sign in ((m, row < planes - m, 1.0), (planes - m, row >= m, -1.0)):
            keep = own if inside else jnp.logical_not(own)
            weights.append((shift, jnp.where(keep, sign * w, 0.0)))
    return weights


def axial_part(tile, weights):
    planes, width = tile.shape
    weights = [(shift, jnp.concatenate([weight] * (width // LANES), axis=1)) for shift, weight in weights]
    total = None
    for shift, weight in weights:
        term = weight * pltpu.roll(tile, planes - shift, 0)
        total = term if total is None else total + term
    return total


def mirror_kernel(v_ref, op_ref, mirror_ref, n_in_ref, n_ref, grad_ref):
    comps, points, planes, radial = v_ref.shape
    tiles = mirror_ref.shape[1]
    count = points // tiles
    width = LANES // count
    rows = tiles * planes
    right = split(jnp.concatenate([op_ref[radial:]] * count, axis=0))
    lane = lax.broadcasted_iota(jnp.int32, (rows, LANES), 1)
    for c in range(comps):
        high, low = split(MIRROR_SIGNS[c] * mirror_ref[c].reshape(rows, LANES))
        zero = jnp.zeros_like(high)
        parts = [
            [jnp.where((lane >= q * width) & (lane < (q + 1) * width), x, zero) for q in range(count)]
            for x in (high, low)
        ]
        left = [jnp.concatenate(x, axis=0) for x in parts]
        grad_ref[c * points * planes : (c + 1) * points * planes] = product(left, right)

    def finish(t):
        for c in range(comps):
            start = pl.multiple_of((c * points + t) * planes, planes)
            n_ref[c, t] = n_in_ref[c, t] + v_ref[0, t] * grad_ref[pl.ds(start, planes)]

    each(points, finish)


def mirror_terms(v, op, mirror, n):
    return pl.pallas_call(
        mirror_kernel,
        name="mirror_terms",
        out_shape=held(*v.shape),
        in_specs=[VMEM] * 4,
        out_specs=VMEM,
        scratch_shapes=[pltpu.VMEM((v.size // v.shape[3], v.shape[3]), jnp.float32)],
        input_output_aliases={3: 0},
        compiler_params=params(v.size * 4, 8),
        cost_estimate=pl.CostEstimate(flops=MIRROR, bytes_accessed=16 * v.size, transcendentals=0),
    )(v, op, mirror, n)


def inner_kernel(tap_ref, v_ref, op_ref, n_ref, grad_ref):
    comps, points, planes, radial = v_ref.shape
    reach = (tap_ref.shape[0] - 1) // 2
    rows = points * planes
    right = split(op_ref[:radial])
    for c in range(comps):
        grad_ref[c * rows : (c + 1) * rows] = product(split(v_ref[c].reshape(rows, radial)), right)
    weights = axial_weights(planes, True)

    @pl.loop(0, radial // LANES)
    def column(k):
        lanes = pl.ds(pl.multiple_of(k * LANES, LANES), LANES)
        inv_r = inverse_radius(LANES, k * LANES)
        for c in range(comps):
            for t in range(points):
                a, b, e = [v_ref[i, t, :, lanes] for i in range(3)]
                b_inv = b * inv_r
                around = None
                for m in range(max(-reach, -t), min(reach, points - 1 - t) + 1):
                    term = tap_ref[m + reach] * v_ref[c, t + m, :, lanes]
                    around = term if around is None else around + term
                start = c * rows + t * planes
                n = a * grad_ref[start : start + planes, lanes] + b_inv * around
                n = n + e * axial_part(v_ref[c, t, :, lanes], weights)
                if c == 0:
                    n = n - b_inv * b
                elif c == 1:
                    n = n + a * b_inv
                n_ref[c, t, :, lanes] = n


def inner_terms(taps, v, op):
    return pl.pallas_call(
        inner_kernel,
        name="inner_terms",
        out_shape=held(*v.shape),
        in_specs=[VMEM] * 3,
        out_specs=VMEM,
        scratch_shapes=[pltpu.VMEM((v.size // v.shape[3], v.shape[3]), jnp.float32)],
        compiler_params=params(v.size * 4, 7),
        cost_estimate=pl.CostEstimate(flops=INNER, bytes_accessed=16 * v.size, transcendentals=0),
    )(taps, v, op)


def add_side(tap_ref, v_ref, side_ref, n_in_ref, n_ref, before, columns):
    comps, points, _, radial = v_ref.shape
    reach = side_ref.shape[1]
    first = 0 if before else reach + 1

    start, count = columns

    @pl.loop(0, count)
    def column(i):
        k = start + i
        lanes = pl.ds(pl.multiple_of(k * LANES, LANES), LANES)
        inv_r = inverse_radius(LANES, k * LANES)
        weights = [tap_ref[first + i] for i in range(reach)]
        for c in range(comps):
            side = [side_ref[c, h, :, lanes] for h in range(reach)]
            for u in range(reach):
                t = u if before else points - reach + u
                taps = [(h, h - u) for h in range(u, reach)] if before else [(h, reach - 1 + h - u) for h in range(u + 1)]
                around = None
                for h, w in taps:
                    term = weights[w] * side[h]
                    around = term if around is None else around + term
                n_ref[c, t, :, lanes] = n_in_ref[c, t, :, lanes] + v_ref[1, t, :, lanes] * inv_r * around


def core_kernel(me_ref, tap_ref, v_ref, core_ref, n_in_ref, n_ref):
    even = me_ref[0] % 2 == 0
    columns = (0, v_ref.shape[3] // LANES)
    add = functools.partial(add_side, tap_ref, v_ref, core_ref, n_in_ref, n_ref, columns=columns)
    pl.when(even)(lambda: add(before=False))
    pl.when(jnp.logical_not(even))(lambda: add(before=True))


def late_kernel(me_ref, tap_ref, v_ref, chip_ref, n_in_ref, ready_ref, n_ref, *, own):
    core = me_ref[0] % 2
    count = v_ref.shape[3] // (2 * LANES)
    columns = ((core if own else 1 - core) * count, count)
    add = functools.partial(add_side, tap_ref, v_ref, chip_ref, n_in_ref, n_ref, columns=columns)
    pl.when(core == 0)(lambda: add(before=True))
    pl.when(core == 1)(lambda: add(before=False))


def side_terms(kernel, name, me, taps, v, side, n, ready=()):
    return pl.pallas_call(
        kernel,
        name=name,
        out_shape=held(*v.shape),
        in_specs=[SMEM] + [VMEM] * 4 + [ANY] * len(ready),
        out_specs=VMEM,
        input_output_aliases={4: 0},
        compiler_params=params(v.size * 4, 5),
        cost_estimate=pl.CostEstimate(flops=SIDE, bytes_accessed=12 * v.size, transcendentals=0),
    )(me, taps, v, side, n, *ready)


def share_kernel(v_ref, e_ref, power_ref, ends_ref, tile_ref):
    comps, points, planes, radial = v_ref.shape
    carriers = e_ref.shape[1]
    weights = axial_weights(planes, False)
    rebuild_tiles(e_ref, tile_ref)
    decay = power_ref[1:2]
    ends_ref[...] = jnp.zeros_like(ends_ref)
    for t in range(points):
        e = STEP_WEIGHT * (e_ref[0, t] if t < carriers else tile_ref[0, t - carriers])
        for c in range(comps):
            right_side = e * axial_part(v_ref[c, t], weights)
            ends_ref[0, c] = decay * ends_ref[0, c] - right_side
            ends_ref[1, c] = ends_ref[1, c] - power_ref[t : t + 1] * right_side


def share_terms(v, e, power):
    comps, points, planes, radial = v.shape
    return pl.pallas_call(
        share_kernel,
        name="share_terms",
        out_shape=held(2, comps, planes, radial),
        in_specs=[VMEM] * 3,
        out_specs=VMEM,
        scratch_shapes=[pltpu.VMEM((1, points - e.shape[1], planes, radial), jnp.float32)],
        compiler_params=params(v.size * 4, 4),
        cost_estimate=pl.CostEstimate(flops=20 * v.size, bytes_accessed=8 * v.size, transcendentals=0),
    )(v, e, power)


def ends_kernel(me_ref, v_ref, share_ref, power_ref, n_ref, ends_ref, *, own):
    comps, points, _, radial = v_ref.shape
    lanes = half_lanes(me_ref, radial // 2, own)
    decay = power_ref[1:2, lanes]
    for c in range(comps):
        low = high = None
        for t in range(points):
            right_side = v_ref[c, t, :, lanes] - STEP_WEIGHT * n_ref[c, t, :, lanes]
            low = right_side if t == 0 else decay * low + right_side
            high = right_side if t == 0 else high + power_ref[t : t + 1, lanes] * right_side
        ends_ref[0, c] = low + share_ref[0, c, :, lanes]
        ends_ref[1, c] = high + share_ref[1, c, :, lanes]


def ends_terms(me, v, share, power, n, own):
    comps, _, planes, radial = v.shape
    return pl.pallas_call(
        functools.partial(ends_kernel, own=own),
        name="ends_own" if own else "ends_other",
        out_shape=held(2, comps, planes, radial // 2),
        in_specs=[SMEM] + [VMEM] * 4,
        out_specs=VMEM,
        compiler_params=params(v.size * 4, 4),
        cost_estimate=pl.CostEstimate(flops=20 * v.size, bytes_accessed=8 * v.size, transcendentals=0),
    )(me, v, share, power, n)


def planes_kernel(v_ref, y_ref, e_ref, ready_ref, n_in_ref, n_ref, y_tile_ref, e_tile_ref):
    comps, points, planes, _ = v_ref.shape
    carriers = y_ref.shape[1]
    weights = axial_weights(planes, False)
    rebuild_tiles(y_ref, y_tile_ref)
    rebuild_tiles(e_ref, e_tile_ref)
    for t in range(points):
        for c in range(comps):
            ref, tile_ref, i = (y_ref, y_tile_ref, c) if c < comps - 1 else (e_ref, e_tile_ref, 0)
            tile = ref[i, t] if t < carriers else tile_ref[i, t - carriers]
            n_ref[c, t] = n_in_ref[c, t] + v_ref[2, t] * axial_part(tile, weights)


def planes_terms(v, y, e, ready, n):
    comps, points, planes, radial = v.shape
    riders = points - y.shape[1]
    return pl.pallas_call(
        planes_kernel,
        name="planes_terms",
        out_shape=held(*v.shape),
        in_specs=[VMEM] * 3 + [ANY, VMEM],
        out_specs=VMEM,
        scratch_shapes=[pltpu.VMEM((k, riders, planes, radial), jnp.float32) for k in (comps - 1, 1)],
        input_output_aliases={4: 0},
        compiler_params=params(v.size * 4, 6),
        cost_estimate=pl.CostEstimate(flops=20 * v.size, bytes_accessed=16 * v.size, transcendentals=0),
    )(v, y, e, ready, n)


def table_kernel(me_ref, factor_ref, stencil_ref, row_ref, tap_ref, *, points, sectors):
    radial = row_ref.shape[1]
    one = jnp.ones((1, radial), jnp.float32)
    half = (0.5 * lax.rsqrt(factor_ref[0] * one)) / inverse_radius(radial)
    root = jnp.sqrt(1.0 + half * half)
    loss = 2.0 * half * (root - half)
    rows = [one]
    for _ in range(points):
        rows.append(rows[-1] * (1.0 - loss))
    total = loss
    left, result = points * sectors, None
    while left:
        if left & 1:
            result = total if result is None else result + total - result * total
        total = total * (2.0 - total)
        left >>= 1
    across = rows[points] * rows[points]
    rows += [half / root, 1.0 / result]
    before = after = one
    for bit in range(1, sectors.bit_length() - 1):
        upper = (me_ref[0] >> bit) % 2 == 1
        rows += [across, before, after]
        before, after = jnp.where(upper, before * across, before), jnp.where(upper, after, after * across)
        across = across * across
    for k, row in enumerate(rows + [before, after]):
        row_ref[k : k + 1] = row
    for k in range(tap_ref.shape[0]):
        tap_ref[k] = jnp.full(tap_ref.shape[1:], stencil_ref[k], jnp.float32)


def table(me, viscous_factor, stencil, points, sectors, planes, radial):
    count = points + 5 + 3 * (sectors.bit_length() - 2)
    return pl.pallas_call(
        functools.partial(table_kernel, points=points, sectors=sectors),
        name="table",
        out_shape=(held(count, radial), held(stencil.shape[0], planes, LANES)),
        in_specs=[SMEM, SMEM, SMEM],
        out_specs=(VMEM, VMEM),
        compiler_params=params(1 << 20, 1),
        cost_estimate=pl.CostEstimate(flops=1000 * radial, bytes_accessed=400 * radial, transcendentals=0),
    )(me, viscous_factor, stencil)


def sweep_kernel(v_ref, n_ref, power_ref, s_ref, nonlinear_ref, sem):
    leave = pltpu.make_async_copy(n_ref, nonlinear_ref, sem)
    leave.start()
    comps, points, planes, radial = v_ref.shape
    decay = power_ref[1:2]
    height = power_ref[points + 1 : points + 2]
    for c in range(comps):
        s_ref[c, 0] = height * (v_ref[c, 0] - STEP_WEIGHT * n_ref[c, 0])

        def forward(i):
            t = i + 1
            s_ref[c, t] = decay * s_ref[c, t - 1] + height * (v_ref[c, t] - STEP_WEIGHT * n_ref[c, t])

        each(points - 1, forward)

    def backward(i, carry):
        t = points - 1 - i
        after = []
        for c in range(comps):
            s_ref[c, t] = s_ref[c, t] + carry[c]
            after.append(decay * (carry[c] + height * (v_ref[c, t] - STEP_WEIGHT * n_ref[c, t])))
        return tuple(after)

    start = (jnp.zeros((planes, radial), jnp.float32),) * comps
    lax.fori_loop(0, points, backward, start, unroll=points <= UNROLL)
    leave.wait()


def sweep(v, n, power):
    return pl.pallas_call(
        sweep_kernel,
        name="sweep",
        out_shape=(held(*v.shape), jax.ShapeDtypeStruct(v.shape, v.dtype)),
        in_specs=[VMEM] * 3,
        out_specs=(VMEM, ANY),
        scratch_shapes=[pltpu.SemaphoreType.DMA],
        compiler_params=params(v.size * 4, 4),
        cost_estimate=pl.CostEstimate(flops=10 * v.size, bytes_accessed=12 * v.size, transcendentals=0),
    )(v, n, power)


def half_lanes(me_ref, half, own=True):
    core = me_ref[0] % 2
    return pl.ds(pl.multiple_of((core if own else 1 - core) * half, half), half)


def pair_kernel(me_ref, power_ref, own_ref, other_ref, block_ref, *, points):
    half = own_ref.shape[3]
    hop = power_ref[points : points + 1, half_lanes(me_ref, half)]
    odd = me_ref[0] % 2 == 1
    for c in range(own_ref.shape[1]):
        for side in range(2):
            own, other = own_ref[side, c], other_ref[side, c]
            far, near = (own, other) if side == 0 else (other, own)
            block_ref[side, c] = jnp.where(odd, hop * near + far, hop * far + near)


def pair(me, power, own, other, points):
    return pl.pallas_call(
        functools.partial(pair_kernel, points=points),
        name="pair",
        out_shape=held(*own.shape),
        in_specs=[SMEM, VMEM, VMEM, VMEM],
        out_specs=VMEM,
        compiler_params=params(own.size * 4, 8),
    )(me, power, own, other)


def merge_kernel(me_ref, power_ref, block_ref, other_ref, *refs, points, bit):
    *entry_refs, block_out_ref, entry_out_ref = refs
    comps, half = block_ref.shape[1], block_ref.shape[3]
    lanes = half_lanes(me_ref, half)
    first = points + 3 * bit
    across, before, after = [power_ref[first + k : first + k + 1, lanes] for k in range(3)]
    upper = (me_ref[0] >> bit) % 2 == 1
    before = jnp.where(upper, before, 0.0)
    after = jnp.where(upper, 0.0, after)
    for c in range(comps):
        low, high = block_ref[0, c], block_ref[1, c]
        other_low, other_high = other_ref[0, c], other_ref[1, c]
        block_out_ref[0, c] = jnp.where(upper, across * other_low + low, across * low + other_low)
        block_out_ref[1, c] = jnp.where(upper, other_high + across * high, high + across * other_high)
        for side, enters in enumerate((before * other_low, after * other_high)):
            entry_out_ref[side, c] = entry_refs[0][side, c] + enters if entry_refs else enters


def merge(me, power, block, other, entries, points, bit):
    return pl.pallas_call(
        functools.partial(merge_kernel, points=points, bit=bit),
        name="merge",
        out_shape=(held(*block.shape), held(*block.shape)),
        in_specs=[SMEM] + [VMEM] * (3 + len(entries)),
        out_specs=(VMEM, VMEM),
        compiler_params=params(block.size * 4, 8),
    )(me, power, block, other, *entries)


def enter_kernel(me_ref, power_ref, block_ref, entry_ref, own_ref, other_ref, ready_ref, mine_ref, send_ref, *, points):
    comps, half = block_ref.shape[1], block_ref.shape[3]
    lanes = half_lanes(me_ref, half)
    row = lambda k: power_ref[k : k + 1, lanes]
    hop, height, wrap = row(points), row(points + 1), row(points + 2)
    last = power_ref.shape[0]
    before, after = row(last - 2) * wrap, row(last - 1) * wrap
    odd = me_ref[0] % 2 == 1
    for c in range(comps):
        low = height * (entry_ref[0, c] + before * block_ref[0, c])
        high = height * (entry_ref[1, c] + after * block_ref[1, c])
        even_low = height * jnp.where(odd, other_ref[0, c], own_ref[0, c])
        odd_high = height * jnp.where(odd, own_ref[1, c], other_ref[1, c])
        even_in = (low, odd_high + hop * high)
        odd_in = (even_low + hop * low, high)
        for side in range(2):
            mine_ref[side, c] = jnp.where(odd, odd_in[side], even_in[side])
            send_ref[side, c] = jnp.where(odd, even_in[side], odd_in[side])


def enter(me, power, block, entry, own, other, ready, points):
    return pl.pallas_call(
        functools.partial(enter_kernel, points=points),
        name="enter",
        out_shape=(held(*block.shape), held(*block.shape)),
        in_specs=[SMEM] + [VMEM] * 5 + [ANY],
        out_specs=(VMEM, VMEM),
        compiler_params=params(block.size * 4, 12),
    )(me, power, block, entry, own, other, ready)


def close_kernel(me_ref, s_ref, power_ref, entry_ref, *refs, own):
    out_ref, x_ref, sems = refs[-3:]
    comps, points, _, _ = s_ref.shape
    lanes = half_lanes(me_ref, entry_ref.shape[3], own)
    leaves = []
    for c in range(comps):
        before, after = entry_ref[0, c], entry_ref[1, c]

        def point(t):
            decayed = power_ref[pl.ds(t + 1, 1), lanes] * before + power_ref[pl.ds(points - t, 1), lanes] * after
            x_ref[c, t] = s_ref[c, t, :, lanes] + decayed

        each(points, point)
        leaves.append(pltpu.make_async_copy(x_ref.at[c], out_ref.at[c, :, :, lanes], sems.at[c]))
        leaves[c].start()
    for leave in leaves:
        leave.wait()


def close(me, s, power, entry, out, own):
    comps, points, planes, radial = s.shape
    return pl.pallas_call(
        functools.partial(close_kernel, own=own),
        name="close_own" if own else "close_other",
        out_shape=jax.ShapeDtypeStruct(s.shape, s.dtype),
        in_specs=[SMEM] + [VMEM] * 3 + [ANY] * len(out),
        out_specs=ANY,
        scratch_shapes=[
            pltpu.VMEM((comps, points, planes, radial // 2), jnp.float32),
            pltpu.SemaphoreType.DMA((comps,)),
        ],
        input_output_aliases={4: 0} if out else {},
        compiler_params=params(s.size * 4, 5),
        cost_estimate=pl.CostEstimate(flops=4 * s.size, bytes_accessed=8 * s.size, transcendentals=0),
    )(me, s, power, entry, *out)


def local(velocity, radial_op, azimuth_stencil, viscous_factor):
    sectors = lax.axis_size("theta")
    comps, points, planes, radial = velocity.shape
    reach = (azimuth_stencil.shape[0] - 1) // 2
    width = radial_op.shape[1] - radial
    me = lax.axis_index("theta").astype(jnp.int32).reshape(1)
    op = radial_op.T

    axial_out = load_axial(pltpu.with_memory_space_constraint(velocity, pltpu.HBM))
    axial_in = swap(axial_out, "gz", 1)
    chip_out = pack_side(me, velocity, axial_out, reach, False)
    chip_in = swap_across(chip_out, "theta")
    mirror_out = pack_mirror(velocity, chip_out, width)
    mirror_in = swap(mirror_out, "theta", sectors // 2)
    core_out = pack_side(me, velocity, axial_in, reach, True)
    core_in = swap(core_out, "theta", 1)
    power, taps = table(me, viscous_factor, azimuth_stencil, points, sectors, planes, radial)
    n = inner_terms(taps, velocity, op)
    share_out = share_terms(velocity, axial_in, power)
    share_in = swap(share_out, "gz", 1)
    planes_in = swap(pack_planes(velocity, share_out), "gz", 1)
    n = side_terms(core_kernel, "core_terms", me, taps, velocity, core_in, n)
    n = mirror_terms(velocity, op, mirror_in, n)
    late = functools.partial(late_kernel, own=False)
    n = side_terms(late, "late_other", me, taps, velocity, chip_in, n, (share_in,))
    send = ends_terms(me, velocity, share_in, power, n, False)
    other = swap(send, "theta", 1)
    late = functools.partial(late_kernel, own=True)
    n = side_terms(late, "late_own", me, taps, velocity, chip_in, n, (send,))
    own = ends_terms(me, velocity, share_in, power, n, True)
    block = pair(me, power, own, other, points)
    entries = ()
    last = sectors.bit_length() - 2
    for bit in range(1, last + 1):
        if bit == last:
            n = planes_terms(velocity, planes_in, axial_in, block, n)
            s, nonlinear = sweep(velocity, n, power)
        block, entry = merge(me, power, block, swap(block, "theta", 1 << bit), entries, points, bit)
        entries = (entry,)
    mine, send = enter(me, power, block, entry, own, other, s, points)
    got = swap(send, "theta", 1)
    new_velocity = close(me, s, power, mine, (), True)
    new_velocity = close(me, s, power, got, (new_velocity,), False)
    return (new_velocity, nonlinear)


def solution(mesh):
    in_specs = (P(None, "theta", "gz", None), P(), P(), P())
    out_specs = (P(None, "theta", "gz", None), P(None, "theta", "gz", None))
    return jax.shard_map(local, mesh=mesh, in_specs=in_specs, out_specs=out_specs, check_vma=False)
```

```python
import functools

import jax
import jax.numpy as jnp
from jax import lax
from jax.experimental import pallas as pl
from jax.experimental.pallas import tpu as pltpu
from jax.sharding import PartitionSpec as P

AXIAL_WEIGHTS = (0.75, -0.15, 1.0 / 60.0)
AXIAL_REACH = len(AXIAL_WEIGHTS)
STEP_WEIGHT = 0.2
MIRROR_SIGNS = (-1.0, -1.0, 1.0)
LANES = 128
UNROLL = 16
INNER = 10 << 29
MIRROR = 1 << 26
SIDE = 1 << 26

VMEM = pl.BlockSpec(memory_space=pltpu.VMEM)
SMEM = pl.BlockSpec(memory_space=pltpu.SMEM)
ANY = pl.BlockSpec(memory_space=pl.ANY)
HBM = pl.BlockSpec(memory_space=pltpu.HBM)


def params(block_bytes, blocks):
    return pltpu.CompilerParams(vmem_limit_bytes=(2 << 20) + blocks * block_bytes)


def held(*shape):
    return pltpu.VMEM(shape, jnp.float32)


def each(count, body):
    if count <= UNROLL:
        for i in range(count):
            body(i)
    else:
        pl.loop(0, count)(body)


def swap(block, axis, bit):
    size = lax.axis_size(axis)
    return lax.ppermute(block, axis, [(i, i ^ bit) for i in range(size)])


def swap_across(block, axis):
    size = lax.axis_size(axis)
    route = []
    for odd in range(1, size, 2):
        route += [(odd, (odd + 1) % size), ((odd + 1) % size, odd)]
    return lax.ppermute(block, axis, route)


def split(x):
    high = x.astype(jnp.bfloat16)
    return high, (x - high.astype(jnp.float32)).astype(jnp.bfloat16)


def product(left, right):
    dot = functools.partial(jnp.dot, preferred_element_type=jnp.float32)
    return dot(left[0], right[0]) + (dot(left[0], right[1]) + dot(left[1], right[0]))


def pack_tiles(v_ref, y_ref, comps):
    points, planes = v_ref.shape[1:3]
    carriers = y_ref.shape[1]
    lo, hi = AXIAL_REACH, planes - AXIAL_REACH
    for i, c in enumerate(comps):

        def carry(t):
            y_ref[i, t] = v_ref[c, t]

        def ride(j):
            t = carriers + j
            y_ref[i, 3 * j, lo:hi] = v_ref[c, t, 0:2]
            y_ref[i, 3 * j + 1, lo : lo + 1] = v_ref[c, t, 2:3]
            y_ref[i, 3 * j + 1, lo + 1 : hi] = v_ref[c, t, hi : hi + 1]
            y_ref[i, 3 * j + 2, lo:hi] = v_ref[c, t, hi + 1 :]

        each(carriers, carry)
        each(points - carriers, ride)


def rebuild_tiles(y_ref, tile_ref):
    carriers = y_ref.shape[1]
    comps, riders, planes, radial = tile_ref.shape
    lo, hi = AXIAL_REACH, planes - AXIAL_REACH
    for c in range(comps):
        for j in range(riders):
            tile_ref[c, j, 0:2] = y_ref[c, 3 * j, lo:hi]
            tile_ref[c, j, 2:3] = y_ref[c, 3 * j + 1, lo : lo + 1]
            tile_ref[c, j, lo:hi] = jnp.zeros((hi - lo, radial), jnp.float32)
            tile_ref[c, j, hi : hi + 1] = y_ref[c, 3 * j + 1, lo + 1 : hi]
            tile_ref[c, j, hi + 1 :] = y_ref[c, 3 * j + 2, lo:hi]


def load_kernel(hbm_ref, v_ref, y_ref, sems):
    order = list(range(v_ref.shape[0]))
    loads = [pltpu.make_async_copy(hbm_ref.at[c], v_ref.at[c], sems.at[c]) for c in order]
    for c in reversed(order):
        loads[c].start()
    loads[-1].wait()
    pack_tiles(v_ref, y_ref, order[-1:])
    for c in order[:-1]:
        loads[c].wait()


def load(v):
    comps, points, planes, radial = v.shape
    return pl.pallas_call(
        load_kernel,
        name="load",
        out_shape=(held(*v.shape), held(1, points - points // 4, planes, radial)),
        in_specs=[HBM],
        out_specs=(VMEM, VMEM),
        scratch_shapes=[pltpu.SemaphoreType.DMA((comps,))],
        compiler_params=params(v.size * 4, 2),
    )(v)


def pack_planes_kernel(v_ref, first_ref, y_ref):
    pack_tiles(v_ref, y_ref, range(y_ref.shape[0]))


def pack_planes(v, first):
    comps, points, planes, radial = v.shape
    return pl.pallas_call(
        pack_planes_kernel,
        name="pack_planes",
        out_shape=held(comps - 1, points - points // 4, planes, radial),
        in_specs=[VMEM, ANY],
        out_specs=VMEM,
        compiler_params=params(v.size * 4, 2),
    )(v, first)


def pack_side_kernel(me_ref, v_ref, first_ref, side_ref, *, after):
    points, reach = v_ref.shape[1], side_ref.shape[1]

    def put(start):
        for c in range(v_ref.shape[0]):
            for h in range(reach):
                side_ref[c, h] = v_ref[c, start + h]

    even = me_ref[0] % 2 == 0
    last = even if after else jnp.logical_not(even)
    pl.when(last)(lambda: put(points - reach))
    pl.when(jnp.logical_not(last))(lambda: put(0))


def pack_side(me, v, first, reach, after):
    comps, _, planes, radial = v.shape
    return pl.pallas_call(
        functools.partial(pack_side_kernel, after=after),
        name="pack_core" if after else "pack_chip",
        out_shape=held(comps, reach, planes, radial),
        in_specs=[SMEM, VMEM, ANY],
        out_specs=VMEM,
        compiler_params=params(v.size * 4, 3),
    )(me, v, first)


def pack_mirror_kernel(v_ref, first_ref, mirror_ref):
    points, tiles = v_ref.shape[1], mirror_ref.shape[1]
    width = LANES // (points // tiles)
    lane = lax.broadcasted_iota(jnp.int32, mirror_ref.shape[2:], 1)

    def put(p):
        for c in range(v_ref.shape[0]):
            tile = v_ref[c, p, :, :LANES]
            for q in range(1, points // tiles):
                part = pltpu.roll(v_ref[c, q * tiles + p, :, :LANES], q * width, 1)
                tile = jnp.where(lane < q * width, tile, part)
            mirror_ref[c, p] = tile

    each(tiles, put)


def pack_mirror(v, first, width):
    comps, points, planes, _ = v.shape
    return pl.pallas_call(
        pack_mirror_kernel,
        name="pack_mirror",
        out_shape=held(comps, points // (LANES // width), planes, LANES),
        in_specs=[VMEM, ANY],
        out_specs=VMEM,
        compiler_params=params(v.size * 4, 2),
    )(v, first)


def inverse_radius(radial, start=0):
    return 1.0 / ((lax.broadcasted_iota(jnp.int32, (1, radial), 1) + start).astype(jnp.float32) + 0.5)


def axial_weights(planes, inside):
    row = lax.broadcasted_iota(jnp.int32, (planes, LANES), 0)
    weights = []
    for m, w in enumerate(AXIAL_WEIGHTS, 1):
        for shift, own, sign in ((m, row < planes - m, 1.0), (planes - m, row >= m, -1.0)):
            keep = own if inside else jnp.logical_not(own)
            weights.append((shift, jnp.where(keep, sign * w, 0.0)))
    return weights


def axial_part(tile, weights):
    planes, width = tile.shape
    weights = [(shift, jnp.concatenate([weight] * (width // LANES), axis=1)) for shift, weight in weights]
    total = None
    for shift, weight in weights:
        term = weight * pltpu.roll(tile, planes - shift, 0)
        total = term if total is None else total + term
    return total


def mirror_kernel(v_ref, op_ref, mirror_ref, n_in_ref, n_ref, grad_ref):
    comps, points, planes, radial = v_ref.shape
    tiles = mirror_ref.shape[1]
    count = points // tiles
    width = LANES // count
    rows = tiles * planes
    right = split(jnp.concatenate([op_ref[radial:]] * count, axis=0))
    lane = lax.broadcasted_iota(jnp.int32, (rows, LANES), 1)
    for c in range(comps):
        high, low = split(MIRROR_SIGNS[c] * mirror_ref[c].reshape(rows, LANES))
        zero = jnp.zeros_like(high)
        parts = [
            [jnp.where((lane >= q * width) & (lane < (q + 1) * width), x, zero) for q in range(count)]
            for x in (high, low)
        ]
        left = [jnp.concatenate(x, axis=0) for x in parts]
        grad_ref[c * points * planes : (c + 1) * points * planes] = product(left, right)

    def finish(t):
        for c in range(comps):
            start = pl.multiple_of((c * points + t) * planes, planes)
            n_ref[c, t] = n_in_ref[c, t] + v_ref[0, t] * grad_ref[pl.ds(start, planes)]

    each(points, finish)


def mirror_terms(v, op, mirror, n):
    return pl.pallas_call(
        mirror_kernel,
        name="mirror_terms",
        out_shape=held(*v.shape),
        in_specs=[VMEM] * 4,
        out_specs=VMEM,
        scratch_shapes=[pltpu.VMEM((v.size // v.shape[3], v.shape[3]), jnp.float32)],
        input_output_aliases={3: 0},
        compiler_params=params(v.size * 4, 8),
        cost_estimate=pl.CostEstimate(flops=MIRROR, bytes_accessed=16 * v.size, transcendentals=0),
    )(v, op, mirror, n)


def inner_kernel(tap_ref, v_ref, op_ref, n_ref, grad_ref):
    comps, points, planes, radial = v_ref.shape
    reach = (tap_ref.shape[0] - 1) // 2
    rows = points * planes
    right = split(op_ref[:radial])
    for c in range(comps):
        grad_ref[c * rows : (c + 1) * rows] = product(split(v_ref[c].reshape(rows, radial)), right)
    weights = axial_weights(planes, True)

    @pl.loop(0, radial // LANES)
    def column(k):
        lanes = pl.ds(pl.multiple_of(k * LANES, LANES), LANES)
        inv_r = inverse_radius(LANES, k * LANES)
        for c in range(comps):
            for t in range(points):
                a, b, e = [v_ref[i, t, :, lanes] for i in range(3)]
                b_inv = b * inv_r
                around = None
                for m in range(max(-reach, -t), min(reach, points - 1 - t) + 1):
                    term = tap_ref[m + reach] * v_ref[c, t + m, :, lanes]
                    around = term if around is None else around + term
                start = c * rows + t * planes
                n = a * grad_ref[start : start + planes, lanes] + b_inv * around
                n = n + e * axial_part(v_ref[c, t, :, lanes], weights)
                if c == 0:
                    n = n - b_inv * b
                elif c == 1:
                    n = n + a * b_inv
                n_ref[c, t, :, lanes] = n


def inner_terms(taps, v, op):
    return pl.pallas_call(
        inner_kernel,
        name="inner_terms",
        out_shape=held(*v.shape),
        in_specs=[VMEM] * 3,
        out_specs=VMEM,
        scratch_shapes=[pltpu.VMEM((v.size // v.shape[3], v.shape[3]), jnp.float32)],
        compiler_params=params(v.size * 4, 7),
        cost_estimate=pl.CostEstimate(flops=INNER, bytes_accessed=16 * v.size, transcendentals=0),
    )(taps, v, op)


def add_side(tap_ref, v_ref, side_ref, n_in_ref, n_ref, before, columns):
    comps, points, _, radial = v_ref.shape
    reach = side_ref.shape[1]
    first = 0 if before else reach + 1

    start, count = columns

    @pl.loop(0, count)
    def column(i):
        k = start + i
        lanes = pl.ds(pl.multiple_of(k * LANES, LANES), LANES)
        inv_r = inverse_radius(LANES, k * LANES)
        weights = [tap_ref[first + i] for i in range(reach)]
        for c in range(comps):
            side = [side_ref[c, h, :, lanes] for h in range(reach)]
            for u in range(reach):
                t = u if before else points - reach + u
                taps = [(h, h - u) for h in range(u, reach)] if before else [(h, reach - 1 + h - u) for h in range(u + 1)]
                around = None
                for h, w in taps:
                    term = weights[w] * side[h]
                    around = term if around is None else around + term
                n_ref[c, t, :, lanes] = n_in_ref[c, t, :, lanes] + v_ref[1, t, :, lanes] * inv_r * around


def core_kernel(me_ref, tap_ref, v_ref, core_ref, n_in_ref, n_ref):
    even = me_ref[0] % 2 == 0
    columns = (0, v_ref.shape[3] // LANES)
    add = functools.partial(add_side, tap_ref, v_ref, core_ref, n_in_ref, n_ref, columns=columns)
    pl.when(even)(lambda: add(before=False))
    pl.when(jnp.logical_not(even))(lambda: add(before=True))


def late_kernel(me_ref, tap_ref, v_ref, chip_ref, n_in_ref, ready_ref, n_ref):
    even = me_ref[0] % 2 == 0
    columns = (0, v_ref.shape[3] // LANES)
    add = functools.partial(add_side, tap_ref, v_ref, chip_ref, n_in_ref, n_ref, columns=columns)
    pl.when(even)(lambda: add(before=True))
    pl.when(jnp.logical_not(even))(lambda: add(before=False))


def side_terms(kernel, name, me, taps, v, side, n, ready=()):
    return pl.pallas_call(
        kernel,
        name=name,
        out_shape=held(*v.shape),
        in_specs=[SMEM] + [VMEM] * 4 + [ANY] * len(ready),
        out_specs=VMEM,
        input_output_aliases={4: 0},
        compiler_params=params(v.size * 4, 5),
        cost_estimate=pl.CostEstimate(flops=SIDE, bytes_accessed=12 * v.size, transcendentals=0),
    )(me, taps, v, side, n, *ready)


def share_kernel(v_ref, e_ref, power_ref, ends_ref, tile_ref):
    comps, points, planes, radial = v_ref.shape
    carriers = e_ref.shape[1]
    weights = axial_weights(planes, False)
    rebuild_tiles(e_ref, tile_ref)
    decay = power_ref[1:2]
    ends_ref[...] = jnp.zeros_like(ends_ref)
    for t in range(points):
        e = STEP_WEIGHT * (e_ref[0, t] if t < carriers else tile_ref[0, t - carriers])
        for c in range(comps):
            right_side = e * axial_part(v_ref[c, t], weights)
            ends_ref[0, c] = decay * ends_ref[0, c] - right_side
            ends_ref[1, c] = ends_ref[1, c] - power_ref[t : t + 1] * right_side


def share_terms(v, e, power):
    comps, points, planes, radial = v.shape
    return pl.pallas_call(
        share_kernel,
        name="share_terms",
        out_shape=held(2, comps, planes, radial),
        in_specs=[VMEM] * 3,
        out_specs=VMEM,
        scratch_shapes=[pltpu.VMEM((1, points - e.shape[1], planes, radial), jnp.float32)],
        compiler_params=params(v.size * 4, 4),
        cost_estimate=pl.CostEstimate(flops=20 * v.size, bytes_accessed=8 * v.size, transcendentals=0),
    )(v, e, power)


def ends_kernel(me_ref, v_ref, share_ref, power_ref, n_ref, ends_ref, *, own):
    comps, points, _, radial = v_ref.shape
    lanes = half_lanes(me_ref, radial // 2, own)
    decay = power_ref[1:2, lanes]
    for c in range(comps):
        low = high = None
        for t in range(points):
            right_side = v_ref[c, t, :, lanes] - STEP_WEIGHT * n_ref[c, t, :, lanes]
            low = right_side if t == 0 else decay * low + right_side
            high = right_side if t == 0 else high + power_ref[t : t + 1, lanes] * right_side
        ends_ref[0, c] = low + share_ref[0, c, :, lanes]
        ends_ref[1, c] = high + share_ref[1, c, :, lanes]


def ends_terms(me, v, share, power, n, own):
    comps, _, planes, radial = v.shape
    return pl.pallas_call(
        functools.partial(ends_kernel, own=own),
        name="ends_own" if own else "ends_other",
        out_shape=held(2, comps, planes, radial // 2),
        in_specs=[SMEM] + [VMEM] * 4,
        out_specs=VMEM,
        compiler_params=params(v.size * 4, 4),
        cost_estimate=pl.CostEstimate(flops=20 * v.size, bytes_accessed=8 * v.size, transcendentals=0),
    )(me, v, share, power, n)


def chip_ends_kernel(me_ref, tap_ref, v_ref, chip_ref, power_ref, inner_ref, ready_ref, ends_ref, *, own):
    comps, points, _, radial = v_ref.shape
    reach = chip_ref.shape[1]
    core = me_ref[0] % 2
    count = radial // (2 * LANES)
    start = (core if own else 1 - core) * count

    def add(before):
        first = 0 if before else reach + 1

        @pl.loop(0, count)
        def column(i):
            k = start + i
            lanes = pl.ds(pl.multiple_of(k * LANES, LANES), LANES)
            here = pl.ds(pl.multiple_of(i * LANES, LANES), LANES)
            inv_r = STEP_WEIGHT * inverse_radius(LANES, k * LANES)
            weights = [tap_ref[first + j] for j in range(reach)]
            for c in range(comps):
                side = [chip_ref[c, h, :, lanes] for h in range(reach)]
                low, high = inner_ref[0, c, :, here], inner_ref[1, c, :, here]
                for u in range(reach):
                    t = u if before else points - reach + u
                    taps = [(h, h - u) for h in range(u, reach)] if before else [(h, reach - 1 + h - u) for h in range(u + 1)]
                    around = None
                    for h, w in taps:
                        term = weights[w] * side[h]
                        around = term if around is None else around + term
                    x = v_ref[1, t, :, lanes] * inv_r * around
                    low = low - power_ref[points - 1 - t : points - t, lanes] * x
                    high = high - power_ref[t : t + 1, lanes] * x
                ends_ref[0, c, :, here] = low
                ends_ref[1, c, :, here] = high

    pl.when(core == 0)(lambda: add(True))
    pl.when(core == 1)(lambda: add(False))


def chip_ends(me, taps, v, chip, power, inner, ready, own):
    return pl.pallas_call(
        functools.partial(chip_ends_kernel, own=own),
        name="chip_own" if own else "chip_other",
        out_shape=held(*inner.shape),
        in_specs=[SMEM] + [VMEM] * 5 + [ANY],
        out_specs=VMEM,
        compiler_params=params(v.size * 4, 4),
        cost_estimate=pl.CostEstimate(flops=SIDE, bytes_accessed=8 * v.size, transcendentals=0),
    )(me, taps, v, chip, power, inner, ready)


def planes_kernel(v_ref, y_ref, e_ref, ready_ref, n_in_ref, n_ref, y_tile_ref, e_tile_ref):
    comps, points, planes, _ = v_ref.shape
    carriers = y_ref.shape[1]
    weights = axial_weights(planes, False)
    rebuild_tiles(y_ref, y_tile_ref)
    rebuild_tiles(e_ref, e_tile_ref)
    for t in range(points):
        for c in range(comps):
            ref, tile_ref, i = (y_ref, y_tile_ref, c) if c < comps - 1 else (e_ref, e_tile_ref, 0)
            tile = ref[i, t] if t < carriers else tile_ref[i, t - carriers]
            n_ref[c, t] = n_in_ref[c, t] + v_ref[2, t] * axial_part(tile, weights)


def planes_terms(v, y, e, ready, n):
    comps, points, planes, radial = v.shape
    riders = points - y.shape[1]
    return pl.pallas_call(
        planes_kernel,
        name="planes_terms",
        out_shape=held(*v.shape),
        in_specs=[VMEM] * 3 + [ANY, VMEM],
        out_specs=VMEM,
        scratch_shapes=[pltpu.VMEM((k, riders, planes, radial), jnp.float32) for k in (comps - 1, 1)],
        input_output_aliases={4: 0},
        compiler_params=params(v.size * 4, 6),
        cost_estimate=pl.CostEstimate(flops=20 * v.size, bytes_accessed=16 * v.size, transcendentals=0),
    )(v, y, e, ready, n)


def table_kernel(me_ref, factor_ref, stencil_ref, row_ref, tap_ref, *, points, sectors):
    radial = row_ref.shape[1]
    one = jnp.ones((1, radial), jnp.float32)
    half = (0.5 * lax.rsqrt(factor_ref[0] * one)) / inverse_radius(radial)
    root = jnp.sqrt(1.0 + half * half)
    loss = 2.0 * half * (root - half)
    rows = [one]
    for _ in range(points):
        rows.append(rows[-1] * (1.0 - loss))
    total = loss
    left, result = points * sectors, None
    while left:
        if left & 1:
            result = total if result is None else result + total - result * total
        total = total * (2.0 - total)
        left >>= 1
    across = rows[points] * rows[points]
    rows += [half / root, 1.0 / result]
    before = after = one
    for bit in range(1, sectors.bit_length() - 1):
        upper = (me_ref[0] >> bit) % 2 == 1
        rows += [across, before, after]
        before, after = jnp.where(upper, before * across, before), jnp.where(upper, after, after * across)
        across = across * across
    for k, row in enumerate(rows + [before, after]):
        row_ref[k : k + 1] = row
    for k in range(tap_ref.shape[0]):
        tap_ref[k] = jnp.full(tap_ref.shape[1:], stencil_ref[k], jnp.float32)


def table(me, viscous_factor, stencil, points, sectors, planes, radial):
    count = points + 5 + 3 * (sectors.bit_length() - 2)
    return pl.pallas_call(
        functools.partial(table_kernel, points=points, sectors=sectors),
        name="table",
        out_shape=(held(count, radial), held(stencil.shape[0], planes, LANES)),
        in_specs=[SMEM, SMEM, SMEM],
        out_specs=(VMEM, VMEM),
        compiler_params=params(1 << 20, 1),
        cost_estimate=pl.CostEstimate(flops=1000 * radial, bytes_accessed=400 * radial, transcendentals=0),
    )(me, viscous_factor, stencil)


def sweep_kernel(v_ref, n_ref, power_ref, s_ref, nonlinear_ref, sem):
    leave = pltpu.make_async_copy(n_ref, nonlinear_ref, sem)
    leave.start()
    comps, points, planes, radial = v_ref.shape
    decay = power_ref[1:2]
    height = power_ref[points + 1 : points + 2]
    for c in range(comps):
        s_ref[c, 0] = height * (v_ref[c, 0] - STEP_WEIGHT * n_ref[c, 0])

        def forward(i):
            t = i + 1
            s_ref[c, t] = decay * s_ref[c, t - 1] + height * (v_ref[c, t] - STEP_WEIGHT * n_ref[c, t])

        each(points - 1, forward)

    def backward(i, carry):
        t = points - 1 - i
        after = []
        for c in range(comps):
            s_ref[c, t] = s_ref[c, t] + carry[c]
            after.append(decay * (carry[c] + height * (v_ref[c, t] - STEP_WEIGHT * n_ref[c, t])))
        return tuple(after)

    start = (jnp.zeros((planes, radial), jnp.float32),) * comps
    lax.fori_loop(0, points, backward, start, unroll=points <= UNROLL)
    leave.wait()


def sweep(v, n, power):
    return pl.pallas_call(
        sweep_kernel,
        name="sweep",
        out_shape=(held(*v.shape), jax.ShapeDtypeStruct(v.shape, v.dtype)),
        in_specs=[VMEM] * 3,
        out_specs=(VMEM, ANY),
        scratch_shapes=[pltpu.SemaphoreType.DMA],
        compiler_params=params(v.size * 4, 4),
        cost_estimate=pl.CostEstimate(flops=10 * v.size, bytes_accessed=12 * v.size, transcendentals=0),
    )(v, n, power)


def half_lanes(me_ref, half, own=True):
    core = me_ref[0] % 2
    return pl.ds(pl.multiple_of((core if own else 1 - core) * half, half), half)


def pair_kernel(me_ref, power_ref, own_ref, other_ref, block_ref, *, points):
    half = own_ref.shape[3]
    hop = power_ref[points : points + 1, half_lanes(me_ref, half)]
    odd = me_ref[0] % 2 == 1
    for c in range(own_ref.shape[1]):
        for side in range(2):
            own, other = own_ref[side, c], other_ref[side, c]
            far, near = (own, other) if side == 0 else (other, own)
            block_ref[side, c] = jnp.where(odd, hop * near + far, hop * far + near)


def pair(me, power, own, other, points):
    return pl.pallas_call(
        functools.partial(pair_kernel, points=points),
        name="pair",
        out_shape=held(*own.shape),
        in_specs=[SMEM, VMEM, VMEM, VMEM],
        out_specs=VMEM,
        compiler_params=params(own.size * 4, 8),
    )(me, power, own, other)


def merge_kernel(me_ref, power_ref, block_ref, other_ref, *refs, points, bit):
    *entry_refs, block_out_ref, entry_out_ref = refs
    comps, half = block_ref.shape[1], block_ref.shape[3]
    lanes = half_lanes(me_ref, half)
    first = points + 3 * bit
    across, before, after = [power_ref[first + k : first + k + 1, lanes] for k in range(3)]
    upper = (me_ref[0] >> bit) % 2 == 1
    before = jnp.where(upper, before, 0.0)
    after = jnp.where(upper, 0.0, after)
    for c in range(comps):
        low, high = block_ref[0, c], block_ref[1, c]
        other_low, other_high = other_ref[0, c], other_ref[1, c]
        block_out_ref[0, c] = jnp.where(upper, across * other_low + low, across * low + other_low)
        block_out_ref[1, c] = jnp.where(upper, other_high + across * high, high + across * other_high)
        for side, enters in enumerate((before * other_low, after * other_high)):
            entry_out_ref[side, c] = entry_refs[0][side, c] + enters if entry_refs else enters


def merge(me, power, block, other, entries, points, bit):
    return pl.pallas_call(
        functools.partial(merge_kernel, points=points, bit=bit),
        name="merge",
        out_shape=(held(*block.shape), held(*block.shape)),
        in_specs=[SMEM] + [VMEM] * (3 + len(entries)),
        out_specs=(VMEM, VMEM),
        compiler_params=params(block.size * 4, 8),
    )(me, power, block, other, *entries)


def enter_kernel(me_ref, power_ref, block_ref, entry_ref, own_ref, other_ref, ready_ref, mine_ref, send_ref, *, points):
    comps, half = block_ref.shape[1], block_ref.shape[3]
    lanes = half_lanes(me_ref, half)
    row = lambda k: power_ref[k : k + 1, lanes]
    hop, height, wrap = row(points), row(points + 1), row(points + 2)
    last = power_ref.shape[0]
    before, after = row(last - 2) * wrap, row(last - 1) * wrap
    odd = me_ref[0] % 2 == 1
    for c in range(comps):
        low = height * (entry_ref[0, c] + before * block_ref[0, c])
        high = height * (entry_ref[1, c] + after * block_ref[1, c])
        even_low = height * jnp.where(odd, other_ref[0, c], own_ref[0, c])
        odd_high = height * jnp.where(odd, own_ref[1, c], other_ref[1, c])
        even_in = (low, odd_high + hop * high)
        odd_in = (even_low + hop * low, high)
        for side in range(2):
            mine_ref[side, c] = jnp.where(odd, odd_in[side], even_in[side])
            send_ref[side, c] = jnp.where(odd, even_in[side], odd_in[side])


def enter(me, power, block, entry, own, other, ready, points):
    return pl.pallas_call(
        functools.partial(enter_kernel, points=points),
        name="enter",
        out_shape=(held(*block.shape), held(*block.shape)),
        in_specs=[SMEM] + [VMEM] * 5 + [ANY],
        out_specs=(VMEM, VMEM),
        compiler_params=params(block.size * 4, 12),
    )(me, power, block, entry, own, other, ready)


def close_kernel(me_ref, s_ref, power_ref, entry_ref, *refs, own):
    out_ref, x_ref, sems = refs[-3:]
    comps, points, _, _ = s_ref.shape
    lanes = half_lanes(me_ref, entry_ref.shape[3], own)
    leaves = []
    for c in range(comps):
        before, after = entry_ref[0, c], entry_ref[1, c]

        def point(t):
            decayed = power_ref[pl.ds(t + 1, 1), lanes] * before + power_ref[pl.ds(points - t, 1), lanes] * after
            x_ref[c, t] = s_ref[c, t, :, lanes] + decayed

        each(points, point)
        leaves.append(pltpu.make_async_copy(x_ref.at[c], out_ref.at[c, :, :, lanes], sems.at[c]))
        leaves[c].start()
    for leave in leaves:
        leave.wait()


def close(me, s, power, entry, out, own):
    comps, points, planes, radial = s.shape
    return pl.pallas_call(
        functools.partial(close_kernel, own=own),
        name="close_own" if own else "close_other",
        out_shape=jax.ShapeDtypeStruct(s.shape, s.dtype),
        in_specs=[SMEM] + [VMEM] * 3 + [ANY] * len(out),
        out_specs=ANY,
        scratch_shapes=[
            pltpu.VMEM((comps, points, planes, radial // 2), jnp.float32),
            pltpu.SemaphoreType.DMA((comps,)),
        ],
        input_output_aliases={4: 0} if out else {},
        compiler_params=params(s.size * 4, 5),
        cost_estimate=pl.CostEstimate(flops=4 * s.size, bytes_accessed=8 * s.size, transcendentals=0),
    )(me, s, power, entry, *out)


def local(velocity, radial_op, azimuth_stencil, viscous_factor):
    sectors = lax.axis_size("theta")
    comps, points, planes, radial = velocity.shape
    reach = (azimuth_stencil.shape[0] - 1) // 2
    width = radial_op.shape[1] - radial
    me = lax.axis_index("theta").astype(jnp.int32).reshape(1)
    op = radial_op.T

    velocity, axial_out = load(pltpu.with_memory_space_constraint(velocity, pltpu.HBM))
    axial_in = swap(axial_out, "gz", 1)
    chip_out = pack_side(me, velocity, axial_out, reach, False)
    chip_in = swap_across(chip_out, "theta")
    mirror_out = pack_mirror(velocity, chip_out, width)
    mirror_in = swap(mirror_out, "theta", sectors // 2)
    core_out = pack_side(me, velocity, axial_in, reach, True)
    core_in = swap(core_out, "theta", 1)
    power, taps = table(me, viscous_factor, azimuth_stencil, points, sectors, planes, radial)
    n = inner_terms(taps, velocity, op)
    share_out = share_terms(velocity, axial_in, power)
    share_in = swap(share_out, "gz", 1)
    planes_in = swap(pack_planes(velocity, share_out), "gz", 1)
    n = side_terms(core_kernel, "core_terms", me, taps, velocity, core_in, n)
    n = mirror_terms(velocity, op, mirror_in, n)
    inner_other = ends_terms(me, velocity, share_in, power, n, False)
    inner_own = ends_terms(me, velocity, share_in, power, n, True)
    send = chip_ends(me, taps, velocity, chip_in, power, inner_other, inner_own, False)
    other = swap(send, "theta", 1)
    own = chip_ends(me, taps, velocity, chip_in, power, inner_own, send, True)
    n = side_terms(late_kernel, "late_terms", me, taps, velocity, chip_in, n, (own,))
    block = pair(me, power, own, other, points)
    entries = ()
    last = sectors.bit_length() - 2
    for bit in range(1, last + 1):
        if bit == last:
            n = planes_terms(velocity, planes_in, axial_in, block, n)
            s, nonlinear = sweep(velocity, n, power)
        block, entry = merge(me, power, block, swap(block, "theta", 1 << bit), entries, points, bit)
        entries = (entry,)
    mine, send = enter(me, power, block, entry, own, other, s, points)
    got = swap(send, "theta", 1)
    new_velocity = close(me, s, power, mine, (), True)
    new_velocity = close(me, s, power, got, (new_velocity,), False)
    return (new_velocity, nonlinear)


def solution(mesh):
    in_specs = (P(None, "theta", "gz", None), P(), P(), P())
    out_specs = (P(None, "theta", "gz", None), P(None, "theta", "gz", None))
    return jax.shard_map(local, mesh=mesh, in_specs=in_specs, out_specs=out_specs, check_vma=False)
```

```python
import functools

import jax
import jax.numpy as jnp
from jax import lax
from jax.experimental import pallas as pl
from jax.experimental.pallas import tpu as pltpu
from jax.sharding import PartitionSpec as P

AXIAL_WEIGHTS = (0.75, -0.15, 1.0 / 60.0)
AXIAL_REACH = len(AXIAL_WEIGHTS)
STEP_WEIGHT = 0.2
MIRROR_SIGNS = (-1.0, -1.0, 1.0)
LANES = 128
UNROLL = 16
INNER = 10 << 29
MIRROR = 1 << 26
SIDE = 1 << 26

VMEM = pl.BlockSpec(memory_space=pltpu.VMEM)
SMEM = pl.BlockSpec(memory_space=pltpu.SMEM)
ANY = pl.BlockSpec(memory_space=pl.ANY)
HBM = pl.BlockSpec(memory_space=pltpu.HBM)


def params(block_bytes, blocks):
    return pltpu.CompilerParams(vmem_limit_bytes=(2 << 20) + blocks * block_bytes)


def held(*shape):
    return pltpu.VMEM(shape, jnp.float32)


def each(count, body):
    if count <= UNROLL:
        for i in range(count):
            body(i)
    else:
        pl.loop(0, count)(body)


def swap(block, axis, bit):
    size = lax.axis_size(axis)
    return lax.ppermute(block, axis, [(i, i ^ bit) for i in range(size)])


def swap_across(block, axis):
    size = lax.axis_size(axis)
    route = []
    for odd in range(1, size, 2):
        route += [(odd, (odd + 1) % size), ((odd + 1) % size, odd)]
    return lax.ppermute(block, axis, route)


def split(x):
    high = x.astype(jnp.bfloat16)
    return high, (x - high.astype(jnp.float32)).astype(jnp.bfloat16)


def product(left, right):
    dot = functools.partial(jnp.dot, preferred_element_type=jnp.float32)
    return dot(left[0], right[0]) + (dot(left[0], right[1]) + dot(left[1], right[0]))


def pack_tiles(v_ref, y_ref, comps):
    points, planes = v_ref.shape[1:3]
    carriers = y_ref.shape[1]
    lo, hi = AXIAL_REACH, planes - AXIAL_REACH
    for i, c in enumerate(comps):

        def carry(t):
            y_ref[i, t] = v_ref[c, t]

        def ride(j):
            t = carriers + j
            y_ref[i, 3 * j, lo:hi] = v_ref[c, t, 0:2]
            y_ref[i, 3 * j + 1, lo : lo + 1] = v_ref[c, t, 2:3]
            y_ref[i, 3 * j + 1, lo + 1 : hi] = v_ref[c, t, hi : hi + 1]
            y_ref[i, 3 * j + 2, lo:hi] = v_ref[c, t, hi + 1 :]

        each(carriers, carry)
        each(points - carriers, ride)


def rebuild_tiles(y_ref, tile_ref):
    carriers = y_ref.shape[1]
    comps, riders, planes, radial = tile_ref.shape
    lo, hi = AXIAL_REACH, planes - AXIAL_REACH
    for c in range(comps):
        for j in range(riders):
            tile_ref[c, j, 0:2] = y_ref[c, 3 * j, lo:hi]
            tile_ref[c, j, 2:3] = y_ref[c, 3 * j + 1, lo : lo + 1]
            tile_ref[c, j, lo:hi] = jnp.zeros((hi - lo, radial), jnp.float32)
            tile_ref[c, j, hi : hi + 1] = y_ref[c, 3 * j + 1, lo + 1 : hi]
            tile_ref[c, j, hi + 1 :] = y_ref[c, 3 * j + 2, lo:hi]


def load_kernel(hbm_ref, v_ref, y_ref, sems):
    order = list(range(v_ref.shape[0]))
    loads = [pltpu.make_async_copy(hbm_ref.at[c], v_ref.at[c], sems.at[c]) for c in order]
    for c in reversed(order):
        loads[c].start()
    loads[-1].wait()
    pack_tiles(v_ref, y_ref, order[-1:])
    for c in order[:-1]:
        loads[c].wait()


def load(v):
    comps, points, planes, radial = v.shape
    return pl.pallas_call(
        load_kernel,
        name="load",
        out_shape=(held(*v.shape), held(1, points - points // 4, planes, radial)),
        in_specs=[HBM],
        out_specs=(VMEM, VMEM),
        scratch_shapes=[pltpu.SemaphoreType.DMA((comps,))],
        compiler_params=params(v.size * 4, 2),
    )(v)


def pack_planes_kernel(v_ref, first_ref, y_ref):
    pack_tiles(v_ref, y_ref, range(y_ref.shape[0]))


def pack_planes(v, first):
    comps, points, planes, radial = v.shape
    return pl.pallas_call(
        pack_planes_kernel,
        name="pack_planes",
        out_shape=held(comps - 1, points - points // 4, planes, radial),
        in_specs=[VMEM, ANY],
        out_specs=VMEM,
        compiler_params=params(v.size * 4, 2),
    )(v, first)


def pack_side_kernel(me_ref, v_ref, first_ref, side_ref, *, after):
    points, reach = v_ref.shape[1], side_ref.shape[1]

    def put(start):
        for c in range(v_ref.shape[0]):
            for h in range(reach):
                side_ref[c, h] = v_ref[c, start + h]

    even = me_ref[0] % 2 == 0
    last = even if after else jnp.logical_not(even)
    pl.when(last)(lambda: put(points - reach))
    pl.when(jnp.logical_not(last))(lambda: put(0))


def pack_side(me, v, first, reach, after):
    comps, _, planes, radial = v.shape
    return pl.pallas_call(
        functools.partial(pack_side_kernel, after=after),
        name="pack_core" if after else "pack_chip",
        out_shape=held(comps, reach, planes, radial),
        in_specs=[SMEM, VMEM, ANY],
        out_specs=VMEM,
        compiler_params=params(v.size * 4, 3),
    )(me, v, first)


def pack_mirror_kernel(v_ref, first_ref, mirror_ref):
    points, tiles = v_ref.shape[1], mirror_ref.shape[1]
    width = LANES // (points // tiles)
    lane = lax.broadcasted_iota(jnp.int32, mirror_ref.shape[2:], 1)

    def put(p):
        for c in range(v_ref.shape[0]):
            tile = v_ref[c, p, :, :LANES]
            for q in range(1, points // tiles):
                part = pltpu.roll(v_ref[c, q * tiles + p, :, :LANES], q * width, 1)
                tile = jnp.where(lane < q * width, tile, part)
            mirror_ref[c, p] = tile

    each(tiles, put)


def pack_mirror(v, first, width):
    comps, points, planes, _ = v.shape
    return pl.pallas_call(
        pack_mirror_kernel,
        name="pack_mirror",
        out_shape=held(comps, points // (LANES // width), planes, LANES),
        in_specs=[VMEM, ANY],
        out_specs=VMEM,
        compiler_params=params(v.size * 4, 2),
    )(v, first)


def inverse_radius(radial, start=0):
    return 1.0 / ((lax.broadcasted_iota(jnp.int32, (1, radial), 1) + start).astype(jnp.float32) + 0.5)


def axial_weights(planes, inside):
    row = lax.broadcasted_iota(jnp.int32, (planes, LANES), 0)
    weights = []
    for m, w in enumerate(AXIAL_WEIGHTS, 1):
        for shift, own, sign in ((m, row < planes - m, 1.0), (planes - m, row >= m, -1.0)):
            keep = own if inside else jnp.logical_not(own)
            weights.append((shift, jnp.where(keep, sign * w, 0.0)))
    return weights


def axial_part(tile, weights):
    planes, width = tile.shape
    weights = [(shift, jnp.concatenate([weight] * (width // LANES), axis=1)) for shift, weight in weights]
    total = None
    for shift, weight in weights:
        term = weight * pltpu.roll(tile, planes - shift, 0)
        total = term if total is None else total + term
    return total


def mirror_kernel(v_ref, op_ref, mirror_ref, n_in_ref, n_ref, grad_ref):
    comps, points, planes, radial = v_ref.shape
    tiles = mirror_ref.shape[1]
    count = points // tiles
    width = LANES // count
    rows = tiles * planes
    right = split(jnp.concatenate([op_ref[radial:]] * count, axis=0))
    lane = lax.broadcasted_iota(jnp.int32, (rows, LANES), 1)
    for c in range(comps):
        high, low = split(MIRROR_SIGNS[c] * mirror_ref[c].reshape(rows, LANES))
        zero = jnp.zeros_like(high)
        parts = [
            [jnp.where((lane >= q * width) & (lane < (q + 1) * width), x, zero) for q in range(count)]
            for x in (high, low)
        ]
        left = [jnp.concatenate(x, axis=0) for x in parts]
        grad_ref[c * points * planes : (c + 1) * points * planes] = product(left, right)

    def finish(t):
        for c in range(comps):
            start = pl.multiple_of((c * points + t) * planes, planes)
            n_ref[c, t] = n_in_ref[c, t] + v_ref[0, t] * grad_ref[pl.ds(start, planes)]

    each(points, finish)


def mirror_terms(v, op, mirror, n):
    return pl.pallas_call(
        mirror_kernel,
        name="mirror_terms",
        out_shape=held(*v.shape),
        in_specs=[VMEM] * 4,
        out_specs=VMEM,
        scratch_shapes=[pltpu.VMEM((v.size // v.shape[3], v.shape[3]), jnp.float32)],
        input_output_aliases={3: 0},
        compiler_params=params(v.size * 4, 8),
        cost_estimate=pl.CostEstimate(flops=MIRROR, bytes_accessed=16 * v.size, transcendentals=0),
    )(v, op, mirror, n)


def inner_kernel(tap_ref, v_ref, op_ref, n_ref, grad_ref):
    comps, points, planes, radial = v_ref.shape
    reach = (tap_ref.shape[0] - 1) // 2
    rows = points * planes
    right = split(op_ref[:radial])
    for c in range(comps):
        grad_ref[c * rows : (c + 1) * rows] = product(split(v_ref[c].reshape(rows, radial)), right)
    weights = axial_weights(planes, True)

    @pl.loop(0, radial // LANES)
    def column(k):
        lanes = pl.ds(pl.multiple_of(k * LANES, LANES), LANES)
        inv_r = inverse_radius(LANES, k * LANES)
        for c in range(comps):
            for t in range(points):
                a, b, e = [v_ref[i, t, :, lanes] for i in range(3)]
                b_inv = b * inv_r
                around = None
                for m in range(max(-reach, -t), min(reach, points - 1 - t) + 1):
                    term = tap_ref[m + reach] * v_ref[c, t + m, :, lanes]
                    around = term if around is None else around + term
                start = c * rows + t * planes
                n = a * grad_ref[start : start + planes, lanes] + b_inv * around
                n = n + e * axial_part(v_ref[c, t, :, lanes], weights)
                if c == 0:
                    n = n - b_inv * b
                elif c == 1:
                    n = n + a * b_inv
                n_ref[c, t, :, lanes] = n


def inner_terms(taps, v, op):
    return pl.pallas_call(
        inner_kernel,
        name="inner_terms",
        out_shape=held(*v.shape),
        in_specs=[VMEM] * 3,
        out_specs=VMEM,
        scratch_shapes=[pltpu.VMEM((v.size // v.shape[3], v.shape[3]), jnp.float32)],
        compiler_params=params(v.size * 4, 7),
        cost_estimate=pl.CostEstimate(flops=INNER, bytes_accessed=16 * v.size, transcendentals=0),
    )(taps, v, op)


def add_side(tap_ref, v_ref, side_ref, n_in_ref, n_ref, before, columns):
    comps, points, _, radial = v_ref.shape
    reach = side_ref.shape[1]
    first = 0 if before else reach + 1

    start, count = columns

    @pl.loop(0, count)
    def column(i):
        k = start + i
        lanes = pl.ds(pl.multiple_of(k * LANES, LANES), LANES)
        inv_r = inverse_radius(LANES, k * LANES)
        weights = [tap_ref[first + i] for i in range(reach)]
        for c in range(comps):
            side = [side_ref[c, h, :, lanes] for h in range(reach)]
            for u in range(reach):
                t = u if before else points - reach + u
                taps = [(h, h - u) for h in range(u, reach)] if before else [(h, reach - 1 + h - u) for h in range(u + 1)]
                around = None
                for h, w in taps:
                    term = weights[w] * side[h]
                    around = term if around is None else around + term
                n_ref[c, t, :, lanes] = n_in_ref[c, t, :, lanes] + v_ref[1, t, :, lanes] * inv_r * around


def core_kernel(me_ref, tap_ref, v_ref, core_ref, n_in_ref, n_ref):
    even = me_ref[0] % 2 == 0
    columns = (0, v_ref.shape[3] // LANES)
    add = functools.partial(add_side, tap_ref, v_ref, core_ref, n_in_ref, n_ref, columns=columns)
    pl.when(even)(lambda: add(before=False))
    pl.when(jnp.logical_not(even))(lambda: add(before=True))


def late_kernel(me_ref, tap_ref, v_ref, chip_ref, n_in_ref, ready_ref, n_ref):
    even = me_ref[0] % 2 == 0
    columns = (0, v_ref.shape[3] // LANES)
    add = functools.partial(add_side, tap_ref, v_ref, chip_ref, n_in_ref, n_ref, columns=columns)
    pl.when(even)(lambda: add(before=True))
    pl.when(jnp.logical_not(even))(lambda: add(before=False))


def side_terms(kernel, name, me, taps, v, side, n, ready=()):
    return pl.pallas_call(
        kernel,
        name=name,
        out_shape=held(*v.shape),
        in_specs=[SMEM] + [VMEM] * 4 + [ANY] * len(ready),
        out_specs=VMEM,
        input_output_aliases={4: 0},
        compiler_params=params(v.size * 4, 5),
        cost_estimate=pl.CostEstimate(flops=SIDE, bytes_accessed=12 * v.size, transcendentals=0),
    )(me, taps, v, side, n, *ready)


def share_kernel(v_ref, e_ref, power_ref, ends_ref, tile_ref):
    comps, points, planes, radial = v_ref.shape
    carriers = e_ref.shape[1]
    weights = axial_weights(planes, False)
    rebuild_tiles(e_ref, tile_ref)
    decay = power_ref[1:2]
    ends_ref[...] = jnp.zeros_like(ends_ref)
    for t in range(points):
        e = STEP_WEIGHT * (e_ref[0, t] if t < carriers else tile_ref[0, t - carriers])
        for c in range(comps):
            right_side = e * axial_part(v_ref[c, t], weights)
            ends_ref[0, c] = decay * ends_ref[0, c] - right_side
            ends_ref[1, c] = ends_ref[1, c] - power_ref[t : t + 1] * right_side


def share_terms(v, e, power):
    comps, points, planes, radial = v.shape
    return pl.pallas_call(
        share_kernel,
        name="share_terms",
        out_shape=held(2, comps, planes, radial),
        in_specs=[VMEM] * 3,
        out_specs=VMEM,
        scratch_shapes=[pltpu.VMEM((1, points - e.shape[1], planes, radial), jnp.float32)],
        compiler_params=params(v.size * 4, 4),
        cost_estimate=pl.CostEstimate(flops=20 * v.size, bytes_accessed=8 * v.size, transcendentals=0),
    )(v, e, power)


def ends_kernel(me_ref, v_ref, share_ref, power_ref, n_ref, ends_ref, *, own):
    comps, points, _, radial = v_ref.shape
    lanes = half_lanes(me_ref, radial // 2, own)
    decay = power_ref[1:2, lanes]
    for c in range(comps):
        low = high = None
        for t in range(points):
            right_side = v_ref[c, t, :, lanes] - STEP_WEIGHT * n_ref[c, t, :, lanes]
            low = right_side if t == 0 else decay * low + right_side
            high = right_side if t == 0 else high + power_ref[t : t + 1, lanes] * right_side
        ends_ref[0, c] = low + share_ref[0, c, :, lanes]
        ends_ref[1, c] = high + share_ref[1, c, :, lanes]


def ends_terms(me, v, share, power, n, own):
    comps, _, planes, radial = v.shape
    return pl.pallas_call(
        functools.partial(ends_kernel, own=own),
        name="ends_own" if own else "ends_other",
        out_shape=held(2, comps, planes, radial // 2),
        in_specs=[SMEM] + [VMEM] * 4,
        out_specs=VMEM,
        compiler_params=params(v.size * 4, 4),
        cost_estimate=pl.CostEstimate(flops=20 * v.size, bytes_accessed=8 * v.size, transcendentals=0),
    )(me, v, share, power, n)


def chip_ends_kernel(me_ref, tap_ref, v_ref, chip_ref, power_ref, inner_ref, ready_ref, ends_ref, *, own):
    comps, points, _, radial = v_ref.shape
    reach = chip_ref.shape[1]
    core = me_ref[0] % 2
    count = radial // (2 * LANES)
    start = (core if own else 1 - core) * count

    def add(before):
        first = 0 if before else reach + 1

        @pl.loop(0, count)
        def column(i):
            k = start + i
            lanes = pl.ds(pl.multiple_of(k * LANES, LANES), LANES)
            here = pl.ds(pl.multiple_of(i * LANES, LANES), LANES)
            inv_r = STEP_WEIGHT * inverse_radius(LANES, k * LANES)
            weights = [tap_ref[first + j] for j in range(reach)]
            for c in range(comps):
                side = [chip_ref[c, h, :, lanes] for h in range(reach)]
                low, high = inner_ref[0, c, :, here], inner_ref[1, c, :, here]
                for u in range(reach):
                    t = u if before else points - reach + u
                    taps = [(h, h - u) for h in range(u, reach)] if before else [(h, reach - 1 + h - u) for h in range(u + 1)]
                    around = None
                    for h, w in taps:
                        term = weights[w] * side[h]
                        around = term if around is None else around + term
                    x = v_ref[1, t, :, lanes] * inv_r * around
                    low = low - power_ref[points - 1 - t : points - t, lanes] * x
                    high = high - power_ref[t : t + 1, lanes] * x
                ends_ref[0, c, :, here] = low
                ends_ref[1, c, :, here] = high

    pl.when(core == 0)(lambda: add(True))
    pl.when(core == 1)(lambda: add(False))


def chip_ends(me, taps, v, chip, power, inner, ready, own):
    return pl.pallas_call(
        functools.partial(chip_ends_kernel, own=own),
        name="chip_own" if own else "chip_other",
        out_shape=held(*inner.shape),
        in_specs=[SMEM] + [VMEM] * 5 + [ANY],
        out_specs=VMEM,
        compiler_params=params(v.size * 4, 4),
        cost_estimate=pl.CostEstimate(flops=SIDE, bytes_accessed=8 * v.size, transcendentals=0),
    )(me, taps, v, chip, power, inner, ready)


def planes_kernel(v_ref, y_ref, e_ref, ready_ref, n_in_ref, n_ref, y_tile_ref, e_tile_ref):
    comps, points, planes, _ = v_ref.shape
    carriers = y_ref.shape[1]
    weights = axial_weights(planes, False)
    rebuild_tiles(y_ref, y_tile_ref)
    rebuild_tiles(e_ref, e_tile_ref)
    for t in range(points):
        for c in range(comps):
            ref, tile_ref, i = (y_ref, y_tile_ref, c) if c < comps - 1 else (e_ref, e_tile_ref, 0)
            tile = ref[i, t] if t < carriers else tile_ref[i, t - carriers]
            n_ref[c, t] = n_in_ref[c, t] + v_ref[2, t] * axial_part(tile, weights)


def planes_terms(v, y, e, ready, n):
    comps, points, planes, radial = v.shape
    riders = points - y.shape[1]
    return pl.pallas_call(
        planes_kernel,
        name="planes_terms",
        out_shape=held(*v.shape),
        in_specs=[VMEM] * 3 + [ANY, VMEM],
        out_specs=VMEM,
        scratch_shapes=[pltpu.VMEM((k, riders, planes, radial), jnp.float32) for k in (comps - 1, 1)],
        input_output_aliases={4: 0},
        compiler_params=params(v.size * 4, 6),
        cost_estimate=pl.CostEstimate(flops=20 * v.size, bytes_accessed=16 * v.size, transcendentals=0),
    )(v, y, e, ready, n)


def table_kernel(me_ref, factor_ref, stencil_ref, row_ref, tap_ref, *, points, sectors):
    radial = row_ref.shape[1]
    one = jnp.ones((1, radial), jnp.float32)
    half = (0.5 * lax.rsqrt(factor_ref[0] * one)) / inverse_radius(radial)
    root = jnp.sqrt(1.0 + half * half)
    loss = 2.0 * half * (root - half)
    rows = [one]
    for _ in range(points):
        rows.append(rows[-1] * (1.0 - loss))
    total = loss
    left, result = points * sectors, None
    while left:
        if left & 1:
            result = total if result is None else result + total - result * total
        total = total * (2.0 - total)
        left >>= 1
    across = rows[points] * rows[points]
    rows += [half / root, 1.0 / result]
    before = after = one
    for bit in range(1, sectors.bit_length() - 1):
        upper = (me_ref[0] >> bit) % 2 == 1
        rows += [across, before, after]
        before, after = jnp.where(upper, before * across, before), jnp.where(upper, after, after * across)
        across = across * across
    for k, row in enumerate(rows + [before, after]):
        row_ref[k : k + 1] = row
    for k in range(tap_ref.shape[0]):
        tap_ref[k] = jnp.full(tap_ref.shape[1:], stencil_ref[k], jnp.float32)


def table(me, viscous_factor, stencil, points, sectors, planes, radial):
    count = points + 5 + 3 * (sectors.bit_length() - 2)
    return pl.pallas_call(
        functools.partial(table_kernel, points=points, sectors=sectors),
        name="table",
        out_shape=(held(count, radial), held(stencil.shape[0], planes, LANES)),
        in_specs=[SMEM, SMEM, SMEM],
        out_specs=(VMEM, VMEM),
        compiler_params=params(1 << 20, 1),
        cost_estimate=pl.CostEstimate(flops=1000 * radial, bytes_accessed=400 * radial, transcendentals=0),
    )(me, viscous_factor, stencil)


def sweep_kernel(v_ref, n_ref, power_ref, s_ref, nonlinear_ref, sem):
    leave = pltpu.make_async_copy(n_ref, nonlinear_ref, sem)
    leave.start()
    comps, points, planes, radial = v_ref.shape
    decay = power_ref[1:2]
    height = power_ref[points + 1 : points + 2]
    for c in range(comps):
        s_ref[c, 0] = height * (v_ref[c, 0] - STEP_WEIGHT * n_ref[c, 0])

        def forward(i):
            t = i + 1
            s_ref[c, t] = decay * s_ref[c, t - 1] + height * (v_ref[c, t] - STEP_WEIGHT * n_ref[c, t])

        each(points - 1, forward)

    def backward(i, carry):
        t = points - 1 - i
        after = []
        for c in range(comps):
            s_ref[c, t] = s_ref[c, t] + carry[c]
            after.append(decay * (carry[c] + height * (v_ref[c, t] - STEP_WEIGHT * n_ref[c, t])))
        return tuple(after)

    start = (jnp.zeros((planes, radial), jnp.float32),) * comps
    lax.fori_loop(0, points, backward, start, unroll=points <= UNROLL)
    leave.wait()


def sweep(v, n, power):
    return pl.pallas_call(
        sweep_kernel,
        name="sweep",
        out_shape=(held(*v.shape), jax.ShapeDtypeStruct(v.shape, v.dtype)),
        in_specs=[VMEM] * 3,
        out_specs=(VMEM, ANY),
        scratch_shapes=[pltpu.SemaphoreType.DMA],
        compiler_params=params(v.size * 4, 4),
        cost_estimate=pl.CostEstimate(flops=10 * v.size, bytes_accessed=12 * v.size, transcendentals=0),
    )(v, n, power)


def half_lanes(me_ref, half, own=True):
    core = me_ref[0] % 2
    return pl.ds(pl.multiple_of((core if own else 1 - core) * half, half), half)


def pair_kernel(me_ref, power_ref, own_ref, other_ref, block_ref, *, points):
    half = own_ref.shape[3]
    hop = power_ref[points : points + 1, half_lanes(me_ref, half)]
    odd = me_ref[0] % 2 == 1
    for c in range(own_ref.shape[1]):
        for side in range(2):
            own, other = own_ref[side, c], other_ref[side, c]
            far, near = (own, other) if side == 0 else (other, own)
            block_ref[side, c] = jnp.where(odd, hop * near + far, hop * far + near)


def pair(me, power, own, other, points):
    return pl.pallas_call(
        functools.partial(pair_kernel, points=points),
        name="pair",
        out_shape=held(*own.shape),
        in_specs=[SMEM, VMEM, VMEM, VMEM],
        out_specs=VMEM,
        compiler_params=params(own.size * 4, 8),
    )(me, power, own, other)


def merge_kernel(me_ref, power_ref, block_ref, other_ref, *refs, points, bit):
    *entry_refs, block_out_ref, entry_out_ref = refs
    comps, half = block_ref.shape[1], block_ref.shape[3]
    lanes = half_lanes(me_ref, half)
    first = points + 3 * bit
    across, before, after = [power_ref[first + k : first + k + 1, lanes] for k in range(3)]
    upper = (me_ref[0] >> bit) % 2 == 1
    before = jnp.where(upper, before, 0.0)
    after = jnp.where(upper, 0.0, after)
    for c in range(comps):
        low, high = block_ref[0, c], block_ref[1, c]
        other_low, other_high = other_ref[0, c], other_ref[1, c]
        block_out_ref[0, c] = jnp.where(upper, across * other_low + low, across * low + other_low)
        block_out_ref[1, c] = jnp.where(upper, other_high + across * high, high + across * other_high)
        for side, enters in enumerate((before * other_low, after * other_high)):
            entry_out_ref[side, c] = entry_refs[0][side, c] + enters if entry_refs else enters


def merge(me, power, block, other, entries, points, bit):
    return pl.pallas_call(
        functools.partial(merge_kernel, points=points, bit=bit),
        name="merge",
        out_shape=(held(*block.shape), held(*block.shape)),
        in_specs=[SMEM] + [VMEM] * (3 + len(entries)),
        out_specs=(VMEM, VMEM),
        compiler_params=params(block.size * 4, 8),
    )(me, power, block, other, *entries)


def enter_kernel(me_ref, power_ref, block_ref, entry_ref, own_ref, other_ref, ready_ref, mine_ref, send_ref, *, points):
    comps, half = block_ref.shape[1], block_ref.shape[3]
    lanes = half_lanes(me_ref, half)
    row = lambda k: power_ref[k : k + 1, lanes]
    hop, height, wrap = row(points), row(points + 1), row(points + 2)
    last = power_ref.shape[0]
    before, after = row(last - 2) * wrap, row(last - 1) * wrap
    odd = me_ref[0] % 2 == 1
    for c in range(comps):
        low = height * (entry_ref[0, c] + before * block_ref[0, c])
        high = height * (entry_ref[1, c] + after * block_ref[1, c])
        even_low = height * jnp.where(odd, other_ref[0, c], own_ref[0, c])
        odd_high = height * jnp.where(odd, own_ref[1, c], other_ref[1, c])
        even_in = (low, odd_high + hop * high)
        odd_in = (even_low + hop * low, high)
        for side in range(2):
            mine_ref[side, c] = jnp.where(odd, odd_in[side], even_in[side])
            send_ref[side, c] = jnp.where(odd, even_in[side], odd_in[side])


def enter(me, power, block, entry, own, other, ready, points):
    return pl.pallas_call(
        functools.partial(enter_kernel, points=points),
        name="enter",
        out_shape=(held(*block.shape), held(*block.shape)),
        in_specs=[SMEM] + [VMEM] * 5 + [ANY],
        out_specs=(VMEM, VMEM),
        compiler_params=params(block.size * 4, 12),
    )(me, power, block, entry, own, other, ready)


def close_kernel(me_ref, s_ref, power_ref, entry_ref, *refs, own):
    out_ref, x_ref, sems = refs[-3:]
    comps, points, _, _ = s_ref.shape
    chunk = points // sems.shape[1]
    lanes = half_lanes(me_ref, entry_ref.shape[3], own)
    leaves = []
    for c in range(comps):
        before, after = entry_ref[0, c], entry_ref[1, c]
        for k in range(sems.shape[1]):
            for t in range(k * chunk, (k + 1) * chunk):
                decayed = power_ref[t + 1 : t + 2, lanes] * before + power_ref[points - t : points - t + 1, lanes] * after
                x_ref[c, t] = s_ref[c, t, :, lanes] + decayed
            some = pl.ds(k * chunk, chunk)
            leaves.append(pltpu.make_async_copy(x_ref.at[c, some], out_ref.at[c, some, :, lanes], sems.at[c, k]))
            leaves[-1].start()
    for leave in leaves:
        leave.wait()


def close(me, s, power, entry, out, own):
    comps, points, planes, radial = s.shape
    return pl.pallas_call(
        functools.partial(close_kernel, own=own),
        name="close_own" if own else "close_other",
        out_shape=jax.ShapeDtypeStruct(s.shape, s.dtype),
        in_specs=[SMEM] + [VMEM] * 3 + [ANY] * len(out),
        out_specs=ANY,
        scratch_shapes=[
            pltpu.VMEM((comps, points, planes, radial // 2), jnp.float32),
            pltpu.SemaphoreType.DMA((comps, 4 if points % 4 == 0 else 1)),
        ],
        input_output_aliases={4: 0} if out else {},
        compiler_params=params(s.size * 4, 5),
        cost_estimate=pl.CostEstimate(flops=4 * s.size, bytes_accessed=8 * s.size, transcendentals=0),
    )(me, s, power, entry, *out)


def local(velocity, radial_op, azimuth_stencil, viscous_factor):
    sectors = lax.axis_size("theta")
    comps, points, planes, radial = velocity.shape
    reach = (azimuth_stencil.shape[0] - 1) // 2
    width = radial_op.shape[1] - radial
    me = lax.axis_index("theta").astype(jnp.int32).reshape(1)
    op = radial_op.T

    velocity, axial_out = load(pltpu.with_memory_space_constraint(velocity, pltpu.HBM))
    axial_in = swap(axial_out, "gz", 1)
    chip_out = pack_side(me, velocity, axial_out, reach, False)
    chip_in = swap_across(chip_out, "theta")
    mirror_out = pack_mirror(velocity, chip_out, width)
    mirror_in = swap(mirror_out, "theta", sectors // 2)
    core_out = pack_side(me, velocity, axial_in, reach, True)
    core_in = swap(core_out, "theta", 1)
    power, taps = table(me, viscous_factor, azimuth_stencil, points, sectors, planes, radial)
    n = inner_terms(taps, velocity, op)
    share_out = share_terms(velocity, axial_in, power)
    share_in = swap(share_out, "gz", 1)
    planes_in = swap(pack_planes(velocity, share_out), "gz", 1)
    n = side_terms(core_kernel, "core_terms", me, taps, velocity, core_in, n)
    n = mirror_terms(velocity, op, mirror_in, n)
    inner_other = ends_terms(me, velocity, share_in, power, n, False)
    inner_own = ends_terms(me, velocity, share_in, power, n, True)
    send = chip_ends(me, taps, velocity, chip_in, power, inner_other, inner_own, False)
    other = swap(send, "theta", 1)
    own = chip_ends(me, taps, velocity, chip_in, power, inner_own, send, True)
    n = side_terms(late_kernel, "late_terms", me, taps, velocity, chip_in, n, (own,))
    block = pair(me, power, own, other, points)
    entries = ()
    last = sectors.bit_length() - 2
    for bit in range(1, last + 1):
        if bit == last:
            n = planes_terms(velocity, planes_in, axial_in, block, n)
            s, nonlinear = sweep(velocity, n, power)
        block, entry = merge(me, power, block, swap(block, "theta", 1 << bit), entries, points, bit)
        entries = (entry,)
    mine, send = enter(me, power, block, entry, own, other, s, points)
    got = swap(send, "theta", 1)
    new_velocity = close(me, s, power, mine, (), True)
    new_velocity = close(me, s, power, got, (new_velocity,), False)
    return (new_velocity, nonlinear)


def solution(mesh):
    in_specs = (P(None, "theta", "gz", None), P(), P(), P())
    out_specs = (P(None, "theta", "gz", None), P(None, "theta", "gz", None))
    return jax.shard_map(local, mesh=mesh, in_specs=in_specs, out_specs=out_specs, check_vma=False)
```

```python
import functools

import jax
import jax.numpy as jnp
from jax import lax
from jax.experimental import pallas as pl
from jax.experimental.pallas import tpu as pltpu
from jax.sharding import PartitionSpec as P

AXIAL_WEIGHTS = (0.75, -0.15, 1.0 / 60.0)
AXIAL_REACH = len(AXIAL_WEIGHTS)
STEP_WEIGHT = 0.2
MIRROR_SIGNS = (-1.0, -1.0, 1.0)
LANES = 128
UNROLL = 16
INNER = 10 << 29
MIRROR = 1 << 26
SIDE = 1 << 26

VMEM = pl.BlockSpec(memory_space=pltpu.VMEM)
SMEM = pl.BlockSpec(memory_space=pltpu.SMEM)
ANY = pl.BlockSpec(memory_space=pl.ANY)
HBM = pl.BlockSpec(memory_space=pltpu.HBM)


def params(block_bytes, blocks):
    return pltpu.CompilerParams(vmem_limit_bytes=(2 << 20) + blocks * block_bytes)


def held(*shape):
    return pltpu.VMEM(shape, jnp.float32)


def each(count, body):
    if count <= UNROLL:
        for i in range(count):
            body(i)
    else:
        pl.loop(0, count)(body)


def swap(block, axis, bit):
    size = lax.axis_size(axis)
    return lax.ppermute(block, axis, [(i, i ^ bit) for i in range(size)])


def swap_across(block, axis):
    size = lax.axis_size(axis)
    route = []
    for odd in range(1, size, 2):
        route += [(odd, (odd + 1) % size), ((odd + 1) % size, odd)]
    return lax.ppermute(block, axis, route)


def split(x):
    high = x.astype(jnp.bfloat16)
    return high, (x - high.astype(jnp.float32)).astype(jnp.bfloat16)


def product(left, right):
    dot = functools.partial(jnp.dot, preferred_element_type=jnp.float32)
    return dot(left[0], right[0]) + (dot(left[0], right[1]) + dot(left[1], right[0]))


def pack_tiles(v_ref, y_ref, comps):
    points, planes = v_ref.shape[1:3]
    carriers = y_ref.shape[1]
    lo, hi = AXIAL_REACH, planes - AXIAL_REACH
    for i, c in enumerate(comps):

        def carry(t):
            y_ref[i, t] = v_ref[c, t]

        def ride(j):
            t = carriers + j
            y_ref[i, 3 * j, lo:hi] = v_ref[c, t, 0:2]
            y_ref[i, 3 * j + 1, lo : lo + 1] = v_ref[c, t, 2:3]
            y_ref[i, 3 * j + 1, lo + 1 : hi] = v_ref[c, t, hi : hi + 1]
            y_ref[i, 3 * j + 2, lo:hi] = v_ref[c, t, hi + 1 :]

        each(carriers, carry)
        each(points - carriers, ride)


def rebuild_tiles(y_ref, tile_ref):
    carriers = y_ref.shape[1]
    comps, riders, planes, radial = tile_ref.shape
    lo, hi = AXIAL_REACH, planes - AXIAL_REACH
    for c in range(comps):
        for j in range(riders):
            tile_ref[c, j, 0:2] = y_ref[c, 3 * j, lo:hi]
            tile_ref[c, j, 2:3] = y_ref[c, 3 * j + 1, lo : lo + 1]
            tile_ref[c, j, lo:hi] = jnp.zeros((hi - lo, radial), jnp.float32)
            tile_ref[c, j, hi : hi + 1] = y_ref[c, 3 * j + 1, lo + 1 : hi]
            tile_ref[c, j, hi + 1 :] = y_ref[c, 3 * j + 2, lo:hi]


def load_axial_kernel(hbm_ref, y_ref, e_ref, sem):
    load = pltpu.make_async_copy(hbm_ref.at[pl.ds(hbm_ref.shape[0] - 1, 1)], e_ref, sem)
    load.start()
    load.wait()
    pack_tiles(e_ref, y_ref, (0,))


def load_axial(v):
    comps, points, planes, radial = v.shape
    return pl.pallas_call(
        load_axial_kernel,
        name="load_axial",
        out_shape=held(1, points - points // 4, planes, radial),
        in_specs=[HBM],
        out_specs=VMEM,
        scratch_shapes=[pltpu.VMEM((1, points, planes, radial), jnp.float32), pltpu.SemaphoreType.DMA],
        compiler_params=params(v.size * 4, 2),
    )(v)


def pack_planes_kernel(v_ref, first_ref, y_ref):
    pack_tiles(v_ref, y_ref, range(y_ref.shape[0]))


def pack_planes(v, first):
    comps, points, planes, radial = v.shape
    return pl.pallas_call(
        pack_planes_kernel,
        name="pack_planes",
        out_shape=held(comps - 1, points - points // 4, planes, radial),
        in_specs=[VMEM, ANY],
        out_specs=VMEM,
        compiler_params=params(v.size * 4, 2),
    )(v, first)


def pack_side_kernel(me_ref, v_ref, first_ref, side_ref, *, after):
    points, reach = v_ref.shape[1], side_ref.shape[1]

    def put(start):
        for c in range(v_ref.shape[0]):
            for h in range(reach):
                side_ref[c, h] = v_ref[c, start + h]

    even = me_ref[0] % 2 == 0
    last = even if after else jnp.logical_not(even)
    pl.when(last)(lambda: put(points - reach))
    pl.when(jnp.logical_not(last))(lambda: put(0))


def pack_side(me, v, first, reach, after):
    comps, _, planes, radial = v.shape
    return pl.pallas_call(
        functools.partial(pack_side_kernel, after=after),
        name="pack_core" if after else "pack_chip",
        out_shape=held(comps, reach, planes, radial),
        in_specs=[SMEM, VMEM, ANY],
        out_specs=VMEM,
        compiler_params=params(v.size * 4, 3),
    )(me, v, first)


def pack_mirror_kernel(v_ref, first_ref, mirror_ref):
    points, tiles = v_ref.shape[1], mirror_ref.shape[1]
    width = LANES // (points // tiles)
    lane = lax.broadcasted_iota(jnp.int32, mirror_ref.shape[2:], 1)

    def put(p):
        for c in range(v_ref.shape[0]):
            tile = v_ref[c, p, :, :LANES]
            for q in range(1, points // tiles):
                part = pltpu.roll(v_ref[c, q * tiles + p, :, :LANES], q * width, 1)
                tile = jnp.where(lane < q * width, tile, part)
            mirror_ref[c, p] = tile

    each(tiles, put)


def pack_mirror(v, first, width):
    comps, points, planes, _ = v.shape
    return pl.pallas_call(
        pack_mirror_kernel,
        name="pack_mirror",
        out_shape=held(comps, points // (LANES // width), planes, LANES),
        in_specs=[VMEM, ANY],
        out_specs=VMEM,
        compiler_params=params(v.size * 4, 2),
    )(v, first)


def inverse_radius(radial, start=0):
    return 1.0 / ((lax.broadcasted_iota(jnp.int32, (1, radial), 1) + start).astype(jnp.float32) + 0.5)


def axial_weights(planes, inside):
    row = lax.broadcasted_iota(jnp.int32, (planes, LANES), 0)
    weights = []
    for m, w in enumerate(AXIAL_WEIGHTS, 1):
        for shift, own, sign in ((m, row < planes - m, 1.0), (planes - m, row >= m, -1.0)):
            keep = own if inside else jnp.logical_not(own)
            weights.append((shift, jnp.where(keep, sign * w, 0.0)))
    return weights


def axial_part(tile, weights):
    planes, width = tile.shape
    weights = [(shift, jnp.concatenate([weight] * (width // LANES), axis=1)) for shift, weight in weights]
    total = None
    for shift, weight in weights:
        term = weight * pltpu.roll(tile, planes - shift, 0)
        total = term if total is None else total + term
    return total


def mirror_kernel(v_ref, op_ref, mirror_ref, n_in_ref, n_ref, grad_ref):
    comps, points, planes, radial = v_ref.shape
    tiles = mirror_ref.shape[1]
    count = points // tiles
    width = LANES // count
    rows = tiles * planes
    right = split(jnp.concatenate([op_ref[radial:]] * count, axis=0))
    lane = lax.broadcasted_iota(jnp.int32, (rows, LANES), 1)
    for c in range(comps):
        high, low = split(MIRROR_SIGNS[c] * mirror_ref[c].reshape(rows, LANES))
        zero = jnp.zeros_like(high)
        parts = [
            [jnp.where((lane >= q * width) & (lane < (q + 1) * width), x, zero) for q in range(count)]
            for x in (high, low)
        ]
        left = [jnp.concatenate(x, axis=0) for x in parts]
        grad_ref[c * points * planes : (c + 1) * points * planes] = product(left, right)

    def finish(t):
        for c in range(comps):
            start = pl.multiple_of((c * points + t) * planes, planes)
            n_ref[c, t] = n_in_ref[c, t] + v_ref[0, t] * grad_ref[pl.ds(start, planes)]

    each(points, finish)


def mirror_terms(v, op, mirror, n):
    return pl.pallas_call(
        mirror_kernel,
        name="mirror_terms",
        out_shape=held(*v.shape),
        in_specs=[VMEM] * 4,
        out_specs=VMEM,
        scratch_shapes=[pltpu.VMEM((v.size // v.shape[3], v.shape[3]), jnp.float32)],
        input_output_aliases={3: 0},
        compiler_params=params(v.size * 4, 8),
        cost_estimate=pl.CostEstimate(flops=MIRROR, bytes_accessed=16 * v.size, transcendentals=0),
    )(v, op, mirror, n)


def inner_kernel(tap_ref, v_ref, op_ref, n_ref, grad_ref):
    comps, points, planes, radial = v_ref.shape
    reach = (tap_ref.shape[0] - 1) // 2
    rows = points * planes
    right = split(op_ref[:radial])
    for c in range(comps):
        grad_ref[c * rows : (c + 1) * rows] = product(split(v_ref[c].reshape(rows, radial)), right)
    weights = axial_weights(planes, True)

    @pl.loop(0, radial // LANES)
    def column(k):
        lanes = pl.ds(pl.multiple_of(k * LANES, LANES), LANES)
        inv_r = inverse_radius(LANES, k * LANES)
        for c in range(comps):
            for t in range(points):
                a, b, e = [v_ref[i, t, :, lanes] for i in range(3)]
                b_inv = b * inv_r
                around = None
                for m in range(max(-reach, -t), min(reach, points - 1 - t) + 1):
                    term = tap_ref[m + reach] * v_ref[c, t + m, :, lanes]
                    around = term if around is None else around + term
                start = c * rows + t * planes
                n = a * grad_ref[start : start + planes, lanes] + b_inv * around
                n = n + e * axial_part(v_ref[c, t, :, lanes], weights)
                if c == 0:
                    n = n - b_inv * b
                elif c == 1:
                    n = n + a * b_inv
                n_ref[c, t, :, lanes] = n


def inner_terms(taps, v, op):
    return pl.pallas_call(
        inner_kernel,
        name="inner_terms",
        out_shape=held(*v.shape),
        in_specs=[VMEM] * 3,
        out_specs=VMEM,
        scratch_shapes=[pltpu.VMEM((v.size // v.shape[3], v.shape[3]), jnp.float32)],
        compiler_params=params(v.size * 4, 7),
        cost_estimate=pl.CostEstimate(flops=INNER, bytes_accessed=16 * v.size, transcendentals=0),
    )(taps, v, op)


def add_side(tap_ref, v_ref, side_ref, n_in_ref, n_ref, before, columns):
    comps, points, _, radial = v_ref.shape
    reach = side_ref.shape[1]
    first = 0 if before else reach + 1

    start, count = columns

    @pl.loop(0, count)
    def column(i):
        k = start + i
        lanes = pl.ds(pl.multiple_of(k * LANES, LANES), LANES)
        inv_r = inverse_radius(LANES, k * LANES)
        weights = [tap_ref[first + i] for i in range(reach)]
        for c in range(comps):
            side = [side_ref[c, h, :, lanes] for h in range(reach)]
            for u in range(reach):
                t = u if before else points - reach + u
                taps = [(h, h - u) for h in range(u, reach)] if before else [(h, reach - 1 + h - u) for h in range(u + 1)]
                around = None
                for h, w in taps:
                    term = weights[w] * side[h]
                    around = term if around is None else around + term
                n_ref[c, t, :, lanes] = n_in_ref[c, t, :, lanes] + v_ref[1, t, :, lanes] * inv_r * around


def core_kernel(me_ref, tap_ref, v_ref, core_ref, n_in_ref, n_ref):
    even = me_ref[0] % 2 == 0
    columns = (0, v_ref.shape[3] // LANES)
    add = functools.partial(add_side, tap_ref, v_ref, core_ref, n_in_ref, n_ref, columns=columns)
    pl.when(even)(lambda: add(before=False))
    pl.when(jnp.logical_not(even))(lambda: add(before=True))


def late_kernel(me_ref, tap_ref, v_ref, chip_ref, n_in_ref, ready_ref, n_ref):
    even = me_ref[0] % 2 == 0
    columns = (0, v_ref.shape[3] // LANES)
    add = functools.partial(add_side, tap_ref, v_ref, chip_ref, n_in_ref, n_ref, columns=columns)
    pl.when(even)(lambda: add(before=True))
    pl.when(jnp.logical_not(even))(lambda: add(before=False))


def side_terms(kernel, name, me, taps, v, side, n, ready=()):
    return pl.pallas_call(
        kernel,
        name=name,
        out_shape=held(*v.shape),
        in_specs=[SMEM] + [VMEM] * 4 + [ANY] * len(ready),
        out_specs=VMEM,
        input_output_aliases={4: 0},
        compiler_params=params(v.size * 4, 5),
        cost_estimate=pl.CostEstimate(flops=SIDE, bytes_accessed=12 * v.size, transcendentals=0),
    )(me, taps, v, side, n, *ready)


def share_kernel(v_ref, e_ref, power_ref, ends_ref, tile_ref):
    comps, points, planes, radial = v_ref.shape
    carriers = e_ref.shape[1]
    weights = axial_weights(planes, False)
    rebuild_tiles(e_ref, tile_ref)
    decay = power_ref[1:2]
    ends_ref[...] = jnp.zeros_like(ends_ref)
    for t in range(points):
        e = STEP_WEIGHT * (e_ref[0, t] if t < carriers else tile_ref[0, t - carriers])
        for c in range(comps):
            right_side = e * axial_part(v_ref[c, t], weights)
            ends_ref[0, c] = decay * ends_ref[0, c] - right_side
            ends_ref[1, c] = ends_ref[1, c] - power_ref[t : t + 1] * right_side


def share_terms(v, e, power):
    comps, points, planes, radial = v.shape
    return pl.pallas_call(
        share_kernel,
        name="share_terms",
        out_shape=held(2, comps, planes, radial),
        in_specs=[VMEM] * 3,
        out_specs=VMEM,
        scratch_shapes=[pltpu.VMEM((1, points - e.shape[1], planes, radial), jnp.float32)],
        compiler_params=params(v.size * 4, 4),
        cost_estimate=pl.CostEstimate(flops=20 * v.size, bytes_accessed=8 * v.size, transcendentals=0),
    )(v, e, power)


def ends_kernel(me_ref, v_ref, share_ref, power_ref, n_ref, ends_ref, *, own):
    comps, points, _, radial = v_ref.shape
    lanes = half_lanes(me_ref, radial // 2, own)
    decay = power_ref[1:2, lanes]
    for c in range(comps):
        low = high = None
        for t in range(points):
            right_side = v_ref[c, t, :, lanes] - STEP_WEIGHT * n_ref[c, t, :, lanes]
            low = right_side if t == 0 else decay * low + right_side
            high = right_side if t == 0 else high + power_ref[t : t + 1, lanes] * right_side
        ends_ref[0, c] = low + share_ref[0, c, :, lanes]
        ends_ref[1, c] = high + share_ref[1, c, :, lanes]


def ends_terms(me, v, share, power, n, own):
    comps, _, planes, radial = v.shape
    return pl.pallas_call(
        functools.partial(ends_kernel, own=own),
        name="ends_own" if own else "ends_other",
        out_shape=held(2, comps, planes, radial // 2),
        in_specs=[SMEM] + [VMEM] * 4,
        out_specs=VMEM,
        compiler_params=params(v.size * 4, 4),
        cost_estimate=pl.CostEstimate(flops=20 * v.size, bytes_accessed=8 * v.size, transcendentals=0),
    )(me, v, share, power, n)


def chip_ends_kernel(me_ref, tap_ref, v_ref, chip_ref, power_ref, inner_ref, ready_ref, ends_ref, *, own):
    comps, points, _, radial = v_ref.shape
    reach = chip_ref.shape[1]
    core = me_ref[0] % 2
    count = radial // (2 * LANES)
    start = (core if own else 1 - core) * count

    def add(before):
        first = 0 if before else reach + 1

        @pl.loop(0, count)
        def column(i):
            k = start + i
            lanes = pl.ds(pl.multiple_of(k * LANES, LANES), LANES)
            here = pl.ds(pl.multiple_of(i * LANES, LANES), LANES)
            inv_r = STEP_WEIGHT * inverse_radius(LANES, k * LANES)
            weights = [tap_ref[first + j] for j in range(reach)]
            for c in range(comps):
                side = [chip_ref[c, h, :, lanes] for h in range(reach)]
                low, high = inner_ref[0, c, :, here], inner_ref[1, c, :, here]
                for u in range(reach):
                    t = u if before else points - reach + u
                    taps = [(h, h - u) for h in range(u, reach)] if before else [(h, reach - 1 + h - u) for h in range(u + 1)]
                    around = None
                    for h, w in taps:
                        term = weights[w] * side[h]
                        around = term if around is None else around + term
                    x = v_ref[1, t, :, lanes] * inv_r * around
                    low = low - power_ref[points - 1 - t : points - t, lanes] * x
                    high = high - power_ref[t : t + 1, lanes] * x
                ends_ref[0, c, :, here] = low
                ends_ref[1, c, :, here] = high

    pl.when(core == 0)(lambda: add(True))
    pl.when(core == 1)(lambda: add(False))


def chip_ends(me, taps, v, chip, power, inner, ready, own):
    return pl.pallas_call(
        functools.partial(chip_ends_kernel, own=own),
        name="chip_own" if own else "chip_other",
        out_shape=held(*inner.shape),
        in_specs=[SMEM] + [VMEM] * 5 + [ANY],
        out_specs=VMEM,
        compiler_params=params(v.size * 4, 4),
        cost_estimate=pl.CostEstimate(flops=SIDE, bytes_accessed=8 * v.size, transcendentals=0),
    )(me, taps, v, chip, power, inner, ready)


def planes_kernel(v_ref, y_ref, e_ref, ready_ref, n_in_ref, n_ref, y_tile_ref, e_tile_ref):
    comps, points, planes, _ = v_ref.shape
    carriers = y_ref.shape[1]
    weights = axial_weights(planes, False)
    rebuild_tiles(y_ref, y_tile_ref)
    rebuild_tiles(e_ref, e_tile_ref)
    for t in range(points):
        for c in range(comps):
            ref, tile_ref, i = (y_ref, y_tile_ref, c) if c < comps - 1 else (e_ref, e_tile_ref, 0)
            tile = ref[i, t] if t < carriers else tile_ref[i, t - carriers]
            n_ref[c, t] = n_in_ref[c, t] + v_ref[2, t] * axial_part(tile, weights)


def planes_terms(v, y, e, ready, n):
    comps, points, planes, radial = v.shape
    riders = points - y.shape[1]
    return pl.pallas_call(
        planes_kernel,
        name="planes_terms",
        out_shape=held(*v.shape),
        in_specs=[VMEM] * 3 + [ANY, VMEM],
        out_specs=VMEM,
        scratch_shapes=[pltpu.VMEM((k, riders, planes, radial), jnp.float32) for k in (comps - 1, 1)],
        input_output_aliases={4: 0},
        compiler_params=params(v.size * 4, 6),
        cost_estimate=pl.CostEstimate(flops=20 * v.size, bytes_accessed=16 * v.size, transcendentals=0),
    )(v, y, e, ready, n)


def table_kernel(me_ref, factor_ref, stencil_ref, row_ref, tap_ref, *, points, sectors):
    radial = row_ref.shape[1]
    one = jnp.ones((1, radial), jnp.float32)
    half = (0.5 * lax.rsqrt(factor_ref[0] * one)) / inverse_radius(radial)
    root = jnp.sqrt(1.0 + half * half)
    loss = 2.0 * half * (root - half)
    rows = [one]
    for _ in range(points):
        rows.append(rows[-1] * (1.0 - loss))
    total = loss
    left, result = points * sectors, None
    while left:
        if left & 1:
            result = total if result is None else result + total - result * total
        total = total * (2.0 - total)
        left >>= 1
    across = rows[points] * rows[points]
    rows += [half / root, 1.0 / result]
    before = after = one
    for bit in range(1, sectors.bit_length() - 1):
        upper = (me_ref[0] >> bit) % 2 == 1
        rows += [across, before, after]
        before, after = jnp.where(upper, before * across, before), jnp.where(upper, after, after * across)
        across = across * across
    for k, row in enumerate(rows + [before, after]):
        row_ref[k : k + 1] = row
    for k in range(tap_ref.shape[0]):
        tap_ref[k] = jnp.full(tap_ref.shape[1:], stencil_ref[k], jnp.float32)


def table(me, viscous_factor, stencil, points, sectors, planes, radial):
    count = points + 5 + 3 * (sectors.bit_length() - 2)
    return pl.pallas_call(
        functools.partial(table_kernel, points=points, sectors=sectors),
        name="table",
        out_shape=(held(count, radial), held(stencil.shape[0], planes, LANES)),
        in_specs=[SMEM, SMEM, SMEM],
        out_specs=(VMEM, VMEM),
        compiler_params=params(1 << 20, 1),
        cost_estimate=pl.CostEstimate(flops=1000 * radial, bytes_accessed=400 * radial, transcendentals=0),
    )(me, viscous_factor, stencil)


def sweep_kernel(v_ref, n_ref, power_ref, s_ref, nonlinear_ref, sem):
    leave = pltpu.make_async_copy(n_ref, nonlinear_ref, sem)
    leave.start()
    comps, points, planes, radial = v_ref.shape
    decay = power_ref[1:2]
    height = power_ref[points + 1 : points + 2]
    for c in range(comps):
        s_ref[c, 0] = height * (v_ref[c, 0] - STEP_WEIGHT * n_ref[c, 0])

        def forward(i):
            t = i + 1
            s_ref[c, t] = decay * s_ref[c, t - 1] + height * (v_ref[c, t] - STEP_WEIGHT * n_ref[c, t])

        each(points - 1, forward)

    def backward(i, carry):
        t = points - 1 - i
        after = []
        for c in range(comps):
            s_ref[c, t] = s_ref[c, t] + carry[c]
            after.append(decay * (carry[c] + height * (v_ref[c, t] - STEP_WEIGHT * n_ref[c, t])))
        return tuple(after)

    start = (jnp.zeros((planes, radial), jnp.float32),) * comps
    lax.fori_loop(0, points, backward, start, unroll=points <= UNROLL)
    leave.wait()


def sweep(v, n, power):
    return pl.pallas_call(
        sweep_kernel,
        name="sweep",
        out_shape=(held(*v.shape), jax.ShapeDtypeStruct(v.shape, v.dtype)),
        in_specs=[VMEM] * 3,
        out_specs=(VMEM, ANY),
        scratch_shapes=[pltpu.SemaphoreType.DMA],
        compiler_params=params(v.size * 4, 4),
        cost_estimate=pl.CostEstimate(flops=10 * v.size, bytes_accessed=12 * v.size, transcendentals=0),
    )(v, n, power)


def half_lanes(me_ref, half, own=True):
    core = me_ref[0] % 2
    return pl.ds(pl.multiple_of((core if own else 1 - core) * half, half), half)


def pair_kernel(me_ref, power_ref, own_ref, other_ref, block_ref, *, points):
    half = own_ref.shape[3]
    hop = power_ref[points : points + 1, half_lanes(me_ref, half)]
    odd = me_ref[0] % 2 == 1
    for c in range(own_ref.shape[1]):
        for side in range(2):
            own, other = own_ref[side, c], other_ref[side, c]
            far, near = (own, other) if side == 0 else (other, own)
            block_ref[side, c] = jnp.where(odd, hop * near + far, hop * far + near)


def pair(me, power, own, other, points):
    return pl.pallas_call(
        functools.partial(pair_kernel, points=points),
        name="pair",
        out_shape=held(*own.shape),
        in_specs=[SMEM, VMEM, VMEM, VMEM],
        out_specs=VMEM,
        compiler_params=params(own.size * 4, 8),
    )(me, power, own, other)


def merge_kernel(me_ref, power_ref, block_ref, other_ref, *refs, points, bit):
    *entry_refs, block_out_ref, entry_out_ref = refs
    comps, half = block_ref.shape[1], block_ref.shape[3]
    lanes = half_lanes(me_ref, half)
    first = points + 3 * bit
    across, before, after = [power_ref[first + k : first + k + 1, lanes] for k in range(3)]
    upper = (me_ref[0] >> bit) % 2 == 1
    before = jnp.where(upper, before, 0.0)
    after = jnp.where(upper, 0.0, after)
    for c in range(comps):
        low, high = block_ref[0, c], block_ref[1, c]
        other_low, other_high = other_ref[0, c], other_ref[1, c]
        block_out_ref[0, c] = jnp.where(upper, across * other_low + low, across * low + other_low)
        block_out_ref[1, c] = jnp.where(upper, other_high + across * high, high + across * other_high)
        for side, enters in enumerate((before * other_low, after * other_high)):
            entry_out_ref[side, c] = entry_refs[0][side, c] + enters if entry_refs else enters


def merge(me, power, block, other, entries, points, bit):
    return pl.pallas_call(
        functools.partial(merge_kernel, points=points, bit=bit),
        name="merge",
        out_shape=(held(*block.shape), held(*block.shape)),
        in_specs=[SMEM] + [VMEM] * (3 + len(entries)),
        out_specs=(VMEM, VMEM),
        compiler_params=params(block.size * 4, 8),
    )(me, power, block, other, *entries)


def enter_kernel(me_ref, power_ref, block_ref, entry_ref, own_ref, other_ref, ready_ref, mine_ref, send_ref, *, points):
    comps, half = block_ref.shape[1], block_ref.shape[3]
    lanes = half_lanes(me_ref, half)
    row = lambda k: power_ref[k : k + 1, lanes]
    hop, height, wrap = row(points), row(points + 1), row(points + 2)
    last = power_ref.shape[0]
    before, after = row(last - 2) * wrap, row(last - 1) * wrap
    odd = me_ref[0] % 2 == 1
    for c in range(comps):
        low = height * (entry_ref[0, c] + before * block_ref[0, c])
        high = height * (entry_ref[1, c] + after * block_ref[1, c])
        even_low = height * jnp.where(odd, other_ref[0, c], own_ref[0, c])
        odd_high = height * jnp.where(odd, own_ref[1, c], other_ref[1, c])
        even_in = (low, odd_high + hop * high)
        odd_in = (even_low + hop * low, high)
        for side in range(2):
            mine_ref[side, c] = jnp.where(odd, odd_in[side], even_in[side])
            send_ref[side, c] = jnp.where(odd, even_in[side], odd_in[side])


def enter(me, power, block, entry, own, other, ready, points):
    return pl.pallas_call(
        functools.partial(enter_kernel, points=points),
        name="enter",
        out_shape=(held(*block.shape), held(*block.shape)),
        in_specs=[SMEM] + [VMEM] * 5 + [ANY],
        out_specs=(VMEM, VMEM),
        compiler_params=params(block.size * 4, 12),
    )(me, power, block, entry, own, other, ready)


def close_kernel(me_ref, s_ref, power_ref, entry_ref, *refs, own):
    out_ref, x_ref, sems = refs[-3:]
    comps, points, _, _ = s_ref.shape
    lanes = half_lanes(me_ref, entry_ref.shape[3], own)
    leaves = []
    for c in range(comps):
        before, after = entry_ref[0, c], entry_ref[1, c]

        def point(t):
            decayed = power_ref[pl.ds(t + 1, 1), lanes] * before + power_ref[pl.ds(points - t, 1), lanes] * after
            x_ref[c, t] = s_ref[c, t, :, lanes] + decayed

        each(points, point)
        leaves.append(pltpu.make_async_copy(x_ref.at[c], out_ref.at[c, :, :, lanes], sems.at[c]))
        leaves[c].start()
    for leave in leaves:
        leave.wait()


def close(me, s, power, entry, out, own):
    comps, points, planes, radial = s.shape
    return pl.pallas_call(
        functools.partial(close_kernel, own=own),
        name="close_own" if own else "close_other",
        out_shape=jax.ShapeDtypeStruct(s.shape, s.dtype),
        in_specs=[SMEM] + [VMEM] * 3 + [ANY] * len(out),
        out_specs=ANY,
        scratch_shapes=[
            pltpu.VMEM((comps, points, planes, radial // 2), jnp.float32),
            pltpu.SemaphoreType.DMA((comps,)),
        ],
        input_output_aliases={4: 0} if out else {},
        compiler_params=params(s.size * 4, 5),
        cost_estimate=pl.CostEstimate(flops=4 * s.size, bytes_accessed=8 * s.size, transcendentals=0),
    )(me, s, power, entry, *out)


def local(velocity, radial_op, azimuth_stencil, viscous_factor):
    sectors = lax.axis_size("theta")
    comps, points, planes, radial = velocity.shape
    reach = (azimuth_stencil.shape[0] - 1) // 2
    width = radial_op.shape[1] - radial
    me = lax.axis_index("theta").astype(jnp.int32).reshape(1)
    op = radial_op.T

    axial_out = load_axial(pltpu.with_memory_space_constraint(velocity, pltpu.HBM))
    axial_in = swap(axial_out, "gz", 1)
    chip_out = pack_side(me, velocity, axial_out, reach, False)
    chip_in = swap_across(chip_out, "theta")
    mirror_out = pack_mirror(velocity, chip_out, width)
    mirror_in = swap(mirror_out, "theta", sectors // 2)
    core_out = pack_side(me, velocity, axial_in, reach, True)
    core_in = swap(core_out, "theta", 1)
    power, taps = table(me, viscous_factor, azimuth_stencil, points, sectors, planes, radial)
    n = inner_terms(taps, velocity, op)
    share_out = share_terms(velocity, axial_in, power)
    share_in = swap(share_out, "gz", 1)
    planes_in = swap(pack_planes(velocity, share_out), "gz", 1)
    n = side_terms(core_kernel, "core_terms", me, taps, velocity, core_in, n)
    n = mirror_terms(velocity, op, mirror_in, n)
    inner_other = ends_terms(me, velocity, share_in, power, n, False)
    inner_own = ends_terms(me, velocity, share_in, power, n, True)
    send = chip_ends(me, taps, velocity, chip_in, power, inner_other, inner_own, False)
    other = swap(send, "theta", 1)
    own = chip_ends(me, taps, velocity, chip_in, power, inner_own, send, True)
    n = side_terms(late_kernel, "late_terms", me, taps, velocity, chip_in, n, (own,))
    block = pair(me, power, own, other, points)
    entries = ()
    last = sectors.bit_length() - 2
    for bit in range(1, last + 1):
        if bit == last:
            n = planes_terms(velocity, planes_in, axial_in, block, n)
            s, nonlinear = sweep(velocity, n, power)
        block, entry = merge(me, power, block, swap(block, "theta", 1 << bit), entries, points, bit)
        entries = (entry,)
    mine, send = enter(me, power, block, entry, own, other, s, points)
    got = swap(send, "theta", 1)
    new_velocity = close(me, s, power, mine, (), True)
    new_velocity = close(me, s, power, got, (new_velocity,), False)
    return (new_velocity, nonlinear)


def solution(mesh):
    in_specs = (P(None, "theta", "gz", None), P(), P(), P())
    out_specs = (P(None, "theta", "gz", None), P(None, "theta", "gz", None))
    return jax.shard_map(local, mesh=mesh, in_specs=in_specs, out_specs=out_specs, check_vma=False)
```

```python
import functools

import jax
import jax.numpy as jnp
from jax import lax
from jax.experimental import pallas as pl
from jax.experimental.pallas import tpu as pltpu
from jax.sharding import PartitionSpec as P

AXIAL_WEIGHTS = (0.75, -0.15, 1.0 / 60.0)
AXIAL_REACH = len(AXIAL_WEIGHTS)
STEP_WEIGHT = 0.2
MIRROR_SIGNS = (-1.0, -1.0, 1.0)
LANES = 128
UNROLL = 16
INNER = 10 << 29
MIRROR = 1 << 26
SIDE = 1 << 26

VMEM = pl.BlockSpec(memory_space=pltpu.VMEM)
SMEM = pl.BlockSpec(memory_space=pltpu.SMEM)
ANY = pl.BlockSpec(memory_space=pl.ANY)
HBM = pl.BlockSpec(memory_space=pltpu.HBM)


def params(block_bytes, blocks):
    return pltpu.CompilerParams(vmem_limit_bytes=(2 << 20) + blocks * block_bytes)


def held(*shape):
    return pltpu.VMEM(shape, jnp.float32)


def each(count, body):
    if count <= UNROLL:
        for i in range(count):
            body(i)
    else:
        pl.loop(0, count)(body)


def swap(block, axis, bit):
    size = lax.axis_size(axis)
    return lax.ppermute(block, axis, [(i, i ^ bit) for i in range(size)])


def swap_across(block, axis):
    size = lax.axis_size(axis)
    route = []
    for odd in range(1, size, 2):
        route += [(odd, (odd + 1) % size), ((odd + 1) % size, odd)]
    return lax.ppermute(block, axis, route)


def split(x):
    high = x.astype(jnp.bfloat16)
    return high, (x - high.astype(jnp.float32)).astype(jnp.bfloat16)


def product(left, right):
    dot = functools.partial(jnp.dot, preferred_element_type=jnp.float32)
    return dot(left[0], right[0]) + (dot(left[0], right[1]) + dot(left[1], right[0]))


def pack_tiles(v_ref, y_ref, comps):
    points, planes = v_ref.shape[1:3]
    carriers = y_ref.shape[1]
    lo, hi = AXIAL_REACH, planes - AXIAL_REACH
    for i, c in enumerate(comps):

        def carry(t):
            y_ref[i, t] = v_ref[c, t]

        def ride(j):
            t = carriers + j
            y_ref[i, 3 * j, lo:hi] = v_ref[c, t, 0:2]
            y_ref[i, 3 * j + 1, lo : lo + 1] = v_ref[c, t, 2:3]
            y_ref[i, 3 * j + 1, lo + 1 : hi] = v_ref[c, t, hi : hi + 1]
            y_ref[i, 3 * j + 2, lo:hi] = v_ref[c, t, hi + 1 :]

        each(carriers, carry)
        each(points - carriers, ride)


def rebuild_tiles(y_ref, tile_ref):
    carriers = y_ref.shape[1]
    comps, riders, planes, radial = tile_ref.shape
    lo, hi = AXIAL_REACH, planes - AXIAL_REACH
    for c in range(comps):
        for j in range(riders):
            tile_ref[c, j, 0:2] = y_ref[c, 3 * j, lo:hi]
            tile_ref[c, j, 2:3] = y_ref[c, 3 * j + 1, lo : lo + 1]
            tile_ref[c, j, lo:hi] = jnp.zeros((hi - lo, radial), jnp.float32)
            tile_ref[c, j, hi : hi + 1] = y_ref[c, 3 * j + 1, lo + 1 : hi]
            tile_ref[c, j, hi + 1 :] = y_ref[c, 3 * j + 2, lo:hi]


def load_axial_kernel(hbm_ref, y_ref, e_ref, sems):
    count = sems.shape[0]
    part = e_ref.shape[1] // count
    loads = []
    for k in range(count):
        some = pl.ds(k * part, part)
        loads.append(pltpu.make_async_copy(hbm_ref.at[hbm_ref.shape[0] - 1, some], e_ref.at[0, some], sems.at[k]))
        loads[k].start()
    for load in loads:
        load.wait()
    pack_tiles(e_ref, y_ref, (0,))


def load_axial(v):
    comps, points, planes, radial = v.shape
    return pl.pallas_call(
        load_axial_kernel,
        name="load_axial",
        out_shape=held(1, points - points // 4, planes, radial),
        in_specs=[HBM],
        out_specs=VMEM,
        scratch_shapes=[
            pltpu.VMEM((1, points, planes, radial), jnp.float32),
            pltpu.SemaphoreType.DMA((4 if points % 4 == 0 else 1,)),
        ],
        compiler_params=params(v.size * 4, 2),
    )(v)


def pack_planes_kernel(v_ref, first_ref, y_ref):
    pack_tiles(v_ref, y_ref, range(y_ref.shape[0]))


def pack_planes(v, first):
    comps, points, planes, radial = v.shape
    return pl.pallas_call(
        pack_planes_kernel,
        name="pack_planes",
        out_shape=held(comps - 1, points - points // 4, planes, radial),
        in_specs=[VMEM, ANY],
        out_specs=VMEM,
        compiler_params=params(v.size * 4, 2),
    )(v, first)


def pack_side_kernel(me_ref, v_ref, first_ref, side_ref, *, after):
    points, reach = v_ref.shape[1], side_ref.shape[1]

    def put(start):
        for c in range(v_ref.shape[0]):
            for h in range(reach):
                side_ref[c, h] = v_ref[c, start + h]

    even = me_ref[0] % 2 == 0
    last = even if after else jnp.logical_not(even)
    pl.when(last)(lambda: put(points - reach))
    pl.when(jnp.logical_not(last))(lambda: put(0))


def pack_side(me, v, first, reach, after):
    comps, _, planes, radial = v.shape
    return pl.pallas_call(
        functools.partial(pack_side_kernel, after=after),
        name="pack_core" if after else "pack_chip",
        out_shape=held(comps, reach, planes, radial),
        in_specs=[SMEM, VMEM, ANY],
        out_specs=VMEM,
        compiler_params=params(v.size * 4, 3),
    )(me, v, first)


def pack_mirror_kernel(v_ref, first_ref, mirror_ref):
    points, tiles = v_ref.shape[1], mirror_ref.shape[1]
    width = LANES // (points // tiles)
    lane = lax.broadcasted_iota(jnp.int32, mirror_ref.shape[2:], 1)

    def put(p):
        for c in range(v_ref.shape[0]):
            tile = v_ref[c, p, :, :LANES]
            for q in range(1, points // tiles):
                part = pltpu.roll(v_ref[c, q * tiles + p, :, :LANES], q * width, 1)
                tile = jnp.where(lane < q * width, tile, part)
            mirror_ref[c, p] = tile

    each(tiles, put)


def pack_mirror(v, first, width):
    comps, points, planes, _ = v.shape
    return pl.pallas_call(
        pack_mirror_kernel,
        name="pack_mirror",
        out_shape=held(comps, points // (LANES // width), planes, LANES),
        in_specs=[VMEM, ANY],
        out_specs=VMEM,
        compiler_params=params(v.size * 4, 2),
    )(v, first)


def inverse_radius(radial, start=0):
    return 1.0 / ((lax.broadcasted_iota(jnp.int32, (1, radial), 1) + start).astype(jnp.float32) + 0.5)


def axial_weights(planes, inside):
    row = lax.broadcasted_iota(jnp.int32, (planes, LANES), 0)
    weights = []
    for m, w in enumerate(AXIAL_WEIGHTS, 1):
        for shift, own, sign in ((m, row < planes - m, 1.0), (planes - m, row >= m, -1.0)):
            keep = own if inside else jnp.logical_not(own)
            weights.append((shift, jnp.where(keep, sign * w, 0.0)))
    return weights


def axial_part(tile, weights):
    planes, width = tile.shape
    weights = [(shift, jnp.concatenate([weight] * (width // LANES), axis=1)) for shift, weight in weights]
    total = None
    for shift, weight in weights:
        term = weight * pltpu.roll(tile, planes - shift, 0)
        total = term if total is None else total + term
    return total


def mirror_kernel(v_ref, op_ref, mirror_ref, n_in_ref, n_ref, grad_ref):
    comps, points, planes, radial = v_ref.shape
    tiles = mirror_ref.shape[1]
    count = points // tiles
    width = LANES // count
    rows = tiles * planes
    right = split(jnp.concatenate([op_ref[radial:]] * count, axis=0))
    lane = lax.broadcasted_iota(jnp.int32, (rows, LANES), 1)
    for c in range(comps):
        high, low = split(MIRROR_SIGNS[c] * mirror_ref[c].reshape(rows, LANES))
        zero = jnp.zeros_like(high)
        parts = [
            [jnp.where((lane >= q * width) & (lane < (q + 1) * width), x, zero) for q in range(count)]
            for x in (high, low)
        ]
        left = [jnp.concatenate(x, axis=0) for x in parts]
        grad_ref[c * points * planes : (c + 1) * points * planes] = product(left, right)

    def finish(t):
        for c in range(comps):
            start = pl.multiple_of((c * points + t) * planes, planes)
            n_ref[c, t] = n_in_ref[c, t] + v_ref[0, t] * grad_ref[pl.ds(start, planes)]

    each(points, finish)


def mirror_terms(v, op, mirror, n):
    return pl.pallas_call(
        mirror_kernel,
        name="mirror_terms",
        out_shape=held(*v.shape),
        in_specs=[VMEM] * 4,
        out_specs=VMEM,
        scratch_shapes=[pltpu.VMEM((v.size // v.shape[3], v.shape[3]), jnp.float32)],
        input_output_aliases={3: 0},
        compiler_params=params(v.size * 4, 8),
        cost_estimate=pl.CostEstimate(flops=MIRROR, bytes_accessed=16 * v.size, transcendentals=0),
    )(v, op, mirror, n)


def inner_kernel(tap_ref, v_ref, op_ref, n_ref, grad_ref):
    comps, points, planes, radial = v_ref.shape
    reach = (tap_ref.shape[0] - 1) // 2
    rows = points * planes
    right = split(op_ref[:radial])
    for c in range(comps):
        grad_ref[c * rows : (c + 1) * rows] = product(split(v_ref[c].reshape(rows, radial)), right)
    weights = axial_weights(planes, True)

    @pl.loop(0, radial // LANES)
    def column(k):
        lanes = pl.ds(pl.multiple_of(k * LANES, LANES), LANES)
        inv_r = inverse_radius(LANES, k * LANES)
        for c in range(comps):
            for t in range(points):
                a, b, e = [v_ref[i, t, :, lanes] for i in range(3)]
                b_inv = b * inv_r
                around = None
                for m in range(max(-reach, -t), min(reach, points - 1 - t) + 1):
                    term = tap_ref[m + reach] * v_ref[c, t + m, :, lanes]
                    around = term if around is None else around + term
                start = c * rows + t * planes
                n = a * grad_ref[start : start + planes, lanes] + b_inv * around
                n = n + e * axial_part(v_ref[c, t, :, lanes], weights)
                if c == 0:
                    n = n - b_inv * b
                elif c == 1:
                    n = n + a * b_inv
                n_ref[c, t, :, lanes] = n


def inner_terms(taps, v, op):
    return pl.pallas_call(
        inner_kernel,
        name="inner_terms",
        out_shape=held(*v.shape),
        in_specs=[VMEM] * 3,
        out_specs=VMEM,
        scratch_shapes=[pltpu.VMEM((v.size // v.shape[3], v.shape[3]), jnp.float32)],
        compiler_params=params(v.size * 4, 7),
        cost_estimate=pl.CostEstimate(flops=INNER, bytes_accessed=16 * v.size, transcendentals=0),
    )(taps, v, op)


def add_side(tap_ref, v_ref, side_ref, n_in_ref, n_ref, before, columns):
    comps, points, _, radial = v_ref.shape
    reach = side_ref.shape[1]
    first = 0 if before else reach + 1

    start, count = columns

    @pl.loop(0, count)
    def column(i):
        k = start + i
        lanes = pl.ds(pl.multiple_of(k * LANES, LANES), LANES)
        inv_r = inverse_radius(LANES, k * LANES)
        weights = [tap_ref[first + i] for i in range(reach)]
        for c in range(comps):
            side = [side_ref[c, h, :, lanes] for h in range(reach)]
            for u in range(reach):
                t = u if before else points - reach + u
                taps = [(h, h - u) for h in range(u, reach)] if before else [(h, reach - 1 + h - u) for h in range(u + 1)]
                around = None
                for h, w in taps:
                    term = weights[w] * side[h]
                    around = term if around is None else around + term
                n_ref[c, t, :, lanes] = n_in_ref[c, t, :, lanes] + v_ref[1, t, :, lanes] * inv_r * around


def core_kernel(me_ref, tap_ref, v_ref, core_ref, n_in_ref, n_ref):
    even = me_ref[0] % 2 == 0
    columns = (0, v_ref.shape[3] // LANES)
    add = functools.partial(add_side, tap_ref, v_ref, core_ref, n_in_ref, n_ref, columns=columns)
    pl.when(even)(lambda: add(before=False))
    pl.when(jnp.logical_not(even))(lambda: add(before=True))


def late_kernel(me_ref, tap_ref, v_ref, chip_ref, n_in_ref, ready_ref, n_ref):
    even = me_ref[0] % 2 == 0
    columns = (0, v_ref.shape[3] // LANES)
    add = functools.partial(add_side, tap_ref, v_ref, chip_ref, n_in_ref, n_ref, columns=columns)
    pl.when(even)(lambda: add(before=True))
    pl.when(jnp.logical_not(even))(lambda: add(before=False))


def side_terms(kernel, name, me, taps, v, side, n, ready=()):
    return pl.pallas_call(
        kernel,
        name=name,
        out_shape=held(*v.shape),
        in_specs=[SMEM] + [VMEM] * 4 + [ANY] * len(ready),
        out_specs=VMEM,
        input_output_aliases={4: 0},
        compiler_params=params(v.size * 4, 5),
        cost_estimate=pl.CostEstimate(flops=SIDE, bytes_accessed=12 * v.size, transcendentals=0),
    )(me, taps, v, side, n, *ready)


def share_kernel(v_ref, e_ref, power_ref, ends_ref, tile_ref):
    comps, points, planes, radial = v_ref.shape
    carriers = e_ref.shape[1]
    weights = axial_weights(planes, False)
    rebuild_tiles(e_ref, tile_ref)
    decay = power_ref[1:2]
    ends_ref[...] = jnp.zeros_like(ends_ref)
    for t in range(points):
        e = STEP_WEIGHT * (e_ref[0, t] if t < carriers else tile_ref[0, t - carriers])
        for c in range(comps):
            right_side = e * axial_part(v_ref[c, t], weights)
            ends_ref[0, c] = decay * ends_ref[0, c] - right_side
            ends_ref[1, c] = ends_ref[1, c] - power_ref[t : t + 1] * right_side


def share_terms(v, e, power):
    comps, points, planes, radial = v.shape
    return pl.pallas_call(
        share_kernel,
        name="share_terms",
        out_shape=held(2, comps, planes, radial),
        in_specs=[VMEM] * 3,
        out_specs=VMEM,
        scratch_shapes=[pltpu.VMEM((1, points - e.shape[1], planes, radial), jnp.float32)],
        compiler_params=params(v.size * 4, 4),
        cost_estimate=pl.CostEstimate(flops=20 * v.size, bytes_accessed=8 * v.size, transcendentals=0),
    )(v, e, power)


def ends_kernel(me_ref, v_ref, share_ref, power_ref, n_ref, ends_ref, *, own):
    comps, points, _, radial = v_ref.shape
    lanes = half_lanes(me_ref, radial // 2, own)
    decay = power_ref[1:2, lanes]
    for c in range(comps):
        low = high = None
        for t in range(points):
            right_side = v_ref[c, t, :, lanes] - STEP_WEIGHT * n_ref[c, t, :, lanes]
            low = right_side if t == 0 else decay * low + right_side
            high = right_side if t == 0 else high + power_ref[t : t + 1, lanes] * right_side
        ends_ref[0, c] = low + share_ref[0, c, :, lanes]
        ends_ref[1, c] = high + share_ref[1, c, :, lanes]


def ends_terms(me, v, share, power, n, own):
    comps, _, planes, radial = v.shape
    return pl.pallas_call(
        functools.partial(ends_kernel, own=own),
        name="ends_own" if own else "ends_other",
        out_shape=held(2, comps, planes, radial // 2),
        in_specs=[SMEM] + [VMEM] * 4,
        out_specs=VMEM,
        compiler_params=params(v.size * 4, 4),
        cost_estimate=pl.CostEstimate(flops=20 * v.size, bytes_accessed=8 * v.size, transcendentals=0),
    )(me, v, share, power, n)


def chip_ends_kernel(me_ref, tap_ref, v_ref, chip_ref, power_ref, inner_ref, ready_ref, ends_ref, *, own):
    comps, points, _, radial = v_ref.shape
    reach = chip_ref.shape[1]
    core = me_ref[0] % 2
    count = radial // (2 * LANES)
    start = (core if own else 1 - core) * count

    def add(before):
        first = 0 if before else reach + 1

        @pl.loop(0, count)
        def column(i):
            k = start + i
            lanes = pl.ds(pl.multiple_of(k * LANES, LANES), LANES)
            here = pl.ds(pl.multiple_of(i * LANES, LANES), LANES)
            inv_r = STEP_WEIGHT * inverse_radius(LANES, k * LANES)
            weights = [tap_ref[first + j] for j in range(reach)]
            for c in range(comps):
                side = [chip_ref[c, h, :, lanes] for h in range(reach)]
                low, high = inner_ref[0, c, :, here], inner_ref[1, c, :, here]
                for u in range(reach):
                    t = u if before else points - reach + u
                    taps = [(h, h - u) for h in range(u, reach)] if before else [(h, reach - 1 + h - u) for h in range(u + 1)]
                    around = None
                    for h, w in taps:
                        term = weights[w] * side[h]
                        around = term if around is None else around + term
                    x = v_ref[1, t, :, lanes] * inv_r * around
                    low = low - power_ref[points - 1 - t : points - t, lanes] * x
                    high = high - power_ref[t : t + 1, lanes] * x
                ends_ref[0, c, :, here] = low
                ends_ref[1, c, :, here] = high

    pl.when(core == 0)(lambda: add(True))
    pl.when(core == 1)(lambda: add(False))


def chip_ends(me, taps, v, chip, power, inner, ready, own):
    return pl.pallas_call(
        functools.partial(chip_ends_kernel, own=own),
        name="chip_own" if own else "chip_other",
        out_shape=held(*inner.shape),
        in_specs=[SMEM] + [VMEM] * 5 + [ANY],
        out_specs=VMEM,
        compiler_params=params(v.size * 4, 4),
        cost_estimate=pl.CostEstimate(flops=SIDE, bytes_accessed=8 * v.size, transcendentals=0),
    )(me, taps, v, chip, power, inner, ready)


def planes_kernel(v_ref, y_ref, e_ref, ready_ref, n_in_ref, n_ref, y_tile_ref, e_tile_ref):
    comps, points, planes, _ = v_ref.shape
    carriers = y_ref.shape[1]
    weights = axial_weights(planes, False)
    rebuild_tiles(y_ref, y_tile_ref)
    rebuild_tiles(e_ref, e_tile_ref)
    for t in range(points):
        for c in range(comps):
            ref, tile_ref, i = (y_ref, y_tile_ref, c) if c < comps - 1 else (e_ref, e_tile_ref, 0)
            tile = ref[i, t] if t < carriers else tile_ref[i, t - carriers]
            n_ref[c, t] = n_in_ref[c, t] + v_ref[2, t] * axial_part(tile, weights)


def planes_terms(v, y, e, ready, n):
    comps, points, planes, radial = v.shape
    riders = points - y.shape[1]
    return pl.pallas_call(
        planes_kernel,
        name="planes_terms",
        out_shape=held(*v.shape),
        in_specs=[VMEM] * 3 + [ANY, VMEM],
        out_specs=VMEM,
        scratch_shapes=[pltpu.VMEM((k, riders, planes, radial), jnp.float32) for k in (comps - 1, 1)],
        input_output_aliases={4: 0},
        compiler_params=params(v.size * 4, 6),
        cost_estimate=pl.CostEstimate(flops=20 * v.size, bytes_accessed=16 * v.size, transcendentals=0),
    )(v, y, e, ready, n)


def table_kernel(me_ref, factor_ref, stencil_ref, row_ref, tap_ref, *, points, sectors):
    radial = row_ref.shape[1]
    one = jnp.ones((1, radial), jnp.float32)
    half = (0.5 * lax.rsqrt(factor_ref[0] * one)) / inverse_radius(radial)
    root = jnp.sqrt(1.0 + half * half)
    loss = 2.0 * half * (root - half)
    rows = [one]
    for _ in range(points):
        rows.append(rows[-1] * (1.0 - loss))
    total = loss
    left, result = points * sectors, None
    while left:
        if left & 1:
            result = total if result is None else result + total - result * total
        total = total * (2.0 - total)
        left >>= 1
    across = rows[points] * rows[points]
    rows += [half / root, 1.0 / result]
    before = after = one
    for bit in range(1, sectors.bit_length() - 1):
        upper = (me_ref[0] >> bit) % 2 == 1
        rows += [across, before, after]
        before, after = jnp.where(upper, before * across, before), jnp.where(upper, after, after * across)
        across = across * across
    for k, row in enumerate(rows + [before, after]):
        row_ref[k : k + 1] = row
    for k in range(tap_ref.shape[0]):
        tap_ref[k] = jnp.full(tap_ref.shape[1:], stencil_ref[k], jnp.float32)


def table(me, viscous_factor, stencil, points, sectors, planes, radial):
    count = points + 5 + 3 * (sectors.bit_length() - 2)
    return pl.pallas_call(
        functools.partial(table_kernel, points=points, sectors=sectors),
        name="table",
        out_shape=(held(count, radial), held(stencil.shape[0], planes, LANES)),
        in_specs=[SMEM, SMEM, SMEM],
        out_specs=(VMEM, VMEM),
        compiler_params=params(1 << 20, 1),
        cost_estimate=pl.CostEstimate(flops=1000 * radial, bytes_accessed=400 * radial, transcendentals=0),
    )(me, viscous_factor, stencil)


def sweep_kernel(v_ref, n_ref, power_ref, s_ref, nonlinear_ref, sem):
    leave = pltpu.make_async_copy(n_ref, nonlinear_ref, sem)
    leave.start()
    comps, points, planes, radial = v_ref.shape
    decay = power_ref[1:2]
    height = power_ref[points + 1 : points + 2]
    for c in range(comps):
        s_ref[c, 0] = height * (v_ref[c, 0] - STEP_WEIGHT * n_ref[c, 0])

        def forward(i):
            t = i + 1
            s_ref[c, t] = decay * s_ref[c, t - 1] + height * (v_ref[c, t] - STEP_WEIGHT * n_ref[c, t])

        each(points - 1, forward)

    def backward(i, carry):
        t = points - 1 - i
        after = []
        for c in range(comps):
            s_ref[c, t] = s_ref[c, t] + carry[c]
            after.append(decay * (carry[c] + height * (v_ref[c, t] - STEP_WEIGHT * n_ref[c, t])))
        return tuple(after)

    start = (jnp.zeros((planes, radial), jnp.float32),) * comps
    lax.fori_loop(0, points, backward, start, unroll=points <= UNROLL)
    leave.wait()


def sweep(v, n, power):
    return pl.pallas_call(
        sweep_kernel,
        name="sweep",
        out_shape=(held(*v.shape), jax.ShapeDtypeStruct(v.shape, v.dtype)),
        in_specs=[VMEM] * 3,
        out_specs=(VMEM, ANY),
        scratch_shapes=[pltpu.SemaphoreType.DMA],
        compiler_params=params(v.size * 4, 4),
        cost_estimate=pl.CostEstimate(flops=10 * v.size, bytes_accessed=12 * v.size, transcendentals=0),
    )(v, n, power)


def half_lanes(me_ref, half, own=True):
    core = me_ref[0] % 2
    return pl.ds(pl.multiple_of((core if own else 1 - core) * half, half), half)


def pair_kernel(me_ref, power_ref, own_ref, other_ref, block_ref, *, points):
    half = own_ref.shape[3]
    hop = power_ref[points : points + 1, half_lanes(me_ref, half)]
    odd = me_ref[0] % 2 == 1
    for c in range(own_ref.shape[1]):
        for side in range(2):
            own, other = own_ref[side, c], other_ref[side, c]
            far, near = (own, other) if side == 0 else (other, own)
            block_ref[side, c] = jnp.where(odd, hop * near + far, hop * far + near)


def pair(me, power, own, other, points):
    return pl.pallas_call(
        functools.partial(pair_kernel, points=points),
        name="pair",
        out_shape=held(*own.shape),
        in_specs=[SMEM, VMEM, VMEM, VMEM],
        out_specs=VMEM,
        compiler_params=params(own.size * 4, 8),
    )(me, power, own, other)


def merge_kernel(me_ref, power_ref, block_ref, other_ref, *refs, points, bit):
    *entry_refs, block_out_ref, entry_out_ref = refs
    comps, half = block_ref.shape[1], block_ref.shape[3]
    lanes = half_lanes(me_ref, half)
    first = points + 3 * bit
    across, before, after = [power_ref[first + k : first + k + 1, lanes] for k in range(3)]
    upper = (me_ref[0] >> bit) % 2 == 1
    before = jnp.where(upper, before, 0.0)
    after = jnp.where(upper, 0.0, after)
    for c in range(comps):
        low, high = block_ref[0, c], block_ref[1, c]
        other_low, other_high = other_ref[0, c], other_ref[1, c]
        block_out_ref[0, c] = jnp.where(upper, across * other_low + low, across * low + other_low)
        block_out_ref[1, c] = jnp.where(upper, other_high + across * high, high + across * other_high)
        for side, enters in enumerate((before * other_low, after * other_high)):
            entry_out_ref[side, c] = entry_refs[0][side, c] + enters if entry_refs else enters


def merge(me, power, block, other, entries, points, bit):
    return pl.pallas_call(
        functools.partial(merge_kernel, points=points, bit=bit),
        name="merge",
        out_shape=(held(*block.shape), held(*block.shape)),
        in_specs=[SMEM] + [VMEM] * (3 + len(entries)),
        out_specs=(VMEM, VMEM),
        compiler_params=params(block.size * 4, 8),
    )(me, power, block, other, *entries)


def enter_kernel(me_ref, power_ref, block_ref, entry_ref, own_ref, other_ref, ready_ref, mine_ref, send_ref, *, points):
    comps, half = block_ref.shape[1], block_ref.shape[3]
    lanes = half_lanes(me_ref, half)
    row = lambda k: power_ref[k : k + 1, lanes]
    hop, height, wrap = row(points), row(points + 1), row(points + 2)
    last = power_ref.shape[0]
    before, after = row(last - 2) * wrap, row(last - 1) * wrap
    odd = me_ref[0] % 2 == 1
    for c in range(comps):
        low = height * (entry_ref[0, c] + before * block_ref[0, c])
        high = height * (entry_ref[1, c] + after * block_ref[1, c])
        even_low = height * jnp.where(odd, other_ref[0, c], own_ref[0, c])
        odd_high = height * jnp.where(odd, own_ref[1, c], other_ref[1, c])
        even_in = (low, odd_high + hop * high)
        odd_in = (even_low + hop * low, high)
        for side in range(2):
            mine_ref[side, c] = jnp.where(odd, odd_in[side], even_in[side])
            send_ref[side, c] = jnp.where(odd, even_in[side], odd_in[side])


def enter(me, power, block, entry, own, other, ready, points):
    return pl.pallas_call(
        functools.partial(enter_kernel, points=points),
        name="enter",
        out_shape=(held(*block.shape), held(*block.shape)),
        in_specs=[SMEM] + [VMEM] * 5 + [ANY],
        out_specs=(VMEM, VMEM),
        compiler_params=params(block.size * 4, 12),
    )(me, power, block, entry, own, other, ready)


def close_kernel(me_ref, s_ref, power_ref, entry_ref, *refs, own):
    out_ref, x_ref, sems = refs[-3:]
    comps, points, _, _ = s_ref.shape
    lanes = half_lanes(me_ref, entry_ref.shape[3], own)
    leaves = []
    for c in range(comps):
        before, after = entry_ref[0, c], entry_ref[1, c]

        def point(t):
            decayed = power_ref[pl.ds(t + 1, 1), lanes] * before + power_ref[pl.ds(points - t, 1), lanes] * after
            x_ref[c, t] = s_ref[c, t, :, lanes] + decayed

        each(points, point)
        leaves.append(pltpu.make_async_copy(x_ref.at[c], out_ref.at[c, :, :, lanes], sems.at[c]))
        leaves[c].start()
    for leave in leaves:
        leave.wait()


def close(me, s, power, entry, out, own):
    comps, points, planes, radial = s.shape
    return pl.pallas_call(
        functools.partial(close_kernel, own=own),
        name="close_own" if own else "close_other",
        out_shape=jax.ShapeDtypeStruct(s.shape, s.dtype),
        in_specs=[SMEM] + [VMEM] * 3 + [ANY] * len(out),
        out_specs=ANY,
        scratch_shapes=[
            pltpu.VMEM((comps, points, planes, radial // 2), jnp.float32),
            pltpu.SemaphoreType.DMA((comps,)),
        ],
        input_output_aliases={4: 0} if out else {},
        compiler_params=params(s.size * 4, 5),
        cost_estimate=pl.CostEstimate(flops=4 * s.size, bytes_accessed=8 * s.size, transcendentals=0),
    )(me, s, power, entry, *out)


def local(velocity, radial_op, azimuth_stencil, viscous_factor):
    sectors = lax.axis_size("theta")
    comps, points, planes, radial = velocity.shape
    reach = (azimuth_stencil.shape[0] - 1) // 2
    width = radial_op.shape[1] - radial
    me = lax.axis_index("theta").astype(jnp.int32).reshape(1)
    op = radial_op.T

    axial_out = load_axial(pltpu.with_memory_space_constraint(velocity, pltpu.HBM))
    axial_in = swap(axial_out, "gz", 1)
    chip_out = pack_side(me, velocity, axial_out, reach, False)
    chip_in = swap_across(chip_out, "theta")
    mirror_out = pack_mirror(velocity, chip_out, width)
    mirror_in = swap(mirror_out, "theta", sectors // 2)
    core_out = pack_side(me, velocity, axial_in, reach, True)
    core_in = swap(core_out, "theta", 1)
    power, taps = table(me, viscous_factor, azimuth_stencil, points, sectors, planes, radial)
    n = inner_terms(taps, velocity, op)
    share_out = share_terms(velocity, axial_in, power)
    share_in = swap(share_out, "gz", 1)
    planes_in = swap(pack_planes(velocity, share_out), "gz", 1)
    n = side_terms(core_kernel, "core_terms", me, taps, velocity, core_in, n)
    n = mirror_terms(velocity, op, mirror_in, n)
    inner_other = ends_terms(me, velocity, share_in, power, n, False)
    inner_own = ends_terms(me, velocity, share_in, power, n, True)
    send = chip_ends(me, taps, velocity, chip_in, power, inner_other, inner_own, False)
    other = swap(send, "theta", 1)
    own = chip_ends(me, taps, velocity, chip_in, power, inner_own, send, True)
    n = side_terms(late_kernel, "late_terms", me, taps, velocity, chip_in, n, (own,))
    block = pair(me, power, own, other, points)
    entries = ()
    last = sectors.bit_length() - 2
    for bit in range(1, last + 1):
        if bit == last:
            n = planes_terms(velocity, planes_in, axial_in, block, n)
            s, nonlinear = sweep(velocity, n, power)
        block, entry = merge(me, power, block, swap(block, "theta", 1 << bit), entries, points, bit)
        entries = (entry,)
    mine, send = enter(me, power, block, entry, own, other, s, points)
    got = swap(send, "theta", 1)
    new_velocity = close(me, s, power, mine, (), True)
    new_velocity = close(me, s, power, got, (new_velocity,), False)
    return (new_velocity, nonlinear)


def solution(mesh):
    in_specs = (P(None, "theta", "gz", None), P(), P(), P())
    out_specs = (P(None, "theta", "gz", None), P(None, "theta", "gz", None))
    return jax.shard_map(local, mesh=mesh, in_specs=in_specs, out_specs=out_specs, check_vma=False)
```
